32 devices in a mesh: tower: 2 (over core), dp: 4 (over z), mp: 4 (over y, x).
Axes of the slice: x: 2, y: 2, z: 4, core: 2. Of those that a mesh axis runs over, the one named last changes fastest.
Arguments:
- picture_residual_entry: bfloat16 [64, 50, 768], P(('tower', 'dp')), may hold values from -6 to 6
- sentence_residual_entry: bfloat16 [64, 77, 512], P(('tower', 'dp')), may hold values from -6 to 6
- sentence_lengths_held: int32 [64], P(('tower', 'dp')), may hold values from 2 to 77
- couple_allowed_flags: int32 [64], P(('tower', 'dp')), may hold values from 0 to 1, as said below
- picture_single_matrices: float32 [4, 1769472], P('mp', ('tower', 'dp'))
- picture_mean_state: float32 [4, 1769472], P('mp', ('tower', 'dp'))
- picture_square_state: float32 [4, 1769472], P('mp', ('tower', 'dp')), as said below
- sentence_single_matrices: float32 [4, 786432], P('mp', ('tower', 'dp'))
- sentence_mean_state: float32 [4, 786432], P('mp', ('tower', 'dp'))
- sentence_square_state: float32 [4, 786432], P('mp', ('tower', 'dp')), as said below
- array_single_params: float32 [663040], P(('tower', 'dp'))
- array_mean_state: float32 [663040], P(('tower', 'dp'))
- array_square_state: float32 [663040], P(('tower', 'dp')), as said below
- logit_log_trio: float32 [3], replicated, as said below
Outputs:
- contrast_objective: float32 [], replicated
- global_slope_size: float32 [], replicated
- picture_entry_slope: float32 [64, 50, 768], P(('tower', 'dp'))
- sentence_entry_slope: float32 [64, 77, 512], P(('tower', 'dp'))
- picture_matrices_fresh: float32 [4, 1769472], P('mp', ('tower', 'dp'))
- image_copy: bfloat16 [4, 1769472], P('mp', ('tower', 'dp'))
- picture_mean_fresh: float32 [4, 1769472], P('mp', ('tower', 'dp'))
- picture_square_fresh: float32 [4, 1769472], P('mp', ('tower', 'dp'))
- sentence_matrices_fresh: float32 [4, 786432], P('mp', ('tower', 'dp'))
- text_copy: bfloat16 [4, 786432], P('mp', ('tower', 'dp'))
- sentence_mean_fresh: float32 [4, 786432], P('mp', ('tower', 'dp'))
- sentence_square_fresh: float32 [4, 786432], P('mp', ('tower', 'dp'))
- array_params_fresh: float32 [663040], P(('tower', 'dp'))
- vector_copy: bfloat16 [663040], P(('tower', 'dp'))
- array_mean_fresh: float32 [663040], P(('tower', 'dp'))
- array_square_fresh: float32 [663040], P(('tower', 'dp'))
- temperature_new: float32 [], replicated
The draws below stay inside these ranges and needn't reach their ends.
Inputs may be any that keep to these rules, and one draw needn't show every extreme that they name: `couple_allowed_flags`: 1 marks a pair whose image and caption enter the loss, 0 one that is left out. `picture_square_state`: every entry positive. `sentence_square_state`: every entry positive. `array_square_state`: every entry positive. `logit_log_trio`: the last entry is positive.
All inputs are finite; a program needn't handle non-finite values.
Results may differ from the reference program's by a relative error of at most 0.018.
The reference program's roundings to bfloat16 on the way count: a program that leaves them out, or rounds other values in their place, can miss the bound.
Values may be sent and summed in bfloat16 or wider, within the bound.
No kernel may reach another device: no remote copies, remote signals or barrier semaphores. Data moves between devices by JAX's collectives and lax.ppermute only.
A program may use at most 832 MiB of HBM per device.

```python
import math
import jax
import jax.numpy as jnp
from jax import lax

D_IMG = 768
FF_IMG = 3072
IMG_LEN = 50
D_TXT = 512
FF_TXT = 2048
TXT_LEN = 77
HEAD = 64
EMBED = 512
PAIRS_DEV = 8
STEP = 10
PAIRS = 64
MAT_IMG = 1769472
MAT_TXT = 786432
VECS = 663040
N_MP = 4


CLIP_LEVEL = 0.005


def spread_level():
    return CLIP_LEVEL / math.sqrt(N_MP * (MAT_IMG + MAT_TXT) + VECS + 1)


def matrix_scales(model_width, hidden, total):
    width_piece = model_width // N_MP
    hidden_piece = hidden // N_MP
    first_end = model_width * 3 * width_piece
    second_end = first_end + width_piece * model_width
    third_end = second_end + model_width * hidden_piece
    column = jnp.arange(total, dtype=jnp.int32)
    inner = model_width ** (-0.5)
    return jnp.where(column < first_end, inner, jnp.where(column < second_end, 3.0 * inner, jnp.where(column < third_end, inner, hidden ** (-0.5))))


def vector_levels():
    index = jnp.arange(VECS, dtype=jnp.int32)
    return jnp.where(index < 6 * (D_IMG + D_TXT), 4.0, 1.0) * spread_level()


def draw_picture_single_matrices(key, part):
    key = jax.random.fold_in(key, 1)
    noise = jax.random.normal(key, (N_MP, MAT_IMG), jnp.float32)
    return noise * matrix_scales(D_IMG, FF_IMG, MAT_IMG)[None, :]


def draw_sentence_single_matrices(key, part):
    key = jax.random.fold_in(key, 2)
    noise = jax.random.normal(key, (N_MP, MAT_TXT), jnp.float32)
    return noise * matrix_scales(D_TXT, FF_TXT, MAT_TXT)[None, :]


def draw_picture_mean_state(key, part):
    key = jax.random.fold_in(key, 3)
    noise = jax.random.normal(key, (N_MP, MAT_IMG), jnp.float32)
    return noise * spread_level()


def draw_sentence_mean_state(key, part):
    key = jax.random.fold_in(key, 4)
    noise = jax.random.normal(key, (N_MP, MAT_TXT), jnp.float32)
    return noise * spread_level()


def draw_picture_square_state(key, part):
    key = jax.random.fold_in(key, 5)
    clipping_factor = jnp.exp(jax.random.uniform(key, (N_MP, MAT_IMG), jnp.float32, 0.0, math.log(4.0)))
    return clipping_factor * spread_level() ** 2


def draw_sentence_square_state(key, part):
    key = jax.random.fold_in(key, 6)
    clipping_factor = jnp.exp(jax.random.uniform(key, (N_MP, MAT_TXT), jnp.float32, 0.0, math.log(4.0)))
    return clipping_factor * spread_level() ** 2


def draw_array_single_params(key, part):
    key = jax.random.fold_in(key, 7)
    noise = jax.random.normal(key, (VECS,), jnp.float32)
    index = jnp.arange(VECS, dtype=jnp.int32)
    in_image = index < 6 * D_IMG
    local_index = jnp.where(in_image, index, index - 6 * D_IMG)
    row_width = jnp.where(in_image, D_IMG, D_TXT)
    row_index = local_index // row_width
    column = local_index % row_width
    ramp = 0.5 + column.astype(jnp.float32) / row_width.astype(jnp.float32)
    norm_part = jnp.where(row_index % 2 == 0, ramp * (1.0 + 0.15 * noise), 0.4 * noise)
    norm_end = 6 * (D_IMG + D_TXT)
    proj_part = noise * jnp.where(index < norm_end + D_IMG * EMBED, D_IMG ** (-0.5), D_TXT ** (-0.5))
    return jnp.where(index < norm_end, norm_part, proj_part)


def draw_array_mean_state(key, part):
    key = jax.random.fold_in(key, 8)
    noise = jax.random.normal(key, (VECS,), jnp.float32)
    return noise * vector_levels()


def draw_array_square_state(key, part):
    key = jax.random.fold_in(key, 9)
    clipping_factor = jnp.exp(jax.random.uniform(key, (VECS,), jnp.float32, 0.0, math.log(4.0)))
    levels = vector_levels()
    return clipping_factor * levels * levels


def draw_logit_log_trio(key, part):
    key = jax.random.fold_in(key, 10)
    value_key, first_key, second_key = jax.random.split(key, 3)
    level = 4.0 * spread_level()
    value = jax.random.uniform(value_key, (), jnp.float32, 3.5, 4.0)
    first = level * jax.random.normal(first_key, (), jnp.float32)
    clipping_factor = jnp.exp(jax.random.uniform(second_key, (), jnp.float32, 0.0, math.log(4.0)))
    return jnp.stack([value, first, clipping_factor * level * level])


def draw_couple_allowed_flags(key, part):
    key = jax.random.fold_in(key, 11)
    group_total = PAIRS // PAIRS_DEV
    group_index = jnp.arange(PAIRS, dtype=jnp.int32) // PAIRS_DEV
    limit = 250 + 700 * group_index // max(group_total - 1, 1)
    return (jax.random.randint(key, (PAIRS,), 0, 1000) < limit).astype(jnp.int32)


def touch_ends(entries, own_key, smallest, top_value):
    longest = entries.shape.index(max(entries.shape))
    spots = []
    for shift in (0, 1):
        where = [jax.random.randint(jax.random.fold_in(own_key, axis), (), 0, length) for axis, length in enumerate(entries.shape)]
        where[longest] = (where[longest] + shift) % entries.shape[longest]
        spots.append(tuple(where))
    return entries.at[spots[0]].set(smallest).at[spots[1]].set(top_value)


def block_scale(stream_key, dims, cuts, least, largest):
    level = 1.0
    for axis_at, shards_of in cuts:
        steps = jax.random.uniform(jax.random.fold_in(jax.random.fold_in(stream_key, 6), axis_at), (shards_of,), jnp.float32, least / len(cuts), largest / len(cuts))
        level = level * jnp.repeat(jnp.exp(steps), dims[axis_at] // shards_of).reshape((-1,) + (1,) * (len(dims) - 1 - axis_at))
    return level


def gaussian(stream_key, extent, deviation, most, cuts=(), held_as=jnp.bfloat16):
    drawn = jax.random.normal(stream_key, extent, jnp.float32) * deviation
    if len(cuts) > 0:
        drawn = block_scale(stream_key, extent, cuts, -0.22, 0.18) * drawn
    return jnp.clip(drawn, min=-most, max=most).astype(held_as)


def setup_inputs(seed: int = 0) -> dict:
    key_of = jax.random.split(jax.random.key(seed), 15)
    return {
        "picture_residual_entry": gaussian(key_of[0], (PAIRS, IMG_LEN, D_IMG), 1.0, 6.0, ((0, 8),)),
        "sentence_residual_entry": gaussian(key_of[1], (PAIRS, TXT_LEN, D_TXT), 1.0, 6.0, ((0, 8),)),
        "sentence_lengths_held": touch_ends(jax.random.randint(key_of[2], (PAIRS,), 2, TXT_LEN + 1), jax.random.fold_in(key_of[2], 1), 2, TXT_LEN).astype(jnp.int32),
        "couple_allowed_flags": draw_couple_allowed_flags(jax.random.fold_in(key_of[14], 71), 0),
        "picture_single_matrices": draw_picture_single_matrices(jax.random.fold_in(key_of[14], 71), 0),
        "picture_mean_state": draw_picture_mean_state(jax.random.fold_in(key_of[14], 71), 0),
        "picture_square_state": draw_picture_square_state(jax.random.fold_in(key_of[14], 71), 0),
        "sentence_single_matrices": draw_sentence_single_matrices(jax.random.fold_in(key_of[14], 71), 0),
        "sentence_mean_state": draw_sentence_mean_state(jax.random.fold_in(key_of[14], 71), 0),
        "sentence_square_state": draw_sentence_square_state(jax.random.fold_in(key_of[14], 71), 0),
        "array_single_params": draw_array_single_params(jax.random.fold_in(key_of[14], 71), 0),
        "array_mean_state": draw_array_mean_state(jax.random.fold_in(key_of[14], 71), 0),
        "array_square_state": draw_array_square_state(jax.random.fold_in(key_of[14], 71), 0),
        "logit_log_trio": draw_logit_log_trio(jax.random.fold_in(key_of[14], 71), 0),
    }


NORM_EPS = 1e-05
UNIT_EPS = 1e-06
BETA_ONE = 0.5
BETA_TWO = 0.5
ADAM_EPS = 1e-08
WEIGHT_DECAY = 0.1
RATE_MATRIX = 0.04
RATE_VECTOR = 0.3
LOGIT_SPEED = 0.5
CLIP_LEVEL = 0.005
MASK_LOW = -1e+30
GELU_SLOPE = 1.702

@jax.custom_vjp
def low(v):
    return lax.optimization_barrier(v.astype(jnp.bfloat16)).astype(jnp.float32)

@jax.custom_vjp
def low_back(v):
    return v

def low_keep(v):
    return (low(v), None)

def low_pass(kept, grad):
    return (grad,)

def back_keep(v):
    return (v, None)

def back_low(kept, grad):
    return (low(grad),)
low.defvjp(low_keep, low_pass)
low_back.defvjp(back_keep, back_low)

def matmul_high(left, right):
    return jnp.dot(left, right, precision=lax.Precision.HIGHEST, preferred_element_type=jnp.float32)

def layer_norm(values, norm_gain, norm_shift):
    centered = values - lax.optimization_barrier(jnp.mean(values, axis=-1, keepdims=True))
    inverse = lax.rsqrt(lax.optimization_barrier(jnp.mean(centered * centered, axis=-1, keepdims=True)) + NORM_EPS)
    return centered * inverse * norm_gain + norm_shift

def quick_gelu(values):
    return values * jax.nn.sigmoid(GELU_SLOPE * values)

def split_mats(master, model_width, hidden):
    width_piece = model_width // N_MP
    hidden_piece = hidden // N_MP
    first_end = model_width * 3 * width_piece
    second_end = first_end + width_piece * model_width
    third_end = second_end + model_width * hidden_piece
    qkv_weight = master[:, :first_end].reshape(N_MP, model_width, 3, width_piece).transpose(1, 2, 0, 3).reshape(model_width, 3 * model_width)
    out_weight = master[:, first_end:second_end].reshape(model_width, model_width)
    up_weight = master[:, second_end:third_end].reshape(N_MP, model_width, hidden_piece).transpose(1, 0, 2).reshape(model_width, hidden)
    down_weight = master[:, third_end:].reshape(hidden, model_width)
    return (qkv_weight, out_weight, up_weight, down_weight)

def residual_layer(tokens, weights, norms, causal):
    qkv_weight, out_weight, up_weight, down_weight = weights
    seq_count, seq_length, model_width = tokens.shape
    head_count = model_width // HEAD
    token_rows = tokens.reshape(seq_count * seq_length, model_width)
    first_normed = low(layer_norm(token_rows, norms[0], norms[1]))
    packed = low(low_back(matmul_high(first_normed, qkv_weight)))
    packed = packed.reshape(seq_count, seq_length, 3, head_count, HEAD)
    scores = low_back(jnp.einsum('nqhd,nkhd->nhqk', packed[:, :, 0], packed[:, :, 1], precision=lax.Precision.HIGHEST) * HEAD ** (-0.5))
    if causal:
        position = jnp.arange(seq_length, dtype=jnp.int32)
        scores = jnp.where(position[None, :] <= position[:, None], scores, MASK_LOW)
    probs = low(jax.nn.softmax(scores, axis=-1))
    attended = jnp.einsum('nhqk,nkhd->nqhd', probs, packed[:, :, 2], precision=lax.Precision.HIGHEST)
    attended = low(low_back(attended.reshape(seq_count * seq_length, model_width)))
    middle = token_rows + low_back(matmul_high(attended, out_weight))
    second_normed = low(layer_norm(middle, norms[2], norms[3]))
    pre_act = low_back(matmul_high(second_normed, up_weight))
    activated = low(quick_gelu(pre_act))
    return middle + low_back(matmul_high(activated, down_weight))

def embed_head(picked, norm_gain, norm_shift, projection):
    normed = low(layer_norm(picked, norm_gain, norm_shift))
    raw_embed = low_back(matmul_high(normed, projection))
    return raw_embed * lax.rsqrt(lax.optimization_barrier(jnp.sum(raw_embed * raw_embed, axis=-1, keepdims=True)) + UNIT_EPS)

def contrast_loss(picture_feature_lines, sentence_feature_lines, couple_allowed_flags, log_scale):
    image_low = low(picture_feature_lines)
    text_low = low(sentence_feature_lines)
    logits = jnp.exp(log_scale) * matmul_high(image_low, text_low.T)
    kept = couple_allowed_flags > 0
    row_lse = jax.nn.logsumexp(jnp.where(kept[None, :], logits, MASK_LOW), axis=1)
    col_lse = jax.nn.logsumexp(jnp.where(kept[:, None], logits, MASK_LOW), axis=0)
    count_valid = jnp.sum(kept.astype(jnp.float32))
    return jnp.sum(jnp.where(kept, row_lse + col_lse - 2.0 * jnp.diagonal(logits), 0.0)) / (2.0 * count_valid)

def optimizer_advance(master, first, second, grad, rate, decay):
    first_new = BETA_ONE * first + (1.0 - BETA_ONE) * grad
    second_new = BETA_TWO * second + (1.0 - BETA_TWO) * grad * grad
    update = first_new / (1.0 - BETA_ONE ** STEP) / (jnp.sqrt(second_new / (1.0 - BETA_TWO ** STEP)) + ADAM_EPS)
    return (master - rate * (update + decay * master), first_new, second_new)

def reference(picture_residual_entry, sentence_residual_entry, sentence_lengths_held, couple_allowed_flags, picture_single_matrices, picture_mean_state, picture_square_state, sentence_single_matrices, sentence_mean_state, sentence_square_state, array_single_params, array_mean_state, array_square_state, logit_log_trio):
    group_count = PAIRS // PAIRS_DEV
    norm_end = 6 * (D_IMG + D_TXT)
    image_end = norm_end + D_IMG * EMBED

    def joint_objective(image_in_weights, text_in_weights, vector_in, log_scale, image_in, text_in):
        image_weights = [low(matrix) for matrix in split_mats(image_in_weights, D_IMG, FF_IMG)]
        text_weights = [low(matrix) for matrix in split_mats(text_in_weights, D_TXT, FF_TXT)]
        vector_low = low(vector_in)
        image_norms = vector_low[:6 * D_IMG].reshape(6, D_IMG)
        text_norms = vector_low[6 * D_IMG:norm_end].reshape(6, D_TXT)
        image_proj = vector_low[norm_end:image_end].reshape(D_IMG, EMBED)
        text_proj = vector_low[image_end:].reshape(D_TXT, EMBED)

        def image_group(group_tokens):
            outputs = residual_layer(group_tokens, image_weights, image_norms, False).reshape(PAIRS_DEV, IMG_LEN, D_IMG)
            return embed_head(lax.optimization_barrier(jnp.mean(outputs, axis=1)), image_norms[4], image_norms[5], image_proj)

        def text_group(group_args):
            group_tokens, group_lengths = group_args
            outputs = residual_layer(group_tokens, text_weights, text_norms, True).reshape(PAIRS_DEV, TXT_LEN, D_TXT)
            inside = (jnp.arange(TXT_LEN, dtype=jnp.int32)[None, :] < group_lengths[:, None]).astype(jnp.float32)
            picker = inside / group_lengths[:, None].astype(jnp.float32)
            picked = jnp.einsum('nl,nld->nd', picker, outputs, precision=lax.Precision.HIGHEST)
            return embed_head(picked, text_norms[4], text_norms[5], text_proj)
        picture_feature_lines = lax.map(jax.checkpoint(image_group), image_in.reshape(group_count, PAIRS_DEV, IMG_LEN, D_IMG)).reshape(PAIRS, EMBED)
        sentence_feature_lines = lax.map(jax.checkpoint(text_group), (text_in.reshape(group_count, PAIRS_DEV, TXT_LEN, D_TXT), sentence_lengths_held.reshape(group_count, PAIRS_DEV))).reshape(PAIRS, EMBED)
        return contrast_loss(picture_feature_lines, sentence_feature_lines, couple_allowed_flags, log_scale)
    contrast_objective, derivative_sweep = jax.vjp(joint_objective, picture_single_matrices, sentence_single_matrices, array_single_params, logit_log_trio[0], picture_residual_entry.astype(jnp.float32), sentence_residual_entry.astype(jnp.float32))
    picture_matrix_slope, sentence_matrix_slope, array_param_slope, logit_log_slope, picture_entry_slope, sentence_entry_slope = derivative_sweep(jnp.ones_like(contrast_objective))
    global_slope_size = jnp.sqrt(jnp.sum(picture_matrix_slope * picture_matrix_slope) + jnp.sum(sentence_matrix_slope * sentence_matrix_slope) + jnp.sum(array_param_slope * array_param_slope) + logit_log_slope * logit_log_slope)
    clipping_factor = CLIP_LEVEL / jnp.maximum(global_slope_size, CLIP_LEVEL)
    picture_matrices_fresh, picture_mean_fresh, picture_square_fresh = optimizer_advance(picture_single_matrices, picture_mean_state, picture_square_state, picture_matrix_slope * clipping_factor, RATE_MATRIX, WEIGHT_DECAY)
    sentence_matrices_fresh, sentence_mean_fresh, sentence_square_fresh = optimizer_advance(sentence_single_matrices, sentence_mean_state, sentence_square_state, sentence_matrix_slope * clipping_factor, RATE_MATRIX, WEIGHT_DECAY)
    is_norm = jnp.arange(VECS, dtype=jnp.int32) < norm_end
    array_params_fresh, array_mean_fresh, array_square_fresh = optimizer_advance(array_single_params, array_mean_state, array_square_state, array_param_slope * clipping_factor, jnp.where(is_norm, RATE_VECTOR, RATE_MATRIX), jnp.where(is_norm, 0.0, WEIGHT_DECAY))
    logit_log_fresh, logit_mean_fresh, logit_square_fresh = optimizer_advance(logit_log_trio[0], logit_log_trio[1], logit_log_trio[2], logit_log_slope * clipping_factor, LOGIT_SPEED, 0.0)
    return (contrast_objective, global_slope_size, picture_entry_slope, sentence_entry_slope, picture_matrices_fresh, picture_matrices_fresh.astype(jnp.bfloat16), picture_mean_fresh, picture_square_fresh, sentence_matrices_fresh, sentence_matrices_fresh.astype(jnp.bfloat16), sentence_mean_fresh, sentence_square_fresh, array_params_fresh, array_params_fresh.astype(jnp.bfloat16), array_mean_fresh, array_square_fresh, logit_log_fresh)
```

```python
import functools
import jax
import jax.numpy as jnp
from jax import lax
from jax.experimental import pallas as pl
from jax.experimental.pallas import tpu as pltpu
from jax.sharding import PartitionSpec as P

BF = jnp.bfloat16
F32 = jnp.float32

D_IMG = 768
FF_IMG = 3072
IMG_LEN = 50
D_TXT = 512
FF_TXT = 2048
TXT_LEN = 77
HEAD = 64
EMBED = 512
STEP = 10


NORM_EPS = 1e-05
UNIT_EPS = 1e-06
BETA_ONE = 0.5
BETA_TWO = 0.5
ADAM_EPS = 1e-08
WEIGHT_DECAY = 0.1
RATE_MATRIX = 0.04
RATE_VECTOR = 0.3
LOGIT_SPEED = 0.5
CLIP_LEVEL = 0.005
MASK_LOW = -1e30
GELU_SLOPE = 1.702
BLOCK_TARGET = 512


def branch_sum(partial_sum):
    return lax.psum(partial_sum, "mp")


def branch_back(partial_sum):
    return lax.psum(partial_sum, "mp")


def norm_forward(values, norm_gain, norm_shift):
    centered = values - jnp.mean(values, axis=-1, keepdims=True)
    inverse = lax.rsqrt(jnp.mean(centered * centered, axis=-1, keepdims=True) + NORM_EPS)
    unit_rows = centered * inverse
    return (unit_rows * norm_gain + norm_shift, unit_rows, inverse)


def norm_backward(grad_rows, unit_rows, inverse, norm_gain):
    scaled = grad_rows * norm_gain
    centered_grad = (
        scaled
        - jnp.mean(scaled, axis=-1, keepdims=True)
        - unit_rows * jnp.mean(scaled * unit_rows, axis=-1, keepdims=True)
    )
    return (
        centered_grad * inverse,
        jnp.sum(grad_rows * unit_rows, axis=0),
        jnp.sum(grad_rows, axis=0),
    )


def quick_gelu(values):
    return values * jax.nn.sigmoid(GELU_SLOPE * values)


def gelu_slope(values):
    sigmoid_value = jax.nn.sigmoid(GELU_SLOPE * values)
    return sigmoid_value + GELU_SLOPE * values * sigmoid_value * (1.0 - sigmoid_value)


def block_size(seq_count, seq_length):
    for candidate in range(1, seq_count + 1):
        if seq_count % candidate == 0 and candidate * seq_length >= BLOCK_TARGET:
            return candidate
    return seq_count


def sequence_mask(seq_length, causal):
    position = lax.iota(jnp.int32, seq_length)
    if causal:
        return position[None, :] <= position[:, None]
    return position[None, :] >= 0


def block_scores(block_qkv, allowed):
    scores = jnp.einsum(
        "nqhd,nkhd->nhqk",
        block_qkv[:, :, 0],
        block_qkv[:, :, 1],
        preferred_element_type=jnp.float32,
    ) * HEAD ** (-0.5)
    return jnp.where(allowed[None, None], scores, MASK_LOW)


def attend(packed, seq_count, seq_length, causal):
    head_count = packed.shape[2]
    per_block = block_size(seq_count, seq_length)
    blocks = packed.reshape(seq_count // per_block, per_block, seq_length, 3, head_count, HEAD)
    allowed = sequence_mask(seq_length, causal)

    def one_block(block_qkv):
        scores = block_scores(block_qkv, allowed)
        row_max = jnp.max(scores, axis=-1, keepdims=True)
        exponent = jnp.exp(scores - row_max)
        totals = jnp.sum(exponent, axis=-1, keepdims=True)
        probs = (exponent / totals).astype(jnp.bfloat16)
        result = jnp.einsum(
            "nhqk,nkhd->nqhd", probs, block_qkv[:, :, 2], preferred_element_type=jnp.float32
        ).astype(jnp.bfloat16)
        return (result, (row_max + jnp.log(totals))[..., 0])

    results, log_totals = lax.map(one_block, blocks)
    return (results.reshape(packed.shape[0], head_count * HEAD), log_totals)


def attend_back(packed, attended_grad, log_totals, seq_count, seq_length, causal):
    head_count = packed.shape[2]
    per_block = block_size(seq_count, seq_length)
    block_total = seq_count // per_block
    blocks = packed.reshape(block_total, per_block, seq_length, 3, head_count, HEAD)
    grad_blocks = attended_grad.reshape(block_total, per_block, seq_length, head_count, HEAD)
    allowed = sequence_mask(seq_length, causal)

    def one_block(block_args):
        block_qkv, block_grad, block_totals = block_args
        scores = block_scores(block_qkv, allowed)
        probs = jnp.exp(scores - block_totals[..., None])
        value_grad = jnp.einsum(
            "nhqk,nqhd->nkhd",
            probs.astype(jnp.bfloat16),
            block_grad,
            preferred_element_type=jnp.float32,
        )
        prob_grad = jnp.einsum(
            "nqhd,nkhd->nhqk", block_grad, block_qkv[:, :, 2], preferred_element_type=jnp.float32
        )
        score_grad = (
            probs * (prob_grad - jnp.sum(probs * prob_grad, axis=-1, keepdims=True))
        ).astype(jnp.bfloat16)
        query_grad = jnp.einsum(
            "nhqk,nkhd->nqhd", score_grad, block_qkv[:, :, 1], preferred_element_type=jnp.float32
        ) * HEAD ** (-0.5)
        key_grad = jnp.einsum(
            "nhqk,nqhd->nkhd", score_grad, block_qkv[:, :, 0], preferred_element_type=jnp.float32
        ) * HEAD ** (-0.5)
        return jnp.stack([query_grad, key_grad, value_grad], axis=2).astype(jnp.bfloat16)

    return lax.map(one_block, (blocks, grad_blocks, log_totals)).reshape(packed.shape)


def split_flat(flat_weights, model_width, hidden, model_split):
    width_piece = model_width // model_split
    hidden_piece = hidden // model_split
    first_end = model_width * 3 * width_piece
    second_end = first_end + width_piece * model_width
    third_end = second_end + model_width * hidden_piece
    return (
        flat_weights[:first_end].reshape(model_width, 3, width_piece),
        flat_weights[first_end:second_end].reshape(width_piece, model_width),
        flat_weights[second_end:third_end].reshape(model_width, hidden_piece),
        flat_weights[third_end:].reshape(hidden_piece, model_width),
    )


def layer_forward(tokens, weights, norms, causal):
    qkv_weight, out_weight, up_weight, down_weight = weights
    seq_count, seq_length, model_width = tokens.shape
    token_rows = tokens.reshape(seq_count * seq_length, model_width).astype(jnp.float32)
    first_normed, unit_one, inverse_one = norm_forward(token_rows, norms[0], norms[1])
    first_low = first_normed.astype(jnp.bfloat16)
    packed = jnp.einsum(
        "rd,dtk->rtk", first_low, qkv_weight, preferred_element_type=jnp.float32
    ).astype(jnp.bfloat16)
    packed = packed.reshape(token_rows.shape[0], 3, qkv_weight.shape[2] // HEAD, HEAD)
    attended, log_totals = attend(packed, seq_count, seq_length, causal)
    middle = token_rows + branch_sum(
        jnp.dot(attended, out_weight, preferred_element_type=jnp.float32)
    )
    second_normed, unit_two, inverse_two = norm_forward(middle, norms[2], norms[3])
    second_low = second_normed.astype(jnp.bfloat16)
    pre_act = jnp.dot(second_low, up_weight, preferred_element_type=jnp.float32)
    activated = quick_gelu(pre_act).astype(jnp.bfloat16)
    outputs = middle + branch_sum(
        jnp.dot(activated, down_weight, preferred_element_type=jnp.float32)
    )
    return (
        outputs,
        (
            first_low,
            unit_one,
            inverse_one,
            packed,
            attended,
            log_totals,
            second_low,
            unit_two,
            inverse_two,
            pre_act,
            activated,
        ),
    )


def layer_backward(grad_out, weights, norms, stored, seq_count, seq_length, causal):
    qkv_weight, out_weight, up_weight, down_weight = weights
    (
        first_low,
        unit_one,
        inverse_one,
        packed,
        attended,
        log_totals,
        second_low,
        unit_two,
        inverse_two,
        pre_act,
        activated,
    ) = stored
    grad_low = grad_out.astype(jnp.bfloat16)
    down_grad = jnp.einsum("rf,rd->fd", activated, grad_low, preferred_element_type=jnp.float32)
    act_grad = jnp.einsum("rd,fd->rf", grad_low, down_weight, preferred_element_type=jnp.float32)
    pre_grad = (act_grad * gelu_slope(pre_act)).astype(jnp.bfloat16)
    up_grad = jnp.einsum("rd,rf->df", second_low, pre_grad, preferred_element_type=jnp.float32)
    second_grad = branch_back(
        jnp.einsum("rf,df->rd", pre_grad, up_weight, preferred_element_type=jnp.float32)
    )
    norm_grad_two, gain_two, shift_two = norm_backward(second_grad, unit_two, inverse_two, norms[2])
    middle_grad = grad_out + norm_grad_two
    middle_low = middle_grad.astype(jnp.bfloat16)
    out_grad = jnp.einsum("ra,rd->ad", attended, middle_low, preferred_element_type=jnp.float32)
    attended_grad = jnp.einsum(
        "rd,ad->ra", middle_low, out_weight, preferred_element_type=jnp.float32
    ).astype(jnp.bfloat16)
    packed_grad = attend_back(packed, attended_grad, log_totals, seq_count, seq_length, causal)
    packed_grad = packed_grad.reshape(packed.shape[0], 3, qkv_weight.shape[2])
    qkv_grad = jnp.einsum("rd,rtk->dtk", first_low, packed_grad, preferred_element_type=jnp.float32)
    first_grad = branch_back(
        jnp.einsum("rtk,dtk->rd", packed_grad, qkv_weight, preferred_element_type=jnp.float32)
    )
    norm_grad_one, gain_one, shift_one = norm_backward(first_grad, unit_one, inverse_one, norms[0])
    flat_grads = jnp.concatenate(
        [qkv_grad.reshape(-1), out_grad.reshape(-1), up_grad.reshape(-1), down_grad.reshape(-1)]
    )
    return (middle_grad + norm_grad_one, flat_grads, [gain_one, shift_one, gain_two, shift_two])


def pool_forward(picked, norm_gain, norm_shift, projection):
    normed, unit_rows, inverse = norm_forward(picked, norm_gain, norm_shift)
    normed_low = normed.astype(jnp.bfloat16)
    raw_embed = jnp.dot(normed_low, projection, preferred_element_type=jnp.float32)
    length_inverse = lax.rsqrt(jnp.sum(raw_embed * raw_embed, axis=-1, keepdims=True) + UNIT_EPS)
    embed_rows = raw_embed * length_inverse
    return (
        embed_rows.astype(jnp.bfloat16),
        (unit_rows, inverse, normed_low, embed_rows, length_inverse),
    )


def pool_backward(embed_grad, norm_gain, projection, stored):
    unit_rows, inverse, normed_low, embed_rows, length_inverse = stored
    raw_grad = (
        length_inverse
        * (embed_grad - embed_rows * jnp.sum(embed_grad * embed_rows, axis=-1, keepdims=True))
    ).astype(jnp.bfloat16)
    proj_grad = jnp.einsum("nd,ne->de", normed_low, raw_grad, preferred_element_type=jnp.float32)
    normed_grad = jnp.einsum("ne,de->nd", raw_grad, projection, preferred_element_type=jnp.float32)
    picked_grad, gain_grad, shift_grad = norm_backward(normed_grad, unit_rows, inverse, norm_gain)
    return (picked_grad, proj_grad, gain_grad, shift_grad)


def cosine_logits(picture_feature_lines, sentence_feature_lines, couple_allowed_flags, log_scale):
    image_all, text_all, valid_all = (
        lax.all_gather(picture_feature_lines, ("tower", "dp"), axis=0, tiled=True),
        lax.all_gather(sentence_feature_lines, ("tower", "dp"), axis=0, tiled=True),
        lax.all_gather(
            couple_allowed_flags.astype(jnp.bfloat16), ("tower", "dp"), axis=0, tiled=True
        ),
    )
    count_valid = jnp.sum(valid_all.astype(jnp.float32))
    column_valid = valid_all > 0
    row_valid = couple_allowed_flags > 0
    local_count = picture_feature_lines.shape[0]
    offset_rows = lax.axis_index(("tower", "dp")) * local_count
    on_diagonal = (
        lax.iota(jnp.int32, valid_all.shape[0])[None, :]
        == offset_rows + lax.iota(jnp.int32, local_count)[:, None]
    )
    scale_factor = jnp.exp(log_scale)

    def one_side(mine, others):
        logits = scale_factor * jnp.einsum(
            "ne,me->nm", mine, others, preferred_element_type=jnp.float32
        )
        masked = jnp.where(column_valid[None, :], logits, MASK_LOW)
        row_max = jnp.max(masked, axis=1, keepdims=True)
        exponent = jnp.exp(masked - row_max)
        totals = jnp.sum(exponent, axis=1, keepdims=True)
        own_logit = jnp.sum(jnp.where(on_diagonal, logits, 0.0), axis=1)
        log_sum = row_max[:, 0] + jnp.log(totals[:, 0])
        loss_sum = jnp.sum(jnp.where(row_valid, log_sum - own_logit, 0.0))
        logit_grad = jnp.where(
            row_valid[:, None], exponent / totals - on_diagonal.astype(jnp.float32), 0.0
        ) / (2.0 * count_valid)
        return (loss_sum, logit_grad, jnp.sum(logit_grad * logits), log_sum, logits)

    image_loss, image_logit_grad, image_scale_part, image_lse, image_logits = one_side(
        picture_feature_lines, text_all
    )
    text_loss, text_logit_grad, text_scale_part, text_lse, text_logits = one_side(
        sentence_feature_lines, image_all
    )
    picture_device_share = scale_factor * jnp.dot(
        image_logit_grad, text_all.astype(jnp.float32), precision=lax.Precision.HIGHEST
    )
    sentence_device_share = scale_factor * jnp.dot(
        text_logit_grad, image_all.astype(jnp.float32), precision=lax.Precision.HIGHEST
    )
    text_spread = scale_factor * jnp.einsum(
        "np,ne->pe",
        image_logit_grad,
        picture_feature_lines.astype(jnp.float32),
        precision=lax.Precision.HIGHEST,
    )
    image_spread = scale_factor * jnp.einsum(
        "np,ne->pe",
        text_logit_grad,
        sentence_feature_lines.astype(jnp.float32),
        precision=lax.Precision.HIGHEST,
    )
    picture_reverse, sentence_reverse = (
        lax.psum_scatter(image_spread, ("tower", "dp"), scatter_dimension=0, tiled=True),
        lax.psum_scatter(text_spread, ("tower", "dp"), scatter_dimension=0, tiled=True),
    )
    contrast_objective, logit_log_slope = lax.psum(
        ((image_loss + text_loss) / (2.0 * count_valid), image_scale_part + text_scale_part),
        ("tower", "dp"),
    )
    return (
        picture_device_share + picture_reverse,
        sentence_device_share + sentence_reverse,
        contrast_objective,
        logit_log_slope,
    )


def optimizer_advance(master, first, second, grad, rate, decay):
    first_new = BETA_ONE * first + (1.0 - BETA_ONE) * grad
    second_new = BETA_TWO * second + (1.0 - BETA_TWO) * grad * grad
    update = (
        first_new
        / (1.0 - BETA_ONE**STEP)
        / (jnp.sqrt(second_new / (1.0 - BETA_TWO**STEP)) + ADAM_EPS)
    )
    return (master - rate * (update + decay * master), first_new, second_new)


def local(
    picture_residual_entry,
    sentence_residual_entry,
    sentence_lengths_held,
    couple_allowed_flags,
    picture_single_matrices,
    picture_mean_state,
    picture_square_state,
    sentence_single_matrices,
    sentence_mean_state,
    sentence_square_state,
    array_single_params,
    array_mean_state,
    array_square_state,
    logit_log_trio,
):
    model_split = lax.axis_size("mp")
    norm_end = 6 * (D_IMG + D_TXT)
    image_end = norm_end + D_IMG * EMBED
    image_flat, text_flat, vector_flat = (
        lax.all_gather(
            picture_single_matrices.astype(jnp.bfloat16), ("tower", "dp"), axis=1, tiled=True
        ),
        lax.all_gather(
            sentence_single_matrices.astype(jnp.bfloat16), ("tower", "dp"), axis=1, tiled=True
        ),
        lax.all_gather(
            array_single_params.astype(jnp.bfloat16), ("tower", "dp"), axis=0, tiled=True
        ),
    )
    image_norms = vector_flat[: 6 * D_IMG].reshape(6, D_IMG).astype(jnp.float32)
    text_norms = vector_flat[6 * D_IMG : norm_end].reshape(6, D_TXT).astype(jnp.float32)
    image_proj = vector_flat[norm_end:image_end].reshape(D_IMG, EMBED)
    text_proj = vector_flat[image_end:].reshape(D_TXT, EMBED)
    seq_count = picture_residual_entry.shape[0]
    image_weights = split_flat(image_flat[0], D_IMG, FF_IMG, model_split)
    image_out, image_stored = layer_forward(
        picture_residual_entry, image_weights, image_norms, False
    )
    image_picked = jnp.mean(image_out.reshape(seq_count, IMG_LEN, D_IMG), axis=1)
    picture_feature_lines, image_pool = pool_forward(
        image_picked, image_norms[4], image_norms[5], image_proj
    )
    text_weights = split_flat(text_flat[0], D_TXT, FF_TXT, model_split)
    text_out, text_stored = layer_forward(sentence_residual_entry, text_weights, text_norms, True)
    inside = (lax.iota(jnp.int32, TXT_LEN)[None, :] < sentence_lengths_held[:, None]).astype(
        jnp.float32
    )
    picker = inside / sentence_lengths_held[:, None].astype(jnp.float32)
    text_picked = jnp.einsum(
        "nl,nld->nd",
        picker,
        text_out.reshape(seq_count, TXT_LEN, D_TXT),
        precision=lax.Precision.HIGHEST,
    )
    sentence_feature_lines, text_pool = pool_forward(
        text_picked, text_norms[4], text_norms[5], text_proj
    )
    picture_feature_slope, sentence_feature_slope, contrast_objective, logit_log_slope = (
        cosine_logits(
            picture_feature_lines, sentence_feature_lines, couple_allowed_flags, logit_log_trio[0]
        )
    )
    text_picked_grad, text_proj_grad, text_post_gain, text_post_shift = pool_backward(
        sentence_feature_slope, text_norms[4], text_proj, text_pool
    )
    text_rows_grad = (picker[:, :, None] * text_picked_grad[:, None, :]).reshape(
        seq_count * TXT_LEN, D_TXT
    )
    sentence_entry_slope, text_flat_grad, text_norm_grads = layer_backward(
        text_rows_grad, text_weights, text_norms, text_stored, seq_count, TXT_LEN, True
    )
    image_picked_grad, image_proj_grad, image_post_gain, image_post_shift = pool_backward(
        picture_feature_slope, image_norms[4], image_proj, image_pool
    )
    image_rows_grad = jnp.broadcast_to(
        image_picked_grad[:, None, :] / IMG_LEN, (seq_count, IMG_LEN, D_IMG)
    ).reshape(seq_count * IMG_LEN, D_IMG)
    picture_entry_slope, image_flat_grad, image_norm_grads = layer_backward(
        image_rows_grad, image_weights, image_norms, image_stored, seq_count, IMG_LEN, False
    )
    array_param_slope = jnp.concatenate(
        [
            jnp.stack(image_norm_grads + [image_post_gain, image_post_shift]).reshape(-1),
            jnp.stack(text_norm_grads + [text_post_gain, text_post_shift]).reshape(-1),
            image_proj_grad.reshape(-1),
            text_proj_grad.reshape(-1),
        ]
    )
    image_reduced, text_reduced, vector_reduced = (
        lax.psum_scatter(
            image_flat_grad.reshape(-1, D_IMG), ("tower", "dp"), scatter_dimension=0, tiled=True
        ).reshape(1, -1),
        lax.psum_scatter(
            text_flat_grad.reshape(-1, D_TXT), ("tower", "dp"), scatter_dimension=0, tiled=True
        ).reshape(1, -1),
        lax.psum_scatter(array_param_slope, ("tower", "dp"), scatter_dimension=0, tiled=True),
    )
    matrix_squares = jnp.sum(image_reduced * image_reduced) + jnp.sum(text_reduced * text_reduced)
    vector_squares = jnp.sum(vector_reduced * vector_reduced) / model_split
    tensor_square_sum, array_square_sum = lax.psum(
        (matrix_squares, vector_squares), ("tower", "dp", "mp")
    )
    global_slope_size = jnp.sqrt(
        tensor_square_sum + array_square_sum + logit_log_slope * logit_log_slope
    )
    clipping_factor = CLIP_LEVEL / jnp.maximum(global_slope_size, CLIP_LEVEL)
    picture_matrices_fresh, picture_mean_fresh, picture_square_fresh = optimizer_advance(
        picture_single_matrices,
        picture_mean_state,
        picture_square_state,
        image_reduced * clipping_factor,
        RATE_MATRIX,
        WEIGHT_DECAY,
    )
    sentence_matrices_fresh, sentence_mean_fresh, sentence_square_fresh = optimizer_advance(
        sentence_single_matrices,
        sentence_mean_state,
        sentence_square_state,
        text_reduced * clipping_factor,
        RATE_MATRIX,
        WEIGHT_DECAY,
    )
    shard_length = array_single_params.shape[0]
    vector_index = lax.axis_index(("tower", "dp")) * shard_length + lax.iota(
        jnp.int32, shard_length
    )
    is_norm = vector_index < norm_end
    array_params_fresh, array_mean_fresh, array_square_fresh = optimizer_advance(
        array_single_params,
        array_mean_state,
        array_square_state,
        vector_reduced * clipping_factor,
        jnp.where(is_norm, RATE_VECTOR, RATE_MATRIX),
        jnp.where(is_norm, 0.0, WEIGHT_DECAY),
    )
    logit_log_fresh, logit_mean_fresh, logit_square_fresh = optimizer_advance(
        logit_log_trio[0],
        logit_log_trio[1],
        logit_log_trio[2],
        logit_log_slope * clipping_factor,
        LOGIT_SPEED,
        0.0,
    )
    return (
        contrast_objective,
        global_slope_size,
        picture_entry_slope.reshape(picture_residual_entry.shape),
        sentence_entry_slope.reshape(sentence_residual_entry.shape),
        picture_matrices_fresh,
        picture_matrices_fresh.astype(jnp.bfloat16),
        picture_mean_fresh,
        picture_square_fresh,
        sentence_matrices_fresh,
        sentence_matrices_fresh.astype(jnp.bfloat16),
        sentence_mean_fresh,
        sentence_square_fresh,
        array_params_fresh,
        array_params_fresh.astype(jnp.bfloat16),
        array_mean_fresh,
        array_square_fresh,
        logit_log_fresh,
    )


ZN = 4
MP = 4
SEQS = 8


class Tower:
    def __init__(self, width, length, padded, joint, causal, norm_row):
        self.d = width
        self.w = width // MP
        self.heads = self.w // HEAD
        self.length = length
        self.padded = padded
        self.rows = 2 * padded
        self.all_rows = MP * self.rows
        self.tile = self.rows if joint else padded
        self.tiles = self.rows // self.tile
        self.causal = causal
        self.sr = 3 * width // 8
        self.half = self.sr // 2
        self.q = width // 128
        self.norm_row = norm_row
        self.lin = self.sr * self.q


IMG = Tower(D_IMG, IMG_LEN, 56, True, False, 0)
TXT = Tower(D_TXT, TXT_LEN, 80, False, True, 6 * D_IMG // 128)
NORM_ROWS = 6 * (D_IMG + D_TXT) // 128
VEC_ROWS = 648
TXT_HALF = 64
COMBINED = IMG.half + TXT_HALF
URGENT_TXT = TXT_HALF + 16


def kernel_call(body, name, outs, ins, scratch=(), flops=0):
    def spec(value):
        small = value.dtype == jnp.int32 or (value.ndim == 1 and value.shape[0] <= 8)
        return pl.BlockSpec(memory_space=pltpu.SMEM if small else pltpu.VMEM)

    moved = sum(v.size * v.dtype.itemsize for v in list(ins) + list(outs))
    return pl.pallas_call(
        body,
        out_shape=list(outs),
        in_specs=[spec(v) for v in ins],
        out_specs=[pl.BlockSpec(memory_space=pltpu.VMEM)] * len(outs),
        scratch_shapes=list(scratch),
        compiler_params=pltpu.CompilerParams(vmem_limit_bytes=56 * 1024 * 1024),
        cost_estimate=pl.CostEstimate(
            flops=int(flops), bytes_accessed=int(moved), transcendentals=0
        ),
        name=name,
    )(*ins)


def out(shape, dtype=F32):
    return jax.ShapeDtypeStruct(shape, dtype)


def dot(a, b):
    return lax.dot_general(a, b, (((1,), (0,)), ((), ())), preferred_element_type=F32)


def dot_nt(a, b):
    return lax.dot_general(a, b, (((1,), (1,)), ((), ())), preferred_element_type=F32)


def dot_tn(a, b):
    return lax.dot_general(a, b, (((0,), (0,)), ((), ())), preferred_element_type=F32)


def pieces(a, count):
    parts = []
    for _ in range(count):
        part = a.astype(BF)
        parts.append(part)
        a = a - part.astype(F32)
    return parts


def unit(values):
    width = values.shape[-1]
    centered = values - jnp.sum(values, axis=-1, keepdims=True) * (1.0 / width)
    inverse = lax.rsqrt(
        jnp.sum(centered * centered, axis=-1, keepdims=True) * (1.0 / width) + NORM_EPS
    )
    return centered * inverse, inverse


def unit_back(grad_rows, unit_rows, inverse, gain):
    width = grad_rows.shape[-1]
    scaled = grad_rows * gain
    first = jnp.sum(scaled, axis=-1, keepdims=True) * (1.0 / width)
    second = jnp.sum(scaled * unit_rows, axis=-1, keepdims=True) * (1.0 / width)
    return (scaled - first - unit_rows * second) * inverse


def norm_vector(norms_ref, tower, index):
    start = tower.norm_row + index * tower.q
    return jnp.concatenate([norms_ref[start + i : start + i + 1, :] for i in range(tower.q)], axis=1)


def natural_from_lin(tower, lin_ref, spare):
    d, w = tower.d, tower.w
    if (3 * w) % 128 == 0:
        per = 3 * w // 128
        return jnp.concatenate(
            [lin_ref[pl.ds(i, d // 2, stride=per), :] for i in range(per)], axis=1
        )
    per = 2 * 3 * w // 128
    mid = per // 2
    lines = [lin_ref[pl.ds(i, d // 4, stride=per), :] for i in range(per)]
    empty = jnp.zeros((d // 4, 64), F32)
    even = lines[: mid + 1]
    odd = jnp.concatenate([lines[mid][:, 64:]] + lines[mid + 1 :] + [empty], axis=1)
    for j in range(mid + 1):
        spare.at[j][pl.ds(0, d // 4, stride=2), :] = even[j]
        spare.at[j][pl.ds(1, d // 4, stride=2), :] = odd[:, 128 * j : 128 * (j + 1)]
    return jnp.concatenate([spare[j] for j in range(mid)] + [spare[mid][:, :64]], axis=1)


def natural_to_lin(tower, natural, lin_ref, spare):
    d, w = tower.d, tower.w
    if (3 * w) % 128 == 0:
        per = 3 * w // 128
        for i in range(per):
            lin_ref[pl.ds(i, d // 2, stride=per), :] = natural[:, 128 * i : 128 * (i + 1)]
        return
    per = 2 * 3 * w // 128
    mid = per // 2
    for j in range(mid):
        spare[j] = natural[:, 128 * j : 128 * (j + 1)]
    spare[mid] = jnp.concatenate([natural[:, 128 * mid :], jnp.zeros((d // 2, 64), F32)], axis=1)
    even = [spare.at[j][pl.ds(0, d // 4, stride=2), :] for j in range(mid + 1)]
    odd = jnp.concatenate(
        [spare.at[j][pl.ds(1, d // 4, stride=2), :] for j in range(mid + 1)], axis=1
    )
    for i in range(mid):
        lin_ref[pl.ds(i, d // 4, stride=per), :] = even[i]
    lin_ref[pl.ds(mid, d // 4, stride=per), :] = jnp.concatenate(
        [even[mid][:, :64], odd[:, :64]], axis=1
    )
    for i in range(mid):
        lin_ref[pl.ds(mid + 1 + i, d // 4, stride=per), :] = odd[:, 64 + 128 * i : 192 + 128 * i]


def lin_to_rows(tower, lin_ref, rows_ref, spare, shard):
    d, w, sr, q = tower.d, tower.w, tower.sr, tower.q

    @pl.when(shard >= 2)
    def _():
        for j in range(q):
            rows_ref[:, 128 * j : 128 * (j + 1)] = lin_ref[pl.ds(j, sr, stride=q), :]

    @pl.when(shard < 2)
    def _():
        tail = d // 8
        natural = natural_from_lin(tower, lin_ref, spare)
        rows_ref[:, : 3 * w] = natural[:sr]
        for i in range(3):
            rows_ref[tail * i : tail * (i + 1), 3 * w :] = natural[sr:, w * i : w * (i + 1)]


def rows_to_lin(tower, rows_ref, lin_ref, spare, shard):
    d, w, sr, q = tower.d, tower.w, tower.sr, tower.q

    @pl.when(shard >= 2)
    def _():
        for j in range(q):
            lin_ref[pl.ds(j, sr, stride=q), :] = rows_ref[:, 128 * j : 128 * (j + 1)]

    @pl.when(shard < 2)
    def _():
        tail = d // 8
        rest = jnp.concatenate(
            [rows_ref[tail * i : tail * (i + 1), 3 * w :] for i in range(3)], axis=1
        )
        natural = jnp.concatenate([rows_ref[:, : 3 * w], rest], axis=0)
        natural_to_lin(tower, natural, lin_ref, spare)


SPARE = ((3 * IMG.w + 127) // 128, IMG.d // 2, 128)


def prepare_body(
    ids, flags, lengths, img, txt, vec, keep, send, normblock, vecpay, img_rows, txt_rows, shifted, spare
):
    side, shard = ids[0], ids[3]
    lin_to_rows(IMG, img, img_rows, spare, shard)
    lin_to_rows(TXT, txt, txt_rows, spare, shard)
    for target, which in ((keep, side), (send, 1 - side)):
        target[: IMG.half, :] = img_rows[
            pl.ds(pl.multiple_of(which * IMG.half, 8), IMG.half), :
        ].astype(BF)
        part = txt_rows[pl.ds(pl.multiple_of(which * TXT.half, 8), TXT.half), :].astype(BF)
        target[IMG.half :, : TXT.d] = part[:64]
        target[IMG.half : IMG.half + 32, TXT.d :] = part[64:, :256]
        target[IMG.half + 32 :, TXT.d :] = part[64:, 256:]
    lane = lax.broadcasted_iota(jnp.int32, (1, 128), 1)
    flag_row = jnp.zeros((1, 128), F32)
    length_row = jnp.zeros((1, 128), F32)
    for i in range(SEQS):
        flag_row = jnp.where(lane == i, jnp.where(flags[i] > 0, 1.0, 0.0), flag_row)
        length_row = jnp.where(lane == i, lengths[i].astype(F32), length_row)
    head = jnp.concatenate(
        [vec[:NORM_ROWS, :], flag_row, length_row, jnp.zeros((64 - NORM_ROWS - 2, 128), F32)], axis=0
    )
    for j in range(4):
        normblock[:, 128 * j : 128 * (j + 1)] = head[16 * j : 16 * (j + 1)].astype(BF)
    normblock[:, 512:] = jnp.zeros((16, 256), BF)

    @pl.when(shard % 2 == 0)
    def _():
        vecpay[...] = vec[...].astype(BF)

    @pl.when(shard % 2 == 1)
    def _():
        rolled = pltpu.roll(vec[...], 64, 1)
        shifted[0:8, :] = jnp.zeros((8, 128), F32)
        shifted[8 : 8 + VEC_ROWS, :] = rolled
        before = shifted[7 : 7 + VEC_ROWS, :]
        low_lanes = lax.broadcasted_iota(jnp.int32, (VEC_ROWS, 128), 1) < 64
        vecpay[...] = jnp.where(low_lanes, before, rolled).astype(BF)


def sort_body(ids, keep, received, normblock, urgent_txt, urgent_img, later):
    side = ids[0]

    def fill(early, late):
        urgent_img[...] = early[: IMG.half, :]
        urgent_txt[:TXT_HALF, :] = early[IMG.half :, :]
        later[...] = late[...]

    pl.when(side == 0)(lambda: fill(keep, received))
    pl.when(side != 0)(lambda: fill(received, keep))
    urgent_txt[TXT_HALF:, :] = normblock[...]


def fetch_half(target, start, source, offset, tower):
    if tower is IMG:
        target[start : start + IMG.half, :] = source[
            pl.ds(pl.multiple_of(offset, 16), IMG.half), :
        ]
    else:
        block = source[pl.ds(pl.multiple_of(offset, 16), TXT_HALF), :]
        target[start : start + 64, :] = block[:, : TXT.d]
        target[start + 64 : start + 96, :] = jnp.concatenate(
            [block[:32, TXT.d :], block[32:, TXT.d :]], axis=1
        )


def fetch_shard(target, start, mine, other, side, place, block_rows, inner, tower):
    offset = place * block_rows + inner

    def take(first, second):
        fetch_half(target, start, first, offset, tower)
        fetch_half(target, start + tower.half, second, offset, tower)

    pl.when(side == 0)(lambda: take(mine, other))
    pl.when(side != 0)(lambda: take(other, mine))


def attention_mask(tower):
    shape = (tower.tile, tower.tile)
    row = lax.broadcasted_iota(jnp.int32, shape, 0)
    column = lax.broadcasted_iota(jnp.int32, shape, 1)
    if tower.causal:
        return (column <= row) & (column < tower.length)
    pad = tower.padded
    first = (row < pad) & (column < tower.length)
    second = (row >= pad) & (column >= pad) & (column < pad + tower.length)
    return first | second


def attend_body(tower, ids, x, mine, other, *rest):
    if tower is TXT:
        outs = rest
        (norms, meta, wq, wo, h1, u1, qkv, att, probs, xo, own, s1, s2, s3, xf, xs, pay, wn) = outs
        block_rows = URGENT_TXT
    else:
        norms = rest[0]
        (wq, wo, h1, u1, qkv, att, probs, xo, own, s1, s2, s3, xf, xs, pay, wn) = rest[1:]
        block_rows = IMG.half
    side, z, m = ids[0], ids[1], ids[2]
    d, w, sr = tower.d, tower.w, tower.sr
    if tower is TXT:

        def read_norms(source):
            block = source[pl.ds(pl.multiple_of(z * URGENT_TXT + TXT_HALF, 16), 16), :]
            for j in range(4):
                norms[16 * j : 16 * (j + 1), :] = block[:, 128 * j : 128 * (j + 1)].astype(F32)

        pl.when(side == 0)(lambda: read_norms(mine))
        pl.when(side != 0)(lambda: read_norms(other))

        def read_meta(first, second):
            for half, source in ((0, first), (1, second)):
                for place in range(ZN):
                    start = (z ^ place) * URGENT_TXT + TXT_HALF
                    block = source[pl.ds(pl.multiple_of(start, 16), 16), 384:512].astype(F32)
                    s = half * ZN + place
                    meta[s : s + 1, :] = block[12:13]
                    meta[8 + s : 9 + s, :] = block[13:14]

        pl.when(side == 0)(lambda: read_meta(mine, other))
        pl.when(side != 0)(lambda: read_meta(other, mine))

    tail = d // 8
    for s in range(3):
        fetch_shard(pay, 0, mine, other, side, z ^ s, block_rows, 0, tower)
        if s < 2:
            base = s * (d // 2)
            wq[base : base + sr, :] = pay[:, : 3 * w]
            wq[base + sr : base + sr + tail, :] = jnp.concatenate(
                [pay[tail * i : tail * (i + 1), 3 * w :] for i in range(3)], axis=1
            )
        else:
            wo[...] = pay[:w, :]

    for j in range(tower.q):
        xf[j] = x[:, :, 128 * j : 128 * (j + 1)].astype(F32).reshape(tower.length * SEQS, 128)
    pad = tower.padded - tower.length
    for k in range(MP):
        for j in range(2):
            start = k * tower.rows + j * tower.padded
            seq = 2 * (m ^ k) + j
            for i in range(tower.q):
                xs[start : start + tower.length, 128 * i : 128 * (i + 1)] = xf.at[i][
                    pl.ds(seq, tower.length, stride=SEQS), :
                ]
            xs[start + tower.length : start + tower.padded, :] = jnp.zeros((pad, d), F32)
    xo[...] = xs[: tower.rows, :]
    unit_rows, _ = unit(xs[...])
    u1[...] = unit_rows
    h1[...] = (
        unit_rows * norm_vector(norms, tower, 0) + norm_vector(norms, tower, 1)
    ).astype(BF)
    qkv[...] = dot(h1[...], wq[...]).astype(BF)
    allowed = attention_mask(tower)
    targets = (own, s1, s2, s3)
    for k in range(MP):
        for tile in range(tower.tiles):
            start = k * tower.rows + tile * tower.tile
            rows = slice(start, start + tower.tile)
            heads = []
            for h in range(tower.heads):
                query = qkv[rows, h * HEAD : (h + 1) * HEAD]
                key = qkv[rows, w + h * HEAD : w + (h + 1) * HEAD]
                value = qkv[rows, 2 * w + h * HEAD : 2 * w + (h + 1) * HEAD]
                scores = jnp.where(allowed, dot_nt(query, key) * HEAD ** (-0.5), MASK_LOW)
                exponent = jnp.exp(scores - jnp.max(scores, axis=-1, keepdims=True))
                prob = exponent / jnp.sum(exponent, axis=-1, keepdims=True)
                probs[(k * tower.tiles + tile) * tower.heads + h] = prob
                heads.append(dot(prob.astype(BF), value))
            att[rows, :] = jnp.concatenate(heads, axis=1).astype(BF)
        rows = slice(k * tower.rows, (k + 1) * tower.rows)
        part = dot(att[rows, :], wo[...])
        targets[k][...] = part.astype(targets[k].dtype)


def attend_call(tower, ids, x, mine, other, norms=None):
    d, w, rows, every = tower.d, tower.w, tower.rows, tower.all_rows
    outs = [
        out((d, 3 * w), BF),
        out((w, d), BF),
        out((every, d), BF),
        out((every, d)),
        out((every, 3 * w), BF),
        out((every, w), BF),
        out((MP * tower.tiles * tower.heads, tower.tile, tower.tile)),
        out((rows, d)),
        out((rows, d)),
        out((rows, d), BF),
        out((rows, d), BF),
        out((rows, d), BF),
    ]
    ins = [ids, x, mine, other]
    if tower is TXT:
        outs = [out((64, 128)), out((16, 128))] + outs
    else:
        ins.append(norms)
    return kernel_call(
        functools.partial(attend_body, tower),
        "attend_" + ("txt" if tower is TXT else "img"),
        outs,
        ins,
        [
            pltpu.VMEM((tower.q, tower.length * SEQS, 128), F32),
            pltpu.VMEM((every, d), F32),
            pltpu.VMEM((tower.sr, d), BF),
            pltpu.VMEM((8, 128), F32),
        ],
        flops=2 * every * d * 4 * w + 4 * every * tower.tile * w,
    )


def row_mask(tower, lengths, pair):
    position = lax.broadcasted_iota(jnp.int32, (tower.padded, 1), 0)
    count = lengths[pair] if tower.causal else tower.length
    return position < count, count


def middle_body(tower, ids, lengths, norms, xo, own, r1, r2, r3, x1, h2, pooled):
    m = ids[2]
    total = xo[...] + ((own[...] + r1[...].astype(F32)) + (r2[...].astype(F32) + r3[...].astype(F32)))
    x1[...] = total
    unit_rows, _ = unit(total)
    h2[...] = (
        unit_rows * norm_vector(norms, tower, 2) + norm_vector(norms, tower, 3)
    ).astype(BF)
    for j in range(2):
        inside, count = row_mask(tower, lengths, 2 * m + j)
        part = total[j * tower.padded : (j + 1) * tower.padded]
        summed = jnp.sum(jnp.where(inside, part, 0.0), axis=0, keepdims=True)
        pooled[j : j + 1, :] = summed / jnp.full((1, 1), count, F32)


def middle_call(tower, ids, lengths, norms, xo, own, received):
    rows, d = tower.rows, tower.d
    return kernel_call(
        functools.partial(middle_body, tower),
        "middle_" + ("txt" if tower is TXT else "img"),
        [out((rows, d)), out((rows, d), BF), out((2, d))],
        [ids, lengths, norms, xo, own] + received,
    )


def feed_body(
    tower, ids, lengths, h_own, h1, h2, h3, mine, other, mine_later, other_later, pooled,
    w1, w2, slope, sums, ypart, pay,
):
    side, z, m = ids[0], ids[1], ids[2]
    d, w, sr = tower.d, tower.w, tower.sr
    tail = d // 8
    urgent_rows = URGENT_TXT if tower is TXT else IMG.half
    inner = IMG.half if tower is TXT else 0

    def early(s):
        fetch_shard(pay, 0, mine, other, side, z ^ s, urgent_rows, 0, tower)

    def late(s):
        fetch_shard(pay, 0, mine_later, other_later, side, z ^ s, COMBINED, inner, tower)

    early(2)
    w1[:tail, :] = pay[w:, :]
    early(3)
    w1[tail : tail + sr, :] = pay[...]
    late(0)
    w1[tail + sr : tail + 2 * sr, :] = pay[...]
    late(1)
    w1[tail + 2 * sr :, :] = pay[:tail, :]
    w2[:w, :] = pay[tail:, :]
    late(2)
    w2[w : w + sr, :] = pay[...]
    late(3)
    w2[w + sr :, :] = pay[...]

    for k, block in enumerate((h_own, h1, h2, h3)):
        pre = dot(block[...], w1[...])
        gate = jax.nn.sigmoid(GELU_SLOPE * pre)
        acted = (pre * gate).astype(BF).astype(F32)
        slope[k * tower.rows : (k + 1) * tower.rows, :] = gate + GELU_SLOPE * pre * gate * (
            1.0 - gate
        )
        summed = []
        counts = []
        for j in range(2):
            inside, count = row_mask(tower, lengths, 2 * (m ^ k) + j)
            part = acted[j * tower.padded : (j + 1) * tower.padded]
            summed.append(jnp.sum(jnp.where(inside, part, 0.0), axis=0, keepdims=True))
            counts.append(jnp.full((1, 1), count, F32))
        both = jnp.concatenate(summed, axis=0)
        sums[m ^ k] = both
        high, low, rest = pieces(both, 3)
        y = dot(high, w2[...]) + (dot(low, w2[...]) + dot(rest, w2[...]))
        y = y / jnp.concatenate(counts, axis=0)
        if k == 0:
            y = y + pooled[...]
        ypart[m ^ k] = y


def feed_call(tower, ids, lengths, blocks, urgent, later, pooled):
    d = tower.d
    return kernel_call(
        functools.partial(feed_body, tower),
        "feed_" + ("txt" if tower is TXT else "img"),
        [
            out((d, d), BF),
            out((d, d), BF),
            out((tower.all_rows, d)),
            out((MP, 2, d)),
            out((MP, 2, d)),
        ],
        [ids, lengths] + blocks + list(urgent) + list(later) + [pooled],
        [pltpu.VMEM((tower.sr, d), BF)],
        flops=2 * tower.all_rows * d * d,
    )


def project_body(gathered, pi, pt, flat):
    for e in range(4):
        base = e * (2 * VEC_ROWS - 1)
        flat[base : base + VEC_ROWS, :] = gathered[2 * e].astype(F32)
        odd = gathered[2 * e + 1].astype(F32)
        row = base + VEC_ROWS - 1
        flat[row : row + 1, :] = flat[row : row + 1, :] + odd[:1]
        flat[row + 1 : row + VEC_ROWS, :] = odd[1:]
    for j in range(4):
        pi[:, 128 * j : 128 * (j + 1)] = flat[pl.ds(NORM_ROWS + j, D_IMG, stride=4), :].astype(BF)
        pt[:, 128 * j : 128 * (j + 1)] = flat[
            pl.ds(NORM_ROWS + 4 * D_IMG + j, D_TXT, stride=4), :
        ].astype(BF)


def project_call(gathered):
    return kernel_call(
        project_body,
        "project",
        [out((D_IMG, EMBED), BF), out((D_TXT, EMBED), BF)],
        [gathered],
        [pltpu.VMEM((4 * (2 * VEC_ROWS - 1) + 4, 128), F32)],
    )


def head_body(
    ids, trio, yall, norms, meta, pi, pt,
    misc, dyb_i, dyb_t, own_i, own_t, pg_i, pg_t, ng_i, ng_t, scr_i, scr_t,
):
    shard = ids[3]
    total = yall.shape[0]
    row = lax.broadcasted_iota(jnp.int32, (total, total), 0)
    column = lax.broadcasted_iota(jnp.int32, (total, total), 1)
    eye = row == column
    place = lax.broadcasted_iota(jnp.int32, (total, 128), 0)
    lane = lax.broadcasted_iota(jnp.int32, (total, 128), 1)

    def column_of(first):
        picked = jnp.zeros((total, 128), F32)
        for s in range(total // SEQS):
            picked = jnp.where(place // SEQS == s, meta[first + s : first + s + 1, :], picked)
        return jnp.sum(jnp.where(lane == place % SEQS, picked, 0.0), axis=1, keepdims=True)

    flag_column = column_of(0)
    length_column = column_of(8)
    flag_row = jnp.sum(jnp.where(eye, flag_column, 0.0), axis=0, keepdims=True)
    row_valid = flag_column > 0.5
    column_valid = flag_row > 0.5
    count = jnp.sum(flag_column, axis=0, keepdims=True)

    def forward(tower, values, projection):
        unit_rows, inverse = unit(values)
        z = (
            unit_rows * norm_vector(norms, tower, 4) + norm_vector(norms, tower, 5)
        ).astype(BF)
        raw = dot(z, projection[...])
        scale = lax.rsqrt(jnp.sum(raw * raw, axis=-1, keepdims=True) + UNIT_EPS)
        quotient = raw * scale
        return unit_rows, inverse, z, scale, quotient, quotient.astype(BF)

    image = forward(IMG, yall[:, :D_IMG], pi)
    text = forward(TXT, yall[:, D_IMG:], pt)
    factor = jnp.exp(jnp.full((1, 1), trio[0], F32))
    e_image, e_text = image[5], text[5]

    def side(mine, others):
        logits = factor * dot_nt(mine, others)
        masked = jnp.where(column_valid, logits, MASK_LOW)
        top = jnp.max(masked, axis=1, keepdims=True)
        exponent = jnp.exp(masked - top)
        totals = jnp.sum(exponent, axis=1, keepdims=True)
        own = jnp.sum(jnp.where(eye, logits, 0.0), axis=1, keepdims=True)
        loss = jnp.sum(
            jnp.where(row_valid, top + jnp.log(totals) - own, 0.0), axis=0, keepdims=True
        )
        grad = jnp.where(row_valid, exponent / totals - eye.astype(F32), 0.0) / (2.0 * count)
        scale_part = jnp.sum(jnp.sum(grad * logits, axis=1, keepdims=True), axis=0, keepdims=True)
        return loss, grad, scale_part

    loss_i, grad_i, part_i = side(e_image, e_text)
    loss_t, grad_t, part_t = side(e_text, e_image)
    loss = (loss_i + loss_t) / (2.0 * count)
    slope = part_i + part_t
    misc[...] = jnp.concatenate(
        [
            jnp.broadcast_to(loss, (1, 128)),
            jnp.broadcast_to(slope, (1, 128)),
            jnp.zeros((6, 128), F32),
        ],
        axis=0,
    )

    def product(grad, back, others):
        sums = None
        for part in pieces(grad, 3):
            term = dot(part, others)
            sums = term if sums is None else sums + term
        for part in pieces(back, 3):
            sums = sums + dot_tn(part, others)
        return factor * sums

    def backward(tower, stored, embed_grad, projection, counts, pg, ng, dyb, scratch, own):
        unit_rows, inverse, z, scale, quotient, _ = stored
        raw_grad = (
            scale
            * (embed_grad - quotient * jnp.sum(embed_grad * quotient, axis=-1, keepdims=True))
        ).astype(BF)
        pg[...] = dot_tn(z, raw_grad)
        normed_grad = dot_nt(raw_grad, projection[...])
        ng[0:1, :] = jnp.sum(normed_grad * unit_rows, axis=0, keepdims=True)
        ng[1:2, :] = jnp.sum(normed_grad, axis=0, keepdims=True)
        grad = unit_back(normed_grad, unit_rows, inverse, norm_vector(norms, tower, 4)) / counts
        dyb[...] = grad.astype(BF)
        scratch[...] = grad
        rows = scratch[pl.ds(pl.multiple_of(shard * SEQS, 8), SEQS), :]
        for c in range(MP):
            own[c] = rows[2 * c : 2 * c + 2]

    grad_image = product(grad_i, grad_t, e_text)
    grad_text = product(grad_t, grad_i, e_image)
    backward(
        TXT, text, grad_text, pt, length_column, pg_t, ng_t, dyb_t, scr_t, own_t
    )
    backward(
        IMG, image, grad_image, pi, jnp.full((1, 1), float(IMG_LEN), F32),
        pg_i, ng_i, dyb_i, scr_i, own_i,
    )


def head_call(ids, trio, yall, norms, meta, pi, pt):
    total = yall.shape[0]
    return kernel_call(
        head_body,
        "head",
        [
            out((8, 128)),
            out((total, D_IMG), BF),
            out((total, D_TXT), BF),
            out((MP, 2, D_IMG)),
            out((MP, 2, D_TXT)),
            out((D_IMG, EMBED)),
            out((D_TXT, EMBED)),
            out((2, D_IMG)),
            out((2, D_TXT)),
        ],
        [ids, trio, yall, norms, meta, pi, pt],
        [pltpu.VMEM((total, D_IMG), F32), pltpu.VMEM((total, D_TXT), F32)],
        flops=2 * total * EMBED * (D_IMG + D_TXT) * 3,
    )


def feed_back_body(
    tower, ids, lengths, h_own, h1, h2, h3, slope, dy, w1, w2,
    own, s1, s2, s3, keep, send, h_all, du, grad,
):
    side, m = ids[0], ids[2]
    rows, pad, half = tower.rows, tower.padded, tower.d // 2
    for k, block in enumerate((h_own, h1, h2, h3)):
        h_all[k * rows : (k + 1) * rows, :] = block[...]
    dy_rows = jnp.concatenate([dy[m ^ k] for k in range(MP)], axis=0).astype(BF)
    act = dot_nt(dy_rows, w2[...])
    targets = (own, s1, s2, s3)
    for k in range(MP):
        for j in range(2):
            inside, _ = row_mask(tower, lengths, 2 * (m ^ k) + j)
            start = k * rows + j * pad
            place = 2 * k + j
            piece = slope[start : start + pad, :] * act[place : place + 1, :]
            du[start : start + pad, :] = jnp.where(inside, piece, 0.0).astype(BF)
        part = dot_nt(du[k * rows : (k + 1) * rows, :], w1[...])
        targets[k][...] = part.astype(targets[k].dtype)
    grad[...] = dot_tn(h_all[...], du[...])
    keep[...] = grad[pl.ds(pl.multiple_of(side * half, 8), half), :]
    send[...] = grad[pl.ds(pl.multiple_of((1 - side) * half, 8), half), :].astype(BF)


def feed_back_call(tower, ids, lengths, blocks, slope, dy, w1, w2):
    rows, d, every = tower.rows, tower.d, tower.all_rows
    return kernel_call(
        functools.partial(feed_back_body, tower),
        "feed_back_" + ("txt" if tower is TXT else "img"),
        [
            out((rows, d)),
            out((rows, d), BF),
            out((rows, d), BF),
            out((rows, d), BF),
            out((d // 2, d)),
            out((d // 2, d), BF),
        ],
        [ids, lengths] + blocks + [slope, dy, w1, w2],
        [pltpu.VMEM((every, d), BF), pltpu.VMEM((every, d), BF), pltpu.VMEM((d, d), F32)],
        flops=4 * every * d * d,
    )


def middle_back_body(tower, ids, lengths, norms, x1, dy, own, r1, r2, r3, dx1, dx1b, sums):
    m = ids[2]
    grad = (own[...] + r1[...].astype(F32)) + (r2[...].astype(F32) + r3[...].astype(F32))
    unit_rows, inverse = unit(x1[...])
    sums[0:1, :] = jnp.sum(grad * unit_rows, axis=0, keepdims=True)
    sums[1:2, :] = jnp.sum(grad, axis=0, keepdims=True)
    back = unit_back(grad, unit_rows, inverse, norm_vector(norms, tower, 2))
    rows = dy[m]
    for j in range(2):
        inside, _ = row_mask(tower, lengths, 2 * m + j)
        part = slice(j * tower.padded, (j + 1) * tower.padded)
        total = back[part] + jnp.where(inside, rows[j : j + 1, :], 0.0)
        dx1[part, :] = total
        dx1b[part, :] = total.astype(BF)


def middle_back_call(tower, ids, lengths, norms, x1, dy, own, received):
    rows, d = tower.rows, tower.d
    return kernel_call(
        functools.partial(middle_back_body, tower),
        "middle_back_" + ("txt" if tower is TXT else "img"),
        [out((rows, d)), out((rows, d), BF), out((2, d))],
        [ids, lengths, norms, x1, dy, own] + received,
    )


def attend_back_body(
    tower, d_own, d1, d2, d3, att, qkv, probs, h1, u1, wq, wo,
    own, s1, s2, s3, grads, sums, d_all, dqkv, wide,
):
    rows, d, w, sr = tower.rows, tower.d, tower.w, tower.sr
    tail = d // 8
    for k, block in enumerate((d_own, d1, d2, d3)):
        d_all[k * rows : (k + 1) * rows, :] = block[...]
    targets = (own, s1, s2, s3)
    gain = jnp.zeros((1, d), F32)
    shift = jnp.zeros((1, d), F32)
    for k in range(MP):
        span = slice(k * rows, (k + 1) * rows)
        d_att = dot_nt(d_all[span, :], wo[...]).astype(BF)
        for tile in range(tower.tiles):
            start = k * rows + tile * tower.tile
            part = slice(start, start + tower.tile)
            queries, keys, values = [], [], []
            for h in range(tower.heads):
                query = qkv[part, h * HEAD : (h + 1) * HEAD]
                key = qkv[part, w + h * HEAD : w + (h + 1) * HEAD]
                value = qkv[part, 2 * w + h * HEAD : 2 * w + (h + 1) * HEAD]
                grad = d_att[
                    tile * tower.tile : (tile + 1) * tower.tile, h * HEAD : (h + 1) * HEAD
                ]
                prob = probs[(k * tower.tiles + tile) * tower.heads + h]
                values.append(dot_tn(prob.astype(BF), grad))
                prob_grad = dot_nt(grad, value)
                score = (
                    prob * (prob_grad - jnp.sum(prob * prob_grad, axis=-1, keepdims=True))
                ).astype(BF)
                queries.append(dot(score, key) * HEAD ** (-0.5))
                keys.append(dot_tn(score, query) * HEAD ** (-0.5))
            dqkv[part, :] = jnp.concatenate(queries + keys + values, axis=1).astype(BF)
        back = dot_nt(dqkv[span, :], wq[...])
        gain = gain + jnp.sum(back * u1[span, :], axis=0, keepdims=True)
        shift = shift + jnp.sum(back, axis=0, keepdims=True)
        targets[k][...] = back.astype(targets[k].dtype)
    sums[0:1, :] = gain
    sums[1:2, :] = shift
    wide[...] = dot_tn(h1[...], dqkv[...]).astype(BF)
    for s in range(2):
        base = s * (d // 2)
        rest = wide[base + sr : base + sr + tail, :]
        grads[s * sr : (s + 1) * sr, : 3 * w] = wide[base : base + sr, :]
        grads[s * sr : (s + 1) * sr, 3 * w :] = jnp.concatenate(
            [rest[:, w * i : w * (i + 1)] for i in range(3)], axis=0
        )
    grads[2 * sr :, :] = dot_tn(att[...], d_all[...]).astype(BF)


def attend_back_call(tower, blocks, att, qkv, probs, h1, u1, wq, wo):
    rows, d, w, every = tower.rows, tower.d, tower.w, tower.all_rows
    return kernel_call(
        functools.partial(attend_back_body, tower),
        "attend_back_" + ("txt" if tower is TXT else "img"),
        [
            out((rows, d)),
            out((rows, d), BF),
            out((rows, d), BF),
            out((rows, d), BF),
            out((d, d), BF),
            out((2, d)),
        ],
        blocks + [att, qkv, probs, h1, u1, wq, wo],
        [
            pltpu.VMEM((every, d), BF),
            pltpu.VMEM((every, 3 * w), BF),
            pltpu.VMEM((d, 3 * w), BF),
        ],
        flops=4 * every * d * 4 * w,
    )


def entry_body(tower, norms, xo, dx1, own, r1, r2, r3, dx):
    grad = (own[...] + r1[...].astype(F32)) + (r2[...].astype(F32) + r3[...].astype(F32))
    unit_rows, inverse = unit(xo[...])
    back = unit_back(grad, unit_rows, inverse, norm_vector(norms, tower, 0))
    dx[...] = (dx1[...] + back).astype(BF)


def entry_call(tower, norms, xo, dx1, own, received):
    rows, d = tower.rows, tower.d
    return kernel_call(
        functools.partial(entry_body, tower),
        "entry_" + ("txt" if tower is TXT else "img"),
        [out((rows, d), BF)],
        [norms, xo, dx1, own] + received,
    )[0]


def place_body(tower, ids, own, r1, r2, r3, result, flat):
    m = ids[2]
    for k, block in enumerate((own, r1, r2, r3)):
        for j in range(2):
            seq = 2 * (m ^ k) + j
            part = block[...][j * tower.padded : j * tower.padded + tower.length].astype(F32)
            for i in range(tower.q):
                flat.at[i][pl.ds(seq, tower.length, stride=SEQS), :] = part[
                    :, 128 * i : 128 * (i + 1)
                ]
    for i in range(tower.q):
        result[:, :, 128 * i : 128 * (i + 1)] = flat[i].reshape(tower.length, SEQS, 128)


def place_call(tower, ids, blocks):
    return kernel_call(
        functools.partial(place_body, tower),
        "place_" + ("txt" if tower is TXT else "img"),
        [out((tower.length, SEQS, tower.d))],
        [ids] + blocks,
        [pltpu.VMEM((tower.q, tower.length * SEQS, 128), F32)],
    )[0]


def pack_text(target, start, part):
    target[start : start + 128, : TXT.d] = part[:128]
    target[start : start + 64, TXT.d :] = part[128:, :256]
    target[start + 64 : start + 128, TXT.d :] = part[128:, 256:]


def unpack_text(source, start):
    top = source[start : start + 128, : TXT.d]
    rest = jnp.concatenate(
        [source[start : start + 64, TXT.d :], source[start + 64 : start + 128, TXT.d :]], axis=1
    )
    return jnp.concatenate([top, rest], axis=0)


def feed_split_body(ids, keep_i, recv_i, keep_t, recv_t, own_i, own_t, s1, s2, s3, sum_i, sum_t):
    z = ids[1]
    sum_i[...] = keep_i[...] + recv_i[...].astype(F32)
    sum_t[...] = keep_t[...] + recv_t[...].astype(F32)
    for k, target in enumerate((None, s1, s2, s3)):
        odd = (z ^ k) % 2
        part_i = sum_i[pl.ds(pl.multiple_of(odd * (D_IMG // 8), 8), IMG.sr), :]
        part_t = sum_t[pl.ds(pl.multiple_of(odd * (D_TXT // 8), 8), TXT.sr), :]
        if k == 0:
            own_i[...] = part_i
            own_t[...] = part_t
        else:
            target[: IMG.sr, :] = part_i.astype(BF)
            pack_text(target, IMG.sr, part_t.astype(BF))


def feed_split_call(ids, keep_i, recv_i, keep_t, recv_t):
    payload = out((IMG.sr + 128, 768), BF)
    return kernel_call(
        feed_split_body,
        "feed_split",
        [out((IMG.sr, IMG.d)), out((TXT.sr, TXT.d)), payload, payload, payload],
        [ids, keep_i, recv_i, keep_t, recv_t],
        [pltpu.VMEM((IMG.d // 2, IMG.d), F32), pltpu.VMEM((TXT.d // 2, TXT.d), F32)],
    )


def attend_split_body(tower, ids, mine, received, own, s1, s2, s3, total):
    z = ids[1]
    total[...] = mine[...].astype(F32) + received[...].astype(F32)
    top = tower.d - tower.sr
    for k, target in enumerate((own, s1, s2, s3)):
        start = jnp.minimum((z ^ k) * tower.sr, top)
        part = total[pl.ds(pl.multiple_of(start, 8), tower.sr), :]
        target[...] = part.astype(target.dtype)


def attend_split_call(tower, ids, mine, received):
    payload = out((tower.sr, tower.d), BF)
    return kernel_call(
        functools.partial(attend_split_body, tower),
        "attend_split_" + ("txt" if tower is TXT else "img"),
        [out((tower.sr, tower.d)), payload, payload, payload],
        [ids, mine, received],
        [pltpu.VMEM((tower.d, tower.d), F32)],
    )


def down_body(tower, ids, sums, dyb, result, wide):
    d = tower.d
    tail = d // 8
    wide[:tail, :] = jnp.zeros((tail, d), F32)
    total = None
    for part in pieces(sums[...], 2):
        term = dot_tn(part, dyb[...])
        total = term if total is None else total + term
    wide[tail:, :] = total
    start = jnp.maximum(ids[3] - 5, 0) * tower.sr
    result[...] = wide[pl.ds(pl.multiple_of(start, 8), tower.sr), :]


def down_call(tower, ids, sums, dyb):
    d = tower.d
    return kernel_call(
        functools.partial(down_body, tower),
        "down_" + ("txt" if tower is TXT else "img"),
        [out((tower.sr, d))],
        [ids, sums, dyb],
        [pltpu.VMEM((d + d // 8, d), F32)],
        flops=4 * sums.shape[0] * d * d,
    )[0]


def vector_body(ids, pg_i, pg_t, ng_i, ng_t, window, flat):
    flat[:64, :] = jnp.zeros((64, 128), F32)
    for tower, sums in ((IMG, ng_i), (TXT, ng_t)):
        for i in range(2):
            start = tower.norm_row + (4 + i) * tower.q
            for j in range(tower.q):
                flat[start + j : start + j + 1, :] = sums[i : i + 1, 128 * j : 128 * (j + 1)]
    for j in range(4):
        flat[pl.ds(NORM_ROWS + j, D_IMG, stride=4), :] = pg_i[:, 128 * j : 128 * (j + 1)]
        flat[pl.ds(NORM_ROWS + 4 * D_IMG + j, D_TXT, stride=4), :] = pg_t[
            :, 128 * j : 128 * (j + 1)
        ]
    low_lanes = lax.broadcasted_iota(jnp.int32, (VEC_ROWS, 128), 1) < 64
    last = lax.broadcasted_iota(jnp.int32, (VEC_ROWS, 128), 0) == VEC_ROWS - 1
    for s in range(8):

        def copy(s=s):
            start = (s * (2 * VEC_ROWS - 1)) // 2
            part = flat[start : start + VEC_ROWS, :]
            if s % 2 == 1:
                after = pltpu.roll(flat[start + 1 : start + 1 + VEC_ROWS, :], 64, 1)
                part = jnp.where(low_lanes, pltpu.roll(part, 64, 1), after)
            window[...] = jnp.where(last & jnp.logical_not(low_lanes), 0.0, part)

        pl.when(ids[3] == s)(copy)


def vector_call(ids, pg_i, pg_t, ng_i, ng_t):
    return kernel_call(
        vector_body,
        "vector_window",
        [out((VEC_ROWS, 128))],
        [ids, pg_i, pg_t, ng_i, ng_t],
        [pltpu.VMEM((4 * (2 * VEC_ROWS - 1) + 12, 128), F32)],
    )[0]


def collect_body(
    ids, fa_i, fa_t, fr1, fr2, fr3,
    bi, bi1, bi2, bi3, bt, bt1, bt2, bt3, down_i, down_t, window, norm_sums,
    lin_i, lin_t, vec, squares, rows_i, rows_t, spare,
):
    shard = ids[3]

    @pl.when(shard < 3)
    def _():
        for target, blocks in ((rows_i, (bi, bi1, bi2, bi3)), (rows_t, (bt, bt1, bt2, bt3))):
            target[...] = (blocks[0][...] + blocks[1][...].astype(F32)) + (
                blocks[2][...].astype(F32) + blocks[3][...].astype(F32)
            )

    @pl.when(shard >= 5)
    def _():
        rows_i[...] = down_i[...]
        rows_t[...] = down_t[...]

    @pl.when((shard >= 2) & (shard < 6))
    def _():
        total_i = (fa_i[...] + fr1[: IMG.sr, :].astype(F32)) + (
            fr2[: IMG.sr, :].astype(F32) + fr3[: IMG.sr, :].astype(F32)
        )
        total_t = (fa_t[...] + unpack_text(fr1, IMG.sr).astype(F32)) + (
            unpack_text(fr2, IMG.sr).astype(F32) + unpack_text(fr3, IMG.sr).astype(F32)
        )
        for tower, target, total in ((IMG, rows_i, total_i), (TXT, rows_t, total_t)):
            tail, w = tower.d // 8, tower.w

            @pl.when(shard == 2)
            def _():
                kept = target[tower.sr - w :, :]
                target[:w, :] = kept
                target[w:, :] = total[:tail]

            @pl.when((shard == 3) | (shard == 4))
            def _():
                target[...] = total

            @pl.when(shard == 5)
            def _():
                target[:tail, :] = total[tower.sr - tail :]

    rows_to_lin(IMG, rows_i, lin_i, spare, shard)
    rows_to_lin(TXT, rows_t, lin_t, spare, shard)
    vec[...] = window[...]

    @pl.when(shard == 0)
    def _():
        for tower, first in ((IMG, 0), (TXT, D_IMG)):
            for i in range(4):
                start = tower.norm_row + i * tower.q
                for j in range(tower.q):
                    vec[start + j : start + j + 1, :] = norm_sums[
                        i : i + 1, first + 128 * j : first + 128 * (j + 1)
                    ]

    def total_of(value):
        return jnp.sum(value * value, axis=0, keepdims=True)

    squares[...] = total_of(rows_i[:, :128])
    every = squares[...]
    for j in range(1, IMG.q):
        every = every + total_of(rows_i[:, 128 * j : 128 * (j + 1)])
    for j in range(TXT.q):
        every = every + total_of(rows_t[:, 128 * j : 128 * (j + 1)])
    squares[...] = every + total_of(vec[...]) * (1.0 / MP)


def collect_call(ids, feed, attend_i, attend_t, down_i, down_t, window, norm_sums):
    return kernel_call(
        collect_body,
        "collect",
        [
            out((IMG.lin, 128)),
            out((TXT.lin, 128)),
            out((VEC_ROWS, 128)),
            out((1, 128)),
        ],
        [ids] + feed + attend_i + attend_t + [down_i, down_t, window, norm_sums],
        [
            pltpu.VMEM((IMG.sr, IMG.d), F32),
            pltpu.VMEM((TXT.sr, TXT.d), F32),
            pltpu.VMEM(SPARE, F32),
        ],
    )


def advance_body(
    ids, trio, parts, misc, ip, im, iv, ig, tp, tm, tv, tg, vp, vm, vv, vg,
    scalars, ipn, icn, imn, ivn, tpn, tcn, tmn, tvn, vpn, vcn, vmn, vvn,
):
    slope = misc[1:2, :]
    total = jnp.sum(jnp.sum(parts[...], axis=0, keepdims=True), axis=1, keepdims=True)
    size = jnp.sqrt(total + slope * slope)
    clip = CLIP_LEVEL / jnp.maximum(size, CLIP_LEVEL)

    def step(master, first, second, grad, rate, decay):
        clipped = grad * clip
        first_new = BETA_ONE * first + (1.0 - BETA_ONE) * clipped
        second_new = BETA_TWO * second + (1.0 - BETA_TWO) * clipped * clipped
        update = (first_new * (1.0 / (1.0 - BETA_ONE**STEP))) / (
            jnp.sqrt(second_new * (1.0 / (1.0 - BETA_TWO**STEP))) + ADAM_EPS
        )
        return master - rate * (update + decay * master), first_new, second_new

    for master, first, second, grad, a, b, c, e in (
        (ip, im, iv, ig, ipn, icn, imn, ivn),
        (tp, tm, tv, tg, tpn, tcn, tmn, tvn),
    ):
        new, first_new, second_new = step(
            master[...], first[...], second[...], grad[...], RATE_MATRIX, WEIGHT_DECAY
        )
        a[...] = new
        b[...] = new.astype(BF)
        c[...] = first_new
        e[...] = second_new
    row = lax.broadcasted_iota(jnp.int32, (VEC_ROWS, 128), 0)
    is_norm = row < jnp.where(ids[3] == 0, NORM_ROWS, 0)
    new, first_new, second_new = step(
        vp[...],
        vm[...],
        vv[...],
        vg[...],
        jnp.where(is_norm, RATE_VECTOR, RATE_MATRIX),
        jnp.where(is_norm, 0.0, WEIGHT_DECAY),
    )
    vpn[...] = new
    vcn[...] = new.astype(BF)
    vmn[...] = first_new
    vvn[...] = second_new
    lane_row = jnp.zeros((1, 128), F32)
    new, _, _ = step(
        lane_row + trio[0], lane_row + trio[1], lane_row + trio[2], slope, LOGIT_SPEED, 0.0
    )
    scalars[...] = jnp.concatenate(
        [misc[0:1, :], size, new, jnp.zeros((5, 128), F32)], axis=0
    )


def advance_call(ids, trio, parts, misc, image, text, vector):
    outs = [out((8, 128))]
    for rows in (IMG.lin, TXT.lin, VEC_ROWS):
        outs += [out((rows, 128)), out((rows, 128), BF), out((rows, 128)), out((rows, 128))]
    return kernel_call(
        advance_body, "advance", outs, [ids, trio, parts, misc] + image + text + vector
    )


def hop(value, axis, mask):
    size = lax.axis_size(axis)
    return lax.ppermute(value, axis, [(i, i ^ mask) for i in range(size)])


def peers(values):
    return [hop(value, "mp", k) for k, value in zip((1, 2, 3), values)]


def spread_z(value):
    blocks = [value] + [hop(value, "dp", k) for k in range(1, ZN)]
    mine = jnp.concatenate(blocks, axis=0)
    return mine, hop(mine, "tower", 1)


def merge(value, axis, mask):
    other = hop(value, axis, mask)
    upper = (lax.axis_index(axis) & mask) != 0
    return jnp.where(
        upper, jnp.concatenate([other, value], axis=0), jnp.concatenate([value, other], axis=0)
    )


def feed_perm(mask):
    wanted = ((0, 2), (0, 3), (1, 0), (1, 1))
    return [(t * ZN + (z ^ mask), t * ZN + z) for t, z in wanted]


def attend_perm(mask):
    return [(z ^ mask, z) for z in range(3)]


def fast_local(
    picture_residual_entry,
    sentence_residual_entry,
    sentence_lengths_held,
    couple_allowed_flags,
    picture_single_matrices,
    picture_mean_state,
    picture_square_state,
    sentence_single_matrices,
    sentence_mean_state,
    sentence_square_state,
    array_single_params,
    array_mean_state,
    array_square_state,
    logit_log_trio,
):
    side, z, m = lax.axis_index("tower"), lax.axis_index("dp"), lax.axis_index("mp")
    ids = jnp.stack([side, z, m, side * ZN + z]).astype(jnp.int32)
    lengths = sentence_lengths_held
    vec_size = array_single_params.shape[0]

    def lines(value):
        return value.reshape(-1, 128)

    def vector_lines(value):
        return jnp.pad(value, (0, VEC_ROWS * 128 - vec_size)).reshape(VEC_ROWS, 128)

    vec_lines = vector_lines(array_single_params)
    keep, send, normblock, vecpay = kernel_call(
        prepare_body,
        "prepare",
        [out((COMBINED, 768), BF), out((COMBINED, 768), BF), out((16, 768), BF), out((VEC_ROWS, 128), BF)],
        [
            ids,
            couple_allowed_flags,
            lengths,
            lines(picture_single_matrices),
            lines(sentence_single_matrices),
            vec_lines,
        ],
        [
            pltpu.VMEM((IMG.sr, IMG.d), F32),
            pltpu.VMEM((TXT.sr, TXT.d), F32),
            pltpu.VMEM((VEC_ROWS + 8, 128), F32),
            pltpu.VMEM(SPARE, F32),
        ],
    )
    received = hop(send, "tower", 1)
    urgent_txt, urgent_img, later = kernel_call(
        sort_body,
        "sort",
        [out((URGENT_TXT, 768), BF), out((IMG.half, 768), BF), out((COMBINED, 768), BF)],
        [ids, keep, received, normblock],
    )
    txt_urgent = spread_z(urgent_txt)
    img_urgent = spread_z(urgent_img)
    later_both = spread_z(later)
    gathered = lax.all_gather(vecpay, ("tower", "dp"), axis=0, tiled=False)

    x_txt = jnp.transpose(sentence_residual_entry, (1, 0, 2))
    x_img = jnp.transpose(picture_residual_entry, (1, 0, 2))
    norms, meta, *t_out = attend_call(TXT, ids, x_txt, *txt_urgent)
    i_out = attend_call(IMG, ids, x_img, *img_urgent, norms=norms)
    layers = {}
    for tower, outs in ((TXT, t_out), (IMG, i_out)):
        wq, wo, h1, u1, qkv, att, probs, xo, own, s1, s2, s3 = outs
        layers[tower] = dict(wq=wq, wo=wo, h1=h1, u1=u1, qkv=qkv, att=att, probs=probs, xo=xo)
        x1, h2, pooled = middle_call(tower, ids, lengths, norms, xo, own, peers([s1, s2, s3]))
        blocks = [h2] + peers([h2, h2, h2])
        urgent = txt_urgent if tower is TXT else img_urgent
        w1, w2, slope, sums, ypart = feed_call(
            tower, ids, lengths, blocks, urgent, later_both, pooled
        )
        layers[tower].update(x1=x1, blocks=blocks, w1=w1, w2=w2, slope=slope, sums=sums, y=ypart)

    def joined(key):
        return jnp.concatenate(
            [layers[IMG][key].reshape(SEQS, D_IMG), layers[TXT][key].reshape(SEQS, D_TXT)], axis=1
        )

    y = joined("y")
    y = y + hop(y, "mp", 1)
    y = y + hop(y, "mp", 2)
    held = jnp.concatenate([y, joined("sums")], axis=0)[None]
    held = merge(held, "dp", 1)
    held = merge(held, "dp", 2)
    held = merge(held, "tower", 1)
    yall = held[:, :SEQS].reshape(-1, D_IMG + D_TXT)
    sums_all = held[:, SEQS:].reshape(-1, D_IMG + D_TXT)
    pi, pt = project_call(gathered)
    misc, dyb_i, dyb_t, dy_i, dy_t, pg_i, pg_t, ng_i, ng_t = head_call(
        ids, logit_log_trio, yall, norms, meta, pi, pt
    )

    back = {}
    for tower, dy in ((TXT, dy_t), (IMG, dy_i)):
        s = layers[tower]
        back[tower] = feed_back_call(
            tower, ids, lengths, s["blocks"], s["slope"], dy, s["w1"], s["w2"]
        )
    norm_sums = {}
    entries = {}
    attend_parts = {}
    feed_swapped = {t: hop(back[t][5], "tower", 1) for t in (IMG, TXT)}
    fa_i, fa_t, fs1, fs2, fs3 = feed_split_call(
        ids, back[IMG][4], feed_swapped[IMG], back[TXT][4], feed_swapped[TXT]
    )
    feed_parts = [fa_i, fa_t] + [
        lax.ppermute(value, ("tower", "dp"), feed_perm(k))
        for k, value in ((1, fs1), (2, fs2), (3, fs3))
    ]
    for tower, dy in ((TXT, dy_t), (IMG, dy_i)):
        s = layers[tower]
        own, s1, s2, s3 = back[tower][:4]
        dx1, dx1b, second = middle_back_call(
            tower, ids, lengths, norms, s["x1"], dy, own, peers([s1, s2, s3])
        )
        own, s1, s2, s3, grads, first = attend_back_call(
            tower,
            [dx1b] + peers([dx1b, dx1b, dx1b]),
            s["att"],
            s["qkv"],
            s["probs"],
            s["h1"],
            s["u1"],
            s["wq"],
            s["wo"],
        )
        norm_sums[tower] = jnp.concatenate([first, second], axis=0)
        moved = lax.ppermute(grads, "tower", [(1, 0)])
        pa, p1, p2, p3 = attend_split_call(tower, ids, grads, moved)
        attend_parts[tower] = [pa] + [
            lax.ppermute(value, ("tower", "dp"), attend_perm(k))
            for k, value in ((1, p1), (2, p2), (3, p3))
        ]
        dx = entry_call(tower, norms, s["xo"], dx1, own, peers([s1, s2, s3]))
        entries[tower] = place_call(tower, ids, [dx] + peers([dx, dx, dx]))
    total = jnp.concatenate([norm_sums[IMG], norm_sums[TXT]], axis=1)
    for axis, mask in (("mp", 1), ("mp", 2), ("dp", 1), ("dp", 2), ("tower", 1)):
        total = total + hop(total, axis, mask)
    down_i = down_call(IMG, ids, sums_all[:, :D_IMG], dyb_i)
    down_t = down_call(TXT, ids, sums_all[:, D_IMG:], dyb_t)
    window = vector_call(ids, pg_i, pg_t, ng_i, ng_t)
    lin_i, lin_t, lin_v, squares = collect_call(
        ids, feed_parts, attend_parts[IMG], attend_parts[TXT], down_i, down_t, window, total
    )
    parts = lax.all_to_all(
        jnp.broadcast_to(squares, (2 * ZN * MP, 128)), ("tower", "dp", "mp"), 0, 0, tiled=True
    )
    scalars, *new = advance_call(
        ids,
        logit_log_trio,
        parts,
        misc,
        [lines(picture_single_matrices), lines(picture_mean_state), lines(picture_square_state), lin_i],
        [
            lines(sentence_single_matrices),
            lines(sentence_mean_state),
            lines(sentence_square_state),
            lin_t,
        ],
        [vec_lines, vector_lines(array_mean_state), vector_lines(array_square_state), lin_v],
    )

    def flat(value, like):
        return value.reshape(-1)[: like.size].reshape(like.shape)

    likes = [picture_single_matrices] * 4 + [sentence_single_matrices] * 4 + [array_single_params] * 4
    news = [flat(value, like) for value, like in zip(new, likes)]
    return (
        scalars[0, 0],
        scalars[1, 0],
        jnp.transpose(entries[IMG], (1, 0, 2)),
        jnp.transpose(entries[TXT], (1, 0, 2)),
        *news,
        scalars[2, 0],
    )


def fits(mesh):
    return mesh.shape["tower"] == 2 and mesh.shape["dp"] == ZN and mesh.shape["mp"] == MP


def solution(mesh):
    placed = (
        P(("tower", "dp"), None, None),
        P(("tower", "dp"), None, None),
        P(("tower", "dp")),
        P(("tower", "dp")),
        P("mp", ("tower", "dp")),
        P("mp", ("tower", "dp")),
        P("mp", ("tower", "dp")),
        P("mp", ("tower", "dp")),
        P("mp", ("tower", "dp")),
        P("mp", ("tower", "dp")),
        P(("tower", "dp")),
        P(("tower", "dp")),
        P(("tower", "dp")),
        P(),
    )
    return jax.shard_map(
        fast_local if fits(mesh) else local,
        mesh=mesh,
        in_specs=placed,
        out_specs=(
            P(),
            P(),
            P(("tower", "dp"), None, None),
            P(("tower", "dp"), None, None),
            P("mp", ("tower", "dp")),
            P("mp", ("tower", "dp")),
            P("mp", ("tower", "dp")),
            P("mp", ("tower", "dp")),
            P("mp", ("tower", "dp")),
            P("mp", ("tower", "dp")),
            P("mp", ("tower", "dp")),
            P("mp", ("tower", "dp")),
            P(("tower", "dp")),
            P(("tower", "dp")),
            P(("tower", "dp")),
            P(("tower", "dp")),
            P(),
        ),
        check_vma=False,
    )
```

```python
import functools
import jax
import jax.numpy as jnp
from jax import lax
from jax.experimental import pallas as pl
from jax.experimental.pallas import tpu as pltpu
from jax.sharding import PartitionSpec as P

BF = jnp.bfloat16
F32 = jnp.float32
GROUP = ("tower", "dp")

D_IMG = 768
FF_IMG = 3072
IMG_LEN = 50
D_TXT = 512
FF_TXT = 2048
TXT_LEN = 77
HEAD = 64
EMBED = 512
STEP = 10


NORM_EPS = 1e-05
UNIT_EPS = 1e-06
BETA_ONE = 0.5
BETA_TWO = 0.5
ADAM_EPS = 1e-08
WEIGHT_DECAY = 0.1
RATE_MATRIX = 0.04
RATE_VECTOR = 0.3
LOGIT_SPEED = 0.5
CLIP_LEVEL = 0.005
MASK_LOW = -1e30
GELU_SLOPE = 1.702
BLOCK_TARGET = 512


def branch_sum(partial_sum):
    return lax.psum(partial_sum, "mp")


def branch_back(partial_sum):
    return lax.psum(partial_sum, "mp")


def norm_forward(values, norm_gain, norm_shift):
    centered = values - jnp.mean(values, axis=-1, keepdims=True)
    inverse = lax.rsqrt(jnp.mean(centered * centered, axis=-1, keepdims=True) + NORM_EPS)
    unit_rows = centered * inverse
    return (unit_rows * norm_gain + norm_shift, unit_rows, inverse)


def norm_backward(grad_rows, unit_rows, inverse, norm_gain):
    scaled = grad_rows * norm_gain
    centered_grad = (
        scaled
        - jnp.mean(scaled, axis=-1, keepdims=True)
        - unit_rows * jnp.mean(scaled * unit_rows, axis=-1, keepdims=True)
    )
    return (
        centered_grad * inverse,
        jnp.sum(grad_rows * unit_rows, axis=0),
        jnp.sum(grad_rows, axis=0),
    )


def quick_gelu(values):
    return values * jax.nn.sigmoid(GELU_SLOPE * values)


def gelu_slope(values):
    sigmoid_value = jax.nn.sigmoid(GELU_SLOPE * values)
    return sigmoid_value + GELU_SLOPE * values * sigmoid_value * (1.0 - sigmoid_value)


def block_size(seq_count, seq_length):
    for candidate in range(1, seq_count + 1):
        if seq_count % candidate == 0 and candidate * seq_length >= BLOCK_TARGET:
            return candidate
    return seq_count


def sequence_mask(seq_length, causal):
    position = lax.iota(jnp.int32, seq_length)
    if causal:
        return position[None, :] <= position[:, None]
    return position[None, :] >= 0


def block_scores(block_qkv, allowed):
    scores = jnp.einsum(
        "nqhd,nkhd->nhqk",
        block_qkv[:, :, 0],
        block_qkv[:, :, 1],
        preferred_element_type=jnp.float32,
    ) * HEAD ** (-0.5)
    return jnp.where(allowed[None, None], scores, MASK_LOW)


def attend(packed, seq_count, seq_length, causal):
    head_count = packed.shape[2]
    per_block = block_size(seq_count, seq_length)
    blocks = packed.reshape(seq_count // per_block, per_block, seq_length, 3, head_count, HEAD)
    allowed = sequence_mask(seq_length, causal)

    def one_block(block_qkv):
        scores = block_scores(block_qkv, allowed)
        row_max = jnp.max(scores, axis=-1, keepdims=True)
        exponent = jnp.exp(scores - row_max)
        totals = jnp.sum(exponent, axis=-1, keepdims=True)
        probs = (exponent / totals).astype(jnp.bfloat16)
        result = jnp.einsum(
            "nhqk,nkhd->nqhd", probs, block_qkv[:, :, 2], preferred_element_type=jnp.float32
        ).astype(jnp.bfloat16)
        return (result, (row_max + jnp.log(totals))[..., 0])

    results, log_totals = lax.map(one_block, blocks)
    return (results.reshape(packed.shape[0], head_count * HEAD), log_totals)


def attend_back(packed, attended_grad, log_totals, seq_count, seq_length, causal):
    head_count = packed.shape[2]
    per_block = block_size(seq_count, seq_length)
    block_total = seq_count // per_block
    blocks = packed.reshape(block_total, per_block, seq_length, 3, head_count, HEAD)
    grad_blocks = attended_grad.reshape(block_total, per_block, seq_length, head_count, HEAD)
    allowed = sequence_mask(seq_length, causal)

    def one_block(block_args):
        block_qkv, block_grad, block_totals = block_args
        scores = block_scores(block_qkv, allowed)
        probs = jnp.exp(scores - block_totals[..., None])
        value_grad = jnp.einsum(
            "nhqk,nqhd->nkhd",
            probs.astype(jnp.bfloat16),
            block_grad,
            preferred_element_type=jnp.float32,
        )
        prob_grad = jnp.einsum(
            "nqhd,nkhd->nhqk", block_grad, block_qkv[:, :, 2], preferred_element_type=jnp.float32
        )
        score_grad = (
            probs * (prob_grad - jnp.sum(probs * prob_grad, axis=-1, keepdims=True))
        ).astype(jnp.bfloat16)
        query_grad = jnp.einsum(
            "nhqk,nkhd->nqhd", score_grad, block_qkv[:, :, 1], preferred_element_type=jnp.float32
        ) * HEAD ** (-0.5)
        key_grad = jnp.einsum(
            "nhqk,nqhd->nkhd", score_grad, block_qkv[:, :, 0], preferred_element_type=jnp.float32
        ) * HEAD ** (-0.5)
        return jnp.stack([query_grad, key_grad, value_grad], axis=2).astype(jnp.bfloat16)

    return lax.map(one_block, (blocks, grad_blocks, log_totals)).reshape(packed.shape)


def split_flat(flat_weights, model_width, hidden, model_split):
    width_piece = model_width // model_split
    hidden_piece = hidden // model_split
    first_end = model_width * 3 * width_piece
    second_end = first_end + width_piece * model_width
    third_end = second_end + model_width * hidden_piece
    return (
        flat_weights[:first_end].reshape(model_width, 3, width_piece),
        flat_weights[first_end:second_end].reshape(width_piece, model_width),
        flat_weights[second_end:third_end].reshape(model_width, hidden_piece),
        flat_weights[third_end:].reshape(hidden_piece, model_width),
    )


def layer_forward(tokens, weights, norms, causal):
    qkv_weight, out_weight, up_weight, down_weight = weights
    seq_count, seq_length, model_width = tokens.shape
    token_rows = tokens.reshape(seq_count * seq_length, model_width).astype(jnp.float32)
    first_normed, unit_one, inverse_one = norm_forward(token_rows, norms[0], norms[1])
    first_low = first_normed.astype(jnp.bfloat16)
    packed = jnp.einsum(
        "rd,dtk->rtk", first_low, qkv_weight, preferred_element_type=jnp.float32
    ).astype(jnp.bfloat16)
    packed = packed.reshape(token_rows.shape[0], 3, qkv_weight.shape[2] // HEAD, HEAD)
    attended, log_totals = attend(packed, seq_count, seq_length, causal)
    middle = token_rows + branch_sum(
        jnp.dot(attended, out_weight, preferred_element_type=jnp.float32)
    )
    second_normed, unit_two, inverse_two = norm_forward(middle, norms[2], norms[3])
    second_low = second_normed.astype(jnp.bfloat16)
    pre_act = jnp.dot(second_low, up_weight, preferred_element_type=jnp.float32)
    activated = quick_gelu(pre_act).astype(jnp.bfloat16)
    outputs = middle + branch_sum(
        jnp.dot(activated, down_weight, preferred_element_type=jnp.float32)
    )
    return (
        outputs,
        (
            first_low,
            unit_one,
            inverse_one,
            packed,
            attended,
            log_totals,
            second_low,
            unit_two,
            inverse_two,
            pre_act,
            activated,
        ),
    )


def layer_backward(grad_out, weights, norms, stored, seq_count, seq_length, causal):
    qkv_weight, out_weight, up_weight, down_weight = weights
    (
        first_low,
        unit_one,
        inverse_one,
        packed,
        attended,
        log_totals,
        second_low,
        unit_two,
        inverse_two,
        pre_act,
        activated,
    ) = stored
    grad_low = grad_out.astype(jnp.bfloat16)
    down_grad = jnp.einsum("rf,rd->fd", activated, grad_low, preferred_element_type=jnp.float32)
    act_grad = jnp.einsum("rd,fd->rf", grad_low, down_weight, preferred_element_type=jnp.float32)
    pre_grad = (act_grad * gelu_slope(pre_act)).astype(jnp.bfloat16)
    up_grad = jnp.einsum("rd,rf->df", second_low, pre_grad, preferred_element_type=jnp.float32)
    second_grad = branch_back(
        jnp.einsum("rf,df->rd", pre_grad, up_weight, preferred_element_type=jnp.float32)
    )
    norm_grad_two, gain_two, shift_two = norm_backward(second_grad, unit_two, inverse_two, norms[2])
    middle_grad = grad_out + norm_grad_two
    middle_low = middle_grad.astype(jnp.bfloat16)
    out_grad = jnp.einsum("ra,rd->ad", attended, middle_low, preferred_element_type=jnp.float32)
    attended_grad = jnp.einsum(
        "rd,ad->ra", middle_low, out_weight, preferred_element_type=jnp.float32
    ).astype(jnp.bfloat16)
    packed_grad = attend_back(packed, attended_grad, log_totals, seq_count, seq_length, causal)
    packed_grad = packed_grad.reshape(packed.shape[0], 3, qkv_weight.shape[2])
    qkv_grad = jnp.einsum("rd,rtk->dtk", first_low, packed_grad, preferred_element_type=jnp.float32)
    first_grad = branch_back(
        jnp.einsum("rtk,dtk->rd", packed_grad, qkv_weight, preferred_element_type=jnp.float32)
    )
    norm_grad_one, gain_one, shift_one = norm_backward(first_grad, unit_one, inverse_one, norms[0])
    flat_grads = jnp.concatenate(
        [qkv_grad.reshape(-1), out_grad.reshape(-1), up_grad.reshape(-1), down_grad.reshape(-1)]
    )
    return (middle_grad + norm_grad_one, flat_grads, [gain_one, shift_one, gain_two, shift_two])


def pool_forward(picked, norm_gain, norm_shift, projection):
    normed, unit_rows, inverse = norm_forward(picked, norm_gain, norm_shift)
    normed_low = normed.astype(jnp.bfloat16)
    raw_embed = jnp.dot(normed_low, projection, preferred_element_type=jnp.float32)
    length_inverse = lax.rsqrt(jnp.sum(raw_embed * raw_embed, axis=-1, keepdims=True) + UNIT_EPS)
    embed_rows = raw_embed * length_inverse
    return (
        embed_rows.astype(jnp.bfloat16),
        (unit_rows, inverse, normed_low, embed_rows, length_inverse),
    )


def pool_backward(embed_grad, norm_gain, projection, stored):
    unit_rows, inverse, normed_low, embed_rows, length_inverse = stored
    raw_grad = (
        length_inverse
        * (embed_grad - embed_rows * jnp.sum(embed_grad * embed_rows, axis=-1, keepdims=True))
    ).astype(jnp.bfloat16)
    proj_grad = jnp.einsum("nd,ne->de", normed_low, raw_grad, preferred_element_type=jnp.float32)
    normed_grad = jnp.einsum("ne,de->nd", raw_grad, projection, preferred_element_type=jnp.float32)
    picked_grad, gain_grad, shift_grad = norm_backward(normed_grad, unit_rows, inverse, norm_gain)
    return (picked_grad, proj_grad, gain_grad, shift_grad)


def cosine_logits(picture_feature_lines, sentence_feature_lines, couple_allowed_flags, log_scale):
    image_all, text_all, valid_all = (
        lax.all_gather(picture_feature_lines, GROUP, axis=0, tiled=True),
        lax.all_gather(sentence_feature_lines, GROUP, axis=0, tiled=True),
        lax.all_gather(
            couple_allowed_flags.astype(jnp.bfloat16), GROUP, axis=0, tiled=True
        ),
    )
    count_valid = jnp.sum(valid_all.astype(jnp.float32))
    column_valid = valid_all > 0
    row_valid = couple_allowed_flags > 0
    local_count = picture_feature_lines.shape[0]
    offset_rows = lax.axis_index(GROUP) * local_count
    on_diagonal = (
        lax.iota(jnp.int32, valid_all.shape[0])[None, :]
        == offset_rows + lax.iota(jnp.int32, local_count)[:, None]
    )
    scale_factor = jnp.exp(log_scale)

    def one_side(mine, others):
        logits = scale_factor * jnp.einsum(
            "ne,me->nm", mine, others, preferred_element_type=jnp.float32
        )
        masked = jnp.where(column_valid[None, :], logits, MASK_LOW)
        row_max = jnp.max(masked, axis=1, keepdims=True)
        exponent = jnp.exp(masked - row_max)
        totals = jnp.sum(exponent, axis=1, keepdims=True)
        own_logit = jnp.sum(jnp.where(on_diagonal, logits, 0.0), axis=1)
        log_sum = row_max[:, 0] + jnp.log(totals[:, 0])
        loss_sum = jnp.sum(jnp.where(row_valid, log_sum - own_logit, 0.0))
        logit_grad = jnp.where(
            row_valid[:, None], exponent / totals - on_diagonal.astype(jnp.float32), 0.0
        ) / (2.0 * count_valid)
        return (loss_sum, logit_grad, jnp.sum(logit_grad * logits), log_sum, logits)

    image_loss, image_logit_grad, image_scale_part, image_lse, image_logits = one_side(
        picture_feature_lines, text_all
    )
    text_loss, text_logit_grad, text_scale_part, text_lse, text_logits = one_side(
        sentence_feature_lines, image_all
    )
    picture_device_share = scale_factor * jnp.dot(
        image_logit_grad, text_all.astype(jnp.float32), precision=lax.Precision.HIGHEST
    )
    sentence_device_share = scale_factor * jnp.dot(
        text_logit_grad, image_all.astype(jnp.float32), precision=lax.Precision.HIGHEST
    )
    text_spread = scale_factor * jnp.einsum(
        "np,ne->pe",
        image_logit_grad,
        picture_feature_lines.astype(jnp.float32),
        precision=lax.Precision.HIGHEST,
    )
    image_spread = scale_factor * jnp.einsum(
        "np,ne->pe",
        text_logit_grad,
        sentence_feature_lines.astype(jnp.float32),
        precision=lax.Precision.HIGHEST,
    )
    picture_reverse, sentence_reverse = (
        lax.psum_scatter(image_spread, GROUP, scatter_dimension=0, tiled=True),
        lax.psum_scatter(text_spread, GROUP, scatter_dimension=0, tiled=True),
    )
    contrast_objective, logit_log_slope = lax.psum(
        ((image_loss + text_loss) / (2.0 * count_valid), image_scale_part + text_scale_part),
        GROUP,
    )
    return (
        picture_device_share + picture_reverse,
        sentence_device_share + sentence_reverse,
        contrast_objective,
        logit_log_slope,
    )


def optimizer_advance(master, first, second, grad, rate, decay):
    first_new = BETA_ONE * first + (1.0 - BETA_ONE) * grad
    second_new = BETA_TWO * second + (1.0 - BETA_TWO) * grad * grad
    update = (
        first_new
        / (1.0 - BETA_ONE**STEP)
        / (jnp.sqrt(second_new / (1.0 - BETA_TWO**STEP)) + ADAM_EPS)
    )
    return (master - rate * (update + decay * master), first_new, second_new)


def local(
    picture_residual_entry,
    sentence_residual_entry,
    sentence_lengths_held,
    couple_allowed_flags,
    picture_single_matrices,
    picture_mean_state,
    picture_square_state,
    sentence_single_matrices,
    sentence_mean_state,
    sentence_square_state,
    array_single_params,
    array_mean_state,
    array_square_state,
    logit_log_trio,
):
    model_split = lax.axis_size("mp")
    norm_end = 6 * (D_IMG + D_TXT)
    image_end = norm_end + D_IMG * EMBED
    image_flat, text_flat, vector_flat = (
        lax.all_gather(
            picture_single_matrices.astype(jnp.bfloat16), GROUP, axis=1, tiled=True
        ),
        lax.all_gather(
            sentence_single_matrices.astype(jnp.bfloat16), GROUP, axis=1, tiled=True
        ),
        lax.all_gather(
            array_single_params.astype(jnp.bfloat16), GROUP, axis=0, tiled=True
        ),
    )
    image_norms = vector_flat[: 6 * D_IMG].reshape(6, D_IMG).astype(jnp.float32)
    text_norms = vector_flat[6 * D_IMG : norm_end].reshape(6, D_TXT).astype(jnp.float32)
    image_proj = vector_flat[norm_end:image_end].reshape(D_IMG, EMBED)
    text_proj = vector_flat[image_end:].reshape(D_TXT, EMBED)
    seq_count = picture_residual_entry.shape[0]
    image_weights = split_flat(image_flat[0], D_IMG, FF_IMG, model_split)
    image_out, image_stored = layer_forward(
        picture_residual_entry, image_weights, image_norms, False
    )
    image_picked = jnp.mean(image_out.reshape(seq_count, IMG_LEN, D_IMG), axis=1)
    picture_feature_lines, image_pool = pool_forward(
        image_picked, image_norms[4], image_norms[5], image_proj
    )
    text_weights = split_flat(text_flat[0], D_TXT, FF_TXT, model_split)
    text_out, text_stored = layer_forward(sentence_residual_entry, text_weights, text_norms, True)
    inside = (lax.iota(jnp.int32, TXT_LEN)[None, :] < sentence_lengths_held[:, None]).astype(
        jnp.float32
    )
    picker = inside / sentence_lengths_held[:, None].astype(jnp.float32)
    text_picked = jnp.einsum(
        "nl,nld->nd",
        picker,
        text_out.reshape(seq_count, TXT_LEN, D_TXT),
        precision=lax.Precision.HIGHEST,
    )
    sentence_feature_lines, text_pool = pool_forward(
        text_picked, text_norms[4], text_norms[5], text_proj
    )
    picture_feature_slope, sentence_feature_slope, contrast_objective, logit_log_slope = (
        cosine_logits(
            picture_feature_lines, sentence_feature_lines, couple_allowed_flags, logit_log_trio[0]
        )
    )
    text_picked_grad, text_proj_grad, text_post_gain, text_post_shift = pool_backward(
        sentence_feature_slope, text_norms[4], text_proj, text_pool
    )
    text_rows_grad = (picker[:, :, None] * text_picked_grad[:, None, :]).reshape(
        seq_count * TXT_LEN, D_TXT
    )
    sentence_entry_slope, text_flat_grad, text_norm_grads = layer_backward(
        text_rows_grad, text_weights, text_norms, text_stored, seq_count, TXT_LEN, True
    )
    image_picked_grad, image_proj_grad, image_post_gain, image_post_shift = pool_backward(
        picture_feature_slope, image_norms[4], image_proj, image_pool
    )
    image_rows_grad = jnp.broadcast_to(
        image_picked_grad[:, None, :] / IMG_LEN, (seq_count, IMG_LEN, D_IMG)
    ).reshape(seq_count * IMG_LEN, D_IMG)
    picture_entry_slope, image_flat_grad, image_norm_grads = layer_backward(
        image_rows_grad, image_weights, image_norms, image_stored, seq_count, IMG_LEN, False
    )
    array_param_slope = jnp.concatenate(
        [
            jnp.stack(image_norm_grads + [image_post_gain, image_post_shift]).reshape(-1),
            jnp.stack(text_norm_grads + [text_post_gain, text_post_shift]).reshape(-1),
            image_proj_grad.reshape(-1),
            text_proj_grad.reshape(-1),
        ]
    )
    image_reduced, text_reduced, vector_reduced = (
        lax.psum_scatter(
            image_flat_grad.reshape(-1, D_IMG), GROUP, scatter_dimension=0, tiled=True
        ).reshape(1, -1),
        lax.psum_scatter(
            text_flat_grad.reshape(-1, D_TXT), GROUP, scatter_dimension=0, tiled=True
        ).reshape(1, -1),
        lax.psum_scatter(array_param_slope, GROUP, scatter_dimension=0, tiled=True),
    )
    matrix_squares = jnp.sum(image_reduced * image_reduced) + jnp.sum(text_reduced * text_reduced)
    vector_squares = jnp.sum(vector_reduced * vector_reduced) / model_split
    tensor_square_sum, array_square_sum = lax.psum(
        (matrix_squares, vector_squares), (*GROUP, "mp")
    )
    global_slope_size = jnp.sqrt(
        tensor_square_sum + array_square_sum + logit_log_slope * logit_log_slope
    )
    clipping_factor = CLIP_LEVEL / jnp.maximum(global_slope_size, CLIP_LEVEL)
    picture_matrices_fresh, picture_mean_fresh, picture_square_fresh = optimizer_advance(
        picture_single_matrices,
        picture_mean_state,
        picture_square_state,
        image_reduced * clipping_factor,
        RATE_MATRIX,
        WEIGHT_DECAY,
    )
    sentence_matrices_fresh, sentence_mean_fresh, sentence_square_fresh = optimizer_advance(
        sentence_single_matrices,
        sentence_mean_state,
        sentence_square_state,
        text_reduced * clipping_factor,
        RATE_MATRIX,
        WEIGHT_DECAY,
    )
    shard_length = array_single_params.shape[0]
    vector_index = lax.axis_index(GROUP) * shard_length + lax.iota(
        jnp.int32, shard_length
    )
    is_norm = vector_index < norm_end
    array_params_fresh, array_mean_fresh, array_square_fresh = optimizer_advance(
        array_single_params,
        array_mean_state,
        array_square_state,
        vector_reduced * clipping_factor,
        jnp.where(is_norm, RATE_VECTOR, RATE_MATRIX),
        jnp.where(is_norm, 0.0, WEIGHT_DECAY),
    )
    logit_log_fresh, logit_mean_fresh, logit_square_fresh = optimizer_advance(
        logit_log_trio[0],
        logit_log_trio[1],
        logit_log_trio[2],
        logit_log_slope * clipping_factor,
        LOGIT_SPEED,
        0.0,
    )
    return (
        contrast_objective,
        global_slope_size,
        picture_entry_slope.reshape(picture_residual_entry.shape),
        sentence_entry_slope.reshape(sentence_residual_entry.shape),
        picture_matrices_fresh,
        picture_matrices_fresh.astype(jnp.bfloat16),
        picture_mean_fresh,
        picture_square_fresh,
        sentence_matrices_fresh,
        sentence_matrices_fresh.astype(jnp.bfloat16),
        sentence_mean_fresh,
        sentence_square_fresh,
        array_params_fresh,
        array_params_fresh.astype(jnp.bfloat16),
        array_mean_fresh,
        array_square_fresh,
        logit_log_fresh,
    )


ZN = 4
MP = 4
SEQS = 8


class Tower:
    def __init__(self, tag, width, length, padded, joint, causal, norm_row):
        self.tag = tag
        self.d = width
        self.w = width // MP
        self.heads = self.w // HEAD
        self.length = length
        self.padded = padded
        self.rows = 2 * padded
        self.all_rows = MP * self.rows
        self.tile = self.rows if joint else padded
        self.tiles = self.rows // self.tile
        self.causal = causal
        self.sr = 3 * width // 8
        self.half = self.sr // 2
        self.q = width // 128
        self.norm_row = norm_row
        self.lin = self.sr * self.q


IMG = Tower("_img", D_IMG, IMG_LEN, 56, True, False, 0)
TXT = Tower("_txt", D_TXT, TXT_LEN, 80, False, True, 6 * D_IMG // 128)
NORM_ROWS = 6 * (D_IMG + D_TXT) // 128
VEC_ROWS = 648
HALF = IMG.half + 64
FEED_ROWS = IMG.d // 8 + 48
URGENT = HALF + 16


COST_SCALE = 1.5e9


def kernel_call(body, outs, ins, scratch=(), us=2.0, after=()):
    after = list(after) + LAST

    def spec(value):
        small = value.dtype == jnp.int32 or (value.ndim == 1 and value.shape[0] <= 8)
        return pl.BlockSpec(memory_space=pltpu.SMEM if small else pltpu.VMEM)

    count, late = len(ins), len(after)
    name = getattr(body, "func", body).__name__
    if hasattr(body, "args"):
        name = name + body.args[0].tag
    results = pl.pallas_call(
        lambda *refs: body(*refs[:count], *refs[count + late :]),
        out_shape=list(outs),
        in_specs=[spec(v) for v in ins] + [pl.BlockSpec(memory_space=pl.ANY)] * late,
        out_specs=[pl.BlockSpec(memory_space=pltpu.VMEM)] * len(outs),
        scratch_shapes=list(scratch),
        compiler_params=pltpu.CompilerParams(
            vmem_limit_bytes=VMEM_LIMIT
        ),
        cost_estimate=pl.CostEstimate(
            flops=int(COST_SCALE * us), bytes_accessed=0, transcendentals=0
        ),
        name=name,
    )(*ins, *after)
    LAST[:] = results[:1]
    return results


LAST = []
MIB = 1024 * 1024
VMEM_LIMIT = 62 * MIB


def gate(value, *after):
    anywhere = pl.BlockSpec(memory_space=pl.ANY)
    return pl.pallas_call(
        lambda *refs: None,
        out_shape=out(value.shape, value.dtype),
        in_specs=[anywhere] * (1 + len(after)),
        out_specs=anywhere,
        input_output_aliases={0: 0},
    )(value, *after)


def out(shape, dtype=F32):
    return jax.ShapeDtypeStruct(shape, dtype)


def dot(a, b):
    return lax.dot_general(a, b, (((1,), (0,)), ((), ())), preferred_element_type=F32)


def dot_nt(a, b):
    return lax.dot_general(a, b, (((1,), (1,)), ((), ())), preferred_element_type=F32)


def dot_tn(a, b):
    return lax.dot_general(a, b, (((0,), (0,)), ((), ())), preferred_element_type=F32)


def pieces(a, count):
    parts = []
    for _ in range(count):
        part = a.astype(BF)
        parts.append(part)
        a = a - part.astype(F32)
    return parts


def unit(values):
    width = values.shape[-1]
    centered = values - jnp.sum(values, axis=-1, keepdims=True) * (1.0 / width)
    inverse = lax.rsqrt(
        jnp.sum(centered * centered, axis=-1, keepdims=True) * (1.0 / width) + NORM_EPS
    )
    return centered * inverse, inverse


def unit_back(grad_rows, unit_rows, inverse, gain):
    width = grad_rows.shape[-1]
    scaled = grad_rows * gain
    first = jnp.sum(scaled, axis=-1, keepdims=True) * (1.0 / width)
    second = jnp.sum(scaled * unit_rows, axis=-1, keepdims=True) * (1.0 / width)
    return (scaled - first - unit_rows * second) * inverse


def norm_vector(norms_ref, tower, index):
    start = tower.norm_row + index * tower.q
    return jnp.concatenate([norms_ref[start + i : start + i + 1, :] for i in range(tower.q)], axis=1)


def natural_from_lin(tower, lin_ref, spare):
    d, w = tower.d, tower.w
    if (3 * w) % 128 == 0:
        per = 3 * w // 128
        return jnp.concatenate(
            [lin_ref[pl.ds(i, d // 2, stride=per), :] for i in range(per)], axis=1
        )
    per = 2 * 3 * w // 128
    mid = per // 2
    lines = [lin_ref[pl.ds(i, d // 4, stride=per), :] for i in range(per)]
    empty = jnp.zeros((d // 4, 64), F32)
    even = lines[: mid + 1]
    odd = jnp.concatenate([lines[mid][:, 64:]] + lines[mid + 1 :] + [empty], axis=1)
    for j in range(mid + 1):
        spare.at[j][pl.ds(0, d // 4, stride=2), :] = even[j]
        spare.at[j][pl.ds(1, d // 4, stride=2), :] = odd[:, 128 * j : 128 * (j + 1)]
    return jnp.concatenate([spare[j] for j in range(mid)] + [spare[mid][:, :64]], axis=1)


def natural_to_lin(tower, natural, lin_ref, spare):
    d, w = tower.d, tower.w
    if (3 * w) % 128 == 0:
        per = 3 * w // 128
        for i in range(per):
            lin_ref[pl.ds(i, d // 2, stride=per), :] = natural[:, 128 * i : 128 * (i + 1)]
        return
    per = 2 * 3 * w // 128
    mid = per // 2
    for j in range(mid):
        spare[j] = natural[:, 128 * j : 128 * (j + 1)]
    spare[mid] = jnp.concatenate([natural[:, 128 * mid :], jnp.zeros((d // 2, 64), F32)], axis=1)
    even = [spare.at[j][pl.ds(0, d // 4, stride=2), :] for j in range(mid + 1)]
    odd = jnp.concatenate(
        [spare.at[j][pl.ds(1, d // 4, stride=2), :] for j in range(mid + 1)], axis=1
    )
    for i in range(mid):
        lin_ref[pl.ds(i, d // 4, stride=per), :] = even[i]
    lin_ref[pl.ds(mid, d // 4, stride=per), :] = jnp.concatenate(
        [even[mid][:, :64], odd[:, :64]], axis=1
    )
    for i in range(mid):
        lin_ref[pl.ds(mid + 1 + i, d // 4, stride=per), :] = odd[:, 64 + 128 * i : 192 + 128 * i]


def lin_to_rows(tower, lin_ref, rows_ref, spare, shard):
    d, w, sr, q = tower.d, tower.w, tower.sr, tower.q

    @pl.when(shard >= 2)
    def _():
        for j in range(q):
            rows_ref[:, 128 * j : 128 * (j + 1)] = lin_ref[pl.ds(j, sr, stride=q), :]

    @pl.when(shard < 2)
    def _():
        tail = d // 8
        natural = natural_from_lin(tower, lin_ref, spare)
        rows_ref[:, : 3 * w] = natural[:sr]
        for i in range(3):
            rows_ref[tail * i : tail * (i + 1), 3 * w :] = natural[sr:, w * i : w * (i + 1)]


def rows_to_lin(tower, rows_ref, lin_ref, spare, shard):
    d, w, sr, q = tower.d, tower.w, tower.sr, tower.q

    @pl.when(shard >= 2)
    def _():
        for j in range(q):
            lin_ref[pl.ds(j, sr, stride=q), :] = rows_ref[:, 128 * j : 128 * (j + 1)]

    @pl.when(shard < 2)
    def _():
        tail = d // 8
        rest = jnp.concatenate(
            [rows_ref[tail * i : tail * (i + 1), 3 * w :] for i in range(3)], axis=1
        )
        natural = jnp.concatenate([rows_ref[:, : 3 * w], rest], axis=0)
        natural_to_lin(tower, natural, lin_ref, spare)


SPARE = ((3 * IMG.w + 127) // 128, IMG.d // 2, 128)


def prepare_body(
    ids, flags, lengths, img, txt, head, keep_t, keep_i, send_t, send_i, block, rows_i, rows_t, spare
):
    side, shard = ids[0], ids[3]
    lin_to_rows(IMG, img, rows_i, spare, shard)
    lin_to_rows(TXT, txt, rows_t, spare, shard)
    lane = lax.broadcasted_iota(jnp.int32, (1, 128), 1)
    flag_row = jnp.zeros((1, 128), F32)
    length_row = jnp.zeros((1, 128), F32)
    for i in range(SEQS):
        flag_row = jnp.where(lane == i, jnp.where(flags[i] > 0, 1.0, 0.0), flag_row)
        length_row = jnp.where(lane == i, lengths[i].astype(F32), length_row)
    lines = jnp.concatenate(
        [head[...], flag_row, length_row, jnp.zeros((64 - NORM_ROWS - 2, 128), F32)], axis=0
    )
    for j in range(4):
        block[:, 128 * j : 128 * (j + 1)] = lines[16 * j : 16 * (j + 1)].astype(BF)
    for tower, rows, keep, send in ((TXT, rows_t, keep_t, send_t), (IMG, rows_i, keep_i, send_i)):
        for target, which in ((keep, side), (send, 1 - side)):
            target[...] = rows[
                pl.ds(pl.multiple_of(which * tower.half, 8), tower.half), :
            ].astype(BF)


def sort_body(ids, keep_t, keep_i, got_t, got_i, block, urgent, late):
    def fill(*halves):
        for target, part_t, part_i in ((urgent, *halves[:2]), (late, *halves[2:])):
            target[: IMG.half, :] = part_i[...]
            target[IMG.half : HALF, : TXT.d] = part_t[:64, :]
            target[IMG.half : IMG.half + 32, TXT.d :] = part_t[64:, :256]
            target[IMG.half + 32 : HALF, TXT.d :] = part_t[64:, 256:]

    pl.when(ids[0] == 0)(lambda: fill(keep_t, keep_i, got_t, got_i))
    pl.when(ids[0] != 0)(lambda: fill(got_t, got_i, keep_t, keep_i))
    urgent[HALF:, : TXT.d] = block[...]
    urgent[HALF:, TXT.d :] = jnp.zeros((16, IMG.d - TXT.d), BF)


def vector_pay_body(ids, vec, vecpay, shifted):
    odd = ids[3] % 2

    @pl.when(odd == 0)
    def _():
        vecpay[...] = vec[...].astype(BF)

    @pl.when(odd == 1)
    def _():
        rolled = pltpu.roll(vec[...], 64, 1)
        shifted[0:8, :] = jnp.zeros((8, 128), F32)
        shifted[8 : 8 + VEC_ROWS, :] = rolled
        before = shifted[7 : 7 + VEC_ROWS, :]
        low_lanes = lax.broadcasted_iota(jnp.int32, (VEC_ROWS, 128), 1) < 64
        vecpay[...] = jnp.where(low_lanes, before, rolled).astype(BF)


def with_halves(blocks, side, z, shard, use):
    if len(blocks) == 2:
        rows = blocks[0].shape[0] // ZN
        mine, other = [block.at[pl.ds(shard * rows, rows)] for block in blocks]
        pl.when(side == 0)(lambda: use(mine, other))
        pl.when(side != 0)(lambda: use(other, mine))
        return
    for k in range(ZN):
        mine, other = blocks[k], blocks[ZN + k]
        here = (z ^ shard) == k
        pl.when(here & (side == 0))(functools.partial(use, mine, other))
        pl.when(here & (side != 0))(functools.partial(use, other, mine))


def half_rows(tower, first, second):
    if tower is IMG:
        return jnp.concatenate([first[: IMG.half, :], second[: IMG.half, :]], axis=0)
    parts = []
    for half in (first, second):
        parts += [
            half[IMG.half : HALF, : TXT.d],
            half[IMG.half : IMG.half + 32, TXT.d :],
            half[IMG.half + 32 : HALF, TXT.d :],
        ]
    return jnp.concatenate(
        [
            parts[0],
            jnp.concatenate([parts[1], parts[2]], axis=1),
            parts[3],
            jnp.concatenate([parts[4], parts[5]], axis=1),
        ],
        axis=0,
    )


def attention_mask(tower):
    shape = (tower.tile, tower.tile)
    row = lax.broadcasted_iota(jnp.int32, shape, 0)
    column = lax.broadcasted_iota(jnp.int32, shape, 1)
    if tower.causal:
        return (column <= row) & (column < tower.length)
    pad = tower.padded
    first = (row < pad) & (column < tower.length)
    second = (row >= pad) & (column >= pad) & (column < pad + tower.length)
    return first | second


def read_meta(meta, blocks, side, z):
    for place in range(ZN):

        def use(*halves, place=place):
            for half, block in enumerate(halves):
                lines = block[HALF:, 384:512].astype(F32)
                line = half * ZN + place
                meta[line : line + 1, :] = lines[12:13]
                meta[8 + line : 9 + line, :] = lines[13:14]

        with_halves(blocks, side, z, place, use)


def attend_body(tower, ids, x, *rest):
    count = 2 * ZN
    blocks, rest = rest[:count], rest[count:]
    if tower is TXT:
        (norms, meta, wq, wo, h1, u1, qkv, att, probs, xo, own, s1, s2, s3, xf, xs) = rest
    else:
        norms = rest[0]
        (wq, wo, h1, u1, qkv, att, probs, xo, own, s1, s2, s3, xf, xs) = rest[1:]
    side, z, m = ids[0], ids[1], ids[2]
    d, w, sr = tower.d, tower.w, tower.sr
    if tower is TXT:

        def read_norms(block, _):
            for j in range(4):
                norms[16 * j : 16 * (j + 1), :] = block[HALF:, 128 * j : 128 * (j + 1)].astype(F32)

        with_halves(blocks, side, z, 0, read_norms)
        read_meta(meta, blocks, side, z)

    tail = d // 8
    for s in range(2):

        def read_qkv(first, second, base=s * (d // 2)):
            part = half_rows(tower, first, second)
            wq[base : base + sr, :] = part[:, : 3 * w]
            wq[base + sr : base + sr + tail, :] = jnp.concatenate(
                [part[tail * i : tail * (i + 1), 3 * w :] for i in range(3)], axis=1
            )

        with_halves(blocks, side, z, s, read_qkv)

    def read_out(first, second):
        wo[...] = half_rows(tower, first, second)[:w]

    with_halves(blocks, side, z, 2, read_out)
    for j in range(tower.q):
        xf[j] = x[:, :, 128 * j : 128 * (j + 1)].astype(F32).reshape(tower.length * SEQS, 128)
    pad = tower.padded - tower.length
    for k in range(MP):
        for j in range(2):
            start = k * tower.rows + j * tower.padded
            seq = 2 * (m ^ k) + j
            for i in range(tower.q):
                xs[start : start + tower.length, 128 * i : 128 * (i + 1)] = xf.at[i][
                    pl.ds(seq, tower.length, stride=SEQS), :
                ]
            xs[start + tower.length : start + tower.padded, :] = jnp.zeros((pad, d), F32)
    xo[...] = xs[: tower.rows, :]
    unit_rows, _ = unit(xs[...])
    u1[...] = unit_rows.astype(BF)
    h1[...] = (
        unit_rows * norm_vector(norms, tower, 0) + norm_vector(norms, tower, 1)
    ).astype(BF)
    qkv[...] = dot(h1[...], wq[...]).astype(BF)
    allowed = attention_mask(tower)
    targets = (own, s1, s2, s3)
    for k in range(MP):
        for tile in range(tower.tiles):
            start = k * tower.rows + tile * tower.tile
            rows = slice(start, start + tower.tile)
            heads = []
            for h in range(tower.heads):
                query = qkv[rows, h * HEAD : (h + 1) * HEAD]
                key = qkv[rows, w + h * HEAD : w + (h + 1) * HEAD]
                value = qkv[rows, 2 * w + h * HEAD : 2 * w + (h + 1) * HEAD]
                scores = jnp.where(allowed, dot_nt(query, key) * HEAD ** (-0.5), MASK_LOW)
                exponent = jnp.exp(scores - jnp.max(scores, axis=-1, keepdims=True))
                prob = exponent / jnp.sum(exponent, axis=-1, keepdims=True)
                probs[(k * tower.tiles + tile) * tower.heads + h] = prob
                heads.append(dot(prob.astype(BF), value))
            att[rows, :] = jnp.concatenate(heads, axis=1).astype(BF)
        rows = slice(k * tower.rows, (k + 1) * tower.rows)
        part = dot(att[rows, :], wo[...])
        targets[k][...] = part.astype(targets[k].dtype)


def attend_call(tower, ids, x, blocks, norms=None, after=()):
    d, w, rows, every = tower.d, tower.w, tower.rows, tower.all_rows
    outs = [
        out((d, 3 * w), BF),
        out((w, d), BF),
        out((every, d), BF),
        out((every, d), BF),
        out((every, 3 * w), BF),
        out((every, w), BF),
        out((MP * tower.tiles * tower.heads, tower.tile, tower.tile)),
        out((rows, d)),
        out((rows, d)),
        out((rows, d), BF),
        out((rows, d), BF),
        out((rows, d), BF),
    ]
    ins = [ids, x] + blocks
    if tower is TXT:
        outs = [out((64, 128)), out((16, 128))] + outs
    else:
        ins.append(norms)
    return kernel_call(
        functools.partial(attend_body, tower),
        outs,
        ins,
        [
            pltpu.VMEM((tower.q, tower.length * SEQS, 128), F32),
            pltpu.VMEM((every, d), F32),
        ],
        after=after,
        us=7.2,
    )


def row_mask(tower, lengths, pair):
    position = lax.broadcasted_iota(jnp.int32, (tower.padded, 1), 0)
    count = lengths[pair] if tower.causal else tower.length
    return position < count, count


def middle_body(tower, ids, lengths, norms, xo, own, r1, r2, r3, x1, h2, pooled):
    m = ids[2]
    total = xo[...] + ((own[...] + r1[...].astype(F32)) + (r2[...].astype(F32) + r3[...].astype(F32)))
    x1[...] = total
    unit_rows, _ = unit(total)
    h2[...] = (
        unit_rows * norm_vector(norms, tower, 2) + norm_vector(norms, tower, 3)
    ).astype(BF)
    for j in range(2):
        inside, count = row_mask(tower, lengths, 2 * m + j)
        part = total[j * tower.padded : (j + 1) * tower.padded]
        summed = jnp.sum(jnp.where(inside, part, 0.0), axis=0, keepdims=True)
        pooled[j : j + 1, :] = summed / jnp.full((1, 1), count, F32)


def middle_call(tower, ids, lengths, norms, xo, own, received):
    rows, d = tower.rows, tower.d
    return kernel_call(
        functools.partial(middle_body, tower),
        [out((rows, d)), out((rows, d), BF), out((2, d))],
        [ids, lengths, norms, xo, own] + received,
    )


def feed_body(tower, ids, lengths, h_own, h1, h2, h3, *rest):
    count = 2 * ZN
    urgent, late, rest = rest[:count], rest[count : count + 2], rest[count + 2 :]
    if tower is TXT:
        pooled, w1, w2, slope, sums, ypart = rest
    else:
        pooled, y_txt, sums_txt, w1, w2, slope, sums, ypart = rest
    side, z, m = ids[0], ids[1], ids[2]
    d, w, sr = tower.d, tower.w, tower.sr
    tail = d // 8

    def read(target, start, skip, count):
        def use(first, second):
            part = half_rows(tower, first, second)
            target[start : start + count, :] = part[skip : skip + count]

        return use

    def read_both(first, second):
        part = half_rows(tower, first, second)
        w1[tail + 2 * sr :, :] = part[:tail]
        w2[:w, :] = part[tail:]

    with_halves(urgent, side, z, 2, read(w1, 0, w, tail))
    with_halves(urgent, side, z, 3, read(w1, tail, 0, sr))
    with_halves(late, side, z, 0, read(w1, tail + sr, 0, sr))
    with_halves(late, side, z, 1, read_both)
    with_halves(late, side, z, 2, read(w2, w, 0, sr))
    with_halves(late, side, z, 3, read(w2, w + sr, 0, sr))
    sums_places, y_places = [], []
    for k, block in enumerate((h_own, h1, h2, h3)):
        pre = dot(block[...], w1[...])
        gate = jax.nn.sigmoid(GELU_SLOPE * pre)
        acted = (pre * gate).astype(BF).astype(F32)
        slope[k * tower.rows : (k + 1) * tower.rows, :] = gate + GELU_SLOPE * pre * gate * (
            1.0 - gate
        )
        summed = []
        counts = []
        for j in range(2):
            inside, count = row_mask(tower, lengths, 2 * (m ^ k) + j)
            part = acted[j * tower.padded : (j + 1) * tower.padded]
            summed.append(jnp.sum(jnp.where(inside, part, 0.0), axis=0, keepdims=True))
            counts.append(jnp.full((1, 1), count, F32))
        both = jnp.concatenate(summed, axis=0)
        sums_places.append(both)
        high, low, rest = pieces(both, 3)
        y = dot(high, w2[...]) + (dot(low, w2[...]) + dot(rest, w2[...]))
        y = y / jnp.concatenate(counts, axis=0)
        if k == 0:
            y = y + pooled[...]
        y_places.append(y)

    def in_order(places):
        def chunk(c):
            value = places[c ^ 3]
            for member in range(3):
                value = jnp.where(m == member, places[c ^ member], value)
            return value

        return jnp.concatenate([chunk(c) for c in range(MP)], axis=0)

    if tower is TXT:
        sums[...] = in_order(sums_places)
        ypart[...] = in_order(y_places)
    else:
        sums[:, :d] = in_order(sums_places)
        sums[:, d:] = sums_txt[...]
        ypart[:, :d] = in_order(y_places)
        ypart[:, d:] = y_txt[...]


def feed_call(tower, ids, lengths, blocks, urgent, late, pooled, before=()):
    d = tower.d
    wide = d if tower is TXT else D_IMG + D_TXT
    return kernel_call(
        functools.partial(feed_body, tower),
        [
            out((d, d), BF),
            out((d, d), BF),
            out((tower.all_rows, d)),
            out((SEQS, wide)),
            out((SEQS, wide)),
        ],
        [ids, lengths] + blocks + urgent + late + [pooled] + list(before),
        us=6.4,
    )


def project_body(gathered, pi, pt, flat):
    for e in range(4):
        base = e * (2 * VEC_ROWS - 1)
        flat[base : base + VEC_ROWS, :] = gathered[2 * e].astype(F32)
        odd = gathered[2 * e + 1].astype(F32)
        row = base + VEC_ROWS - 1
        flat[row : row + 1, :] = flat[row : row + 1, :] + odd[:1]
        flat[row + 1 : row + VEC_ROWS, :] = odd[1:]
    for j in range(4):
        pi[:, 128 * j : 128 * (j + 1)] = flat[pl.ds(NORM_ROWS + j, D_IMG, stride=4), :].astype(BF)
        pt[:, 128 * j : 128 * (j + 1)] = flat[
            pl.ds(NORM_ROWS + 4 * D_IMG + j, D_TXT, stride=4), :
        ].astype(BF)


def project_call(gathered):
    return kernel_call(
        project_body,
        [out((D_IMG, EMBED), BF), out((D_TXT, EMBED), BF)],
        [gathered],
        [pltpu.VMEM((4 * (2 * VEC_ROWS - 1) + 4, 128), F32)],
        us=2.8,
    )


def head_body(
    ids, trio, yall, norms, meta, pi, pt,
    misc, dyb_i, dyb_t, own_i, own_t, pg_i, pg_t, ng_i, ng_t, scr_i, scr_t,
):
    shard = ids[3]
    total = yall.shape[0]
    row = lax.broadcasted_iota(jnp.int32, (total, total), 0)
    column = lax.broadcasted_iota(jnp.int32, (total, total), 1)
    eye = row == column
    place = lax.broadcasted_iota(jnp.int32, (total, 128), 0)
    lane = lax.broadcasted_iota(jnp.int32, (total, 128), 1)

    def column_of(first):
        picked = jnp.zeros((total, 128), F32)
        for s in range(2 * ZN):
            picked = jnp.where(place // SEQS == s, meta[first + s : first + s + 1, :], picked)
        return jnp.sum(jnp.where(lane == place % SEQS, picked, 0.0), axis=1, keepdims=True)

    flag_column = column_of(0)
    length_column = column_of(8)
    flag_row = jnp.sum(jnp.where(eye, flag_column, 0.0), axis=0, keepdims=True)
    row_valid = flag_column > 0.5
    column_valid = flag_row > 0.5
    count = jnp.sum(flag_column, axis=0, keepdims=True)

    def forward(tower, values, projection):
        unit_rows, inverse = unit(values)
        z = (
            unit_rows * norm_vector(norms, tower, 4) + norm_vector(norms, tower, 5)
        ).astype(BF)
        raw = dot(z, projection[...])
        scale = lax.rsqrt(jnp.sum(raw * raw, axis=-1, keepdims=True) + UNIT_EPS)
        quotient = raw * scale
        return unit_rows, inverse, z, scale, quotient, quotient.astype(BF)

    image = forward(IMG, yall[:, :D_IMG], pi)
    text = forward(TXT, yall[:, D_IMG:], pt)
    factor = jnp.exp(jnp.full((1, 1), trio[0], F32))
    e_image, e_text = image[5], text[5]

    def side(mine, others):
        logits = factor * dot_nt(mine, others)
        masked = jnp.where(column_valid, logits, MASK_LOW)
        top = jnp.max(masked, axis=1, keepdims=True)
        exponent = jnp.exp(masked - top)
        totals = jnp.sum(exponent, axis=1, keepdims=True)
        own = jnp.sum(jnp.where(eye, logits, 0.0), axis=1, keepdims=True)
        loss = jnp.sum(
            jnp.where(row_valid, top + jnp.log(totals) - own, 0.0), axis=0, keepdims=True
        )
        grad = jnp.where(row_valid, exponent / totals - eye.astype(F32), 0.0) / (2.0 * count)
        scale_part = jnp.sum(jnp.sum(grad * logits, axis=1, keepdims=True), axis=0, keepdims=True)
        return loss, grad, scale_part

    loss_i, grad_i, part_i = side(e_image, e_text)
    loss_t, grad_t, part_t = side(e_text, e_image)
    loss = (loss_i + loss_t) / (2.0 * count)
    slope = part_i + part_t
    misc[...] = jnp.concatenate(
        [
            jnp.broadcast_to(loss, (1, 128)),
            jnp.broadcast_to(slope, (1, 128)),
            jnp.zeros((6, 128), F32),
        ],
        axis=0,
    )

    def product(grad, back, others):
        sums = None
        for part in pieces(grad, 3):
            term = dot(part, others)
            sums = term if sums is None else sums + term
        for part in pieces(back, 3):
            sums = sums + dot_tn(part, others)
        return factor * sums

    def backward(tower, stored, embed_grad, projection, counts, pg, ng, dyb, scratch, own):
        unit_rows, inverse, z, scale, quotient, _ = stored
        raw_grad = (
            scale
            * (embed_grad - quotient * jnp.sum(embed_grad * quotient, axis=-1, keepdims=True))
        ).astype(BF)
        pg[...] = dot_tn(z, raw_grad)
        normed_grad = dot_nt(raw_grad, projection[...])
        ng[0:1, :] = jnp.sum(normed_grad * unit_rows, axis=0, keepdims=True)
        ng[1:2, :] = jnp.sum(normed_grad, axis=0, keepdims=True)
        grad = unit_back(normed_grad, unit_rows, inverse, norm_vector(norms, tower, 4)) / counts
        dyb[...] = grad.astype(BF)
        scratch[...] = grad
        rows = scratch[pl.ds(pl.multiple_of(shard * SEQS, 8), SEQS), :]
        for c in range(MP):
            own[c] = rows[2 * c : 2 * c + 2]

    grad_image = product(grad_i, grad_t, e_text)
    grad_text = product(grad_t, grad_i, e_image)
    backward(
        TXT, text, grad_text, pt, length_column, pg_t, ng_t, dyb_t, scr_t, own_t
    )
    backward(
        IMG, image, grad_image, pi, jnp.full((1, 1), float(IMG_LEN), F32),
        pg_i, ng_i, dyb_i, scr_i, own_i,
    )


def head_call(ids, trio, yall, norms, meta, pi, pt):
    total = yall.shape[0]
    return kernel_call(
        head_body,
        [
            out((8, 128)),
            out((total, D_IMG), BF),
            out((total, D_TXT), BF),
            out((MP, 2, D_IMG)),
            out((MP, 2, D_TXT)),
            out((D_IMG, EMBED)),
            out((D_TXT, EMBED)),
            out((2, D_IMG)),
            out((2, D_TXT)),
        ],
        [ids, trio, yall, norms, meta, pi, pt],
        [pltpu.VMEM((total, D_IMG), F32), pltpu.VMEM((total, D_TXT), F32)],
        us=5.0,
    )


def feed_back_body(
    tower, ids, lengths, h_own, h1, h2, h3, slope, dy, w1, w2, *rest
):
    if tower is TXT:
        grad_i, own, s1, s2, s3, payload, h_all, du = rest
    else:
        own, s1, s2, s3, grads, h_all, du = rest
    m = ids[2]
    rows, pad = tower.rows, tower.padded
    for k, block in enumerate((h_own, h1, h2, h3)):
        h_all[k * rows : (k + 1) * rows, :] = block[...]
    dy_rows = jnp.concatenate([dy[m ^ k] for k in range(MP)], axis=0).astype(BF)
    act = dot_nt(dy_rows, w2[...])
    targets = (own, s1, s2, s3)
    for k in range(MP):
        for j in range(2):
            inside, _ = row_mask(tower, lengths, 2 * (m ^ k) + j)
            start = k * rows + j * pad
            place = 2 * k + j
            piece = slope[start : start + pad, :] * act[place : place + 1, :]
            du[start : start + pad, :] = jnp.where(inside, piece, 0.0).astype(BF)
        part = dot_nt(du[k * rows : (k + 1) * rows, :], w1[...])
        targets[k][...] = part.astype(targets[k].dtype)
    grad = dot_tn(h_all[...], du[...]).astype(BF)
    if tower is IMG:
        grads[...] = grad
        return
    rows_i, rows_t = IMG.d // 8, TXT.d // 8
    for place, e in enumerate(FEED_ORDER):
        payload[place, :rows_i, :] = grad_i[rows_i * e : rows_i * (e + 1), :]
        part = grad[rows_t * e : rows_t * (e + 1)]
        top = FEED_ROWS - rows_i
        payload[place, rows_i:, : TXT.d] = part[:top]
        payload[place, rows_i : rows_i + 16, TXT.d :] = part[top:, :256]
        payload[place, rows_i + 16 : rows_i + 32, TXT.d :] = part[top:, 256:]
        payload[place, rows_i + 32 :, TXT.d :] = jnp.zeros((top - 32, IMG.d - TXT.d), BF)


def feed_back_call(tower, ids, lengths, blocks, slope, dy, w1, w2, grads, after=()):
    rows, d, every = tower.rows, tower.d, tower.all_rows
    return kernel_call(
        functools.partial(feed_back_body, tower),
        [
            out((rows, d)),
            out((rows, d), BF),
            out((rows, d), BF),
            out((rows, d), BF),
            out((d, d), BF) if tower is IMG else out((2 * ZN, FEED_ROWS, IMG.d), BF),
        ],
        [ids, lengths] + blocks + [slope, dy, w1, w2] + grads,
        [pltpu.VMEM((every, d), BF), pltpu.VMEM((every, d), BF)],
        after=after,
        us=5.3,
    )


def middle_back_body(tower, ids, lengths, norms, x1, dy, own, r1, r2, r3, dx1, dx1b):
    m = ids[2]
    grad = (own[...] + r1[...].astype(F32)) + (r2[...].astype(F32) + r3[...].astype(F32))
    unit_rows, inverse = unit(x1[...])
    extra = (
        jnp.sum(grad * unit_rows, axis=0, keepdims=True),
        jnp.sum(grad, axis=0, keepdims=True),
    )
    back = unit_back(grad, unit_rows, inverse, norm_vector(norms, tower, 2))
    rows = dy[m]
    position = lax.broadcasted_iota(jnp.int32, (tower.padded, 1), 0)
    for j in range(2):
        inside, _ = row_mask(tower, lengths, 2 * m + j)
        part = slice(j * tower.padded, (j + 1) * tower.padded)
        total = back[part] + jnp.where(inside, rows[j : j + 1, :], 0.0)
        dx1[part, :] = total
        high, low = [piece.astype(F32) for piece in pieces(extra[j], 2)]
        total = jnp.where(position == tower.length, high, total)
        total = jnp.where(position == tower.length + 1, low, total)
        dx1b[part, :] = total.astype(BF)


def middle_back_call(tower, ids, lengths, norms, x1, dy, own, received, after=()):
    rows, d = tower.rows, tower.d
    return kernel_call(
        functools.partial(middle_back_body, tower),
        [out((rows, d)), out((rows, d), BF)],
        [ids, lengths, norms, x1, dy, own] + received,
        after=after,
    )


def attend_back_body(
    tower, ids, d_own, d1, d2, d3, att, qkv, probs, h1, u1, wq, wo,
    own, s1, s2, s3, *rest
):
    grads, sums, d_all, dqkv, wide, backs = rest
    rows, d, w, sr = tower.rows, tower.d, tower.w, tower.sr
    tail = d // 8
    position = lax.broadcasted_iota(jnp.int32, (tower.padded, 1), 0)
    extra = [[], []]
    for k, block in enumerate((d_own, d1, d2, d3)):
        for j in range(2):
            start = j * tower.padded
            part = block[start : start + tower.padded, :].astype(F32)
            line = tower.length
            extra[j].append(part[line : line + 1] + part[line + 1 : line + 2])
            d_all[k * rows + start : k * rows + start + tower.padded, :] = jnp.where(
                position < line, part, 0.0
            ).astype(BF)
    for j in range(2):
        sums[j : j + 1, :] = (extra[j][0] + extra[j][1]) + (extra[j][2] + extra[j][3])
    targets = (own, s1, s2, s3)
    gain = jnp.zeros((1, d), F32)
    shift = jnp.zeros((1, d), F32)
    for k in range(MP):
        span = slice(k * rows, (k + 1) * rows)
        d_att = dot_nt(d_all[span, :], wo[...]).astype(BF)
        for tile in range(tower.tiles):
            start = k * rows + tile * tower.tile
            part = slice(start, start + tower.tile)
            queries, keys, values = [], [], []
            for h in range(tower.heads):
                query = qkv[part, h * HEAD : (h + 1) * HEAD]
                key = qkv[part, w + h * HEAD : w + (h + 1) * HEAD]
                value = qkv[part, 2 * w + h * HEAD : 2 * w + (h + 1) * HEAD]
                grad = d_att[
                    tile * tower.tile : (tile + 1) * tower.tile, h * HEAD : (h + 1) * HEAD
                ]
                prob = probs[(k * tower.tiles + tile) * tower.heads + h]
                values.append(dot_tn(prob.astype(BF), grad))
                prob_grad = dot_nt(grad, value)
                score = (
                    prob * (prob_grad - jnp.sum(prob * prob_grad, axis=-1, keepdims=True))
                ).astype(BF)
                queries.append(dot(score, key) * HEAD ** (-0.5))
                keys.append(dot_tn(score, query) * HEAD ** (-0.5))
            dqkv[part, :] = jnp.concatenate(queries + keys + values, axis=1).astype(BF)
        back = dot_nt(dqkv[span, :], wq[...])
        gain = gain + jnp.sum(back * u1[span, :].astype(F32), axis=0, keepdims=True)
        shift = shift + jnp.sum(back, axis=0, keepdims=True)
        backs[k, :, :] = back
    for k in range(MP):
        for j, value in enumerate((gain, shift)):
            start = j * tower.padded
            part = backs[k, start : start + tower.padded, :]
            high, low = [piece.astype(F32) for piece in pieces(value, 2)]
            part = jnp.where(position == tower.length, high, part)
            part = jnp.where(position == tower.length + 1, low, part)
            targets[k][start : start + tower.padded, :] = part.astype(targets[k].dtype)
    wide[...] = dot_tn(h1[...], dqkv[...]).astype(BF)
    out_grad = dot_tn(att[...], d_all[...]).astype(BF)
    order = WIDE_ORDER if tower is IMG else range(2 * ZN)
    for place, e in enumerate(order):
        span = slice(place * tail, (place + 1) * tail)
        if e >= 6:
            piece = out_grad[(e - 6) * tail : (e - 5) * tail]
        else:
            s, i = e // 3, e % 3
            base = s * (d // 2)
            rest = wide[base + sr : base + sr + tail, w * i : w * (i + 1)]
            piece = jnp.concatenate(
                [wide[base + i * tail : base + (i + 1) * tail, :], rest], axis=1
            )
        grads[span, :] = piece


def attend_back_call(tower, ids, blocks, att, qkv, probs, h1, u1, wq, wo, after=()):
    rows, d, w, every = tower.rows, tower.d, tower.w, tower.all_rows
    return kernel_call(
        functools.partial(attend_back_body, tower),
        [
            out((rows, d)),
            out((rows, d), BF),
            out((rows, d), BF),
            out((rows, d), BF),
            out((d, d), BF),
            out((2, d)),
        ],
        [ids] + blocks + [att, qkv, probs, h1, u1, wq, wo],
        [
            pltpu.VMEM((every, d), BF),
            pltpu.VMEM((every, 3 * w), BF),
            pltpu.VMEM((d, 3 * w), BF),
            pltpu.VMEM((MP, rows, d), F32),
        ],
        after=after,
        us=10.4,
    )


def entry_body(tower, norms, xo, dx1, second, own, r1, r2, r3, *rest):
    if tower is IMG:
        dx, sums = rest
    else:
        dx_i, payload, sums = rest
    grad = (own[...] + r1[...].astype(F32)) + (r2[...].astype(F32) + r3[...].astype(F32))
    line = tower.length
    sums[0:1, :] = grad[line : line + 1] + grad[line + 1 : line + 2]
    line += tower.padded
    sums[1:2, :] = grad[line : line + 1] + grad[line + 1 : line + 2]
    sums[2:4, :] = second[...]
    unit_rows, inverse = unit(xo[...])
    back = unit_back(grad, unit_rows, inverse, norm_vector(norms, tower, 0))
    result = (dx1[...] + back).astype(BF)
    if tower is IMG:
        dx[...] = result
        return
    top = IMG.rows
    payload[:top, :] = dx_i[...]
    payload[top:, : TXT.d] = result[:top]
    rest = TXT.rows - top
    payload[top : top + rest, TXT.d :] = result[top:, :256]
    payload[top + rest : top + 2 * rest, TXT.d :] = result[top:, 256:]
    payload[top + 2 * rest :, TXT.d :] = jnp.zeros((top - 2 * rest, IMG.d - TXT.d), BF)


def entry_call(tower, norms, xo, dx1, second, own, received, before=(), after=()):
    rows, d = tower.rows, tower.d
    return kernel_call(
        functools.partial(entry_body, tower),
        [out((rows, d), BF) if tower is IMG else out((2 * IMG.rows, IMG.d), BF), out((4, d))],
        [norms, xo, dx1, second, own] + received + list(before),
        after=after,
    )


def place_body(tower, ids, own, r1, r2, r3, result, flat):
    m = ids[2]
    top = IMG.rows
    rest = TXT.rows - top
    for k, block in enumerate((own, r1, r2, r3)):
        if tower is IMG:
            rows = block[:top, :].astype(F32)
        else:
            low = jnp.concatenate(
                [
                    block[top : top + rest, TXT.d :],
                    block[top + rest : top + 2 * rest, TXT.d :],
                ],
                axis=1,
            )
            rows = jnp.concatenate([block[top:, : TXT.d], low], axis=0).astype(F32)
        for j in range(2):
            seq = 2 * (m ^ k) + j
            part = rows[j * tower.padded : j * tower.padded + tower.length]
            for i in range(tower.q):
                flat.at[i][pl.ds(seq, tower.length, stride=SEQS), :] = part[
                    :, 128 * i : 128 * (i + 1)
                ]
    for i in range(tower.q):
        result[:, :, 128 * i : 128 * (i + 1)] = flat[i].reshape(tower.length, SEQS, 128)


def place_call(tower, ids, blocks):
    return kernel_call(
        functools.partial(place_body, tower),
        [out((tower.length, SEQS, tower.d))],
        [ids] + blocks,
        [pltpu.VMEM((tower.q, tower.length * SEQS, 128), F32)],
        us=2.7,
    )[0]


def attend_split_body(tower, ids, mine, received, own, s1, s2, s3, total):
    z = ids[1]
    total[...] = mine[...].astype(F32) + received[...].astype(F32)
    top = tower.d - tower.sr
    for k, target in enumerate((own, s1, s2, s3)):
        start = jnp.minimum((z ^ k) * tower.sr, top)
        part = total[pl.ds(pl.multiple_of(start, 8), tower.sr), :]
        target[...] = part.astype(target.dtype)


def attend_split_call(tower, ids, mine, received, after=()):
    payload = out((tower.sr, tower.d), BF)
    return kernel_call(
        functools.partial(attend_split_body, tower),
        [out((tower.sr, tower.d)), payload, payload, payload],
        [ids, mine, received],
        [pltpu.VMEM((tower.d, tower.d), F32)],
        after=after,
    )


def down_body(tower, ids, sums, dyb, result, wide):
    d = tower.d
    tail = d // 8
    first = 0 if tower is IMG else D_IMG
    high, low = pieces(sums[:, first : first + d], 2)
    wide[:tail, :] = jnp.zeros((tail, d), F32)
    wide[tail:, :] = dot_tn(high, dyb[...]) + dot_tn(low, dyb[...])
    start = jnp.maximum(ids[3] - 5, 0) * tower.sr
    result[...] = wide[pl.ds(pl.multiple_of(start, 8), tower.sr), :]


def down_call(tower, ids, sums, dyb, after=()):
    d = tower.d
    return kernel_call(
        functools.partial(down_body, tower),
        [out((tower.sr, d))],
        [ids, sums, dyb],
        [pltpu.VMEM((d + d // 8, d), F32)],
        after=after,
        us=2.6,
    )[0]


def vector_body(ids, pg_i, pg_t, ng_i, ng_t, window, flat):
    flat[:64, :] = jnp.zeros((64, 128), F32)
    for tower, sums in ((IMG, ng_i), (TXT, ng_t)):
        for i in range(2):
            start = tower.norm_row + (4 + i) * tower.q
            for j in range(tower.q):
                flat[start + j : start + j + 1, :] = sums[i : i + 1, 128 * j : 128 * (j + 1)]
    for j in range(4):
        flat[pl.ds(NORM_ROWS + j, D_IMG, stride=4), :] = pg_i[:, 128 * j : 128 * (j + 1)]
        flat[pl.ds(NORM_ROWS + 4 * D_IMG + j, D_TXT, stride=4), :] = pg_t[
            :, 128 * j : 128 * (j + 1)
        ]
    low_lanes = lax.broadcasted_iota(jnp.int32, (VEC_ROWS, 128), 1) < 64
    last = lax.broadcasted_iota(jnp.int32, (VEC_ROWS, 128), 0) == VEC_ROWS - 1
    for s in range(8):

        def copy(s=s):
            start = (s * (2 * VEC_ROWS - 1)) // 2
            part = flat[start : start + VEC_ROWS, :]
            if s % 2 == 1:
                after = pltpu.roll(flat[start + 1 : start + 1 + VEC_ROWS, :], 64, 1)
                part = jnp.where(low_lanes, pltpu.roll(part, 64, 1), after)
            window[...] = jnp.where(last & jnp.logical_not(low_lanes), 0.0, part)

        pl.when(ids[3] == s)(copy)


def vector_call(ids, pg_i, pg_t, ng_i, ng_t, after=()):
    return kernel_call(
        vector_body,
        [out((VEC_ROWS, 128))],
        [ids, pg_i, pg_t, ng_i, ng_t],
        [pltpu.VMEM((4 * (2 * VEC_ROWS - 1) + 12, 128), F32)],
        after=after,
        us=2.9,
    )[0]


def collect_body(
    ids, f_own, fa, fb, q_own, q1, q2, bt, bt1, bt2, bt3, down_i, down_t, window,
    sums_i, sums_t, lin_i, lin_t, message, rows_i, rows_t, spare,
):
    shard = ids[3]
    q = IMG.d // 8

    def put(*blocks):
        for i, block in enumerate(blocks):
            rows_i[q * i : q * (i + 1), :] = block[...].astype(F32)

    pl.when(shard < 2)(lambda: put(q_own, q1, q2))
    pl.when(shard == 2)(lambda: put(q_own, q1))

    @pl.when(shard < 3)
    def _():
        rows_t[...] = (bt[...] + bt1[...].astype(F32)) + (
            bt2[...].astype(F32) + bt3[...].astype(F32)
        )

    @pl.when(shard >= 5)
    def _():
        rows_i[...] = down_i[...]
        rows_t[...] = down_t[...]

    @pl.when(shard == 2)
    def _():
        kept = rows_t[TXT.sr - TXT.w :, :]
        rows_t[: TXT.w, :] = kept

    tq = TXT.d // 8

    def feed(start, *blocks):
        for i, block in enumerate(blocks):
            rows_i[q * (start + i) : q * (start + i + 1), :] = block[:q, :].astype(F32)
            low = jnp.concatenate([block[q : q + 16, TXT.d :], block[q + 16 : q + 32, TXT.d :]], axis=1)
            part = jnp.concatenate([block[q:, : TXT.d], low], axis=0)
            rows_t[tq * (start + i) : tq * (start + i + 1), :] = part.astype(F32)

    pl.when(shard == 2)(lambda: feed(2, f_own))
    pl.when((shard == 3) | (shard == 4))(lambda: feed(0, f_own, fa, fb))
    pl.when(shard == 5)(lambda: feed(0, f_own))

    rows_to_lin(IMG, rows_i, lin_i, spare, shard)
    rows_to_lin(TXT, rows_t, lin_t, spare, shard)
    def total_of(value):
        return jnp.sum(value * value, axis=0, keepdims=True)

    every = total_of(window[...]) * (1.0 / MP)
    for j in range(IMG.q):
        every = every + total_of(rows_i[:, 128 * j : 128 * (j + 1)])
    for j in range(TXT.q):
        every = every + total_of(rows_t[:, 128 * j : 128 * (j + 1)])
    m = ids[2]

    def own_line(sums):
        line = sums[3:4, :]
        for member in range(3):
            line = jnp.where(m == member, sums[member : member + 1, :], line)
        return line

    line = jnp.concatenate([own_line(sums_i), own_line(sums_t)], axis=1)
    block = jnp.concatenate(
        [every] + [line[:, 128 * j : 128 * (j + 1)] for j in range(IMG.q + TXT.q)], axis=0
    )
    for peer in range(2 * ZN * MP):
        message[peer, : MESSAGE_ROWS, :] = block
        message[peer, MESSAGE_ROWS:, :] = jnp.zeros((16 - MESSAGE_ROWS, 128), F32)


MESSAGE_ROWS = 1 + IMG.q + TXT.q


def collect_call(ids, feed, attend_i, attend_t, down_i, down_t, window, sums_i, sums_t):
    return kernel_call(
        collect_body,
        [out((IMG.lin, 128)), out((TXT.lin, 128)), out((2 * ZN * MP, 16, 128))],
        [ids] + feed + attend_i + attend_t + [down_i, down_t, window, sums_i, sums_t],
        [
            pltpu.VMEM((IMG.sr, IMG.d), F32),
            pltpu.VMEM((TXT.sr, TXT.d), F32),
            pltpu.VMEM(SPARE, F32),
        ],
        us=3.8,
    )


def advance_body(
    ids, trio, parts, misc, ip, im, iv, ig, tp, tm, tv, tg, vp, vm, vv, vg,
    scalars, ipn, icn, imn, ivn, tpn, tcn, tmn, tvn, vpn, vcn, vmn, vvn, grad_v,
):
    slope = misc[1:2, :]
    grad_v[...] = vg[...]
    norm_squares = jnp.zeros((1, 128), F32)
    for member in range(MP):
        lines = parts[member]
        for group in range(1, 2 * ZN):
            lines = lines + parts[group * MP + member]
        if member == 0:
            squares = lines[:1]
        else:
            squares = squares + lines[:1]
        lines = lines[1:MESSAGE_ROWS]
        norm_squares = norm_squares + jnp.sum(lines * lines, axis=0, keepdims=True)

        @pl.when(ids[3] == 0)
        def _(member=member, lines=lines):
            start = member * IMG.q
            grad_v[start : start + IMG.q, :] = lines[: IMG.q]
            start = TXT.norm_row + member * TXT.q
            grad_v[start : start + TXT.q, :] = lines[IMG.q :]

    total = jnp.sum(squares + norm_squares, axis=1, keepdims=True)
    size = jnp.sqrt(total + slope * slope)
    clip = CLIP_LEVEL / jnp.maximum(size, CLIP_LEVEL)

    def step(master, first, second, grad, rate, decay):
        clipped = grad * clip
        first_new = BETA_ONE * first + (1.0 - BETA_ONE) * clipped
        second_new = BETA_TWO * second + (1.0 - BETA_TWO) * clipped * clipped
        update = (first_new * (1.0 / (1.0 - BETA_ONE**STEP))) / (
            jnp.sqrt(second_new * (1.0 / (1.0 - BETA_TWO**STEP))) + ADAM_EPS
        )
        return master - rate * (update + decay * master), first_new, second_new

    for master, first, second, grad, a, b, c, e in (
        (ip, im, iv, ig, ipn, icn, imn, ivn),
        (tp, tm, tv, tg, tpn, tcn, tmn, tvn),
    ):
        new, first_new, second_new = step(
            master[...], first[...], second[...], grad[...], RATE_MATRIX, WEIGHT_DECAY
        )
        a[...] = new
        b[...] = new.astype(BF)
        c[...] = first_new
        e[...] = second_new
    row = lax.broadcasted_iota(jnp.int32, (VEC_ROWS, 128), 0)
    is_norm = row < jnp.where(ids[3] == 0, NORM_ROWS, 0)
    new, first_new, second_new = step(
        vp[...],
        vm[...],
        vv[...],
        grad_v[...],
        jnp.where(is_norm, RATE_VECTOR, RATE_MATRIX),
        jnp.where(is_norm, 0.0, WEIGHT_DECAY),
    )
    vpn[...] = new
    vcn[...] = new.astype(BF)
    vmn[...] = first_new
    vvn[...] = second_new
    lane_row = jnp.zeros((1, 128), F32)
    new, _, _ = step(
        lane_row + trio[0], lane_row + trio[1], lane_row + trio[2], slope, LOGIT_SPEED, 0.0
    )
    scalars[...] = jnp.concatenate(
        [misc[0:1, :], size, new, jnp.zeros((5, 128), F32)], axis=0
    )


def advance_call(ids, trio, parts, misc, image, text, vector):
    outs = [out((8, 128))]
    for rows in (IMG.lin, TXT.lin, VEC_ROWS):
        outs += [out((rows, 128)), out((rows, 128), BF), out((rows, 128)), out((rows, 128))]
    return kernel_call(
        advance_body,
        outs,
        [ids, trio, parts, misc] + image + text + vector,
        [pltpu.VMEM((VEC_ROWS, 128), F32)],
        us=6.8,
    )


def hop(value, axis, mask):
    size = lax.axis_size(axis)
    return lax.ppermute(value, axis, [(i, i ^ mask) for i in range(size)])


def peers(values):
    return [hop(value, "mp", k) for k, value in zip((1, 2, 3), values)]


def spread(value):
    here = [value] + [hop(value, "dp", k) for k in range(1, ZN)]
    return here + [hop(block, "tower", 1) for block in here]


def merge(value, axis, mask):
    other = hop(value, axis, mask)
    upper = (lax.axis_index(axis) & mask) != 0
    return jnp.where(
        upper, jnp.concatenate([other, value], axis=0), jnp.concatenate([value, other], axis=0)
    )


FEED_ORDER = (2, 3, 0, 1, 4, 7, 5, 6)
FEED_MOVES = (((0, 3), (6, 4)), ((1, 3), (7, 4)))
WIDE_ORDER = (0, 3, 6, 1, 2, 4, 5, 7)
WIDE_MOVES = (((3, 0), (5, 1), (7, 2)), ((4, 0), (6, 1)))


def moves(value, rounds):
    return [lax.ppermute(value, GROUP, list(pairs)) for pairs in rounds]


def attend_perm(mask):
    return [(z ^ mask, z) for z in range(3)]


def fast_local(
    picture_residual_entry,
    sentence_residual_entry,
    sentence_lengths_held,
    couple_allowed_flags,
    picture_single_matrices,
    picture_mean_state,
    picture_square_state,
    sentence_single_matrices,
    sentence_mean_state,
    sentence_square_state,
    array_single_params,
    array_mean_state,
    array_square_state,
    logit_log_trio,
):
    LAST.clear()
    side, z, m = lax.axis_index("tower"), lax.axis_index("dp"), lax.axis_index("mp")
    ids = jnp.stack([side, z, m, side * ZN + z]).astype(jnp.int32)
    lengths = sentence_lengths_held
    vec_size = array_single_params.shape[0]

    def lines(value):
        return value.reshape(-1, 128)

    def vector_lines(value):
        return jnp.pad(value, (0, VEC_ROWS * 128 - vec_size)).reshape(VEC_ROWS, 128)

    vec_lines = vector_lines(array_single_params)
    keep_t, keep_i, send_t, send_i, block = kernel_call(
        prepare_body,
        [out((TXT.half, TXT.d), BF), out((IMG.half, IMG.d), BF)] * 2 + [out((16, TXT.d), BF)],
        [
            ids,
            couple_allowed_flags,
            lengths,
            lines(picture_single_matrices),
            lines(sentence_single_matrices),
            lines(array_single_params[: NORM_ROWS * 128]),
        ],
        [
            pltpu.VMEM((IMG.sr, IMG.d), F32),
            pltpu.VMEM((TXT.sr, TXT.d), F32),
            pltpu.VMEM(SPARE, F32),
        ],
        us=2.5,
    )
    urgent, late = kernel_call(
        sort_body,
        [out((URGENT, IMG.d), BF), out((HALF, IMG.d), BF)],
        [ids, keep_t, keep_i, hop(send_t, "tower", 1), hop(send_i, "tower", 1), block],
    )
    urgent = spread(urgent)
    late = lax.all_gather(gate(late, *urgent[1:ZN]), "dp", axis=0, tiled=True)
    vecpay = kernel_call(
        vector_pay_body,
        [out((VEC_ROWS, 128), BF)],
        [ids, vec_lines],
        [pltpu.VMEM((VEC_ROWS + 8, 128), F32)],
    )[0]
    x_txt = jnp.transpose(sentence_residual_entry, (1, 0, 2))
    x_img = jnp.transpose(picture_residual_entry, (1, 0, 2))
    norms, meta, *t_out = attend_call(TXT, ids, x_txt, urgent)
    i_out = attend_call(IMG, ids, x_img, urgent, norms=norms)
    layers = {}
    before = ()
    middles = {}
    for tower, outs in ((TXT, t_out), (IMG, i_out)):
        xo, own, s1, s2, s3 = outs[7:]
        x1, h2, pooled = middle_call(tower, ids, lengths, norms, xo, own, peers([s1, s2, s3]))
        middles[tower] = (x1, pooled, [h2] + peers([h2, h2, h2]))
    late = gate(late, x1, *middles[TXT][2][1:])
    late = [late, hop(late, "tower", 1)]
    gathered = lax.all_gather(gate(vecpay, late[0]), GROUP, axis=0, tiled=False)
    for tower, outs in ((TXT, t_out), (IMG, i_out)):
        wq, wo, h1, u1, qkv, att, probs, xo = outs[:8]
        x1, pooled, blocks = middles[tower]
        w1, w2, slope, sums, y = feed_call(
            tower, ids, lengths, blocks, urgent, late, pooled, before
        )
        before = (y, sums)
        layers[tower] = dict(
            wq=wq, wo=wo, h1=h1, u1=u1, qkv=qkv, att=att, probs=probs, xo=xo,
            x1=x1, blocks=blocks, w1=w1, w2=w2, slope=slope,
        )

    pi, pt = project_call(gathered)
    y = gate(y + hop(y, "mp", 1), pi)
    y = y + hop(y, "mp", 2)
    held = jnp.concatenate([y, sums], axis=0)[None]
    held = merge(merge(merge(held, "dp", 1), "dp", 2), "tower", 1)
    yall = held[:, :SEQS].reshape(-1, D_IMG + D_TXT)
    sums_all = held[:, SEQS:].reshape(-1, D_IMG + D_TXT)
    misc, dyb_i, dyb_t, dy_i, dy_t, pg_i, pg_t, ng_i, ng_t = head_call(
        ids, logit_log_trio, yall, norms, meta, pi, pt
    )

    dy = {IMG: dy_i, TXT: dy_t}
    back, dx1, dx1b, second = {}, {}, {}, {}
    entries, norm_sums = {}, {}
    grads = []
    for tower in (IMG, TXT):
        s = layers[tower]
        back[tower] = feed_back_call(
            tower, ids, lengths, s["blocks"], s["slope"], dy[tower], s["w1"], s["w2"], grads
        )
        grads = [back[tower][4]]
    feed_own = lax.psum_scatter(back[TXT][4], GROUP, scatter_dimension=0, tiled=False)
    for tower in (IMG, TXT):
        own, s1, s2, s3 = back[tower][:4]
        dx1[tower], dx1b[tower] = middle_back_call(
            tower, ids, lengths, norms, layers[tower]["x1"], dy[tower], own, peers([s1, s2, s3])
        )
        if tower is IMG:
            down = {IMG: down_call(IMG, ids, sums_all, dyb_i)}
    for tower in (IMG, TXT):
        s = layers[tower]
        block = dx1b[tower]
        *back[tower], grads, second[tower] = attend_back_call(
            tower, ids, [block] + peers([block] * 3),
            s["att"], s["qkv"], s["probs"], s["h1"], s["u1"], s["wq"], s["wo"],
        )
        if tower is IMG:
            quarter = lax.psum_scatter(
                gate(grads.reshape(2 * ZN, IMG.d // 8, IMG.d), feed_own), GROUP, scatter_dimension=0, tiled=False
            )
    moved = lax.ppermute(grads, "tower", [(1, 0)])
    before = ()
    for tower in (IMG, TXT):
        own, s1, s2, s3 = back[tower]
        dx, norm_sums[tower] = entry_call(
            tower, norms, layers[tower]["xo"], dx1[tower], second[tower], own,
            peers([s1, s2, s3]), before,
        )
        before = (dx,)
        if tower is IMG:
            window = vector_call(ids, pg_i, pg_t, ng_i, ng_t)
            down[TXT] = down_call(TXT, ids, sums_all, dyb_t)
            pa, p1, p2, p3 = attend_split_call(TXT, ids, grads, moved)
            text_parts = [pa] + [
                lax.ppermute(value, GROUP, attend_perm(k))
                for k, value in ((1, p1), (2, p2), (3, p3))
            ]
    feed_parts = [feed_own] + moves(feed_own, FEED_MOVES)
    image_parts = [quarter] + moves(quarter, WIDE_MOVES)
    placed = [dx] + peers([dx, dx, dx])
    lin_i, lin_t, message = collect_call(
        ids, feed_parts, image_parts, text_parts, down[IMG], down[TXT], window,
        norm_sums[IMG], norm_sums[TXT],
    )
    parts = lax.all_to_all(message, (*GROUP, "mp"), 0, 0, tiled=True)
    for tower in (IMG, TXT):
        entries[tower] = place_call(tower, ids, placed)
    scalars, *new = advance_call(
        ids,
        logit_log_trio,
        parts,
        misc,
        [lines(picture_single_matrices), lines(picture_mean_state), lines(picture_square_state), lin_i],
        [
            lines(sentence_single_matrices),
            lines(sentence_mean_state),
            lines(sentence_square_state),
            lin_t,
        ],
        [vec_lines, vector_lines(array_mean_state), vector_lines(array_square_state), window],
    )

    def flat(value, like):
        return value.reshape(-1)[: like.size].reshape(like.shape)

    likes = [picture_single_matrices] * 4 + [sentence_single_matrices] * 4 + [array_single_params] * 4
    news = [flat(value, like) for value, like in zip(new, likes)]
    return (
        scalars[0, 0],
        scalars[1, 0],
        jnp.transpose(entries[IMG], (1, 0, 2)),
        jnp.transpose(entries[TXT], (1, 0, 2)),
        *news,
        scalars[2, 0],
    )


def fits(mesh):
    return mesh.shape["tower"] == 2 and mesh.shape["dp"] == ZN and mesh.shape["mp"] == MP


def solution(mesh):
    placed = (
        P(GROUP, None, None),
        P(GROUP, None, None),
        P(GROUP),
        P(GROUP),
        P("mp", GROUP),
        P("mp", GROUP),
        P("mp", GROUP),
        P("mp", GROUP),
        P("mp", GROUP),
        P("mp", GROUP),
        P(GROUP),
        P(GROUP),
        P(GROUP),
        P(),
    )
    return jax.shard_map(
        fast_local if fits(mesh) else local,
        mesh=mesh,
        in_specs=placed,
        out_specs=(
            P(),
            P(),
            P(GROUP, None, None),
            P(GROUP, None, None),
            P("mp", GROUP),
            P("mp", GROUP),
            P("mp", GROUP),
            P("mp", GROUP),
            P("mp", GROUP),
            P("mp", GROUP),
            P("mp", GROUP),
            P("mp", GROUP),
            P(GROUP),
            P(GROUP),
            P(GROUP),
            P(GROUP),
            P(),
        ),
        check_vma=False,
    )
```

```python
import functools
import jax
import jax.numpy as jnp
from jax import lax
from jax.experimental import pallas as pl
from jax.experimental.pallas import tpu as pltpu
from jax.sharding import PartitionSpec as P

BF = jnp.bfloat16
F32 = jnp.float32
GROUP = ("tower", "dp")

D_IMG = 768
FF_IMG = 3072
IMG_LEN = 50
D_TXT = 512
FF_TXT = 2048
TXT_LEN = 77
HEAD = 64
EMBED = 512
STEP = 10


NORM_EPS = 1e-05
UNIT_EPS = 1e-06
BETA_ONE = 0.5
BETA_TWO = 0.5
ADAM_EPS = 1e-08
WEIGHT_DECAY = 0.1
RATE_MATRIX = 0.04
RATE_VECTOR = 0.3
LOGIT_SPEED = 0.5
CLIP_LEVEL = 0.005
MASK_LOW = -1e30
GELU_SLOPE = 1.702
BLOCK_TARGET = 512


def branch_sum(partial_sum):
    return lax.psum(partial_sum, "mp")


def branch_back(partial_sum):
    return lax.psum(partial_sum, "mp")


def norm_forward(values, norm_gain, norm_shift):
    centered = values - jnp.mean(values, axis=-1, keepdims=True)
    inverse = lax.rsqrt(jnp.mean(centered * centered, axis=-1, keepdims=True) + NORM_EPS)
    unit_rows = centered * inverse
    return (unit_rows * norm_gain + norm_shift, unit_rows, inverse)


def norm_backward(grad_rows, unit_rows, inverse, norm_gain):
    scaled = grad_rows * norm_gain
    centered_grad = (
        scaled
        - jnp.mean(scaled, axis=-1, keepdims=True)
        - unit_rows * jnp.mean(scaled * unit_rows, axis=-1, keepdims=True)
    )
    return (
        centered_grad * inverse,
        jnp.sum(grad_rows * unit_rows, axis=0),
        jnp.sum(grad_rows, axis=0),
    )


def quick_gelu(values):
    return values * jax.nn.sigmoid(GELU_SLOPE * values)


def gelu_slope(values):
    sigmoid_value = jax.nn.sigmoid(GELU_SLOPE * values)
    return sigmoid_value + GELU_SLOPE * values * sigmoid_value * (1.0 - sigmoid_value)


def block_size(seq_count, seq_length):
    for candidate in range(1, seq_count + 1):
        if seq_count % candidate == 0 and candidate * seq_length >= BLOCK_TARGET:
            return candidate
    return seq_count


def sequence_mask(seq_length, causal):
    position = lax.iota(jnp.int32, seq_length)
    if causal:
        return position[None, :] <= position[:, None]
    return position[None, :] >= 0


def block_scores(block_qkv, allowed):
    scores = jnp.einsum(
        "nqhd,nkhd->nhqk",
        block_qkv[:, :, 0],
        block_qkv[:, :, 1],
        preferred_element_type=jnp.float32,
    ) * HEAD ** (-0.5)
    return jnp.where(allowed[None, None], scores, MASK_LOW)


def attend(packed, seq_count, seq_length, causal):
    head_count = packed.shape[2]
    per_block = block_size(seq_count, seq_length)
    blocks = packed.reshape(seq_count // per_block, per_block, seq_length, 3, head_count, HEAD)
    allowed = sequence_mask(seq_length, causal)

    def one_block(block_qkv):
        scores = block_scores(block_qkv, allowed)
        row_max = jnp.max(scores, axis=-1, keepdims=True)
        exponent = jnp.exp(scores - row_max)
        totals = jnp.sum(exponent, axis=-1, keepdims=True)
        probs = (exponent / totals).astype(jnp.bfloat16)
        result = jnp.einsum(
            "nhqk,nkhd->nqhd", probs, block_qkv[:, :, 2], preferred_element_type=jnp.float32
        ).astype(jnp.bfloat16)
        return (result, (row_max + jnp.log(totals))[..., 0])

    results, log_totals = lax.map(one_block, blocks)
    return (results.reshape(packed.shape[0], head_count * HEAD), log_totals)


def attend_back(packed, attended_grad, log_totals, seq_count, seq_length, causal):
    head_count = packed.shape[2]
    per_block = block_size(seq_count, seq_length)
    block_total = seq_count // per_block
    blocks = packed.reshape(block_total, per_block, seq_length, 3, head_count, HEAD)
    grad_blocks = attended_grad.reshape(block_total, per_block, seq_length, head_count, HEAD)
    allowed = sequence_mask(seq_length, causal)

    def one_block(block_args):
        block_qkv, block_grad, block_totals = block_args
        scores = block_scores(block_qkv, allowed)
        probs = jnp.exp(scores - block_totals[..., None])
        value_grad = jnp.einsum(
            "nhqk,nqhd->nkhd",
            probs.astype(jnp.bfloat16),
            block_grad,
            preferred_element_type=jnp.float32,
        )
        prob_grad = jnp.einsum(
            "nqhd,nkhd->nhqk", block_grad, block_qkv[:, :, 2], preferred_element_type=jnp.float32
        )
        score_grad = (
            probs * (prob_grad - jnp.sum(probs * prob_grad, axis=-1, keepdims=True))
        ).astype(jnp.bfloat16)
        query_grad = jnp.einsum(
            "nhqk,nkhd->nqhd", score_grad, block_qkv[:, :, 1], preferred_element_type=jnp.float32
        ) * HEAD ** (-0.5)
        key_grad = jnp.einsum(
            "nhqk,nqhd->nkhd", score_grad, block_qkv[:, :, 0], preferred_element_type=jnp.float32
        ) * HEAD ** (-0.5)
        return jnp.stack([query_grad, key_grad, value_grad], axis=2).astype(jnp.bfloat16)

    return lax.map(one_block, (blocks, grad_blocks, log_totals)).reshape(packed.shape)


def split_flat(flat_weights, model_width, hidden, model_split):
    width_piece = model_width // model_split
    hidden_piece = hidden // model_split
    first_end = model_width * 3 * width_piece
    second_end = first_end + width_piece * model_width
    third_end = second_end + model_width * hidden_piece
    return (
        flat_weights[:first_end].reshape(model_width, 3, width_piece),
        flat_weights[first_end:second_end].reshape(width_piece, model_width),
        flat_weights[second_end:third_end].reshape(model_width, hidden_piece),
        flat_weights[third_end:].reshape(hidden_piece, model_width),
    )


def layer_forward(tokens, weights, norms, causal):
    qkv_weight, out_weight, up_weight, down_weight = weights
    seq_count, seq_length, model_width = tokens.shape
    token_rows = tokens.reshape(seq_count * seq_length, model_width).astype(jnp.float32)
    first_normed, unit_one, inverse_one = norm_forward(token_rows, norms[0], norms[1])
    first_low = first_normed.astype(jnp.bfloat16)
    packed = jnp.einsum(
        "rd,dtk->rtk", first_low, qkv_weight, preferred_element_type=jnp.float32
    ).astype(jnp.bfloat16)
    packed = packed.reshape(token_rows.shape[0], 3, qkv_weight.shape[2] // HEAD, HEAD)
    attended, log_totals = attend(packed, seq_count, seq_length, causal)
    middle = token_rows + branch_sum(
        jnp.dot(attended, out_weight, preferred_element_type=jnp.float32)
    )
    second_normed, unit_two, inverse_two = norm_forward(middle, norms[2], norms[3])
    second_low = second_normed.astype(jnp.bfloat16)
    pre_act = jnp.dot(second_low, up_weight, preferred_element_type=jnp.float32)
    activated = quick_gelu(pre_act).astype(jnp.bfloat16)
    outputs = middle + branch_sum(
        jnp.dot(activated, down_weight, preferred_element_type=jnp.float32)
    )
    return (
        outputs,
        (
            first_low,
            unit_one,
            inverse_one,
            packed,
            attended,
            log_totals,
            second_low,
            unit_two,
            inverse_two,
            pre_act,
            activated,
        ),
    )


def layer_backward(grad_out, weights, norms, stored, seq_count, seq_length, causal):
    qkv_weight, out_weight, up_weight, down_weight = weights
    (
        first_low,
        unit_one,
        inverse_one,
        packed,
        attended,
        log_totals,
        second_low,
        unit_two,
        inverse_two,
        pre_act,
        activated,
    ) = stored
    grad_low = grad_out.astype(jnp.bfloat16)
    down_grad = jnp.einsum("rf,rd->fd", activated, grad_low, preferred_element_type=jnp.float32)
    act_grad = jnp.einsum("rd,fd->rf", grad_low, down_weight, preferred_element_type=jnp.float32)
    pre_grad = (act_grad * gelu_slope(pre_act)).astype(jnp.bfloat16)
    up_grad = jnp.einsum("rd,rf->df", second_low, pre_grad, preferred_element_type=jnp.float32)
    second_grad = branch_back(
        jnp.einsum("rf,df->rd", pre_grad, up_weight, preferred_element_type=jnp.float32)
    )
    norm_grad_two, gain_two, shift_two = norm_backward(second_grad, unit_two, inverse_two, norms[2])
    middle_grad = grad_out + norm_grad_two
    middle_low = middle_grad.astype(jnp.bfloat16)
    out_grad = jnp.einsum("ra,rd->ad", attended, middle_low, preferred_element_type=jnp.float32)
    attended_grad = jnp.einsum(
        "rd,ad->ra", middle_low, out_weight, preferred_element_type=jnp.float32
    ).astype(jnp.bfloat16)
    packed_grad = attend_back(packed, attended_grad, log_totals, seq_count, seq_length, causal)
    packed_grad = packed_grad.reshape(packed.shape[0], 3, qkv_weight.shape[2])
    qkv_grad = jnp.einsum("rd,rtk->dtk", first_low, packed_grad, preferred_element_type=jnp.float32)
    first_grad = branch_back(
        jnp.einsum("rtk,dtk->rd", packed_grad, qkv_weight, preferred_element_type=jnp.float32)
    )
    norm_grad_one, gain_one, shift_one = norm_backward(first_grad, unit_one, inverse_one, norms[0])
    flat_grads = jnp.concatenate(
        [qkv_grad.reshape(-1), out_grad.reshape(-1), up_grad.reshape(-1), down_grad.reshape(-1)]
    )
    return (middle_grad + norm_grad_one, flat_grads, [gain_one, shift_one, gain_two, shift_two])


def pool_forward(picked, norm_gain, norm_shift, projection):
    normed, unit_rows, inverse = norm_forward(picked, norm_gain, norm_shift)
    normed_low = normed.astype(jnp.bfloat16)
    raw_embed = jnp.dot(normed_low, projection, preferred_element_type=jnp.float32)
    length_inverse = lax.rsqrt(jnp.sum(raw_embed * raw_embed, axis=-1, keepdims=True) + UNIT_EPS)
    embed_rows = raw_embed * length_inverse
    return (
        embed_rows.astype(jnp.bfloat16),
        (unit_rows, inverse, normed_low, embed_rows, length_inverse),
    )


def pool_backward(embed_grad, norm_gain, projection, stored):
    unit_rows, inverse, normed_low, embed_rows, length_inverse = stored
    raw_grad = (
        length_inverse
        * (embed_grad - embed_rows * jnp.sum(embed_grad * embed_rows, axis=-1, keepdims=True))
    ).astype(jnp.bfloat16)
    proj_grad = jnp.einsum("nd,ne->de", normed_low, raw_grad, preferred_element_type=jnp.float32)
    normed_grad = jnp.einsum("ne,de->nd", raw_grad, projection, preferred_element_type=jnp.float32)
    picked_grad, gain_grad, shift_grad = norm_backward(normed_grad, unit_rows, inverse, norm_gain)
    return (picked_grad, proj_grad, gain_grad, shift_grad)


def cosine_logits(picture_feature_lines, sentence_feature_lines, couple_allowed_flags, log_scale):
    image_all, text_all, valid_all = (
        lax.all_gather(picture_feature_lines, GROUP, axis=0, tiled=True),
        lax.all_gather(sentence_feature_lines, GROUP, axis=0, tiled=True),
        lax.all_gather(
            couple_allowed_flags.astype(jnp.bfloat16), GROUP, axis=0, tiled=True
        ),
    )
    count_valid = jnp.sum(valid_all.astype(jnp.float32))
    column_valid = valid_all > 0
    row_valid = couple_allowed_flags > 0
    local_count = picture_feature_lines.shape[0]
    offset_rows = lax.axis_index(GROUP) * local_count
    on_diagonal = (
        lax.iota(jnp.int32, valid_all.shape[0])[None, :]
        == offset_rows + lax.iota(jnp.int32, local_count)[:, None]
    )
    scale_factor = jnp.exp(log_scale)

    def one_side(mine, others):
        logits = scale_factor * jnp.einsum(
            "ne,me->nm", mine, others, preferred_element_type=jnp.float32
        )
        masked = jnp.where(column_valid[None, :], logits, MASK_LOW)
        row_max = jnp.max(masked, axis=1, keepdims=True)
        exponent = jnp.exp(masked - row_max)
        totals = jnp.sum(exponent, axis=1, keepdims=True)
        own_logit = jnp.sum(jnp.where(on_diagonal, logits, 0.0), axis=1)
        log_sum = row_max[:, 0] + jnp.log(totals[:, 0])
        loss_sum = jnp.sum(jnp.where(row_valid, log_sum - own_logit, 0.0))
        logit_grad = jnp.where(
            row_valid[:, None], exponent / totals - on_diagonal.astype(jnp.float32), 0.0
        ) / (2.0 * count_valid)
        return (loss_sum, logit_grad, jnp.sum(logit_grad * logits), log_sum, logits)

    image_loss, image_logit_grad, image_scale_part, image_lse, image_logits = one_side(
        picture_feature_lines, text_all
    )
    text_loss, text_logit_grad, text_scale_part, text_lse, text_logits = one_side(
        sentence_feature_lines, image_all
    )
    picture_device_share = scale_factor * jnp.dot(
        image_logit_grad, text_all.astype(jnp.float32), precision=lax.Precision.HIGHEST
    )
    sentence_device_share = scale_factor * jnp.dot(
        text_logit_grad, image_all.astype(jnp.float32), precision=lax.Precision.HIGHEST
    )
    text_spread = scale_factor * jnp.einsum(
        "np,ne->pe",
        image_logit_grad,
        picture_feature_lines.astype(jnp.float32),
        precision=lax.Precision.HIGHEST,
    )
    image_spread = scale_factor * jnp.einsum(
        "np,ne->pe",
        text_logit_grad,
        sentence_feature_lines.astype(jnp.float32),
        precision=lax.Precision.HIGHEST,
    )
    picture_reverse, sentence_reverse = (
        lax.psum_scatter(image_spread, GROUP, scatter_dimension=0, tiled=True),
        lax.psum_scatter(text_spread, GROUP, scatter_dimension=0, tiled=True),
    )
    contrast_objective, logit_log_slope = lax.psum(
        ((image_loss + text_loss) / (2.0 * count_valid), image_scale_part + text_scale_part),
        GROUP,
    )
    return (
        picture_device_share + picture_reverse,
        sentence_device_share + sentence_reverse,
        contrast_objective,
        logit_log_slope,
    )


def optimizer_advance(master, first, second, grad, rate, decay):
    first_new = BETA_ONE * first + (1.0 - BETA_ONE) * grad
    second_new = BETA_TWO * second + (1.0 - BETA_TWO) * grad * grad
    update = (
        first_new
        / (1.0 - BETA_ONE**STEP)
        / (jnp.sqrt(second_new / (1.0 - BETA_TWO**STEP)) + ADAM_EPS)
    )
    return (master - rate * (update + decay * master), first_new, second_new)


def local(
    picture_residual_entry,
    sentence_residual_entry,
    sentence_lengths_held,
    couple_allowed_flags,
    picture_single_matrices,
    picture_mean_state,
    picture_square_state,
    sentence_single_matrices,
    sentence_mean_state,
    sentence_square_state,
    array_single_params,
    array_mean_state,
    array_square_state,
    logit_log_trio,
):
    model_split = lax.axis_size("mp")
    norm_end = 6 * (D_IMG + D_TXT)
    image_end = norm_end + D_IMG * EMBED
    image_flat, text_flat, vector_flat = (
        lax.all_gather(
            picture_single_matrices.astype(jnp.bfloat16), GROUP, axis=1, tiled=True
        ),
        lax.all_gather(
            sentence_single_matrices.astype(jnp.bfloat16), GROUP, axis=1, tiled=True
        ),
        lax.all_gather(
            array_single_params.astype(jnp.bfloat16), GROUP, axis=0, tiled=True
        ),
    )
    image_norms = vector_flat[: 6 * D_IMG].reshape(6, D_IMG).astype(jnp.float32)
    text_norms = vector_flat[6 * D_IMG : norm_end].reshape(6, D_TXT).astype(jnp.float32)
    image_proj = vector_flat[norm_end:image_end].reshape(D_IMG, EMBED)
    text_proj = vector_flat[image_end:].reshape(D_TXT, EMBED)
    seq_count = picture_residual_entry.shape[0]
    image_weights = split_flat(image_flat[0], D_IMG, FF_IMG, model_split)
    image_out, image_stored = layer_forward(
        picture_residual_entry, image_weights, image_norms, False
    )
    image_picked = jnp.mean(image_out.reshape(seq_count, IMG_LEN, D_IMG), axis=1)
    picture_feature_lines, image_pool = pool_forward(
        image_picked, image_norms[4], image_norms[5], image_proj
    )
    text_weights = split_flat(text_flat[0], D_TXT, FF_TXT, model_split)
    text_out, text_stored = layer_forward(sentence_residual_entry, text_weights, text_norms, True)
    inside = (lax.iota(jnp.int32, TXT_LEN)[None, :] < sentence_lengths_held[:, None]).astype(
        jnp.float32
    )
    picker = inside / sentence_lengths_held[:, None].astype(jnp.float32)
    text_picked = jnp.einsum(
        "nl,nld->nd",
        picker,
        text_out.reshape(seq_count, TXT_LEN, D_TXT),
        precision=lax.Precision.HIGHEST,
    )
    sentence_feature_lines, text_pool = pool_forward(
        text_picked, text_norms[4], text_norms[5], text_proj
    )
    picture_feature_slope, sentence_feature_slope, contrast_objective, logit_log_slope = (
        cosine_logits(
            picture_feature_lines, sentence_feature_lines, couple_allowed_flags, logit_log_trio[0]
        )
    )
    text_picked_grad, text_proj_grad, text_post_gain, text_post_shift = pool_backward(
        sentence_feature_slope, text_norms[4], text_proj, text_pool
    )
    text_rows_grad = (picker[:, :, None] * text_picked_grad[:, None, :]).reshape(
        seq_count * TXT_LEN, D_TXT
    )
    sentence_entry_slope, text_flat_grad, text_norm_grads = layer_backward(
        text_rows_grad, text_weights, text_norms, text_stored, seq_count, TXT_LEN, True
    )
    image_picked_grad, image_proj_grad, image_post_gain, image_post_shift = pool_backward(
        picture_feature_slope, image_norms[4], image_proj, image_pool
    )
    image_rows_grad = jnp.broadcast_to(
        image_picked_grad[:, None, :] / IMG_LEN, (seq_count, IMG_LEN, D_IMG)
    ).reshape(seq_count * IMG_LEN, D_IMG)
    picture_entry_slope, image_flat_grad, image_norm_grads = layer_backward(
        image_rows_grad, image_weights, image_norms, image_stored, seq_count, IMG_LEN, False
    )
    array_param_slope = jnp.concatenate(
        [
            jnp.stack(image_norm_grads + [image_post_gain, image_post_shift]).reshape(-1),
            jnp.stack(text_norm_grads + [text_post_gain, text_post_shift]).reshape(-1),
            image_proj_grad.reshape(-1),
            text_proj_grad.reshape(-1),
        ]
    )
    image_reduced, text_reduced, vector_reduced = (
        lax.psum_scatter(
            image_flat_grad.reshape(-1, D_IMG), GROUP, scatter_dimension=0, tiled=True
        ).reshape(1, -1),
        lax.psum_scatter(
            text_flat_grad.reshape(-1, D_TXT), GROUP, scatter_dimension=0, tiled=True
        ).reshape(1, -1),
        lax.psum_scatter(array_param_slope, GROUP, scatter_dimension=0, tiled=True),
    )
    matrix_squares = jnp.sum(image_reduced * image_reduced) + jnp.sum(text_reduced * text_reduced)
    vector_squares = jnp.sum(vector_reduced * vector_reduced) / model_split
    tensor_square_sum, array_square_sum = lax.psum(
        (matrix_squares, vector_squares), (*GROUP, "mp")
    )
    global_slope_size = jnp.sqrt(
        tensor_square_sum + array_square_sum + logit_log_slope * logit_log_slope
    )
    clipping_factor = CLIP_LEVEL / jnp.maximum(global_slope_size, CLIP_LEVEL)
    picture_matrices_fresh, picture_mean_fresh, picture_square_fresh = optimizer_advance(
        picture_single_matrices,
        picture_mean_state,
        picture_square_state,
        image_reduced * clipping_factor,
        RATE_MATRIX,
        WEIGHT_DECAY,
    )
    sentence_matrices_fresh, sentence_mean_fresh, sentence_square_fresh = optimizer_advance(
        sentence_single_matrices,
        sentence_mean_state,
        sentence_square_state,
        text_reduced * clipping_factor,
        RATE_MATRIX,
        WEIGHT_DECAY,
    )
    shard_length = array_single_params.shape[0]
    vector_index = lax.axis_index(GROUP) * shard_length + lax.iota(
        jnp.int32, shard_length
    )
    is_norm = vector_index < norm_end
    array_params_fresh, array_mean_fresh, array_square_fresh = optimizer_advance(
        array_single_params,
        array_mean_state,
        array_square_state,
        vector_reduced * clipping_factor,
        jnp.where(is_norm, RATE_VECTOR, RATE_MATRIX),
        jnp.where(is_norm, 0.0, WEIGHT_DECAY),
    )
    logit_log_fresh, logit_mean_fresh, logit_square_fresh = optimizer_advance(
        logit_log_trio[0],
        logit_log_trio[1],
        logit_log_trio[2],
        logit_log_slope * clipping_factor,
        LOGIT_SPEED,
        0.0,
    )
    return (
        contrast_objective,
        global_slope_size,
        picture_entry_slope.reshape(picture_residual_entry.shape),
        sentence_entry_slope.reshape(sentence_residual_entry.shape),
        picture_matrices_fresh,
        picture_matrices_fresh.astype(jnp.bfloat16),
        picture_mean_fresh,
        picture_square_fresh,
        sentence_matrices_fresh,
        sentence_matrices_fresh.astype(jnp.bfloat16),
        sentence_mean_fresh,
        sentence_square_fresh,
        array_params_fresh,
        array_params_fresh.astype(jnp.bfloat16),
        array_mean_fresh,
        array_square_fresh,
        logit_log_fresh,
    )


ZN = 4
MP = 4
SEQS = 8


class Tower:
    def __init__(self, tag, width, length, padded, joint, causal, norm_row):
        self.tag = tag
        self.d = width
        self.w = width // MP
        self.heads = self.w // HEAD
        self.length = length
        self.padded = padded
        self.rows = 2 * padded
        self.all_rows = MP * self.rows
        self.tile = self.rows if joint else padded
        self.tiles = self.rows // self.tile
        self.causal = causal
        self.sr = 3 * width // 8
        self.half = self.sr // 2
        self.q = width // 128
        self.norm_row = norm_row
        self.lin = self.sr * self.q


IMG = Tower("_img", D_IMG, IMG_LEN, 56, True, False, 0)
TXT = Tower("_txt", D_TXT, TXT_LEN, 80, False, True, 6 * D_IMG // 128)
NORM_ROWS = 6 * (D_IMG + D_TXT) // 128
VEC_ROWS = 648
HALF = IMG.half + 64
FEED_ROWS = IMG.d // 8 + 48
URGENT = HALF + 16


COST_SCALE = 1.5e9


def kernel_call(body, outs, ins, scratch=(), us=2.0, after=(), vmem=62):
    after = list(after) + LAST

    def spec(value):
        small = value.dtype == jnp.int32 or (value.ndim == 1 and value.shape[0] <= 8)
        return pl.BlockSpec(memory_space=pltpu.SMEM if small else pltpu.VMEM)

    count, late = len(ins), len(after)
    name = getattr(body, "func", body).__name__
    if hasattr(body, "args"):
        name = name + body.args[0].tag
    results = pl.pallas_call(
        lambda *refs: body(*refs[:count], *refs[count + late :]),
        out_shape=list(outs),
        in_specs=[spec(v) for v in ins] + [pl.BlockSpec(memory_space=pl.ANY)] * late,
        out_specs=[pl.BlockSpec(memory_space=pltpu.VMEM)] * len(outs),
        scratch_shapes=list(scratch),
        compiler_params=pltpu.CompilerParams(
            vmem_limit_bytes=vmem * MIB
        ),
        cost_estimate=pl.CostEstimate(
            flops=int(COST_SCALE * us), bytes_accessed=0, transcendentals=0
        ),
        name=name,
    )(*ins, *after)
    LAST[:] = results[:1]
    return results


LAST = []
MIB = 1024 * 1024


def gate(value, *after):
    anywhere = pl.BlockSpec(memory_space=pl.ANY)
    return pl.pallas_call(
        lambda *refs: None,
        out_shape=out(value.shape, value.dtype),
        in_specs=[anywhere] * (1 + len(after)),
        out_specs=anywhere,
        input_output_aliases={0: 0},
    )(value, *after)


def out(shape, dtype=F32):
    return jax.ShapeDtypeStruct(shape, dtype)


def dot(a, b):
    return lax.dot_general(a, b, (((1,), (0,)), ((), ())), preferred_element_type=F32)


def dot_nt(a, b):
    return lax.dot_general(a, b, (((1,), (1,)), ((), ())), preferred_element_type=F32)


def dot_tn(a, b):
    return lax.dot_general(a, b, (((0,), (0,)), ((), ())), preferred_element_type=F32)


def pieces(a, count):
    parts = []
    for _ in range(count):
        part = a.astype(BF)
        parts.append(part)
        a = a - part.astype(F32)
    return parts


def unit(values):
    width = values.shape[-1]
    centered = values - jnp.sum(values, axis=-1, keepdims=True) * (1.0 / width)
    inverse = lax.rsqrt(
        jnp.sum(centered * centered, axis=-1, keepdims=True) * (1.0 / width) + NORM_EPS
    )
    return centered * inverse, inverse


def unit_back(grad_rows, unit_rows, inverse, gain):
    width = grad_rows.shape[-1]
    scaled = grad_rows * gain
    first = jnp.sum(scaled, axis=-1, keepdims=True) * (1.0 / width)
    second = jnp.sum(scaled * unit_rows, axis=-1, keepdims=True) * (1.0 / width)
    return (scaled - first - unit_rows * second) * inverse


def norm_vector(norms_ref, tower, index):
    start = tower.norm_row + index * tower.q
    return jnp.concatenate([norms_ref[start + i : start + i + 1, :] for i in range(tower.q)], axis=1)


def natural_from_lin(tower, lin_ref, spare):
    d, w = tower.d, tower.w
    if (3 * w) % 128 == 0:
        per = 3 * w // 128
        return jnp.concatenate(
            [lin_ref[pl.ds(i, d // 2, stride=per), :] for i in range(per)], axis=1
        )
    per = 2 * 3 * w // 128
    mid = per // 2
    lines = [lin_ref[pl.ds(i, d // 4, stride=per), :] for i in range(per)]
    empty = jnp.zeros((d // 4, 64), F32)
    even = lines[: mid + 1]
    odd = jnp.concatenate([lines[mid][:, 64:]] + lines[mid + 1 :] + [empty], axis=1)
    for j in range(mid + 1):
        spare.at[j][pl.ds(0, d // 4, stride=2), :] = even[j]
        spare.at[j][pl.ds(1, d // 4, stride=2), :] = odd[:, 128 * j : 128 * (j + 1)]
    return jnp.concatenate([spare[j] for j in range(mid)] + [spare[mid][:, :64]], axis=1)


def natural_to_lin(tower, natural, lin_ref, spare):
    d, w = tower.d, tower.w
    if (3 * w) % 128 == 0:
        per = 3 * w // 128
        for i in range(per):
            lin_ref[pl.ds(i, d // 2, stride=per), :] = natural[:, 128 * i : 128 * (i + 1)]
        return
    per = 2 * 3 * w // 128
    mid = per // 2
    for j in range(mid):
        spare[j] = natural[:, 128 * j : 128 * (j + 1)]
    spare[mid] = jnp.concatenate([natural[:, 128 * mid :], jnp.zeros((d // 2, 64), F32)], axis=1)
    even = [spare.at[j][pl.ds(0, d // 4, stride=2), :] for j in range(mid + 1)]
    odd = jnp.concatenate(
        [spare.at[j][pl.ds(1, d // 4, stride=2), :] for j in range(mid + 1)], axis=1
    )
    for i in range(mid):
        lin_ref[pl.ds(i, d // 4, stride=per), :] = even[i]
    lin_ref[pl.ds(mid, d // 4, stride=per), :] = jnp.concatenate(
        [even[mid][:, :64], odd[:, :64]], axis=1
    )
    for i in range(mid):
        lin_ref[pl.ds(mid + 1 + i, d // 4, stride=per), :] = odd[:, 64 + 128 * i : 192 + 128 * i]


def lin_to_rows(tower, lin_ref, rows_ref, spare, shard):
    d, w, sr, q = tower.d, tower.w, tower.sr, tower.q

    @pl.when(shard >= 2)
    def _():
        for j in range(q):
            rows_ref[:, 128 * j : 128 * (j + 1)] = lin_ref[pl.ds(j, sr, stride=q), :]

    @pl.when(shard < 2)
    def _():
        tail = d // 8
        natural = natural_from_lin(tower, lin_ref, spare)
        rows_ref[:, : 3 * w] = natural[:sr]
        for i in range(3):
            rows_ref[tail * i : tail * (i + 1), 3 * w :] = natural[sr:, w * i : w * (i + 1)]


def rows_to_lin(tower, rows_ref, lin_ref, spare, shard):
    d, w, sr, q = tower.d, tower.w, tower.sr, tower.q

    @pl.when(shard >= 2)
    def _():
        for j in range(q):
            lin_ref[pl.ds(j, sr, stride=q), :] = rows_ref[:, 128 * j : 128 * (j + 1)]

    @pl.when(shard < 2)
    def _():
        tail = d // 8
        rest = jnp.concatenate(
            [rows_ref[tail * i : tail * (i + 1), 3 * w :] for i in range(3)], axis=1
        )
        natural = jnp.concatenate([rows_ref[:, : 3 * w], rest], axis=0)
        natural_to_lin(tower, natural, lin_ref, spare)


SPARE = ((3 * IMG.w + 127) // 128, IMG.d // 2, 128)


def prepare_body(
    ids, flags, lengths, img, txt, head, keep_t, keep_i, send_t, send_i, block, rows_i, rows_t, spare
):
    side, shard = ids[0], ids[3]
    lin_to_rows(IMG, img, rows_i, spare, shard)
    lin_to_rows(TXT, txt, rows_t, spare, shard)
    lane = lax.broadcasted_iota(jnp.int32, (1, 128), 1)
    flag_row = jnp.zeros((1, 128), F32)
    length_row = jnp.zeros((1, 128), F32)
    for i in range(SEQS):
        flag_row = jnp.where(lane == i, jnp.where(flags[i] > 0, 1.0, 0.0), flag_row)
        length_row = jnp.where(lane == i, lengths[i].astype(F32), length_row)
    lines = jnp.concatenate(
        [head[:NORM_ROWS, :], flag_row, length_row, jnp.zeros((64 - NORM_ROWS - 2, 128), F32)], axis=0
    )
    for j in range(4):
        block[:, 128 * j : 128 * (j + 1)] = lines[16 * j : 16 * (j + 1)].astype(BF)
    for tower, rows, keep, send in ((TXT, rows_t, keep_t, send_t), (IMG, rows_i, keep_i, send_i)):
        for target, which in ((keep, side), (send, 1 - side)):
            target[...] = rows[
                pl.ds(pl.multiple_of(which * tower.half, 8), tower.half), :
            ].astype(BF)


def sort_body(ids, keep_t, keep_i, got_t, got_i, block, urgent, late):
    def fill(*halves):
        for target, part_t, part_i in ((urgent, *halves[:2]), (late, *halves[2:])):
            target[: IMG.half, :] = part_i[...]
            target[IMG.half : HALF, : TXT.d] = part_t[:64, :]
            target[IMG.half : IMG.half + 32, TXT.d :] = part_t[64:, :256]
            target[IMG.half + 32 : HALF, TXT.d :] = part_t[64:, 256:]

    pl.when(ids[0] == 0)(lambda: fill(keep_t, keep_i, got_t, got_i))
    pl.when(ids[0] != 0)(lambda: fill(got_t, got_i, keep_t, keep_i))
    urgent[HALF:, : TXT.d] = block[...]
    urgent[HALF:, TXT.d :] = jnp.zeros((16, IMG.d - TXT.d), BF)


def vector_pay_body(ids, vec, vecpay, shifted):
    odd = ids[3] % 2

    @pl.when(odd == 0)
    def _():
        vecpay[...] = vec[...].astype(BF)

    @pl.when(odd == 1)
    def _():
        rolled = pltpu.roll(vec[...], 64, 1)
        shifted[0:8, :] = jnp.zeros((8, 128), F32)
        shifted[8 : 8 + VEC_ROWS, :] = rolled
        before = shifted[7 : 7 + VEC_ROWS, :]
        low_lanes = lax.broadcasted_iota(jnp.int32, (VEC_ROWS, 128), 1) < 64
        vecpay[...] = jnp.where(low_lanes, before, rolled).astype(BF)


def with_halves(blocks, side, z, shard, use):
    if len(blocks) == 2:
        rows = blocks[0].shape[0] // ZN
        mine, other = [block.at[pl.ds(shard * rows, rows)] for block in blocks]
        pl.when(side == 0)(lambda: use(mine, other))
        pl.when(side != 0)(lambda: use(other, mine))
        return
    for k in range(ZN):
        mine, other = blocks[k], blocks[ZN + k]
        here = (z ^ shard) == k
        pl.when(here & (side == 0))(functools.partial(use, mine, other))
        pl.when(here & (side != 0))(functools.partial(use, other, mine))


def half_rows(tower, first, second):
    if tower is IMG:
        return jnp.concatenate([first[: IMG.half, :], second[: IMG.half, :]], axis=0)
    parts = []
    for half in (first, second):
        parts += [
            half[IMG.half : HALF, : TXT.d],
            half[IMG.half : IMG.half + 32, TXT.d :],
            half[IMG.half + 32 : HALF, TXT.d :],
        ]
    return jnp.concatenate(
        [
            parts[0],
            jnp.concatenate([parts[1], parts[2]], axis=1),
            parts[3],
            jnp.concatenate([parts[4], parts[5]], axis=1),
        ],
        axis=0,
    )


def attention_mask(tower):
    shape = (tower.tile, tower.tile)
    row = lax.broadcasted_iota(jnp.int32, shape, 0)
    column = lax.broadcasted_iota(jnp.int32, shape, 1)
    if tower.causal:
        return (column <= row) & (column < tower.length)
    pad = tower.padded
    first = (row < pad) & (column < tower.length)
    second = (row >= pad) & (column >= pad) & (column < pad + tower.length)
    return first | second


def read_meta(meta, blocks, side, z):
    for place in range(ZN):

        def use(*halves, place=place):
            for half, block in enumerate(halves):
                lines = block[HALF:, 384:512].astype(F32)
                line = half * ZN + place
                meta[line : line + 1, :] = lines[12:13]
                meta[8 + line : 9 + line, :] = lines[13:14]

        with_halves(blocks, side, z, place, use)


def attend_body(tower, ids, x, *rest):
    count = 2 * ZN
    blocks, rest = rest[:count], rest[count:]
    if tower is TXT:
        (norms, meta, wq, wo, h1, u1, qkv, att, probs, xo, own, s1, s2, s3, xf, xs) = rest
    else:
        norms = rest[0]
        (wq, wo, h1, u1, qkv, att, probs, xo, own, s1, s2, s3, xf, xs) = rest[1:]
    side, z, m = ids[0], ids[1], ids[2]
    d, w, sr = tower.d, tower.w, tower.sr
    if tower is TXT:

        def read_norms(block, _):
            for j in range(4):
                norms[16 * j : 16 * (j + 1), :] = block[HALF:, 128 * j : 128 * (j + 1)].astype(F32)

        with_halves(blocks, side, z, 0, read_norms)
        read_meta(meta, blocks, side, z)

    tail = d // 8
    for s in range(2):

        def read_qkv(first, second, base=s * (d // 2)):
            part = half_rows(tower, first, second)
            wq[base : base + sr, :] = part[:, : 3 * w]
            wq[base + sr : base + sr + tail, :] = jnp.concatenate(
                [part[tail * i : tail * (i + 1), 3 * w :] for i in range(3)], axis=1
            )

        with_halves(blocks, side, z, s, read_qkv)

    def read_out(first, second):
        wo[...] = half_rows(tower, first, second)[:w]

    with_halves(blocks, side, z, 2, read_out)
    for j in range(tower.q):
        xf[j] = x[:, :, 128 * j : 128 * (j + 1)].astype(F32).reshape(tower.length * SEQS, 128)
    pad = tower.padded - tower.length
    for k in range(MP):
        for j in range(2):
            start = k * tower.rows + j * tower.padded
            seq = 2 * (m ^ k) + j
            for i in range(tower.q):
                xs[start : start + tower.length, 128 * i : 128 * (i + 1)] = xf.at[i][
                    pl.ds(seq, tower.length, stride=SEQS), :
                ]
            xs[start + tower.length : start + tower.padded, :] = jnp.zeros((pad, d), F32)
    xo[...] = xs[: tower.rows, :]
    unit_rows, _ = unit(xs[...])
    u1[...] = unit_rows.astype(BF)
    h1[...] = (
        unit_rows * norm_vector(norms, tower, 0) + norm_vector(norms, tower, 1)
    ).astype(BF)
    qkv[...] = dot(h1[...], wq[...]).astype(BF)
    allowed = attention_mask(tower)
    targets = (own, s1, s2, s3)
    for k in range(MP):
        for tile in range(tower.tiles):
            start = k * tower.rows + tile * tower.tile
            rows = slice(start, start + tower.tile)
            heads = []
            for h in range(tower.heads):
                query = qkv[rows, h * HEAD : (h + 1) * HEAD]
                key = qkv[rows, w + h * HEAD : w + (h + 1) * HEAD]
                value = qkv[rows, 2 * w + h * HEAD : 2 * w + (h + 1) * HEAD]
                scores = jnp.where(allowed, dot_nt(query, key) * HEAD ** (-0.5), MASK_LOW)
                exponent = jnp.exp(scores - jnp.max(scores, axis=-1, keepdims=True))
                prob = exponent / jnp.sum(exponent, axis=-1, keepdims=True)
                probs[(k * tower.tiles + tile) * tower.heads + h] = prob
                heads.append(dot(prob.astype(BF), value))
            att[rows, :] = jnp.concatenate(heads, axis=1).astype(BF)
        rows = slice(k * tower.rows, (k + 1) * tower.rows)
        part = dot(att[rows, :], wo[...])
        targets[k][...] = part.astype(targets[k].dtype)


def attend_call(tower, ids, x, blocks, norms=None, after=()):
    d, w, rows, every = tower.d, tower.w, tower.rows, tower.all_rows
    outs = [
        out((d, 3 * w), BF),
        out((w, d), BF),
        out((every, d), BF),
        out((every, d), BF),
        out((every, 3 * w), BF),
        out((every, w), BF),
        out((MP * tower.tiles * tower.heads, tower.tile, tower.tile)),
        out((rows, d)),
        out((rows, d)),
        out((rows, d), BF),
        out((rows, d), BF),
        out((rows, d), BF),
    ]
    ins = [ids, x] + blocks
    if tower is TXT:
        outs = [out((64, 128)), out((16, 128))] + outs
    else:
        ins.append(norms)
    return kernel_call(
        functools.partial(attend_body, tower),
        outs,
        ins,
        [
            pltpu.VMEM((tower.q, tower.length * SEQS, 128), F32),
            pltpu.VMEM((every, d), F32),
        ],
        after=after,
        us=7.2,
    )


def row_mask(tower, lengths, pair):
    position = lax.broadcasted_iota(jnp.int32, (tower.padded, 1), 0)
    count = lengths[pair] if tower.causal else tower.length
    return position < count, count


def middle_body(tower, ids, lengths, norms, xo, own, r1, r2, r3, x1, h2, pooled):
    m = ids[2]
    total = xo[...] + ((own[...] + r1[...].astype(F32)) + (r2[...].astype(F32) + r3[...].astype(F32)))
    x1[...] = total
    unit_rows, _ = unit(total)
    h2[...] = (
        unit_rows * norm_vector(norms, tower, 2) + norm_vector(norms, tower, 3)
    ).astype(BF)
    for j in range(2):
        inside, count = row_mask(tower, lengths, 2 * m + j)
        part = total[j * tower.padded : (j + 1) * tower.padded]
        summed = jnp.sum(jnp.where(inside, part, 0.0), axis=0, keepdims=True)
        pooled[j : j + 1, :] = summed / jnp.full((1, 1), count, F32)


def middle_call(tower, ids, lengths, norms, xo, own, received, after=()):
    rows, d = tower.rows, tower.d
    return kernel_call(
        functools.partial(middle_body, tower),
        [out((rows, d)), out((rows, d), BF), out((2, d))],
        [ids, lengths, norms, xo, own] + received,
        after=after,
    )


def feed_body(tower, ids, lengths, h_own, h1, h2, h3, *rest):
    count = 2 * ZN
    urgent, late, rest = rest[:count], rest[count : count + 2], rest[count + 2 :]
    if tower is TXT:
        pooled, w1, w2, slope, sums, *y_out = rest
    else:
        pooled, *y_txt, sums_txt, w1, w2, slope, sums, y0, y1, y2, y3 = rest
        y_out = (y0, y1, y2, y3)
    side, z, m = ids[0], ids[1], ids[2]
    d, w, sr = tower.d, tower.w, tower.sr
    tail = d // 8

    def read(target, start, skip, count):
        def use(first, second):
            part = half_rows(tower, first, second)
            target[start : start + count, :] = part[skip : skip + count]

        return use

    def read_both(first, second):
        part = half_rows(tower, first, second)
        w1[tail + 2 * sr :, :] = part[:tail]
        w2[:w, :] = part[tail:]

    with_halves(urgent, side, z, 2, read(w1, 0, w, tail))
    with_halves(urgent, side, z, 3, read(w1, tail, 0, sr))
    with_halves(late, side, z, 0, read(w1, tail + sr, 0, sr))
    with_halves(late, side, z, 1, read_both)
    with_halves(late, side, z, 2, read(w2, w, 0, sr))
    with_halves(late, side, z, 3, read(w2, w + sr, 0, sr))
    sums_places, y_places = [], []
    for k, block in enumerate((h_own, h1, h2, h3)):
        pre = dot(block[...], w1[...])
        gate = jax.nn.sigmoid(GELU_SLOPE * pre)
        acted = (pre * gate).astype(BF).astype(F32)
        slope[k * tower.rows : (k + 1) * tower.rows, :] = gate + GELU_SLOPE * pre * gate * (
            1.0 - gate
        )
        summed = []
        counts = []
        for j in range(2):
            inside, count = row_mask(tower, lengths, 2 * (m ^ k) + j)
            part = acted[j * tower.padded : (j + 1) * tower.padded]
            summed.append(jnp.sum(jnp.where(inside, part, 0.0), axis=0, keepdims=True))
            counts.append(jnp.full((1, 1), count, F32))
        both = jnp.concatenate(summed, axis=0)
        sums_places.append(both)
        high, low, rest = pieces(both, 3)
        y = dot(high, w2[...]) + (dot(low, w2[...]) + dot(rest, w2[...]))
        y = y / jnp.concatenate(counts, axis=0)
        if k == 0:
            y = y + pooled[...]
        y_places.append(y)

    def in_order(places):
        def chunk(c):
            value = places[c ^ 3]
            for member in range(3):
                value = jnp.where(m == member, places[c ^ member], value)
            return value

        return jnp.concatenate([chunk(c) for c in range(MP)], axis=0)

    ordered = in_order(sums_places)
    if tower is TXT:
        sums[...] = ordered
        for target, value in zip(y_out, y_places):
            target[...] = value
        return
    for target, value, other in zip(y_out, y_places, y_txt):
        target[:, :d] = value
        target[:, d:] = other[...]
    sums[...] = jnp.zeros(sums.shape, F32)
    for part, values, first in ((IMG, ordered, 0), (TXT, sums_txt[...], SUM_TXT)):
        start = part.d // 8
        sums[5, :, first + start : first + part.sr] = values[:, : part.sr - start]
        for s in (6, 7):
            at = part.sr * (s - 5) - start
            sums[s, :, first : first + part.sr] = values[:, at : at + part.sr]


SUM_TXT = 384
SUM_WIDTH = SUM_TXT + 256


def feed_call(tower, ids, lengths, blocks, urgent, late, pooled, before=()):
    d = tower.d
    wide = d if tower is TXT else D_IMG + D_TXT
    sums = (SEQS, d) if tower is TXT else (2 * ZN, SEQS, SUM_WIDTH)
    return kernel_call(
        functools.partial(feed_body, tower),
        [
            out((d, d), BF),
            out((d, d), BF),
            out((tower.all_rows, d)),
            out(sums),
        ]
        + [out((2, wide))] * MP,
        [ids, lengths] + blocks + urgent + late + [pooled] + list(before),
        us=6.4,
    )


def project_body(gathered, pi, pt, flat):
    for e in range(4):
        base = e * (2 * VEC_ROWS - 1)
        flat[base : base + VEC_ROWS, :] = gathered[2 * e].astype(F32)
        odd = gathered[2 * e + 1].astype(F32)
        row = base + VEC_ROWS - 1
        flat[row : row + 1, :] = flat[row : row + 1, :] + odd[:1]
        flat[row + 1 : row + VEC_ROWS, :] = odd[1:]
    for j in range(4):
        pi[:, 128 * j : 128 * (j + 1)] = flat[pl.ds(NORM_ROWS + j, D_IMG, stride=4), :].astype(BF)
        pt[:, 128 * j : 128 * (j + 1)] = flat[
            pl.ds(NORM_ROWS + 4 * D_IMG + j, D_TXT, stride=4), :
        ].astype(BF)


def project_call(gathered):
    return kernel_call(
        project_body,
        [out((D_IMG, EMBED), BF), out((D_TXT, EMBED), BF)],
        [gathered],
        [pltpu.VMEM((4 * (2 * VEC_ROWS - 1) + 4, 128), F32)],
        us=2.8,
    )


def head_body(
    ids, trio, parts, norms, meta, pi, pt,
    misc, dyb_i, dyb_t, own_i, own_t, pg_i, pg_t, ng_i, ng_t, scr_i, scr_t, yall,
):
    shard = ids[3]
    total = yall.shape[0]
    for i in range(parts.shape[0]):
        yall[2 * i : 2 * i + 2, :] = parts[i]
    row = lax.broadcasted_iota(jnp.int32, (total, total), 0)
    column = lax.broadcasted_iota(jnp.int32, (total, total), 1)
    eye = row == column
    place = lax.broadcasted_iota(jnp.int32, (total, 128), 0)
    lane = lax.broadcasted_iota(jnp.int32, (total, 128), 1)

    def column_of(first):
        picked = jnp.zeros((total, 128), F32)
        for s in range(2 * ZN):
            picked = jnp.where(place // SEQS == s, meta[first + s : first + s + 1, :], picked)
        return jnp.sum(jnp.where(lane == place % SEQS, picked, 0.0), axis=1, keepdims=True)

    flag_column = column_of(0)
    length_column = column_of(8)
    flag_row = jnp.sum(jnp.where(eye, flag_column, 0.0), axis=0, keepdims=True)
    row_valid = flag_column > 0.5
    column_valid = flag_row > 0.5
    count = jnp.sum(flag_column, axis=0, keepdims=True)

    def forward(tower, values, projection):
        unit_rows, inverse = unit(values)
        z = (
            unit_rows * norm_vector(norms, tower, 4) + norm_vector(norms, tower, 5)
        ).astype(BF)
        raw = dot(z, projection[...])
        scale = lax.rsqrt(jnp.sum(raw * raw, axis=-1, keepdims=True) + UNIT_EPS)
        quotient = raw * scale
        return unit_rows, inverse, z, scale, quotient, quotient.astype(BF)

    image = forward(IMG, yall[:, :D_IMG], pi)
    text = forward(TXT, yall[:, D_IMG:], pt)
    factor = jnp.exp(jnp.full((1, 1), trio[0], F32))
    e_image, e_text = image[5], text[5]

    def side(mine, others):
        logits = factor * dot_nt(mine, others)
        masked = jnp.where(column_valid, logits, MASK_LOW)
        top = jnp.max(masked, axis=1, keepdims=True)
        exponent = jnp.exp(masked - top)
        totals = jnp.sum(exponent, axis=1, keepdims=True)
        own = jnp.sum(jnp.where(eye, logits, 0.0), axis=1, keepdims=True)
        loss = jnp.sum(
            jnp.where(row_valid, top + jnp.log(totals) - own, 0.0), axis=0, keepdims=True
        )
        grad = jnp.where(row_valid, exponent / totals - eye.astype(F32), 0.0) / (2.0 * count)
        scale_part = jnp.sum(jnp.sum(grad * logits, axis=1, keepdims=True), axis=0, keepdims=True)
        return loss, grad, scale_part

    loss_i, grad_i, part_i = side(e_image, e_text)
    loss_t, grad_t, part_t = side(e_text, e_image)
    loss = (loss_i + loss_t) / (2.0 * count)
    slope = part_i + part_t
    misc[...] = jnp.concatenate(
        [
            jnp.broadcast_to(loss, (1, 128)),
            jnp.broadcast_to(slope, (1, 128)),
            jnp.zeros((6, 128), F32),
        ],
        axis=0,
    )

    def product(grad, back, others):
        sums = None
        for part in pieces(grad, 3):
            term = dot(part, others)
            sums = term if sums is None else sums + term
        for part in pieces(back, 3):
            sums = sums + dot_tn(part, others)
        return factor * sums

    def backward(tower, stored, embed_grad, projection, counts, pg, ng, dyb, scratch, own):
        unit_rows, inverse, z, scale, quotient, _ = stored
        raw_grad = (
            scale
            * (embed_grad - quotient * jnp.sum(embed_grad * quotient, axis=-1, keepdims=True))
        ).astype(BF)
        pg[...] = dot_tn(z, raw_grad)
        normed_grad = dot_nt(raw_grad, projection[...])
        ng[0:1, :] = jnp.sum(normed_grad * unit_rows, axis=0, keepdims=True)
        ng[1:2, :] = jnp.sum(normed_grad, axis=0, keepdims=True)
        grad = unit_back(normed_grad, unit_rows, inverse, norm_vector(norms, tower, 4)) / counts
        dyb[...] = grad.astype(BF)
        scratch[...] = grad
        rows = scratch[pl.ds(pl.multiple_of(shard * SEQS, 8), SEQS), :]
        for c in range(MP):
            own[c] = rows[2 * c : 2 * c + 2]

    grad_image = product(grad_i, grad_t, e_text)
    grad_text = product(grad_t, grad_i, e_image)
    backward(
        TXT, text, grad_text, pt, length_column, pg_t, ng_t, dyb_t, scr_t, own_t
    )
    backward(
        IMG, image, grad_image, pi, jnp.full((1, 1), float(IMG_LEN), F32),
        pg_i, ng_i, dyb_i, scr_i, own_i,
    )


def head_call(ids, trio, parts, norms, meta, pi, pt):
    total = 2 * parts.shape[0]
    return kernel_call(
        head_body,
        [
            out((8, 128)),
            out((total, D_IMG), BF),
            out((total, D_TXT), BF),
            out((MP, 2, D_IMG)),
            out((MP, 2, D_TXT)),
            out((D_IMG, EMBED)),
            out((D_TXT, EMBED)),
            out((2, D_IMG)),
            out((2, D_TXT)),
        ],
        [ids, trio, parts, norms, meta, pi, pt],
        [
            pltpu.VMEM((total, D_IMG), F32),
            pltpu.VMEM((total, D_TXT), F32),
            pltpu.VMEM((total, D_IMG + D_TXT), F32),
        ],
        us=5.0,
    )


def feed_back_body(
    tower, ids, lengths, h_own, h1, h2, h3, slope, dy, w1, w2, *rest
):
    if tower is TXT:
        grad_i, own, s1, s2, s3, payload, h_all, du = rest
    else:
        own, s1, s2, s3, grads, h_all, du = rest
    m = ids[2]
    rows, pad = tower.rows, tower.padded
    for k, block in enumerate((h_own, h1, h2, h3)):
        h_all[k * rows : (k + 1) * rows, :] = block[...]
    dy_rows = jnp.concatenate([dy[m ^ k] for k in range(MP)], axis=0).astype(BF)
    act = dot_nt(dy_rows, w2[...])
    targets = (own, s1, s2, s3)
    for k in range(MP):
        for j in range(2):
            inside, _ = row_mask(tower, lengths, 2 * (m ^ k) + j)
            start = k * rows + j * pad
            place = 2 * k + j
            piece = slope[start : start + pad, :] * act[place : place + 1, :]
            du[start : start + pad, :] = jnp.where(inside, piece, 0.0).astype(BF)
        part = dot_nt(du[k * rows : (k + 1) * rows, :], w1[...])
        targets[k][...] = part.astype(targets[k].dtype)
    grad = dot_tn(h_all[...], du[...]).astype(BF)
    if tower is IMG:
        grads[...] = grad
        return
    rows_i, rows_t = IMG.d // 8, TXT.d // 8
    for place, e in enumerate(FEED_ORDER):
        payload[place, :rows_i, :] = grad_i[rows_i * e : rows_i * (e + 1), :]
        part = grad[rows_t * e : rows_t * (e + 1)]
        top = FEED_ROWS - rows_i
        payload[place, rows_i:, : TXT.d] = part[:top]
        payload[place, rows_i : rows_i + 16, TXT.d :] = part[top:, :256]
        payload[place, rows_i + 16 : rows_i + 32, TXT.d :] = part[top:, 256:]
        payload[place, rows_i + 32 :, TXT.d :] = jnp.zeros((top - 32, IMG.d - TXT.d), BF)


def feed_back_call(tower, ids, lengths, blocks, slope, dy, w1, w2, grads, after=()):
    rows, d, every = tower.rows, tower.d, tower.all_rows
    return kernel_call(
        functools.partial(feed_back_body, tower),
        [
            out((rows, d)),
            out((rows, d), BF),
            out((rows, d), BF),
            out((rows, d), BF),
            out((d, d), BF) if tower is IMG else out((2 * ZN, FEED_ROWS, IMG.d), BF),
        ],
        [ids, lengths] + blocks + [slope, dy, w1, w2] + grads,
        [pltpu.VMEM((every, d), BF), pltpu.VMEM((every, d), BF)],
        after=after,
        us=5.3,
    )


def middle_back_body(tower, ids, lengths, norms, x1, dy, own, r1, r2, r3, dx1, dx1b):
    m = ids[2]
    grad = (own[...] + r1[...].astype(F32)) + (r2[...].astype(F32) + r3[...].astype(F32))
    unit_rows, inverse = unit(x1[...])
    extra = (
        jnp.sum(grad * unit_rows, axis=0, keepdims=True),
        jnp.sum(grad, axis=0, keepdims=True),
    )
    back = unit_back(grad, unit_rows, inverse, norm_vector(norms, tower, 2))
    rows = dy[m]
    position = lax.broadcasted_iota(jnp.int32, (tower.padded, 1), 0)
    for j in range(2):
        inside, _ = row_mask(tower, lengths, 2 * m + j)
        part = slice(j * tower.padded, (j + 1) * tower.padded)
        total = back[part] + jnp.where(inside, rows[j : j + 1, :], 0.0)
        dx1[part, :] = total
        high, low = [piece.astype(F32) for piece in pieces(extra[j], 2)]
        total = jnp.where(position == tower.length, high, total)
        total = jnp.where(position == tower.length + 1, low, total)
        dx1b[part, :] = total.astype(BF)


def middle_back_call(tower, ids, lengths, norms, x1, dy, own, received, after=()):
    rows, d = tower.rows, tower.d
    return kernel_call(
        functools.partial(middle_back_body, tower),
        [out((rows, d)), out((rows, d), BF)],
        [ids, lengths, norms, x1, dy, own] + received,
        after=after,
    )


def attend_back_body(
    tower, ids, d_own, d1, d2, d3, att, qkv, probs, h1, u1, wq, wo,
    own, s1, s2, s3, *rest
):
    grads, sums, d_all, dqkv, wide, backs = rest
    rows, d, w, sr = tower.rows, tower.d, tower.w, tower.sr
    tail = d // 8
    position = lax.broadcasted_iota(jnp.int32, (tower.padded, 1), 0)
    extra = [[], []]
    for k, block in enumerate((d_own, d1, d2, d3)):
        for j in range(2):
            start = j * tower.padded
            part = block[start : start + tower.padded, :].astype(F32)
            line = tower.length
            extra[j].append(part[line : line + 1] + part[line + 1 : line + 2])
            d_all[k * rows + start : k * rows + start + tower.padded, :] = jnp.where(
                position < line, part, 0.0
            ).astype(BF)
    for j in range(2):
        sums[j : j + 1, :] = (extra[j][0] + extra[j][1]) + (extra[j][2] + extra[j][3])
    targets = (own, s1, s2, s3)
    gain = jnp.zeros((1, d), F32)
    shift = jnp.zeros((1, d), F32)
    for k in range(MP):
        span = slice(k * rows, (k + 1) * rows)
        d_att = dot_nt(d_all[span, :], wo[...]).astype(BF)
        for tile in range(tower.tiles):
            start = k * rows + tile * tower.tile
            part = slice(start, start + tower.tile)
            queries, keys, values = [], [], []
            for h in range(tower.heads):
                query = qkv[part, h * HEAD : (h + 1) * HEAD]
                key = qkv[part, w + h * HEAD : w + (h + 1) * HEAD]
                value = qkv[part, 2 * w + h * HEAD : 2 * w + (h + 1) * HEAD]
                grad = d_att[
                    tile * tower.tile : (tile + 1) * tower.tile, h * HEAD : (h + 1) * HEAD
                ]
                prob = probs[(k * tower.tiles + tile) * tower.heads + h]
                values.append(dot_tn(prob.astype(BF), grad))
                prob_grad = dot_nt(grad, value)
                score = (
                    prob * (prob_grad - jnp.sum(prob * prob_grad, axis=-1, keepdims=True))
                ).astype(BF)
                queries.append(dot(score, key) * HEAD ** (-0.5))
                keys.append(dot_tn(score, query) * HEAD ** (-0.5))
            dqkv[part, :] = jnp.concatenate(queries + keys + values, axis=1).astype(BF)
        back = dot_nt(dqkv[span, :], wq[...])
        gain = gain + jnp.sum(back * u1[span, :].astype(F32), axis=0, keepdims=True)
        shift = shift + jnp.sum(back, axis=0, keepdims=True)
        backs[k, :, :] = back
    for k in range(MP):
        for j, value in enumerate((gain, shift)):
            start = j * tower.padded
            part = backs[k, start : start + tower.padded, :]
            high, low = [piece.astype(F32) for piece in pieces(value, 2)]
            part = jnp.where(position == tower.length, high, part)
            part = jnp.where(position == tower.length + 1, low, part)
            targets[k][start : start + tower.padded, :] = part.astype(targets[k].dtype)
    wide[...] = dot_tn(h1[...], dqkv[...]).astype(BF)
    out_grad = dot_tn(att[...], d_all[...]).astype(BF)
    order = WIDE_ORDER if tower is IMG else range(2 * ZN)
    for place, e in enumerate(order):
        span = slice(place * tail, (place + 1) * tail)
        if e >= 6:
            piece = out_grad[(e - 6) * tail : (e - 5) * tail]
        else:
            s, i = e // 3, e % 3
            base = s * (d // 2)
            rest = wide[base + sr : base + sr + tail, w * i : w * (i + 1)]
            piece = jnp.concatenate(
                [wide[base + i * tail : base + (i + 1) * tail, :], rest], axis=1
            )
        grads[span, :] = piece


def attend_back_call(tower, ids, blocks, att, qkv, probs, h1, u1, wq, wo, after=()):
    rows, d, w, every = tower.rows, tower.d, tower.w, tower.all_rows
    return kernel_call(
        functools.partial(attend_back_body, tower),
        [
            out((rows, d)),
            out((rows, d), BF),
            out((rows, d), BF),
            out((rows, d), BF),
            out((d, d), BF),
            out((2, d)),
        ],
        [ids] + blocks + [att, qkv, probs, h1, u1, wq, wo],
        [
            pltpu.VMEM((every, d), BF),
            pltpu.VMEM((every, 3 * w), BF),
            pltpu.VMEM((d, 3 * w), BF),
            pltpu.VMEM((MP, rows, d), F32),
        ],
        after=after,
        us=10.4,
    )


def entry_body(tower, norms, xo, dx1, second, own, r1, r2, r3, *rest):
    if tower is IMG:
        dx, sums = rest
    else:
        dx_i, payload, sums = rest
    grad = (own[...] + r1[...].astype(F32)) + (r2[...].astype(F32) + r3[...].astype(F32))
    line = tower.length
    sums[0:1, :] = grad[line : line + 1] + grad[line + 1 : line + 2]
    line += tower.padded
    sums[1:2, :] = grad[line : line + 1] + grad[line + 1 : line + 2]
    sums[2:4, :] = second[...]
    unit_rows, inverse = unit(xo[...])
    back = unit_back(grad, unit_rows, inverse, norm_vector(norms, tower, 0))
    result = (dx1[...] + back).astype(BF)
    if tower is IMG:
        dx[...] = result
        return
    top = IMG.rows
    rest = TXT.rows - top
    for member in range(MP):
        payload[member, :top, :] = dx_i[...]
        payload[member, top:, : TXT.d] = result[:top]
        payload[member, top : top + rest, TXT.d :] = result[top:, :256]
        payload[member, top + rest : top + 2 * rest, TXT.d :] = result[top:, 256:]
        payload[member, top + 2 * rest :, TXT.d :] = jnp.zeros(
            (top - 2 * rest, IMG.d - TXT.d), BF
        )


def entry_call(tower, norms, xo, dx1, second, own, received, before=(), after=()):
    rows, d = tower.rows, tower.d
    return kernel_call(
        functools.partial(entry_body, tower),
        [out((rows, d), BF) if tower is IMG else out((MP, 2 * IMG.rows, IMG.d), BF), out((4, d))],
        [norms, xo, dx1, second, own] + received + list(before),
        after=after,
    )


def place_body(tower, blocks, result, flat):
    top = IMG.rows
    rest = TXT.rows - top
    for c in range(MP):
        block = blocks.at[c]
        if tower is IMG:
            rows = block[:top, :].astype(F32)
        else:
            low = jnp.concatenate(
                [
                    block[top : top + rest, TXT.d :],
                    block[top + rest : top + 2 * rest, TXT.d :],
                ],
                axis=1,
            )
            rows = jnp.concatenate([block[top:, : TXT.d], low], axis=0).astype(F32)
        for j in range(2):
            seq = 2 * c + j
            part = rows[j * tower.padded : j * tower.padded + tower.length]
            for i in range(tower.q):
                flat.at[i][pl.ds(seq, tower.length, stride=SEQS), :] = part[
                    :, 128 * i : 128 * (i + 1)
                ]
    for i in range(tower.q):
        result[:, :, 128 * i : 128 * (i + 1)] = flat[i].reshape(tower.length, SEQS, 128)


def place_call(tower, blocks):
    return kernel_call(
        functools.partial(place_body, tower),
        [out((tower.length, SEQS, tower.d))],
        [blocks],
        [pltpu.VMEM((tower.q, tower.length * SEQS, 128), F32)],
        vmem=PLACE_VMEM,
        us=2.7,
    )[0]


def attend_split_body(tower, ids, mine, received, own, s1, s2, s3, total):
    z = ids[1]
    total[...] = mine[...].astype(F32) + received[...].astype(F32)
    top = tower.d - tower.sr
    for k, target in enumerate((own, s1, s2, s3)):
        start = jnp.minimum((z ^ k) * tower.sr, top)
        part = total[pl.ds(pl.multiple_of(start, 8), tower.sr), :]
        target[...] = part.astype(target.dtype)


def attend_split_call(tower, ids, mine, received, after=()):
    payload = out((tower.sr, tower.d), BF)
    return kernel_call(
        functools.partial(attend_split_body, tower),
        [out((tower.sr, tower.d)), payload, payload, payload],
        [ids, mine, received],
        [pltpu.VMEM((tower.d, tower.d), F32)],
        after=after,
    )


def down_body(tower, sums, dyb, result):
    first = 0 if tower is IMG else SUM_TXT
    rows = jnp.concatenate([sums[s] for s in range(2 * ZN)], axis=0)
    high, low = pieces(rows[:, first : first + tower.sr], 2)
    result[...] = dot_tn(high, dyb[...]) + dot_tn(low, dyb[...])


def down_call(tower, sums, dyb):
    return kernel_call(
        functools.partial(down_body, tower),
        [out((tower.sr, tower.d))],
        [sums, dyb],
        us=1.8,
    )[0]


def vector_body(ids, pg_i, pg_t, ng_i, ng_t, window, flat):
    flat[:64, :] = jnp.zeros((64, 128), F32)
    for tower, sums in ((IMG, ng_i), (TXT, ng_t)):
        for i in range(2):
            start = tower.norm_row + (4 + i) * tower.q
            for j in range(tower.q):
                flat[start + j : start + j + 1, :] = sums[i : i + 1, 128 * j : 128 * (j + 1)]
    for j in range(4):
        flat[pl.ds(NORM_ROWS + j, D_IMG, stride=4), :] = pg_i[:, 128 * j : 128 * (j + 1)]
        flat[pl.ds(NORM_ROWS + 4 * D_IMG + j, D_TXT, stride=4), :] = pg_t[
            :, 128 * j : 128 * (j + 1)
        ]
    low_lanes = lax.broadcasted_iota(jnp.int32, (VEC_ROWS, 128), 1) < 64
    last = lax.broadcasted_iota(jnp.int32, (VEC_ROWS, 128), 0) == VEC_ROWS - 1
    for s in range(8):

        def copy(s=s):
            start = (s * (2 * VEC_ROWS - 1)) // 2
            part = flat[start : start + VEC_ROWS, :]
            if s % 2 == 1:
                after = pltpu.roll(flat[start + 1 : start + 1 + VEC_ROWS, :], 64, 1)
                part = jnp.where(low_lanes, pltpu.roll(part, 64, 1), after)
            window[...] = jnp.where(last & jnp.logical_not(low_lanes), 0.0, part)

        pl.when(ids[3] == s)(copy)


def vector_call(ids, pg_i, pg_t, ng_i, ng_t, after=()):
    return kernel_call(
        vector_body,
        [out((VEC_ROWS, 128))],
        [ids, pg_i, pg_t, ng_i, ng_t],
        [pltpu.VMEM((4 * (2 * VEC_ROWS - 1) + 12, 128), F32)],
        after=after,
        us=2.9,
    )[0]


def collect_body(
    ids, f_own, q_own, ra, rb, bt, bt1, bt2, bt3, down_i, down_t, window,
    sums_i, sums_t, lin_i, lin_t, message, rows_i, rows_t, spare,
):
    shard = ids[3]
    q = IMG.d // 8

    def put(*blocks):
        for i, block in enumerate(blocks):
            rows_i[q * i : q * (i + 1), :] = block[:q, :].astype(F32)

    pl.when(shard < 2)(lambda: put(q_own, ra, rb))
    pl.when(shard == 2)(lambda: put(q_own, ra))

    @pl.when(shard < 3)
    def _():
        rows_t[...] = (bt[...] + bt1[...].astype(F32)) + (
            bt2[...].astype(F32) + bt3[...].astype(F32)
        )

    @pl.when(shard >= 5)
    def _():
        rows_i[...] = down_i[...]
        rows_t[...] = down_t[...]

    @pl.when(shard == 2)
    def _():
        kept = rows_t[TXT.sr - TXT.w :, :]
        rows_t[: TXT.w, :] = kept

    tq = TXT.d // 8

    def feed(start, *blocks):
        for i, block in enumerate(blocks):
            rows_i[q * (start + i) : q * (start + i + 1), :] = block[:q, :].astype(F32)
            low = jnp.concatenate([block[q : q + 16, TXT.d :], block[q + 16 : q + 32, TXT.d :]], axis=1)
            part = jnp.concatenate([block[q:, : TXT.d], low], axis=0)
            rows_t[tq * (start + i) : tq * (start + i + 1), :] = part.astype(F32)

    pl.when(shard == 2)(lambda: feed(2, f_own))
    pl.when((shard == 3) | (shard == 4))(lambda: feed(0, f_own, ra, rb))
    pl.when(shard == 5)(lambda: feed(0, f_own))

    rows_to_lin(IMG, rows_i, lin_i, spare, shard)
    rows_to_lin(TXT, rows_t, lin_t, spare, shard)
    def total_of(value):
        return jnp.sum(value * value, axis=0, keepdims=True)

    every = total_of(window[...]) * (1.0 / MP)
    for j in range(IMG.q):
        every = every + total_of(rows_i[:, 128 * j : 128 * (j + 1)])
    for j in range(TXT.q):
        every = every + total_of(rows_t[:, 128 * j : 128 * (j + 1)])
    m = ids[2]

    def own_line(sums):
        line = sums[3:4, :]
        for member in range(3):
            line = jnp.where(m == member, sums[member : member + 1, :], line)
        return line

    line = jnp.concatenate([own_line(sums_i), own_line(sums_t)], axis=1)
    block = jnp.concatenate(
        [every] + [line[:, 128 * j : 128 * (j + 1)] for j in range(IMG.q + TXT.q)], axis=0
    )
    for peer in range(2 * ZN * MP):
        message[peer, : MESSAGE_ROWS, :] = block
        message[peer, MESSAGE_ROWS:, :] = jnp.zeros((16 - MESSAGE_ROWS, 128), F32)


MESSAGE_ROWS = 1 + IMG.q + TXT.q


def collect_call(ids, moved, attend_t, down_i, down_t, window, sums_i, sums_t, after):
    return kernel_call(
        collect_body,
        [out((IMG.lin, 128)), out((TXT.lin, 128)), out((2 * ZN * MP, 16, 128))],
        [ids] + moved + attend_t + [down_i, down_t, window, sums_i, sums_t],
        [
            pltpu.VMEM((IMG.sr, IMG.d), F32),
            pltpu.VMEM((TXT.sr, TXT.d), F32),
            pltpu.VMEM(SPARE, F32),
        ],
        us=3.8,
        after=after,
    )


def advance_body(
    ids, trio, parts, misc, ip, im, iv, ig, tp, tm, tv, tg, vp, vm, vv, vg,
    loss_out, size_out, trio_out, ipn, icn, imn, ivn, tpn, tcn, tmn, tvn, vpn, vcn, vmn, vvn, grad_v,
):
    slope = misc[1:2, :]
    grad_v[...] = vg[...]
    norm_squares = jnp.zeros((1, 128), F32)
    for member in range(MP):
        lines = parts[member]
        for group in range(1, 2 * ZN):
            lines = lines + parts[group * MP + member]
        if member == 0:
            squares = lines[:1]
        else:
            squares = squares + lines[:1]
        lines = lines[1:MESSAGE_ROWS]
        norm_squares = norm_squares + jnp.sum(lines * lines, axis=0, keepdims=True)

        @pl.when((ids[3] == 0) & (pl.program_id(0) == 0))
        def _(member=member, lines=lines):
            start = member * IMG.q
            grad_v[start : start + IMG.q, :] = lines[: IMG.q]
            start = TXT.norm_row + member * TXT.q
            grad_v[start : start + TXT.q, :] = lines[IMG.q :]

    total = jnp.sum(squares + norm_squares, axis=1, keepdims=True)
    size = jnp.sqrt(total + slope * slope)
    clip = CLIP_LEVEL / jnp.maximum(size, CLIP_LEVEL)

    def step(master, first, second, grad, rate, decay):
        clipped = grad * clip
        first_new = BETA_ONE * first + (1.0 - BETA_ONE) * clipped
        second_new = BETA_TWO * second + (1.0 - BETA_TWO) * clipped * clipped
        update = (first_new * (1.0 / (1.0 - BETA_ONE**STEP))) / (
            jnp.sqrt(second_new * (1.0 / (1.0 - BETA_TWO**STEP))) + ADAM_EPS
        )
        return master - rate * (update + decay * master), first_new, second_new

    for master, first, second, grad, a, b, c, e in (
        (ip, im, iv, ig, ipn, icn, imn, ivn),
        (tp, tm, tv, tg, tpn, tcn, tmn, tvn),
    ):
        new, first_new, second_new = step(
            master[...], first[...], second[...], grad[...], RATE_MATRIX, WEIGHT_DECAY
        )
        a[...] = new
        b[:, 0, :] = new.astype(BF)
        c[...] = first_new
        e[...] = second_new
    rows = VEC_ROWS // ADVANCE_STEPS
    row = lax.broadcasted_iota(jnp.int32, (rows, 128), 0) + pl.program_id(0) * rows
    is_norm = row < jnp.where(ids[3] == 0, NORM_ROWS, 0)
    new, first_new, second_new = step(
        vp[...],
        vm[...],
        vv[...],
        grad_v[...],
        jnp.where(is_norm, RATE_VECTOR, RATE_MATRIX),
        jnp.where(is_norm, 0.0, WEIGHT_DECAY),
    )
    vpn[...] = new
    vcn[...] = new.astype(BF)
    vmn[...] = first_new
    vvn[...] = second_new
    lane_row = jnp.zeros((1, 128), F32)
    new, _, _ = step(
        lane_row + trio[0], lane_row + trio[1], lane_row + trio[2], slope, LOGIT_SPEED, 0.0
    )
    loss_out[...] = misc[0:1, :1]
    size_out[...] = size[:, :1]
    trio_out[...] = new[:, :1]


PLACE_VMEM = 62
ADVANCE_STEPS = 3


def advance_call(ids, trio, parts, misc, image, text, vector):
    ins = [ids, trio, parts, misc] + image + text + vector

    def spec(shape, cut):
        block = (shape[0] // ADVANCE_STEPS if cut else shape[0],) + tuple(shape[1:])
        rest = (0,) * (len(shape) - 1)
        return pl.BlockSpec(block, lambda i: ((i if cut else 0),) + rest)

    outs = [out((1, 1))] * 3
    for rows in (IMG.lin, TXT.lin, VEC_ROWS):
        copied = (rows, 128) if rows == VEC_ROWS else (rows, 1, 128)
        outs += [out((rows, 128)), out(copied, BF), out((rows, 128)), out((rows, 128))]
    scalars = pl.BlockSpec(memory_space=pltpu.SMEM)
    return pl.pallas_call(
        advance_body,
        grid=(ADVANCE_STEPS,),
        out_shape=outs,
        in_specs=[scalars, scalars] + [spec(v.shape, i > 1) for i, v in enumerate(ins[2:])],
        out_specs=[spec(v.shape, i > 2) for i, v in enumerate(outs)],
        scratch_shapes=[pltpu.VMEM((VEC_ROWS // ADVANCE_STEPS, 128), F32)],
        compiler_params=pltpu.CompilerParams(vmem_limit_bytes=62 * MIB),
        cost_estimate=pl.CostEstimate(
            flops=int(COST_SCALE * 7), bytes_accessed=0, transcendentals=0
        ),
    )(*ins)


def hop(value, axis, mask):
    size = lax.axis_size(axis)
    return lax.ppermute(value, axis, [(i, i ^ mask) for i in range(size)])


def peers(values):
    return [hop(value, "mp", k) for k, value in zip((1, 2, 3), values)]


def spread(value):
    near, far = hop(value, "dp", 1), hop(value, "dp", 2)
    here = [value, near, far, hop(far, "dp", 1)]
    return here + [hop(block, "tower", 1) for block in here]


def merge(value, axis, mask):
    other = hop(value, axis, mask)
    upper = (lax.axis_index(axis) & mask) != 0
    return jnp.where(
        upper, jnp.concatenate([other, value], axis=0), jnp.concatenate([value, other], axis=0)
    )


FEED_ORDER = (5, 6, 0, 1, 4, 7, 3, 2)
WIDE_ORDER = (0, 3, 6, 5, 1, 4, 7, 2)
MOVES = (
    ((7, 0), ((7, 3), (0, 4), (4, 0), (5, 1), (6, 2))),
    ((6, 1), ((6, 3), (1, 4), (7, 0), (3, 1))),
)


def moves(feed, wide, shard):
    wide = jnp.pad(wide, ((0, feed.shape[0] - wide.shape[0]), (0, 0)))
    results = []
    for senders, pairs in MOVES:
        first, second = senders
        chosen = jnp.where((shard == first) | (shard == second), feed, wide)
        results.append(lax.ppermute(chosen, GROUP, list(pairs)))
    return results


def attend_perm(mask):
    return [(z ^ mask, z) for z in range(3)]


def fast_local(
    picture_residual_entry,
    sentence_residual_entry,
    sentence_lengths_held,
    couple_allowed_flags,
    picture_single_matrices,
    picture_mean_state,
    picture_square_state,
    sentence_single_matrices,
    sentence_mean_state,
    sentence_square_state,
    array_single_params,
    array_mean_state,
    array_square_state,
    logit_log_trio,
):
    LAST.clear()
    side, z, m = lax.axis_index("tower"), lax.axis_index("dp"), lax.axis_index("mp")
    ids = jnp.stack([side, z, m, side * ZN + z]).astype(jnp.int32)
    lengths = sentence_lengths_held
    vec_size = array_single_params.shape[0]

    def lines(value):
        return value.reshape(-1, 128)

    def vector_lines(value):
        return jnp.pad(value, (0, VEC_ROWS * 128 - vec_size)).reshape(VEC_ROWS, 128)

    vec_lines = vector_lines(array_single_params)
    keep_t, keep_i, send_t, send_i, block = kernel_call(
        prepare_body,
        [out((TXT.half, TXT.d), BF), out((IMG.half, IMG.d), BF)] * 2 + [out((16, TXT.d), BF)],
        [
            ids,
            couple_allowed_flags,
            lengths,
            lines(picture_single_matrices),
            lines(sentence_single_matrices),
            vec_lines,
        ],
        [
            pltpu.VMEM((IMG.sr, IMG.d), F32),
            pltpu.VMEM((TXT.sr, TXT.d), F32),
            pltpu.VMEM(SPARE, F32),
        ],
        us=2.5,
    )
    urgent, late = kernel_call(
        sort_body,
        [out((URGENT, IMG.d), BF), out((HALF, IMG.d), BF)],
        [ids, keep_t, keep_i, hop(send_t, "tower", 1), hop(send_i, "tower", 1), block],
    )
    urgent = spread(urgent)
    late = lax.all_gather(gate(late, *urgent[1:ZN]), "dp", axis=0, tiled=True)
    vecpay = kernel_call(
        vector_pay_body,
        [out((VEC_ROWS, 128), BF)],
        [ids, vec_lines],
        [pltpu.VMEM((VEC_ROWS + 8, 128), F32)],
    )[0]
    x_txt = jnp.transpose(sentence_residual_entry, (1, 0, 2))
    x_img = jnp.transpose(picture_residual_entry, (1, 0, 2))
    norms, meta, *t_out = attend_call(TXT, ids, x_txt, urgent)
    i_out = attend_call(IMG, ids, x_img, urgent, norms=norms)
    layers = {}
    before = ()
    middles = {}
    for tower, outs in ((TXT, t_out), (IMG, i_out)):
        xo, own, s1, s2, s3 = outs[7:]
        x1, h2, pooled = middle_call(
            tower, ids, lengths, norms, xo, own, peers([s1, s2, s3])
        )
        middles[tower] = (x1, pooled, [h2] + peers([h2, h2, h2]))
    late = gate(late, x1, *middles[TXT][2][1:])
    late = [late, hop(late, "tower", 1)]
    gathered = lax.all_gather(gate(vecpay, late[0]), GROUP, axis=0, tiled=False)
    for tower, outs in ((TXT, t_out), (IMG, i_out)):
        wq, wo, h1, u1, qkv, att, probs, xo = outs[:8]
        x1, pooled, blocks = middles[tower]
        w1, w2, slope, sums, *y = feed_call(
            tower, ids, lengths, blocks, urgent, late, pooled, before
        )
        before = (*y, sums)
        layers[tower] = dict(
            wq=wq, wo=wo, h1=h1, u1=u1, qkv=qkv, att=att, probs=probs, xo=xo,
            x1=x1, blocks=blocks, w1=w1, w2=w2, slope=slope,
        )

    received = peers(y[1:])
    y = (y[0] + received[0]) + (received[1] + received[2])
    parts = lax.all_to_all(
        jnp.broadcast_to(y, (2 * ZN * MP, *y.shape)), (*GROUP, "mp"), 0, 0, tiled=True
    )
    pi, pt = project_call(gathered)
    misc, dyb_i, dyb_t, dy_i, dy_t, pg_i, pg_t, ng_i, ng_t = head_call(
        ids, logit_log_trio, parts, norms, meta, pi, pt
    )

    dy = {IMG: dy_i, TXT: dy_t}
    back, dx1, dx1b, second = {}, {}, {}, {}
    entries, norm_sums = {}, {}
    grads = []
    for tower in (IMG, TXT):
        s = layers[tower]
        back[tower] = feed_back_call(
            tower, ids, lengths, s["blocks"], s["slope"], dy[tower], s["w1"], s["w2"], grads
        )
        grads = [back[tower][4]]
    feed_own = lax.psum_scatter(back[TXT][4], GROUP, scatter_dimension=0, tiled=False)
    window = vector_call(ids, pg_i, pg_t, ng_i, ng_t)
    for tower in (IMG, TXT):
        own, s1, s2, s3 = back[tower][:4]
        dx1[tower], dx1b[tower] = middle_back_call(
            tower, ids, lengths, norms, layers[tower]["x1"], dy[tower], own, peers([s1, s2, s3])
        )
    sums = lax.all_to_all(gate(sums, dx1[TXT]), GROUP, 0, 0, tiled=True)
    for tower in (IMG, TXT):
        s = layers[tower]
        block = dx1b[tower]
        *back[tower], grads, second[tower] = attend_back_call(
            tower, ids, [block] + peers([block] * 3),
            s["att"], s["qkv"], s["probs"], s["h1"], s["u1"], s["wq"], s["wo"],
        )
        if tower is IMG:
            quarter = lax.psum_scatter(
                gate(grads.reshape(2 * ZN, IMG.d // 8, IMG.d), feed_own), GROUP, scatter_dimension=0, tiled=False
            )
    moved = lax.ppermute(grads, "tower", [(1, 0)])
    before = ()
    for tower in (IMG, TXT):
        own, s1, s2, s3 = back[tower]
        dx, norm_sums[tower] = entry_call(
            tower, norms, layers[tower]["xo"], dx1[tower], second[tower], own,
            peers([s1, s2, s3]), before,
        )
        before = (dx,)
        if tower is IMG:
            down = {IMG: down_call(IMG, sums, dyb_i)}
    pa, p1, p2, p3 = attend_split_call(TXT, ids, grads, moved)
    text_parts = [pa] + [
        lax.ppermute(value, GROUP, attend_perm(k)) for k, value in ((1, p1), (2, p2), (3, p3))
    ]
    down[TXT] = down_call(TXT, sums, dyb_t)
    moved = moves(feed_own, quarter, ids[3])
    placed = lax.all_to_all(dx, "mp", 0, 0, tiled=True)
    lin_i, lin_t, message = collect_call(
        ids, [feed_own, quarter, *moved], text_parts, down[IMG], down[TXT], window,
        norm_sums[IMG], norm_sums[TXT], [placed],
    )
    parts = lax.all_to_all(message, (*GROUP, "mp"), 0, 0, tiled=True)
    for tower in (IMG, TXT):
        entries[tower] = place_call(tower, placed)
    loss, size, temperature, *new = advance_call(
        ids,
        logit_log_trio,
        parts,
        misc,
        [lines(picture_single_matrices), lines(picture_mean_state), lines(picture_square_state), lin_i],
        [
            lines(sentence_single_matrices),
            lines(sentence_mean_state),
            lines(sentence_square_state),
            lin_t,
        ],
        [vec_lines, vector_lines(array_mean_state), vector_lines(array_square_state), window],
    )

    def flat(value, like):
        return value.reshape(-1)[: like.size].reshape(like.shape)

    likes = [picture_single_matrices] * 4 + [sentence_single_matrices] * 4 + [array_single_params] * 4
    news = [flat(value, like) for value, like in zip(new, likes)]
    return (
        loss.reshape(()),
        size.reshape(()),
        jnp.transpose(entries[IMG], (1, 0, 2)),
        jnp.transpose(entries[TXT], (1, 0, 2)),
        *news,
        temperature.reshape(()),
    )


def fits(mesh):
    return mesh.shape["tower"] == 2 and mesh.shape["dp"] == ZN and mesh.shape["mp"] == MP


def solution(mesh):
    placed = (
        P(GROUP, None, None),
        P(GROUP, None, None),
        P(GROUP),
        P(GROUP),
        P("mp", GROUP),
        P("mp", GROUP),
        P("mp", GROUP),
        P("mp", GROUP),
        P("mp", GROUP),
        P("mp", GROUP),
        P(GROUP),
        P(GROUP),
        P(GROUP),
        P(),
    )
    return jax.shard_map(
        fast_local if fits(mesh) else local,
        mesh=mesh,
        in_specs=placed,
        out_specs=(
            P(),
            P(),
            P(GROUP, None, None),
            P(GROUP, None, None),
            P("mp", GROUP),
            P("mp", GROUP),
            P("mp", GROUP),
            P("mp", GROUP),
            P("mp", GROUP),
            P("mp", GROUP),
            P("mp", GROUP),
            P("mp", GROUP),
            P(GROUP),
            P(GROUP),
            P(GROUP),
            P(GROUP),
            P(),
        ),
        check_vma=False,
    )
```

```python
import functools
import jax
import jax.numpy as jnp
from jax import lax
from jax.experimental import pallas as pl
from jax.experimental.pallas import tpu as pltpu
from jax.sharding import PartitionSpec as P

BF = jnp.bfloat16
F32 = jnp.float32
GROUP = ("tower", "dp")

D_IMG = 768
FF_IMG = 3072
IMG_LEN = 50
D_TXT = 512
FF_TXT = 2048
TXT_LEN = 77
HEAD = 64
EMBED = 512
STEP = 10


NORM_EPS = 1e-05
UNIT_EPS = 1e-06
BETA_ONE = 0.5
BETA_TWO = 0.5
ADAM_EPS = 1e-08
WEIGHT_DECAY = 0.1
RATE_MATRIX = 0.04
RATE_VECTOR = 0.3
LOGIT_SPEED = 0.5
CLIP_LEVEL = 0.005
MASK_LOW = -1e30
GELU_SLOPE = 1.702
BLOCK_TARGET = 512


def branch_sum(partial_sum):
    return lax.psum(partial_sum, "mp")


def branch_back(partial_sum):
    return lax.psum(partial_sum, "mp")


def norm_forward(values, norm_gain, norm_shift):
    centered = values - jnp.mean(values, axis=-1, keepdims=True)
    inverse = lax.rsqrt(jnp.mean(centered * centered, axis=-1, keepdims=True) + NORM_EPS)
    unit_rows = centered * inverse
    return (unit_rows * norm_gain + norm_shift, unit_rows, inverse)


def norm_backward(grad_rows, unit_rows, inverse, norm_gain):
    scaled = grad_rows * norm_gain
    centered_grad = (
        scaled
        - jnp.mean(scaled, axis=-1, keepdims=True)
        - unit_rows * jnp.mean(scaled * unit_rows, axis=-1, keepdims=True)
    )
    return (
        centered_grad * inverse,
        jnp.sum(grad_rows * unit_rows, axis=0),
        jnp.sum(grad_rows, axis=0),
    )


def quick_gelu(values):
    return values * jax.nn.sigmoid(GELU_SLOPE * values)


def gelu_slope(values):
    sigmoid_value = jax.nn.sigmoid(GELU_SLOPE * values)
    return sigmoid_value + GELU_SLOPE * values * sigmoid_value * (1.0 - sigmoid_value)


def block_size(seq_count, seq_length):
    for candidate in range(1, seq_count + 1):
        if seq_count % candidate == 0 and candidate * seq_length >= BLOCK_TARGET:
            return candidate
    return seq_count


def sequence_mask(seq_length, causal):
    position = lax.iota(jnp.int32, seq_length)
    if causal:
        return position[None, :] <= position[:, None]
    return position[None, :] >= 0


def block_scores(block_qkv, allowed):
    scores = jnp.einsum(
        "nqhd,nkhd->nhqk",
        block_qkv[:, :, 0],
        block_qkv[:, :, 1],
        preferred_element_type=jnp.float32,
    ) * HEAD ** (-0.5)
    return jnp.where(allowed[None, None], scores, MASK_LOW)


def attend(packed, seq_count, seq_length, causal):
    head_count = packed.shape[2]
    per_block = block_size(seq_count, seq_length)
    blocks = packed.reshape(seq_count // per_block, per_block, seq_length, 3, head_count, HEAD)
    allowed = sequence_mask(seq_length, causal)

    def one_block(block_qkv):
        scores = block_scores(block_qkv, allowed)
        row_max = jnp.max(scores, axis=-1, keepdims=True)
        exponent = jnp.exp(scores - row_max)
        totals = jnp.sum(exponent, axis=-1, keepdims=True)
        probs = (exponent / totals).astype(jnp.bfloat16)
        result = jnp.einsum(
            "nhqk,nkhd->nqhd", probs, block_qkv[:, :, 2], preferred_element_type=jnp.float32
        ).astype(jnp.bfloat16)
        return (result, (row_max + jnp.log(totals))[..., 0])

    results, log_totals = lax.map(one_block, blocks)
    return (results.reshape(packed.shape[0], head_count * HEAD), log_totals)


def attend_back(packed, attended_grad, log_totals, seq_count, seq_length, causal):
    head_count = packed.shape[2]
    per_block = block_size(seq_count, seq_length)
    block_total = seq_count // per_block
    blocks = packed.reshape(block_total, per_block, seq_length, 3, head_count, HEAD)
    grad_blocks = attended_grad.reshape(block_total, per_block, seq_length, head_count, HEAD)
    allowed = sequence_mask(seq_length, causal)

    def one_block(block_args):
        block_qkv, block_grad, block_totals = block_args
        scores = block_scores(block_qkv, allowed)
        probs = jnp.exp(scores - block_totals[..., None])
        value_grad = jnp.einsum(
            "nhqk,nqhd->nkhd",
            probs.astype(jnp.bfloat16),
            block_grad,
            preferred_element_type=jnp.float32,
        )
        prob_grad = jnp.einsum(
            "nqhd,nkhd->nhqk", block_grad, block_qkv[:, :, 2], preferred_element_type=jnp.float32
        )
        score_grad = (
            probs * (prob_grad - jnp.sum(probs * prob_grad, axis=-1, keepdims=True))
        ).astype(jnp.bfloat16)
        query_grad = jnp.einsum(
            "nhqk,nkhd->nqhd", score_grad, block_qkv[:, :, 1], preferred_element_type=jnp.float32
        ) * HEAD ** (-0.5)
        key_grad = jnp.einsum(
            "nhqk,nqhd->nkhd", score_grad, block_qkv[:, :, 0], preferred_element_type=jnp.float32
        ) * HEAD ** (-0.5)
        return jnp.stack([query_grad, key_grad, value_grad], axis=2).astype(jnp.bfloat16)

    return lax.map(one_block, (blocks, grad_blocks, log_totals)).reshape(packed.shape)


def split_flat(flat_weights, model_width, hidden, model_split):
    width_piece = model_width // model_split
    hidden_piece = hidden // model_split
    first_end = model_width * 3 * width_piece
    second_end = first_end + width_piece * model_width
    third_end = second_end + model_width * hidden_piece
    return (
        flat_weights[:first_end].reshape(model_width, 3, width_piece),
        flat_weights[first_end:second_end].reshape(width_piece, model_width),
        flat_weights[second_end:third_end].reshape(model_width, hidden_piece),
        flat_weights[third_end:].reshape(hidden_piece, model_width),
    )


def layer_forward(tokens, weights, norms, causal):
    qkv_weight, out_weight, up_weight, down_weight = weights
    seq_count, seq_length, model_width = tokens.shape
    token_rows = tokens.reshape(seq_count * seq_length, model_width).astype(jnp.float32)
    first_normed, unit_one, inverse_one = norm_forward(token_rows, norms[0], norms[1])
    first_low = first_normed.astype(jnp.bfloat16)
    packed = jnp.einsum(
        "rd,dtk->rtk", first_low, qkv_weight, preferred_element_type=jnp.float32
    ).astype(jnp.bfloat16)
    packed = packed.reshape(token_rows.shape[0], 3, qkv_weight.shape[2] // HEAD, HEAD)
    attended, log_totals = attend(packed, seq_count, seq_length, causal)
    middle = token_rows + branch_sum(
        jnp.dot(attended, out_weight, preferred_element_type=jnp.float32)
    )
    second_normed, unit_two, inverse_two = norm_forward(middle, norms[2], norms[3])
    second_low = second_normed.astype(jnp.bfloat16)
    pre_act = jnp.dot(second_low, up_weight, preferred_element_type=jnp.float32)
    activated = quick_gelu(pre_act).astype(jnp.bfloat16)
    outputs = middle + branch_sum(
        jnp.dot(activated, down_weight, preferred_element_type=jnp.float32)
    )
    return (
        outputs,
        (
            first_low,
            unit_one,
            inverse_one,
            packed,
            attended,
            log_totals,
            second_low,
            unit_two,
            inverse_two,
            pre_act,
            activated,
        ),
    )


def layer_backward(grad_out, weights, norms, stored, seq_count, seq_length, causal):
    qkv_weight, out_weight, up_weight, down_weight = weights
    (
        first_low,
        unit_one,
        inverse_one,
        packed,
        attended,
        log_totals,
        second_low,
        unit_two,
        inverse_two,
        pre_act,
        activated,
    ) = stored
    grad_low = grad_out.astype(jnp.bfloat16)
    down_grad = jnp.einsum("rf,rd->fd", activated, grad_low, preferred_element_type=jnp.float32)
    act_grad = jnp.einsum("rd,fd->rf", grad_low, down_weight, preferred_element_type=jnp.float32)
    pre_grad = (act_grad * gelu_slope(pre_act)).astype(jnp.bfloat16)
    up_grad = jnp.einsum("rd,rf->df", second_low, pre_grad, preferred_element_type=jnp.float32)
    second_grad = branch_back(
        jnp.einsum("rf,df->rd", pre_grad, up_weight, preferred_element_type=jnp.float32)
    )
    norm_grad_two, gain_two, shift_two = norm_backward(second_grad, unit_two, inverse_two, norms[2])
    middle_grad = grad_out + norm_grad_two
    middle_low = middle_grad.astype(jnp.bfloat16)
    out_grad = jnp.einsum("ra,rd->ad", attended, middle_low, preferred_element_type=jnp.float32)
    attended_grad = jnp.einsum(
        "rd,ad->ra", middle_low, out_weight, preferred_element_type=jnp.float32
    ).astype(jnp.bfloat16)
    packed_grad = attend_back(packed, attended_grad, log_totals, seq_count, seq_length, causal)
    packed_grad = packed_grad.reshape(packed.shape[0], 3, qkv_weight.shape[2])
    qkv_grad = jnp.einsum("rd,rtk->dtk", first_low, packed_grad, preferred_element_type=jnp.float32)
    first_grad = branch_back(
        jnp.einsum("rtk,dtk->rd", packed_grad, qkv_weight, preferred_element_type=jnp.float32)
    )
    norm_grad_one, gain_one, shift_one = norm_backward(first_grad, unit_one, inverse_one, norms[0])
    flat_grads = jnp.concatenate(
        [qkv_grad.reshape(-1), out_grad.reshape(-1), up_grad.reshape(-1), down_grad.reshape(-1)]
    )
    return (middle_grad + norm_grad_one, flat_grads, [gain_one, shift_one, gain_two, shift_two])


def pool_forward(picked, norm_gain, norm_shift, projection):
    normed, unit_rows, inverse = norm_forward(picked, norm_gain, norm_shift)
    normed_low = normed.astype(jnp.bfloat16)
    raw_embed = jnp.dot(normed_low, projection, preferred_element_type=jnp.float32)
    length_inverse = lax.rsqrt(jnp.sum(raw_embed * raw_embed, axis=-1, keepdims=True) + UNIT_EPS)
    embed_rows = raw_embed * length_inverse
    return (
        embed_rows.astype(jnp.bfloat16),
        (unit_rows, inverse, normed_low, embed_rows, length_inverse),
    )


def pool_backward(embed_grad, norm_gain, projection, stored):
    unit_rows, inverse, normed_low, embed_rows, length_inverse = stored
    raw_grad = (
        length_inverse
        * (embed_grad - embed_rows * jnp.sum(embed_grad * embed_rows, axis=-1, keepdims=True))
    ).astype(jnp.bfloat16)
    proj_grad = jnp.einsum("nd,ne->de", normed_low, raw_grad, preferred_element_type=jnp.float32)
    normed_grad = jnp.einsum("ne,de->nd", raw_grad, projection, preferred_element_type=jnp.float32)
    picked_grad, gain_grad, shift_grad = norm_backward(normed_grad, unit_rows, inverse, norm_gain)
    return (picked_grad, proj_grad, gain_grad, shift_grad)


def cosine_logits(picture_feature_lines, sentence_feature_lines, couple_allowed_flags, log_scale):
    image_all, text_all, valid_all = (
        lax.all_gather(picture_feature_lines, GROUP, axis=0, tiled=True),
        lax.all_gather(sentence_feature_lines, GROUP, axis=0, tiled=True),
        lax.all_gather(
            couple_allowed_flags.astype(jnp.bfloat16), GROUP, axis=0, tiled=True
        ),
    )
    count_valid = jnp.sum(valid_all.astype(jnp.float32))
    column_valid = valid_all > 0
    row_valid = couple_allowed_flags > 0
    local_count = picture_feature_lines.shape[0]
    offset_rows = lax.axis_index(GROUP) * local_count
    on_diagonal = (
        lax.iota(jnp.int32, valid_all.shape[0])[None, :]
        == offset_rows + lax.iota(jnp.int32, local_count)[:, None]
    )
    scale_factor = jnp.exp(log_scale)

    def one_side(mine, others):
        logits = scale_factor * jnp.einsum(
            "ne,me->nm", mine, others, preferred_element_type=jnp.float32
        )
        masked = jnp.where(column_valid[None, :], logits, MASK_LOW)
        row_max = jnp.max(masked, axis=1, keepdims=True)
        exponent = jnp.exp(masked - row_max)
        totals = jnp.sum(exponent, axis=1, keepdims=True)
        own_logit = jnp.sum(jnp.where(on_diagonal, logits, 0.0), axis=1)
        log_sum = row_max[:, 0] + jnp.log(totals[:, 0])
        loss_sum = jnp.sum(jnp.where(row_valid, log_sum - own_logit, 0.0))
        logit_grad = jnp.where(
            row_valid[:, None], exponent / totals - on_diagonal.astype(jnp.float32), 0.0
        ) / (2.0 * count_valid)
        return (loss_sum, logit_grad, jnp.sum(logit_grad * logits), log_sum, logits)

    image_loss, image_logit_grad, image_scale_part, image_lse, image_logits = one_side(
        picture_feature_lines, text_all
    )
    text_loss, text_logit_grad, text_scale_part, text_lse, text_logits = one_side(
        sentence_feature_lines, image_all
    )
    picture_device_share = scale_factor * jnp.dot(
        image_logit_grad, text_all.astype(jnp.float32), precision=lax.Precision.HIGHEST
    )
    sentence_device_share = scale_factor * jnp.dot(
        text_logit_grad, image_all.astype(jnp.float32), precision=lax.Precision.HIGHEST
    )
    text_spread = scale_factor * jnp.einsum(
        "np,ne->pe",
        image_logit_grad,
        picture_feature_lines.astype(jnp.float32),
        precision=lax.Precision.HIGHEST,
    )
    image_spread = scale_factor * jnp.einsum(
        "np,ne->pe",
        text_logit_grad,
        sentence_feature_lines.astype(jnp.float32),
        precision=lax.Precision.HIGHEST,
    )
    picture_reverse, sentence_reverse = (
        lax.psum_scatter(image_spread, GROUP, scatter_dimension=0, tiled=True),
        lax.psum_scatter(text_spread, GROUP, scatter_dimension=0, tiled=True),
    )
    contrast_objective, logit_log_slope = lax.psum(
        ((image_loss + text_loss) / (2.0 * count_valid), image_scale_part + text_scale_part),
        GROUP,
    )
    return (
        picture_device_share + picture_reverse,
        sentence_device_share + sentence_reverse,
        contrast_objective,
        logit_log_slope,
    )


def optimizer_advance(master, first, second, grad, rate, decay):
    first_new = BETA_ONE * first + (1.0 - BETA_ONE) * grad
    second_new = BETA_TWO * second + (1.0 - BETA_TWO) * grad * grad
    update = (
        first_new
        / (1.0 - BETA_ONE**STEP)
        / (jnp.sqrt(second_new / (1.0 - BETA_TWO**STEP)) + ADAM_EPS)
    )
    return (master - rate * (update + decay * master), first_new, second_new)


def local(
    picture_residual_entry,
    sentence_residual_entry,
    sentence_lengths_held,
    couple_allowed_flags,
    picture_single_matrices,
    picture_mean_state,
    picture_square_state,
    sentence_single_matrices,
    sentence_mean_state,
    sentence_square_state,
    array_single_params,
    array_mean_state,
    array_square_state,
    logit_log_trio,
):
    model_split = lax.axis_size("mp")
    norm_end = 6 * (D_IMG + D_TXT)
    image_end = norm_end + D_IMG * EMBED
    image_flat, text_flat, vector_flat = (
        lax.all_gather(
            picture_single_matrices.astype(jnp.bfloat16), GROUP, axis=1, tiled=True
        ),
        lax.all_gather(
            sentence_single_matrices.astype(jnp.bfloat16), GROUP, axis=1, tiled=True
        ),
        lax.all_gather(
            array_single_params.astype(jnp.bfloat16), GROUP, axis=0, tiled=True
        ),
    )
    image_norms = vector_flat[: 6 * D_IMG].reshape(6, D_IMG).astype(jnp.float32)
    text_norms = vector_flat[6 * D_IMG : norm_end].reshape(6, D_TXT).astype(jnp.float32)
    image_proj = vector_flat[norm_end:image_end].reshape(D_IMG, EMBED)
    text_proj = vector_flat[image_end:].reshape(D_TXT, EMBED)
    seq_count = picture_residual_entry.shape[0]
    image_weights = split_flat(image_flat[0], D_IMG, FF_IMG, model_split)
    image_out, image_stored = layer_forward(
        picture_residual_entry, image_weights, image_norms, False
    )
    image_picked = jnp.mean(image_out.reshape(seq_count, IMG_LEN, D_IMG), axis=1)
    picture_feature_lines, image_pool = pool_forward(
        image_picked, image_norms[4], image_norms[5], image_proj
    )
    text_weights = split_flat(text_flat[0], D_TXT, FF_TXT, model_split)
    text_out, text_stored = layer_forward(sentence_residual_entry, text_weights, text_norms, True)
    inside = (lax.iota(jnp.int32, TXT_LEN)[None, :] < sentence_lengths_held[:, None]).astype(
        jnp.float32
    )
    picker = inside / sentence_lengths_held[:, None].astype(jnp.float32)
    text_picked = jnp.einsum(
        "nl,nld->nd",
        picker,
        text_out.reshape(seq_count, TXT_LEN, D_TXT),
        precision=lax.Precision.HIGHEST,
    )
    sentence_feature_lines, text_pool = pool_forward(
        text_picked, text_norms[4], text_norms[5], text_proj
    )
    picture_feature_slope, sentence_feature_slope, contrast_objective, logit_log_slope = (
        cosine_logits(
            picture_feature_lines, sentence_feature_lines, couple_allowed_flags, logit_log_trio[0]
        )
    )
    text_picked_grad, text_proj_grad, text_post_gain, text_post_shift = pool_backward(
        sentence_feature_slope, text_norms[4], text_proj, text_pool
    )
    text_rows_grad = (picker[:, :, None] * text_picked_grad[:, None, :]).reshape(
        seq_count * TXT_LEN, D_TXT
    )
    sentence_entry_slope, text_flat_grad, text_norm_grads = layer_backward(
        text_rows_grad, text_weights, text_norms, text_stored, seq_count, TXT_LEN, True
    )
    image_picked_grad, image_proj_grad, image_post_gain, image_post_shift = pool_backward(
        picture_feature_slope, image_norms[4], image_proj, image_pool
    )
    image_rows_grad = jnp.broadcast_to(
        image_picked_grad[:, None, :] / IMG_LEN, (seq_count, IMG_LEN, D_IMG)
    ).reshape(seq_count * IMG_LEN, D_IMG)
    picture_entry_slope, image_flat_grad, image_norm_grads = layer_backward(
        image_rows_grad, image_weights, image_norms, image_stored, seq_count, IMG_LEN, False
    )
    array_param_slope = jnp.concatenate(
        [
            jnp.stack(image_norm_grads + [image_post_gain, image_post_shift]).reshape(-1),
            jnp.stack(text_norm_grads + [text_post_gain, text_post_shift]).reshape(-1),
            image_proj_grad.reshape(-1),
            text_proj_grad.reshape(-1),
        ]
    )
    image_reduced, text_reduced, vector_reduced = (
        lax.psum_scatter(
            image_flat_grad.reshape(-1, D_IMG), GROUP, scatter_dimension=0, tiled=True
        ).reshape(1, -1),
        lax.psum_scatter(
            text_flat_grad.reshape(-1, D_TXT), GROUP, scatter_dimension=0, tiled=True
        ).reshape(1, -1),
        lax.psum_scatter(array_param_slope, GROUP, scatter_dimension=0, tiled=True),
    )
    matrix_squares = jnp.sum(image_reduced * image_reduced) + jnp.sum(text_reduced * text_reduced)
    vector_squares = jnp.sum(vector_reduced * vector_reduced) / model_split
    tensor_square_sum, array_square_sum = lax.psum(
        (matrix_squares, vector_squares), (*GROUP, "mp")
    )
    global_slope_size = jnp.sqrt(
        tensor_square_sum + array_square_sum + logit_log_slope * logit_log_slope
    )
    clipping_factor = CLIP_LEVEL / jnp.maximum(global_slope_size, CLIP_LEVEL)
    picture_matrices_fresh, picture_mean_fresh, picture_square_fresh = optimizer_advance(
        picture_single_matrices,
        picture_mean_state,
        picture_square_state,
        image_reduced * clipping_factor,
        RATE_MATRIX,
        WEIGHT_DECAY,
    )
    sentence_matrices_fresh, sentence_mean_fresh, sentence_square_fresh = optimizer_advance(
        sentence_single_matrices,
        sentence_mean_state,
        sentence_square_state,
        text_reduced * clipping_factor,
        RATE_MATRIX,
        WEIGHT_DECAY,
    )
    shard_length = array_single_params.shape[0]
    vector_index = lax.axis_index(GROUP) * shard_length + lax.iota(
        jnp.int32, shard_length
    )
    is_norm = vector_index < norm_end
    array_params_fresh, array_mean_fresh, array_square_fresh = optimizer_advance(
        array_single_params,
        array_mean_state,
        array_square_state,
        vector_reduced * clipping_factor,
        jnp.where(is_norm, RATE_VECTOR, RATE_MATRIX),
        jnp.where(is_norm, 0.0, WEIGHT_DECAY),
    )
    logit_log_fresh, logit_mean_fresh, logit_square_fresh = optimizer_advance(
        logit_log_trio[0],
        logit_log_trio[1],
        logit_log_trio[2],
        logit_log_slope * clipping_factor,
        LOGIT_SPEED,
        0.0,
    )
    return (
        contrast_objective,
        global_slope_size,
        picture_entry_slope.reshape(picture_residual_entry.shape),
        sentence_entry_slope.reshape(sentence_residual_entry.shape),
        picture_matrices_fresh,
        picture_matrices_fresh.astype(jnp.bfloat16),
        picture_mean_fresh,
        picture_square_fresh,
        sentence_matrices_fresh,
        sentence_matrices_fresh.astype(jnp.bfloat16),
        sentence_mean_fresh,
        sentence_square_fresh,
        array_params_fresh,
        array_params_fresh.astype(jnp.bfloat16),
        array_mean_fresh,
        array_square_fresh,
        logit_log_fresh,
    )


ZN = 4
MP = 4
SEQS = 8


class Tower:
    def __init__(self, tag, width, length, padded, joint, causal, norm_row):
        self.tag = tag
        self.d = width
        self.w = width // MP
        self.heads = self.w // HEAD
        self.length = length
        self.padded = padded
        self.rows = 2 * padded
        self.all_rows = MP * self.rows
        self.tile = self.rows if joint else padded
        self.tiles = self.rows // self.tile
        self.causal = causal
        self.sr = 3 * width // 8
        self.half = self.sr // 2
        self.q = width // 128
        self.norm_row = norm_row
        self.lin = self.sr * self.q


IMG = Tower("_img", D_IMG, IMG_LEN, 56, True, False, 0)
TXT = Tower("_txt", D_TXT, TXT_LEN, 80, False, True, 6 * D_IMG // 128)
NORM_ROWS = 6 * (D_IMG + D_TXT) // 128
VEC_ROWS = 648
HALF = IMG.half + 64
FEED_ROWS = IMG.d // 8 + 48
URGENT = HALF + 16


COST_SCALE = 1.5e9


def kernel_call(body, outs, ins, scratch=(), us=2.0, after=(), vmem=64):
    after = list(after) + LAST

    def spec(value):
        small = value.dtype == jnp.int32 or (value.ndim == 1 and value.shape[0] <= 8)
        return pl.BlockSpec(memory_space=pltpu.SMEM if small else pltpu.VMEM)

    count, late = len(ins), len(after)
    name = getattr(body, "func", body).__name__
    if hasattr(body, "args"):
        name = name + body.args[0].tag
    results = pl.pallas_call(
        lambda *refs: body(*refs[:count], *refs[count + late :]),
        out_shape=list(outs),
        in_specs=[spec(v) for v in ins] + [pl.BlockSpec(memory_space=pl.ANY)] * late,
        out_specs=[pl.BlockSpec(memory_space=pltpu.VMEM)] * len(outs),
        scratch_shapes=list(scratch),
        compiler_params=pltpu.CompilerParams(
            vmem_limit_bytes=vmem * MIB
        ),
        cost_estimate=pl.CostEstimate(
            flops=int(COST_SCALE * us), bytes_accessed=0, transcendentals=0
        ),
        name=name,
    )(*ins, *after)
    LAST[:] = results[:1]
    return results


LAST = []
MIB = 1024 * 1024


def gate(value, *after):
    anywhere = pl.BlockSpec(memory_space=pl.ANY)
    return pl.pallas_call(
        lambda *refs: None,
        out_shape=out(value.shape, value.dtype),
        in_specs=[anywhere] * (1 + len(after)),
        out_specs=anywhere,
        input_output_aliases={0: 0},
    )(value, *after)


def out(shape, dtype=F32):
    return jax.ShapeDtypeStruct(shape, dtype)


def dot(a, b):
    return lax.dot_general(a, b, (((1,), (0,)), ((), ())), preferred_element_type=F32)


def dot_nt(a, b):
    return lax.dot_general(a, b, (((1,), (1,)), ((), ())), preferred_element_type=F32)


def dot_tn(a, b):
    return lax.dot_general(a, b, (((0,), (0,)), ((), ())), preferred_element_type=F32)


def pieces(a, count):
    parts = []
    for _ in range(count):
        part = a.astype(BF)
        parts.append(part)
        a = a - part.astype(F32)
    return parts


def unit(values):
    width = values.shape[-1]
    centered = values - jnp.sum(values, axis=-1, keepdims=True) * (1.0 / width)
    inverse = lax.rsqrt(
        jnp.sum(centered * centered, axis=-1, keepdims=True) * (1.0 / width) + NORM_EPS
    )
    return centered * inverse, inverse


def unit_back(grad_rows, unit_rows, inverse, gain):
    width = grad_rows.shape[-1]
    scaled = grad_rows * gain
    first = jnp.sum(scaled, axis=-1, keepdims=True) * (1.0 / width)
    second = jnp.sum(scaled * unit_rows, axis=-1, keepdims=True) * (1.0 / width)
    return (scaled - first - unit_rows * second) * inverse


def norm_vector(norms_ref, tower, index):
    start = tower.norm_row + index * tower.q
    return jnp.concatenate([norms_ref[start + i : start + i + 1, :] for i in range(tower.q)], axis=1)


def natural_from_lin(tower, lin_ref, spare):
    d, w = tower.d, tower.w
    if (3 * w) % 128 == 0:
        per = 3 * w // 128
        return jnp.concatenate(
            [lin_ref[pl.ds(i, d // 2, stride=per), :] for i in range(per)], axis=1
        )
    per = 2 * 3 * w // 128
    mid = per // 2
    lines = [lin_ref[pl.ds(i, d // 4, stride=per), :] for i in range(per)]
    empty = jnp.zeros((d // 4, 64), F32)
    even = lines[: mid + 1]
    odd = jnp.concatenate([lines[mid][:, 64:]] + lines[mid + 1 :] + [empty], axis=1)
    for j in range(mid + 1):
        spare.at[j][pl.ds(0, d // 4, stride=2), :] = even[j]
        spare.at[j][pl.ds(1, d // 4, stride=2), :] = odd[:, 128 * j : 128 * (j + 1)]
    return jnp.concatenate([spare[j] for j in range(mid)] + [spare[mid][:, :64]], axis=1)


def natural_to_lin(tower, natural, lin_ref, spare):
    d, w = tower.d, tower.w
    if (3 * w) % 128 == 0:
        per = 3 * w // 128
        for i in range(per):
            lin_ref[pl.ds(i, d // 2, stride=per), :] = natural[:, 128 * i : 128 * (i + 1)]
        return
    per = 2 * 3 * w // 128
    mid = per // 2
    for j in range(mid):
        spare[j] = natural[:, 128 * j : 128 * (j + 1)]
    spare[mid] = jnp.concatenate([natural[:, 128 * mid :], jnp.zeros((d // 2, 64), F32)], axis=1)
    even = [spare.at[j][pl.ds(0, d // 4, stride=2), :] for j in range(mid + 1)]
    odd = jnp.concatenate(
        [spare.at[j][pl.ds(1, d // 4, stride=2), :] for j in range(mid + 1)], axis=1
    )
    for i in range(mid):
        lin_ref[pl.ds(i, d // 4, stride=per), :] = even[i]
    lin_ref[pl.ds(mid, d // 4, stride=per), :] = jnp.concatenate(
        [even[mid][:, :64], odd[:, :64]], axis=1
    )
    for i in range(mid):
        lin_ref[pl.ds(mid + 1 + i, d // 4, stride=per), :] = odd[:, 64 + 128 * i : 192 + 128 * i]


def lin_to_rows(tower, lin_ref, rows_ref, spare, shard):
    d, w, sr, q = tower.d, tower.w, tower.sr, tower.q

    @pl.when(shard >= 2)
    def _():
        for j in range(q):
            rows_ref[:, 128 * j : 128 * (j + 1)] = lin_ref[pl.ds(j, sr, stride=q), :]

    @pl.when(shard < 2)
    def _():
        tail = d // 8
        natural = natural_from_lin(tower, lin_ref, spare)
        rows_ref[:, : 3 * w] = natural[:sr]
        for i in range(3):
            rows_ref[tail * i : tail * (i + 1), 3 * w :] = natural[sr:, w * i : w * (i + 1)]


def rows_to_lin(tower, rows_ref, lin_ref, spare, shard):
    d, w, sr, q = tower.d, tower.w, tower.sr, tower.q

    @pl.when(shard >= 2)
    def _():
        for j in range(q):
            lin_ref[pl.ds(j, sr, stride=q), :] = rows_ref[:, 128 * j : 128 * (j + 1)]

    @pl.when(shard < 2)
    def _():
        tail = d // 8
        rest = jnp.concatenate(
            [rows_ref[tail * i : tail * (i + 1), 3 * w :] for i in range(3)], axis=1
        )
        natural = jnp.concatenate([rows_ref[:, : 3 * w], rest], axis=0)
        natural_to_lin(tower, natural, lin_ref, spare)


SPARE = ((3 * IMG.w + 127) // 128, IMG.d // 2, 128)


def prepare_body(
    ids, flags, lengths, img, txt, head, keep_t, keep_i, send_t, send_i, block, rows_i, rows_t, spare
):
    side, shard = ids[0], ids[3]
    lin_to_rows(IMG, img, rows_i, spare, shard)
    lin_to_rows(TXT, txt, rows_t, spare, shard)
    lane = lax.broadcasted_iota(jnp.int32, (1, 128), 1)
    flag_row = jnp.zeros((1, 128), F32)
    length_row = jnp.zeros((1, 128), F32)
    for i in range(SEQS):
        flag_row = jnp.where(lane == i, jnp.where(flags[i] > 0, 1.0, 0.0), flag_row)
        length_row = jnp.where(lane == i, lengths[i].astype(F32), length_row)
    lines = jnp.concatenate(
        [head[:NORM_ROWS, :], flag_row, length_row, jnp.zeros((64 - NORM_ROWS - 2, 128), F32)], axis=0
    )
    for j in range(4):
        block[:, 128 * j : 128 * (j + 1)] = lines[16 * j : 16 * (j + 1)].astype(BF)
    for tower, rows, keep, send in ((TXT, rows_t, keep_t, send_t), (IMG, rows_i, keep_i, send_i)):
        for target, which in ((keep, side), (send, 1 - side)):
            target[...] = rows[
                pl.ds(pl.multiple_of(which * tower.half, 8), tower.half), :
            ].astype(BF)


def sort_body(ids, keep_t, keep_i, got_t, got_i, block, urgent, late):
    def fill(*halves):
        for target, part_t, part_i in ((urgent, *halves[:2]), (late, *halves[2:])):
            target[: IMG.half, :] = part_i[...]
            target[IMG.half : HALF, : TXT.d] = part_t[:64, :]
            target[IMG.half : IMG.half + 32, TXT.d :] = part_t[64:, :256]
            target[IMG.half + 32 : HALF, TXT.d :] = part_t[64:, 256:]

    pl.when(ids[0] == 0)(lambda: fill(keep_t, keep_i, got_t, got_i))
    pl.when(ids[0] != 0)(lambda: fill(got_t, got_i, keep_t, keep_i))
    urgent[HALF:, : TXT.d] = block[...]
    urgent[HALF:, TXT.d :] = jnp.zeros((16, IMG.d - TXT.d), BF)


def vector_pay_body(ids, vec, vecpay, shifted):
    odd = ids[3] % 2

    @pl.when(odd == 0)
    def _():
        vecpay[...] = vec[...].astype(BF)

    @pl.when(odd == 1)
    def _():
        rolled = pltpu.roll(vec[...], 64, 1)
        shifted[0:8, :] = jnp.zeros((8, 128), F32)
        shifted[8 : 8 + VEC_ROWS, :] = rolled
        before = shifted[7 : 7 + VEC_ROWS, :]
        low_lanes = lax.broadcasted_iota(jnp.int32, (VEC_ROWS, 128), 1) < 64
        vecpay[...] = jnp.where(low_lanes, before, rolled).astype(BF)


def with_halves(blocks, side, z, shard, use):
    if len(blocks) == 2:
        rows = blocks[0].shape[0] // ZN
        mine, other = [block.at[pl.ds(shard * rows, rows)] for block in blocks]
        pl.when(side == 0)(lambda: use(mine, other))
        pl.when(side != 0)(lambda: use(other, mine))
        return
    for k in range(ZN):
        mine, other = blocks[k], blocks[ZN + k]
        here = (z ^ shard) == k
        pl.when(here & (side == 0))(functools.partial(use, mine, other))
        pl.when(here & (side != 0))(functools.partial(use, other, mine))


def half_rows(tower, first, second):
    if tower is IMG:
        return jnp.concatenate([first[: IMG.half, :], second[: IMG.half, :]], axis=0)
    parts = []
    for half in (first, second):
        parts += [
            half[IMG.half : HALF, : TXT.d],
            half[IMG.half : IMG.half + 32, TXT.d :],
            half[IMG.half + 32 : HALF, TXT.d :],
        ]
    return jnp.concatenate(
        [
            parts[0],
            jnp.concatenate([parts[1], parts[2]], axis=1),
            parts[3],
            jnp.concatenate([parts[4], parts[5]], axis=1),
        ],
        axis=0,
    )


def attention_mask(tower):
    shape = (tower.tile, tower.tile)
    row = lax.broadcasted_iota(jnp.int32, shape, 0)
    column = lax.broadcasted_iota(jnp.int32, shape, 1)
    if tower.causal:
        return (column <= row) & (column < tower.length)
    pad = tower.padded
    first = (row < pad) & (column < tower.length)
    second = (row >= pad) & (column >= pad) & (column < pad + tower.length)
    return first | second


def read_meta(meta, blocks, side, z):
    for place in range(ZN):

        def use(*halves, place=place):
            for half, block in enumerate(halves):
                lines = block[HALF:, 384:512].astype(F32)
                line = half * ZN + place
                meta[line : line + 1, :] = lines[12:13]
                meta[8 + line : 9 + line, :] = lines[13:14]

        with_halves(blocks, side, z, place, use)


def attend_body(tower, ids, x, *rest):
    count = 2 * ZN
    blocks, rest = rest[:count], rest[count:]
    if tower is TXT:
        (norms, meta, wq, wo, up, h1, u1, qkv, att, probs, xo, own, s1, s2, s3, xf, xs) = rest
    else:
        norms = rest[0]
        (wq, wo, up, h1, u1, qkv, att, probs, xo, own, s1, s2, s3, xf, xs) = rest[1:]
    side, z, m = ids[0], ids[1], ids[2]
    d, w, sr = tower.d, tower.w, tower.sr
    if tower is TXT:

        def read_norms(block, _):
            for j in range(4):
                norms[16 * j : 16 * (j + 1), :] = block[HALF:, 128 * j : 128 * (j + 1)].astype(F32)

        with_halves(blocks, side, z, 0, read_norms)
        read_meta(meta, blocks, side, z)

    tail = d // 8
    for s in range(2):

        def read_qkv(first, second, base=s * (d // 2)):
            part = half_rows(tower, first, second)
            wq[base : base + sr, :] = part[:, : 3 * w]
            wq[base + sr : base + sr + tail, :] = jnp.concatenate(
                [part[tail * i : tail * (i + 1), 3 * w :] for i in range(3)], axis=1
            )

        with_halves(blocks, side, z, s, read_qkv)

    def read_out(first, second):
        part = half_rows(tower, first, second)
        wo[...] = part[:w]
        up[:tail, :] = part[w:]

    def read_up(first, second):
        up[tail:, :] = half_rows(tower, first, second)

    with_halves(blocks, side, z, 2, read_out)
    with_halves(blocks, side, z, 3, read_up)
    for j in range(tower.q):
        xf[j] = x[:, :, 128 * j : 128 * (j + 1)].astype(F32).reshape(tower.length * SEQS, 128)
    pad = tower.padded - tower.length
    for k in range(MP):
        for j in range(2):
            start = k * tower.rows + j * tower.padded
            seq = 2 * (m ^ k) + j
            for i in range(tower.q):
                xs[start : start + tower.length, 128 * i : 128 * (i + 1)] = xf.at[i][
                    pl.ds(seq, tower.length, stride=SEQS), :
                ]
            xs[start + tower.length : start + tower.padded, :] = jnp.zeros((pad, d), F32)
    xo[...] = xs[: tower.rows, :]
    unit_rows, _ = unit(xs[...])
    u1[...] = unit_rows.astype(BF)
    h1[...] = (
        unit_rows * norm_vector(norms, tower, 0) + norm_vector(norms, tower, 1)
    ).astype(BF)
    qkv[...] = dot(h1[...], wq[...]).astype(BF)
    allowed = attention_mask(tower)
    targets = (own, s1, s2, s3)
    for k in range(MP):
        for tile in range(tower.tiles):
            start = k * tower.rows + tile * tower.tile
            rows = slice(start, start + tower.tile)
            heads = []
            for h in range(tower.heads):
                query = qkv[rows, h * HEAD : (h + 1) * HEAD]
                key = qkv[rows, w + h * HEAD : w + (h + 1) * HEAD]
                value = qkv[rows, 2 * w + h * HEAD : 2 * w + (h + 1) * HEAD]
                scores = jnp.where(allowed, dot_nt(query, key) * HEAD ** (-0.5), MASK_LOW)
                exponent = jnp.exp(scores - jnp.max(scores, axis=-1, keepdims=True))
                prob = exponent / jnp.sum(exponent, axis=-1, keepdims=True)
                probs[(k * tower.tiles + tile) * tower.heads + h] = prob
                heads.append(dot(prob.astype(BF), value))
            att[rows, :] = jnp.concatenate(heads, axis=1).astype(BF)
        rows = slice(k * tower.rows, (k + 1) * tower.rows)
        part = dot(att[rows, :], wo[...])
        targets[k][...] = part.astype(targets[k].dtype)


def attend_call(tower, ids, x, blocks, norms=None, after=()):
    d, w, rows, every = tower.d, tower.w, tower.rows, tower.all_rows
    outs = [
        out((d, 3 * w), BF),
        out((w, d), BF),
        out((d // 2, d), BF),
        out((every, d), BF),
        out((every, d), BF),
        out((every, 3 * w), BF),
        out((every, w), BF),
        out((MP * tower.tiles * tower.heads, tower.tile, tower.tile)),
        out((rows, d)),
        out((rows, d)),
        out((rows, d), BF),
        out((rows, d), BF),
        out((rows, d), BF),
    ]
    ins = [ids, x] + blocks
    if tower is TXT:
        outs = [out((64, 128)), out((16, 128))] + outs
    else:
        ins.append(norms)
    return kernel_call(
        functools.partial(attend_body, tower),
        outs,
        ins,
        [
            pltpu.VMEM((tower.q, tower.length * SEQS, 128), F32),
            pltpu.VMEM((every, d), F32),
        ],
        after=after,
        us=7.2,
    )


def row_mask(tower, lengths, pair):
    position = lax.broadcasted_iota(jnp.int32, (tower.padded, 1), 0)
    count = lengths[pair] if tower.causal else tower.length
    return position < count, count


def middle_body(tower, ids, lengths, norms, xo, own, r1, r2, r3, x1, h2, pooled):
    m = ids[2]
    total = xo[...] + ((own[...] + r1[...].astype(F32)) + (r2[...].astype(F32) + r3[...].astype(F32)))
    x1[...] = total
    unit_rows, _ = unit(total)
    h2[...] = (
        unit_rows * norm_vector(norms, tower, 2) + norm_vector(norms, tower, 3)
    ).astype(BF)
    for j in range(2):
        inside, count = row_mask(tower, lengths, 2 * m + j)
        part = total[j * tower.padded : (j + 1) * tower.padded]
        summed = jnp.sum(jnp.where(inside, part, 0.0), axis=0, keepdims=True)
        pooled[j : j + 1, :] = summed / jnp.full((1, 1), count, F32)


def middle_call(tower, ids, lengths, norms, xo, own, received, after=()):
    rows, d = tower.rows, tower.d
    return kernel_call(
        functools.partial(middle_body, tower),
        [out((rows, d)), out((rows, d), BF), out((2, d))],
        [ids, lengths, norms, xo, own] + received,
        after=after,
    )


def feed_body(tower, ids, lengths, h_own, h1, h2, h3, *rest):
    up, late, rest = rest[0], rest[1:3], rest[3:]
    if tower is TXT:
        pooled, w1, w2, slope, sums, *y_out = rest
    else:
        pooled, *y_txt, sums_txt, w1, w2, slope, sums, y0, y1, y2, y3 = rest
        y_out = (y0, y1, y2, y3)
    side, z, m = ids[0], ids[1], ids[2]
    d, w, sr = tower.d, tower.w, tower.sr
    tail = d // 8

    def read(target, start, skip, count):
        def use(first, second):
            part = half_rows(tower, first, second)
            target[start : start + count, :] = part[skip : skip + count]

        return use

    def read_both(first, second):
        part = half_rows(tower, first, second)
        w1[tail + 2 * sr :, :] = part[:tail]
        w2[:w, :] = part[tail:]

    w1[: d // 2, :] = up[...]
    with_halves(late, side, z, 0, read(w1, tail + sr, 0, sr))
    with_halves(late, side, z, 1, read_both)
    with_halves(late, side, z, 2, read(w2, w, 0, sr))
    with_halves(late, side, z, 3, read(w2, w + sr, 0, sr))
    sums_places, y_places = [], []
    for k, block in enumerate((h_own, h1, h2, h3)):
        pre = dot(block[...], w1[...])
        gate = jax.nn.sigmoid(GELU_SLOPE * pre)
        acted = (pre * gate).astype(BF).astype(F32)
        slope[k * tower.rows : (k + 1) * tower.rows, :] = gate + GELU_SLOPE * pre * gate * (
            1.0 - gate
        )
        summed = []
        counts = []
        for j in range(2):
            inside, count = row_mask(tower, lengths, 2 * (m ^ k) + j)
            part = acted[j * tower.padded : (j + 1) * tower.padded]
            summed.append(jnp.sum(jnp.where(inside, part, 0.0), axis=0, keepdims=True))
            counts.append(jnp.full((1, 1), count, F32))
        both = jnp.concatenate(summed, axis=0)
        sums_places.append(both)
        high, low, rest = pieces(both, 3)
        y = dot(high, w2[...]) + (dot(low, w2[...]) + dot(rest, w2[...]))
        y = y / jnp.concatenate(counts, axis=0)
        if k == 0:
            y = y + pooled[...]
        y_places.append(y)

    def in_order(places):
        def chunk(c):
            value = places[c ^ 3]
            for member in range(3):
                value = jnp.where(m == member, places[c ^ member], value)
            return value

        return jnp.concatenate([chunk(c) for c in range(MP)], axis=0)

    ordered = in_order(sums_places)
    if tower is TXT:
        sums[...] = ordered
        for target, value in zip(y_out, y_places):
            target[...] = value
        return
    for target, value, other in zip(y_out, y_places, y_txt):
        target[:, :d] = value
        target[:, d:] = other[...]
    sums[:, :d] = ordered
    sums[:, d:] = sums_txt[...]


def feed_call(tower, ids, lengths, blocks, up, late, pooled, before=()):
    d = tower.d
    wide = d if tower is TXT else D_IMG + D_TXT
    return kernel_call(
        functools.partial(feed_body, tower),
        [
            out((d, d), BF),
            out((d, d), BF),
            out((tower.all_rows, d)),
            out((SEQS, wide)),
        ]
        + [out((2, wide))] * MP,
        [ids, lengths] + blocks + [up] + late + [pooled] + list(before),
        us=6.4,
    )


def project_body(gathered, pi, pt, flat):
    for e in range(4):
        base = e * (2 * VEC_ROWS - 1)
        flat[base : base + VEC_ROWS, :] = gathered[2 * e].astype(F32)
        odd = gathered[2 * e + 1].astype(F32)
        row = base + VEC_ROWS - 1
        flat[row : row + 1, :] = flat[row : row + 1, :] + odd[:1]
        flat[row + 1 : row + VEC_ROWS, :] = odd[1:]
    for j in range(4):
        pi[:, 128 * j : 128 * (j + 1)] = flat[pl.ds(NORM_ROWS + j, D_IMG, stride=4), :].astype(BF)
        pt[:, 128 * j : 128 * (j + 1)] = flat[
            pl.ds(NORM_ROWS + 4 * D_IMG + j, D_TXT, stride=4), :
        ].astype(BF)


def project_call(gathered, after):
    return kernel_call(
        project_body,
        [out((D_IMG, EMBED), BF), out((D_TXT, EMBED), BF)],
        [gathered],
        [pltpu.VMEM((4 * (2 * VEC_ROWS - 1) + 4, 128), F32)],
        us=2.8,
        after=after,
    )


def head_body(
    ids, trio, parts, norms, meta, pi, pt,
    misc, dyb_i, dyb_t, own_i, own_t, pg_i, pg_t, ng_i, ng_t, scr_i, scr_t, yall,
):
    shard = ids[3]
    total = yall.shape[0]
    for i in range(parts.shape[0]):
        yall[2 * i : 2 * i + 2, :] = parts[i]
    row = lax.broadcasted_iota(jnp.int32, (total, total), 0)
    column = lax.broadcasted_iota(jnp.int32, (total, total), 1)
    eye = row == column
    place = lax.broadcasted_iota(jnp.int32, (total, 128), 0)
    lane = lax.broadcasted_iota(jnp.int32, (total, 128), 1)

    def column_of(first):
        picked = jnp.zeros((total, 128), F32)
        for s in range(2 * ZN):
            picked = jnp.where(place // SEQS == s, meta[first + s : first + s + 1, :], picked)
        return jnp.sum(jnp.where(lane == place % SEQS, picked, 0.0), axis=1, keepdims=True)

    flag_column = column_of(0)
    length_column = column_of(8)
    flag_row = jnp.sum(jnp.where(eye, flag_column, 0.0), axis=0, keepdims=True)
    row_valid = flag_column > 0.5
    column_valid = flag_row > 0.5
    count = jnp.sum(flag_column, axis=0, keepdims=True)

    def forward(tower, values, projection):
        unit_rows, inverse = unit(values)
        z = (
            unit_rows * norm_vector(norms, tower, 4) + norm_vector(norms, tower, 5)
        ).astype(BF)
        raw = dot(z, projection[...])
        scale = lax.rsqrt(jnp.sum(raw * raw, axis=-1, keepdims=True) + UNIT_EPS)
        quotient = raw * scale
        return unit_rows, inverse, z, scale, quotient, quotient.astype(BF)

    image = forward(IMG, yall[:, :D_IMG], pi)
    text = forward(TXT, yall[:, D_IMG:], pt)
    factor = jnp.exp(jnp.full((1, 1), trio[0], F32))
    e_image, e_text = image[5], text[5]

    def side(mine, others):
        logits = factor * dot_nt(mine, others)
        masked = jnp.where(column_valid, logits, MASK_LOW)
        top = jnp.max(masked, axis=1, keepdims=True)
        exponent = jnp.exp(masked - top)
        totals = jnp.sum(exponent, axis=1, keepdims=True)
        own = jnp.sum(jnp.where(eye, logits, 0.0), axis=1, keepdims=True)
        loss = jnp.sum(
            jnp.where(row_valid, top + jnp.log(totals) - own, 0.0), axis=0, keepdims=True
        )
        grad = jnp.where(row_valid, exponent / totals - eye.astype(F32), 0.0) / (2.0 * count)
        scale_part = jnp.sum(jnp.sum(grad * logits, axis=1, keepdims=True), axis=0, keepdims=True)
        return loss, grad, scale_part

    loss_i, grad_i, part_i = side(e_image, e_text)
    loss_t, grad_t, part_t = side(e_text, e_image)
    loss = (loss_i + loss_t) / (2.0 * count)
    slope = part_i + part_t
    misc[...] = jnp.concatenate(
        [
            jnp.broadcast_to(loss, (1, 128)),
            jnp.broadcast_to(slope, (1, 128)),
            jnp.zeros((6, 128), F32),
        ],
        axis=0,
    )

    def product(grad, back, others):
        sums = None
        for part in pieces(grad, 3):
            term = dot(part, others)
            sums = term if sums is None else sums + term
        for part in pieces(back, 3):
            sums = sums + dot_tn(part, others)
        return factor * sums

    def backward(tower, stored, embed_grad, projection, counts, pg, ng, dyb, scratch, own):
        unit_rows, inverse, z, scale, quotient, _ = stored
        raw_grad = (
            scale
            * (embed_grad - quotient * jnp.sum(embed_grad * quotient, axis=-1, keepdims=True))
        ).astype(BF)
        pg[...] = dot_tn(z, raw_grad)
        normed_grad = dot_nt(raw_grad, projection[...])
        ng[0:1, :] = jnp.sum(normed_grad * unit_rows, axis=0, keepdims=True)
        ng[1:2, :] = jnp.sum(normed_grad, axis=0, keepdims=True)
        grad = unit_back(normed_grad, unit_rows, inverse, norm_vector(norms, tower, 4)) / counts
        dyb[...] = grad.astype(BF)
        scratch[...] = grad
        rows = scratch[pl.ds(pl.multiple_of(shard * SEQS, 8), SEQS), :]
        for c in range(MP):
            own[c] = rows[2 * c : 2 * c + 2]

    grad_image = product(grad_i, grad_t, e_text)
    grad_text = product(grad_t, grad_i, e_image)
    backward(
        TXT, text, grad_text, pt, length_column, pg_t, ng_t, dyb_t, scr_t, own_t
    )
    backward(
        IMG, image, grad_image, pi, jnp.full((1, 1), float(IMG_LEN), F32),
        pg_i, ng_i, dyb_i, scr_i, own_i,
    )


def head_call(ids, trio, parts, norms, meta, pi, pt):
    total = 2 * parts.shape[0]
    return kernel_call(
        head_body,
        [
            out((8, 128)),
            out((total, D_IMG), BF),
            out((total, D_TXT), BF),
            out((MP, 2, D_IMG)),
            out((MP, 2, D_TXT)),
            out((D_IMG, EMBED)),
            out((D_TXT, EMBED)),
            out((2, D_IMG)),
            out((2, D_TXT)),
        ],
        [ids, trio, parts, norms, meta, pi, pt],
        [
            pltpu.VMEM((total, D_IMG), F32),
            pltpu.VMEM((total, D_TXT), F32),
            pltpu.VMEM((total, D_IMG + D_TXT), F32),
        ],
        us=5.0,
    )


def feed_back_body(
    tower, ids, lengths, h_own, h1, h2, h3, slope, dy, w1, w2, *rest
):
    if tower is TXT:
        grad_i, own, s1, s2, s3, payload, h_all, du = rest
    else:
        own, s1, s2, s3, grads, h_all, du = rest
    m = ids[2]
    rows, pad = tower.rows, tower.padded
    for k, block in enumerate((h_own, h1, h2, h3)):
        h_all[k * rows : (k + 1) * rows, :] = block[...]
    dy_rows = jnp.concatenate([dy[m ^ k] for k in range(MP)], axis=0).astype(BF)
    act = dot_nt(dy_rows, w2[...])
    targets = (own, s1, s2, s3)
    for k in range(MP):
        for j in range(2):
            inside, _ = row_mask(tower, lengths, 2 * (m ^ k) + j)
            start = k * rows + j * pad
            place = 2 * k + j
            piece = slope[start : start + pad, :] * act[place : place + 1, :]
            du[start : start + pad, :] = jnp.where(inside, piece, 0.0).astype(BF)
        part = dot_nt(du[k * rows : (k + 1) * rows, :], w1[...])
        targets[k][...] = part.astype(targets[k].dtype)
    grad = dot_tn(h_all[...], du[...]).astype(BF)
    if tower is IMG:
        grads[...] = grad
        return
    rows_i, rows_t = IMG.d // 8, TXT.d // 8
    for place, e in enumerate(FEED_ORDER):
        payload[place, :rows_i, :] = grad_i[rows_i * e : rows_i * (e + 1), :]
        pack_eighth(payload.at[place], rows_i, grad[rows_t * e : rows_t * (e + 1)])


def feed_back_call(tower, ids, lengths, blocks, slope, dy, w1, w2, grads, after=()):
    rows, d, every = tower.rows, tower.d, tower.all_rows
    return kernel_call(
        functools.partial(feed_back_body, tower),
        [
            out((rows, d)),
            out((rows, d), BF),
            out((rows, d), BF),
            out((rows, d), BF),
            out((d, d), BF) if tower is IMG else out((2 * ZN, FEED_ROWS, IMG.d), BF),
        ],
        [ids, lengths] + blocks + [slope, dy, w1, w2] + grads,
        [pltpu.VMEM((every, d), BF), pltpu.VMEM((every, d), BF)],
        after=after,
        us=5.3,
    )


def middle_back_body(tower, ids, lengths, norms, x1, dy, own, r1, r2, r3, dx1, dx1b):
    m = ids[2]
    grad = (own[...] + r1[...].astype(F32)) + (r2[...].astype(F32) + r3[...].astype(F32))
    unit_rows, inverse = unit(x1[...])
    extra = (
        jnp.sum(grad * unit_rows, axis=0, keepdims=True),
        jnp.sum(grad, axis=0, keepdims=True),
    )
    back = unit_back(grad, unit_rows, inverse, norm_vector(norms, tower, 2))
    rows = dy[m]
    position = lax.broadcasted_iota(jnp.int32, (tower.padded, 1), 0)
    for j in range(2):
        inside, _ = row_mask(tower, lengths, 2 * m + j)
        part = slice(j * tower.padded, (j + 1) * tower.padded)
        total = back[part] + jnp.where(inside, rows[j : j + 1, :], 0.0)
        dx1[part, :] = total
        high, low = [piece.astype(F32) for piece in pieces(extra[j], 2)]
        total = jnp.where(position == tower.length, high, total)
        total = jnp.where(position == tower.length + 1, low, total)
        dx1b[part, :] = total.astype(BF)


def middle_back_call(tower, ids, lengths, norms, x1, dy, own, received, after=()):
    rows, d = tower.rows, tower.d
    return kernel_call(
        functools.partial(middle_back_body, tower),
        [out((rows, d)), out((rows, d), BF)],
        [ids, lengths, norms, x1, dy, own] + received,
        after=after,
    )


def attend_back_body(
    tower, ids, d_own, d1, d2, d3, att, qkv, probs, h1, u1, wq, wo,
    own, s1, s2, s3, *rest
):
    keep, sent, sums, d_all, dqkv, wide, backs, grads = rest
    rows, d, w, sr = tower.rows, tower.d, tower.w, tower.sr
    tail = d // 8
    position = lax.broadcasted_iota(jnp.int32, (tower.padded, 1), 0)
    extra = [[], []]
    for k, block in enumerate((d_own, d1, d2, d3)):
        for j in range(2):
            start = j * tower.padded
            part = block[start : start + tower.padded, :].astype(F32)
            line = tower.length
            extra[j].append(part[line : line + 1] + part[line + 1 : line + 2])
            d_all[k * rows + start : k * rows + start + tower.padded, :] = jnp.where(
                position < line, part, 0.0
            ).astype(BF)
    for j in range(2):
        sums[j : j + 1, :] = (extra[j][0] + extra[j][1]) + (extra[j][2] + extra[j][3])
    targets = (own, s1, s2, s3)
    gain = jnp.zeros((1, d), F32)
    shift = jnp.zeros((1, d), F32)
    for k in range(MP):
        span = slice(k * rows, (k + 1) * rows)
        d_att = dot_nt(d_all[span, :], wo[...]).astype(BF)
        for tile in range(tower.tiles):
            start = k * rows + tile * tower.tile
            part = slice(start, start + tower.tile)
            queries, keys, values = [], [], []
            for h in range(tower.heads):
                query = qkv[part, h * HEAD : (h + 1) * HEAD]
                key = qkv[part, w + h * HEAD : w + (h + 1) * HEAD]
                value = qkv[part, 2 * w + h * HEAD : 2 * w + (h + 1) * HEAD]
                grad = d_att[
                    tile * tower.tile : (tile + 1) * tower.tile, h * HEAD : (h + 1) * HEAD
                ]
                prob = probs[(k * tower.tiles + tile) * tower.heads + h]
                values.append(dot_tn(prob.astype(BF), grad))
                prob_grad = dot_nt(grad, value)
                score = (
                    prob * (prob_grad - jnp.sum(prob * prob_grad, axis=-1, keepdims=True))
                ).astype(BF)
                queries.append(dot(score, key) * HEAD ** (-0.5))
                keys.append(dot_tn(score, query) * HEAD ** (-0.5))
            dqkv[part, :] = jnp.concatenate(queries + keys + values, axis=1).astype(BF)
        back = dot_nt(dqkv[span, :], wq[...])
        gain = gain + jnp.sum(back * u1[span, :].astype(F32), axis=0, keepdims=True)
        shift = shift + jnp.sum(back, axis=0, keepdims=True)
        backs[k, :, :] = back
    for k in range(MP):
        for j, value in enumerate((gain, shift)):
            start = j * tower.padded
            part = backs[k, start : start + tower.padded, :]
            high, low = [piece.astype(F32) for piece in pieces(value, 2)]
            part = jnp.where(position == tower.length, high, part)
            part = jnp.where(position == tower.length + 1, low, part)
            targets[k][start : start + tower.padded, :] = part.astype(targets[k].dtype)
    wide[...] = dot_tn(h1[...], dqkv[...]).astype(BF)
    out_grad = dot_tn(att[...], d_all[...]).astype(BF)
    for place, e in enumerate(WIDE_ORDER):
        if e >= 6:
            piece = out_grad[(e - 6) * tail : (e - 5) * tail]
        else:
            s, i = e // 3, e % 3
            base = s * (d // 2)
            rest = wide[base + sr : base + sr + tail, w * i : w * (i + 1)]
            piece = jnp.concatenate(
                [wide[base + i * tail : base + (i + 1) * tail, :], rest], axis=1
            )
        grads[place] = piece
    for z in range(ZN):
        keep[z] = grads[ids[0] * ZN + z]
        sent[z] = grads[(1 - ids[0]) * ZN + z]


def attend_back_call(tower, ids, blocks, att, qkv, probs, h1, u1, wq, wo, after=()):
    rows, d, w, every = tower.rows, tower.d, tower.w, tower.all_rows
    return kernel_call(
        functools.partial(attend_back_body, tower),
        [
            out((rows, d)),
            out((rows, d), BF),
            out((rows, d), BF),
            out((rows, d), BF),
            out((ZN, d // 8, d), BF),
            out((ZN, d // 8, d), BF),
            out((2, d)),
        ],
        [ids] + blocks + [att, qkv, probs, h1, u1, wq, wo],
        [
            pltpu.VMEM((every, d), BF),
            pltpu.VMEM((every, 3 * w), BF),
            pltpu.VMEM((d, 3 * w), BF),
            pltpu.VMEM((MP, rows, d), F32),
            pltpu.VMEM((2 * ZN, d // 8, d), BF),
        ],
        after=after,
        us=10.4,
    )


def entry_body(tower, norms, xo, dx1, second, own, r1, r2, r3, *rest):
    if tower is IMG:
        dx, sums = rest
    else:
        dx_i, payload, sums = rest
    grad = (own[...] + r1[...].astype(F32)) + (r2[...].astype(F32) + r3[...].astype(F32))
    line = tower.length
    sums[0:1, :] = grad[line : line + 1] + grad[line + 1 : line + 2]
    line += tower.padded
    sums[1:2, :] = grad[line : line + 1] + grad[line + 1 : line + 2]
    sums[2:4, :] = second[...]
    unit_rows, inverse = unit(xo[...])
    back = unit_back(grad, unit_rows, inverse, norm_vector(norms, tower, 0))
    result = (dx1[...] + back).astype(BF)
    if tower is IMG:
        dx[...] = result
        return
    top = IMG.rows
    rest = TXT.rows - top
    payload[:top, :] = dx_i[...]
    payload[top:, : TXT.d] = result[:top]
    payload[top : top + rest, TXT.d :] = result[top:, :256]
    payload[top + rest : top + 2 * rest, TXT.d :] = result[top:, 256:]
    payload[top + 2 * rest :, TXT.d :] = jnp.zeros((top - 2 * rest, IMG.d - TXT.d), BF)


def entry_call(tower, norms, xo, dx1, second, own, received, before=(), after=()):
    rows, d = tower.rows, tower.d
    return kernel_call(
        functools.partial(entry_body, tower),
        [out((rows, d), BF) if tower is IMG else out((2 * IMG.rows, IMG.d), BF), out((4, d))],
        [norms, xo, dx1, second, own] + received + list(before),
        after=after,
    )


def place_body(tower, ids, own, r1, r2, r3, result, flat):
    m = ids[2]
    top = IMG.rows
    rest = TXT.rows - top
    for k, block in enumerate((own, r1, r2, r3)):
        if tower is IMG:
            rows = block[:top, :].astype(F32)
        else:
            low = jnp.concatenate(
                [
                    block[top : top + rest, TXT.d :],
                    block[top + rest : top + 2 * rest, TXT.d :],
                ],
                axis=1,
            )
            rows = jnp.concatenate([block[top:, : TXT.d], low], axis=0).astype(F32)
        for j in range(2):
            seq = 2 * (m ^ k) + j
            part = rows[j * tower.padded : j * tower.padded + tower.length]
            for i in range(tower.q):
                flat.at[i][pl.ds(seq, tower.length, stride=SEQS), :] = part[
                    :, 128 * i : 128 * (i + 1)
                ]
    for i in range(tower.q):
        result[:, :, 128 * i : 128 * (i + 1)] = flat[i].reshape(tower.length, SEQS, 128)


def place_call(tower, ids, blocks):
    return kernel_call(
        functools.partial(place_body, tower),
        [out((tower.length, SEQS, tower.d))],
        [ids] + blocks,
        [pltpu.VMEM((tower.q, tower.length * SEQS, 128), F32)],
        vmem=PLACE_VMEM,
        us=2.7,
    )[0]


def pack_eighth(target, start, part):
    target[start : start + 48, : TXT.d] = part[:48]
    target[start : start + 16, TXT.d :] = part[48:, :256]
    target[start + 16 : start + 32, TXT.d :] = part[48:, 256:]
    target[start + 32 : start + 48, TXT.d :] = jnp.zeros((16, IMG.d - TXT.d), BF)


def pair_body(keep_i, got_i, keep_t, got_t, payload):
    top = IMG.d // 8
    for z in range(ZN):
        payload[z, :top, :] = (keep_i[z].astype(F32) + got_i[z].astype(F32)).astype(BF)
        total = (keep_t[z].astype(F32) + got_t[z].astype(F32)).astype(BF)
        pack_eighth(payload.at[z], top, total)


def mix_body(ids, feed, got, wide, first, second):
    shard = ids[3]
    part = [got[z].astype(F32) for z in range(ZN)]
    wide[...] = ((part[0] + part[1]) + (part[2] + part[3])).astype(BF)
    for target, (senders, _) in zip((first, second), MOVES):
        passes = (shard == senders[0]) | (shard == senders[1])

        def copy(source, target=target):
            target[...] = source[...]

        pl.when(passes)(functools.partial(copy, feed))
        pl.when(jnp.logical_not(passes))(functools.partial(copy, wide))


def mix_call(ids, feed, got):
    return kernel_call(mix_body, [out((FEED_ROWS, IMG.d), BF)] * 3, [ids, feed, got], us=2.5)


def down_body(tower, ids, b0, b1, b2, b3, b4, b5, b6, b7, dyb, result, wide, sums):
    d = tower.d
    tail = d // 8
    first = 0 if tower is IMG else D_IMG
    for k, block in enumerate((b0, b1, b2, b3, b4, b5, b6, b7)):
        side = ids[0] if k < ZN else 1 - ids[0]
        start = (side * ZN + (ids[1] ^ (k % ZN))) * SEQS
        sums[pl.ds(pl.multiple_of(start, SEQS), SEQS), :] = block[:, first : first + d]
    high, low = pieces(sums[...], 2)
    wide[:tail, :] = jnp.zeros((tail, d), F32)
    wide[tail:, :] = dot_tn(high, dyb[...]) + dot_tn(low, dyb[...])
    start = jnp.maximum(ids[3] - 5, 0) * tower.sr
    result[...] = wide[pl.ds(pl.multiple_of(start, 8), tower.sr), :]


def down_call(tower, ids, sums, dyb):
    d = tower.d
    return kernel_call(
        functools.partial(down_body, tower),
        [out((tower.sr, d))],
        [ids] + sums + [dyb],
        [pltpu.VMEM((d + d // 8, d), F32), pltpu.VMEM((2 * ZN * SEQS, d), F32)],
        us=2.6,
    )[0]


def vector_body(ids, pg_i, pg_t, ng_i, ng_t, window, flat):
    flat[:64, :] = jnp.zeros((64, 128), F32)
    for tower, sums in ((IMG, ng_i), (TXT, ng_t)):
        for i in range(2):
            start = tower.norm_row + (4 + i) * tower.q
            for j in range(tower.q):
                flat[start + j : start + j + 1, :] = sums[i : i + 1, 128 * j : 128 * (j + 1)]
    for j in range(4):
        flat[pl.ds(NORM_ROWS + j, D_IMG, stride=4), :] = pg_i[:, 128 * j : 128 * (j + 1)]
        flat[pl.ds(NORM_ROWS + 4 * D_IMG + j, D_TXT, stride=4), :] = pg_t[
            :, 128 * j : 128 * (j + 1)
        ]
    low_lanes = lax.broadcasted_iota(jnp.int32, (VEC_ROWS, 128), 1) < 64
    last = lax.broadcasted_iota(jnp.int32, (VEC_ROWS, 128), 0) == VEC_ROWS - 1
    for s in range(8):

        def copy(s=s):
            start = (s * (2 * VEC_ROWS - 1)) // 2
            part = flat[start : start + VEC_ROWS, :]
            if s % 2 == 1:
                after = pltpu.roll(flat[start + 1 : start + 1 + VEC_ROWS, :], 64, 1)
                part = jnp.where(low_lanes, pltpu.roll(part, 64, 1), after)
            window[...] = jnp.where(last & jnp.logical_not(low_lanes), 0.0, part)

        pl.when(ids[3] == s)(copy)


def vector_call(ids, pg_i, pg_t, ng_i, ng_t, after=()):
    return kernel_call(
        vector_body,
        [out((VEC_ROWS, 128))],
        [ids, pg_i, pg_t, ng_i, ng_t],
        [pltpu.VMEM((4 * (2 * VEC_ROWS - 1) + 12, 128), F32)],
        after=after,
        us=2.9,
    )[0]


def collect_body(
    ids, f_own, w_own, ra, rb, down_i, down_t, window,
    sums_i, sums_t, lin_i, lin_t, message, rows_i, rows_t, spare,
):
    shard = ids[3]
    q = IMG.d // 8

    @pl.when(shard >= 5)
    def _():
        rows_i[...] = down_i[...]
        rows_t[...] = down_t[...]

    tq = TXT.d // 8

    def feed(start, *blocks):
        for i, block in enumerate(blocks):
            rows_i[q * (start + i) : q * (start + i + 1), :] = block[:q, :].astype(F32)
            low = jnp.concatenate([block[q : q + 16, TXT.d :], block[q + 16 : q + 32, TXT.d :]], axis=1)
            part = jnp.concatenate([block[q:, : TXT.d], low], axis=0)
            rows_t[tq * (start + i) : tq * (start + i + 1), :] = part.astype(F32)

    pl.when(shard < 2)(lambda: feed(0, w_own, ra, rb))
    pl.when(shard == 2)(lambda: feed(0, w_own, ra, f_own))
    pl.when((shard == 3) | (shard == 4))(lambda: feed(0, f_own, ra, rb))
    pl.when(shard == 5)(lambda: feed(0, f_own))

    rows_to_lin(IMG, rows_i, lin_i, spare, shard)
    rows_to_lin(TXT, rows_t, lin_t, spare, shard)
    def total_of(value):
        return jnp.sum(value * value, axis=0, keepdims=True)

    every = total_of(window[...]) * (1.0 / MP)
    for j in range(IMG.q):
        every = every + total_of(rows_i[:, 128 * j : 128 * (j + 1)])
    for j in range(TXT.q):
        every = every + total_of(rows_t[:, 128 * j : 128 * (j + 1)])
    m = ids[2]

    def own_line(sums):
        line = sums[3:4, :]
        for member in range(3):
            line = jnp.where(m == member, sums[member : member + 1, :], line)
        return line

    line = jnp.concatenate([own_line(sums_i), own_line(sums_t)], axis=1)
    block = jnp.concatenate(
        [every] + [line[:, 128 * j : 128 * (j + 1)] for j in range(IMG.q + TXT.q)], axis=0
    )
    for peer in range(2 * ZN * MP):
        message[peer, : MESSAGE_ROWS, :] = block
        message[peer, MESSAGE_ROWS:, :] = jnp.zeros((16 - MESSAGE_ROWS, 128), F32)


MESSAGE_ROWS = 1 + IMG.q + TXT.q


def collect_call(ids, moved, down_i, down_t, window, sums_i, sums_t, after):
    return kernel_call(
        collect_body,
        [out((IMG.lin, 128)), out((TXT.lin, 128)), out((2 * ZN * MP, 16, 128))],
        [ids] + moved + [down_i, down_t, window, sums_i, sums_t],
        [
            pltpu.VMEM((IMG.sr, IMG.d), F32),
            pltpu.VMEM((TXT.sr, TXT.d), F32),
            pltpu.VMEM(SPARE, F32),
        ],
        us=3.8,
        after=after,
    )


def advance_body(
    ids, trio, parts, misc, ip, im, iv, ig, tp, tm, tv, tg, vp, vm, vv, vg,
    loss_out, size_out, trio_out, ipn, icn, imn, ivn, tpn, tcn, tmn, tvn, vpn, vcn, vmn, vvn, grad_v,
):
    slope = misc[1:2, :]
    grad_v[...] = vg[...]
    norm_squares = jnp.zeros((1, 128), F32)
    for member in range(MP):
        lines = parts[member]
        for group in range(1, 2 * ZN):
            lines = lines + parts[group * MP + member]
        if member == 0:
            squares = lines[:1]
        else:
            squares = squares + lines[:1]
        lines = lines[1:MESSAGE_ROWS]
        norm_squares = norm_squares + jnp.sum(lines * lines, axis=0, keepdims=True)

        @pl.when((ids[3] == 0) & (pl.program_id(0) == 0))
        def _(member=member, lines=lines):
            start = member * IMG.q
            grad_v[start : start + IMG.q, :] = lines[: IMG.q]
            start = TXT.norm_row + member * TXT.q
            grad_v[start : start + TXT.q, :] = lines[IMG.q :]

    total = jnp.sum(squares + norm_squares, axis=1, keepdims=True)
    size = jnp.sqrt(total + slope * slope)
    clip = CLIP_LEVEL / jnp.maximum(size, CLIP_LEVEL)

    def step(master, first, second, grad, rate, decay):
        clipped = grad * clip
        first_new = BETA_ONE * first + (1.0 - BETA_ONE) * clipped
        second_new = BETA_TWO * second + (1.0 - BETA_TWO) * clipped * clipped
        update = (first_new * (1.0 / (1.0 - BETA_ONE**STEP))) / (
            jnp.sqrt(second_new * (1.0 / (1.0 - BETA_TWO**STEP))) + ADAM_EPS
        )
        return master - rate * (update + decay * master), first_new, second_new

    for master, first, second, grad, a, b, c, e in (
        (ip, im, iv, ig, ipn, icn, imn, ivn),
        (tp, tm, tv, tg, tpn, tcn, tmn, tvn),
    ):
        new, first_new, second_new = step(
            master[...], first[...], second[...], grad[...], RATE_MATRIX, WEIGHT_DECAY
        )
        a[...] = new
        b[:, 0, :] = new.astype(BF)
        c[...] = first_new
        e[...] = second_new
    rows = VEC_ROWS // ADVANCE_STEPS
    row = lax.broadcasted_iota(jnp.int32, (rows, 128), 0) + pl.program_id(0) * rows
    is_norm = row < jnp.where(ids[3] == 0, NORM_ROWS, 0)
    new, first_new, second_new = step(
        vp[...],
        vm[...],
        vv[...],
        grad_v[...],
        jnp.where(is_norm, RATE_VECTOR, RATE_MATRIX),
        jnp.where(is_norm, 0.0, WEIGHT_DECAY),
    )
    vpn[...] = new
    vcn[...] = new.astype(BF)
    vmn[...] = first_new
    vvn[...] = second_new
    lane_row = jnp.zeros((1, 128), F32)
    new, _, _ = step(
        lane_row + trio[0], lane_row + trio[1], lane_row + trio[2], slope, LOGIT_SPEED, 0.0
    )
    loss_out[...] = misc[0:1, :1]
    size_out[...] = size[:, :1]
    trio_out[...] = new[:, :1]


PLACE_VMEM = 64
ADVANCE_STEPS = 3


def advance_call(ids, trio, parts, misc, image, text, vector):
    ins = [ids, trio, parts, misc] + image + text + vector

    def spec(shape, cut):
        block = (shape[0] // ADVANCE_STEPS if cut else shape[0],) + tuple(shape[1:])
        rest = (0,) * (len(shape) - 1)
        return pl.BlockSpec(block, lambda i: ((i if cut else 0),) + rest)

    outs = [out((1, 1))] * 3
    for rows in (IMG.lin, TXT.lin, VEC_ROWS):
        copied = (rows, 128) if rows == VEC_ROWS else (rows, 1, 128)
        outs += [out((rows, 128)), out(copied, BF), out((rows, 128)), out((rows, 128))]
    scalars = pl.BlockSpec(memory_space=pltpu.SMEM)
    return pl.pallas_call(
        advance_body,
        grid=(ADVANCE_STEPS,),
        out_shape=outs,
        in_specs=[scalars, scalars] + [spec(v.shape, i > 1) for i, v in enumerate(ins[2:])],
        out_specs=[spec(v.shape, i > 2) for i, v in enumerate(outs)],
        scratch_shapes=[pltpu.VMEM((VEC_ROWS // ADVANCE_STEPS, 128), F32)],
        compiler_params=pltpu.CompilerParams(vmem_limit_bytes=64 * MIB),
        cost_estimate=pl.CostEstimate(
            flops=int(COST_SCALE * 7), bytes_accessed=0, transcendentals=0
        ),
    )(*ins)


def hop(value, axis, mask):
    size = lax.axis_size(axis)
    return lax.ppermute(value, axis, [(i, i ^ mask) for i in range(size)])


def peers(values):
    return [hop(value, "mp", k) for k, value in zip((1, 2, 3), values)]


def spread(value):
    near, far = hop(value, "dp", 1), hop(value, "dp", 2)
    here = [value, near, far, hop(far, "dp", 1)]
    return here + [hop(block, "tower", 1) for block in here]


def merge(value, axis, mask):
    other = hop(value, axis, mask)
    upper = (lax.axis_index(axis) & mask) != 0
    return jnp.where(
        upper, jnp.concatenate([other, value], axis=0), jnp.concatenate([value, other], axis=0)
    )


FEED_ORDER = (5, 6, 0, 1, 4, 7, 3, 2)
WIDE_ORDER = (0, 3, 6, 5, 1, 4, 7, 2)
MOVES = (
    ((7, 0), ((7, 3), (0, 4), (4, 0), (5, 1), (6, 2))),
    ((6, 1), ((6, 3), (1, 4), (7, 0), (3, 1))),
)


def fast_local(
    picture_residual_entry,
    sentence_residual_entry,
    sentence_lengths_held,
    couple_allowed_flags,
    picture_single_matrices,
    picture_mean_state,
    picture_square_state,
    sentence_single_matrices,
    sentence_mean_state,
    sentence_square_state,
    array_single_params,
    array_mean_state,
    array_square_state,
    logit_log_trio,
):
    LAST.clear()
    side, z, m = lax.axis_index("tower"), lax.axis_index("dp"), lax.axis_index("mp")
    ids = jnp.stack([side, z, m, side * ZN + z]).astype(jnp.int32)
    lengths = sentence_lengths_held
    vec_size = array_single_params.shape[0]

    def lines(value):
        return value.reshape(-1, 128)

    def vector_lines(value):
        return jnp.pad(value, (0, VEC_ROWS * 128 - vec_size)).reshape(VEC_ROWS, 128)

    vec_lines = vector_lines(array_single_params)
    keep_t, keep_i, send_t, send_i, block = kernel_call(
        prepare_body,
        [out((TXT.half, TXT.d), BF), out((IMG.half, IMG.d), BF)] * 2 + [out((16, TXT.d), BF)],
        [
            ids,
            couple_allowed_flags,
            lengths,
            lines(picture_single_matrices),
            lines(sentence_single_matrices),
            vec_lines,
        ],
        [
            pltpu.VMEM((IMG.sr, IMG.d), F32),
            pltpu.VMEM((TXT.sr, TXT.d), F32),
            pltpu.VMEM(SPARE, F32),
        ],
        us=2.5,
    )
    urgent, late = kernel_call(
        sort_body,
        [out((URGENT, IMG.d), BF), out((HALF, IMG.d), BF)],
        [ids, keep_t, keep_i, hop(send_t, "tower", 1), hop(send_i, "tower", 1), block],
    )
    urgent = spread(urgent)
    late = lax.all_gather(gate(late, *urgent[1:ZN]), "dp", axis=0, tiled=True)
    vecpay = kernel_call(
        vector_pay_body,
        [out((VEC_ROWS, 128), BF)],
        [ids, vec_lines],
        [pltpu.VMEM((VEC_ROWS + 8, 128), F32)],
    )[0]
    x_txt = jnp.transpose(sentence_residual_entry, (1, 0, 2))
    x_img = jnp.transpose(picture_residual_entry, (1, 0, 2))
    norms, meta, *t_out = attend_call(TXT, ids, x_txt, urgent)
    i_out = attend_call(IMG, ids, x_img, urgent, norms=norms)
    layers = {}
    before = ()
    middles = {}
    for tower, outs in ((TXT, t_out), (IMG, i_out)):
        xo, own, s1, s2, s3 = outs[8:]
        x1, h2, pooled = middle_call(
            tower, ids, lengths, norms, xo, own, peers([s1, s2, s3])
        )
        middles[tower] = (x1, pooled, [h2] + peers([h2, h2, h2]))
    late = gate(late, x1, *middles[TXT][2][1:])
    late = [late, hop(late, "tower", 1)]
    gathered = lax.all_gather(gate(vecpay, late[0]), GROUP, axis=0, tiled=False)
    for tower, outs in ((TXT, t_out), (IMG, i_out)):
        wq, wo, up, h1, u1, qkv, att, probs, xo = outs[:9]
        x1, pooled, blocks = middles[tower]
        w1, w2, slope, sums, *y = feed_call(
            tower, ids, lengths, blocks, up, late, pooled, before
        )
        before = (*y, sums)
        layers[tower] = dict(
            wq=wq, wo=wo, h1=h1, u1=u1, qkv=qkv, att=att, probs=probs, xo=xo,
            x1=x1, blocks=blocks, w1=w1, w2=w2, slope=slope,
        )

    received = peers(y[1:])
    y = (y[0] + received[0]) + (received[1] + received[2])
    parts = lax.all_to_all(
        jnp.broadcast_to(y, (2 * ZN * MP, *y.shape)), (*GROUP, "mp"), 0, 0, tiled=True
    )
    sums = gate(sums, y)
    sums = [sums] + [hop(sums, "dp", k) for k in range(1, ZN)]
    pi, pt = project_call(gathered, ())
    sums = sums[:1] + [gate(block, pi) for block in sums[1:]]
    sums = sums + [hop(block, "tower", 1) for block in sums]
    misc, dyb_i, dyb_t, dy_i, dy_t, pg_i, pg_t, ng_i, ng_t = head_call(
        ids, logit_log_trio, parts, norms, meta, pi, pt
    )

    dy = {IMG: dy_i, TXT: dy_t}
    back, dx1, dx1b, second = {}, {}, {}, {}
    entries, norm_sums = {}, {}
    grads = []
    for tower in (IMG, TXT):
        s = layers[tower]
        back[tower] = feed_back_call(
            tower, ids, lengths, s["blocks"], s["slope"], dy[tower], s["w1"], s["w2"], grads,
            sums if tower is TXT else (),
        )
        grads = [back[tower][4]]
    feed_own = lax.psum_scatter(back[TXT][4], GROUP, scatter_dimension=0, tiled=False)
    window = vector_call(ids, pg_i, pg_t, ng_i, ng_t)
    for tower in (IMG, TXT):
        own, s1, s2, s3 = back[tower][:4]
        dx1[tower], dx1b[tower] = middle_back_call(
            tower, ids, lengths, norms, layers[tower]["x1"], dy[tower], own, peers([s1, s2, s3])
        )
    halves = []
    for tower in (IMG, TXT):
        s = layers[tower]
        block = dx1b[tower]
        *back[tower], keep, sent, second[tower] = attend_back_call(
            tower, ids, [block] + peers([block] * 3),
            s["att"], s["qkv"], s["probs"], s["h1"], s["u1"], s["wq"], s["wo"],
        )
        halves += [keep, hop(sent, "tower", 1)]
    payload = kernel_call(pair_body, [out((ZN, FEED_ROWS, IMG.d), BF)], halves, us=2.8)[0]
    got = lax.all_to_all(payload, "dp", 0, 0, tiled=True)
    before = ()
    for tower in (IMG, TXT):
        own, s1, s2, s3 = back[tower]
        dx, norm_sums[tower] = entry_call(
            tower, norms, layers[tower]["xo"], dx1[tower], second[tower], own,
            peers([s1, s2, s3]), before,
        )
        before = (dx,)
        if tower is IMG:
            down = {IMG: down_call(IMG, ids, sums, dyb_i)}
    placed = [dx] + peers([dx, dx, dx])
    down[TXT] = down_call(TXT, ids, sums, dyb_t)
    wide, *passed = mix_call(ids, feed_own, got)
    moved = [lax.ppermute(v, GROUP, list(pairs)) for v, (_, pairs) in zip(passed, MOVES)]
    lin_i, lin_t, message = collect_call(
        ids, [feed_own, wide, *moved], down[IMG], down[TXT], window,
        norm_sums[IMG], norm_sums[TXT], placed[1:],
    )
    parts = lax.all_to_all(message, (*GROUP, "mp"), 0, 0, tiled=True)
    for tower in (IMG, TXT):
        entries[tower] = place_call(tower, ids, placed)
    loss, size, temperature, *new = advance_call(
        ids,
        logit_log_trio,
        parts,
        misc,
        [lines(picture_single_matrices), lines(picture_mean_state), lines(picture_square_state), lin_i],
        [
            lines(sentence_single_matrices),
            lines(sentence_mean_state),
            lines(sentence_square_state),
            lin_t,
        ],
        [vec_lines, vector_lines(array_mean_state), vector_lines(array_square_state), window],
    )

    def flat(value, like):
        return value.reshape(-1)[: like.size].reshape(like.shape)

    likes = [picture_single_matrices] * 4 + [sentence_single_matrices] * 4 + [array_single_params] * 4
    news = [flat(value, like) for value, like in zip(new, likes)]
    return (
        loss.reshape(()),
        size.reshape(()),
        jnp.transpose(entries[IMG], (1, 0, 2)),
        jnp.transpose(entries[TXT], (1, 0, 2)),
        *news,
        temperature.reshape(()),
    )


def fits(mesh):
    return mesh.shape["tower"] == 2 and mesh.shape["dp"] == ZN and mesh.shape["mp"] == MP


def solution(mesh):
    placed = (
        P(GROUP, None, None),
        P(GROUP, None, None),
        P(GROUP),
        P(GROUP),
        P("mp", GROUP),
        P("mp", GROUP),
        P("mp", GROUP),
        P("mp", GROUP),
        P("mp", GROUP),
        P("mp", GROUP),
        P(GROUP),
        P(GROUP),
        P(GROUP),
        P(),
    )
    return jax.shard_map(
        fast_local if fits(mesh) else local,
        mesh=mesh,
        in_specs=placed,
        out_specs=(
            P(),
            P(),
            P(GROUP, None, None),
            P(GROUP, None, None),
            P("mp", GROUP),
            P("mp", GROUP),
            P("mp", GROUP),
            P("mp", GROUP),
            P("mp", GROUP),
            P("mp", GROUP),
            P("mp", GROUP),
            P("mp", GROUP),
            P(GROUP),
            P(GROUP),
            P(GROUP),
            P(GROUP),
            P(),
        ),
        check_vma=False,
    )
```

```python
import functools
import jax
import jax.numpy as jnp
from jax import lax
from jax.experimental import pallas as pl
from jax.experimental.pallas import tpu as pltpu
from jax.sharding import PartitionSpec as P

BF = jnp.bfloat16
F32 = jnp.float32
GROUP = ("tower", "dp")

D_IMG = 768
FF_IMG = 3072
IMG_LEN = 50
D_TXT = 512
FF_TXT = 2048
TXT_LEN = 77
HEAD = 64
EMBED = 512
STEP = 10


NORM_EPS = 1e-05
UNIT_EPS = 1e-06
BETA_ONE = 0.5
BETA_TWO = 0.5
ADAM_EPS = 1e-08
WEIGHT_DECAY = 0.1
RATE_MATRIX = 0.04
RATE_VECTOR = 0.3
LOGIT_SPEED = 0.5
CLIP_LEVEL = 0.005
MASK_LOW = -1e30
GELU_SLOPE = 1.702
BLOCK_TARGET = 512


def branch_sum(partial_sum):
    return lax.psum(partial_sum, "mp")


def branch_back(partial_sum):
    return lax.psum(partial_sum, "mp")


def norm_forward(values, norm_gain, norm_shift):
    centered = values - jnp.mean(values, axis=-1, keepdims=True)
    inverse = lax.rsqrt(jnp.mean(centered * centered, axis=-1, keepdims=True) + NORM_EPS)
    unit_rows = centered * inverse
    return (unit_rows * norm_gain + norm_shift, unit_rows, inverse)


def norm_backward(grad_rows, unit_rows, inverse, norm_gain):
    scaled = grad_rows * norm_gain
    centered_grad = (
        scaled
        - jnp.mean(scaled, axis=-1, keepdims=True)
        - unit_rows * jnp.mean(scaled * unit_rows, axis=-1, keepdims=True)
    )
    return (
        centered_grad * inverse,
        jnp.sum(grad_rows * unit_rows, axis=0),
        jnp.sum(grad_rows, axis=0),
    )


def quick_gelu(values):
    return values * jax.nn.sigmoid(GELU_SLOPE * values)


def gelu_slope(values):
    sigmoid_value = jax.nn.sigmoid(GELU_SLOPE * values)
    return sigmoid_value + GELU_SLOPE * values * sigmoid_value * (1.0 - sigmoid_value)


def block_size(seq_count, seq_length):
    for candidate in range(1, seq_count + 1):
        if seq_count % candidate == 0 and candidate * seq_length >= BLOCK_TARGET:
            return candidate
    return seq_count


def sequence_mask(seq_length, causal):
    position = lax.iota(jnp.int32, seq_length)
    if causal:
        return position[None, :] <= position[:, None]
    return position[None, :] >= 0


def block_scores(block_qkv, allowed):
    scores = jnp.einsum(
        "nqhd,nkhd->nhqk",
        block_qkv[:, :, 0],
        block_qkv[:, :, 1],
        preferred_element_type=jnp.float32,
    ) * HEAD ** (-0.5)
    return jnp.where(allowed[None, None], scores, MASK_LOW)


def attend(packed, seq_count, seq_length, causal):
    head_count = packed.shape[2]
    per_block = block_size(seq_count, seq_length)
    blocks = packed.reshape(seq_count // per_block, per_block, seq_length, 3, head_count, HEAD)
    allowed = sequence_mask(seq_length, causal)

    def one_block(block_qkv):
        scores = block_scores(block_qkv, allowed)
        row_max = jnp.max(scores, axis=-1, keepdims=True)
        exponent = jnp.exp(scores - row_max)
        totals = jnp.sum(exponent, axis=-1, keepdims=True)
        probs = (exponent / totals).astype(jnp.bfloat16)
        result = jnp.einsum(
            "nhqk,nkhd->nqhd", probs, block_qkv[:, :, 2], preferred_element_type=jnp.float32
        ).astype(jnp.bfloat16)
        return (result, (row_max + jnp.log(totals))[..., 0])

    results, log_totals = lax.map(one_block, blocks)
    return (results.reshape(packed.shape[0], head_count * HEAD), log_totals)


def attend_back(packed, attended_grad, log_totals, seq_count, seq_length, causal):
    head_count = packed.shape[2]
    per_block = block_size(seq_count, seq_length)
    block_total = seq_count // per_block
    blocks = packed.reshape(block_total, per_block, seq_length, 3, head_count, HEAD)
    grad_blocks = attended_grad.reshape(block_total, per_block, seq_length, head_count, HEAD)
    allowed = sequence_mask(seq_length, causal)

    def one_block(block_args):
        block_qkv, block_grad, block_totals = block_args
        scores = block_scores(block_qkv, allowed)
        probs = jnp.exp(scores - block_totals[..., None])
        value_grad = jnp.einsum(
            "nhqk,nqhd->nkhd",
            probs.astype(jnp.bfloat16),
            block_grad,
            preferred_element_type=jnp.float32,
        )
        prob_grad = jnp.einsum(
            "nqhd,nkhd->nhqk", block_grad, block_qkv[:, :, 2], preferred_element_type=jnp.float32
        )
        score_grad = (
            probs * (prob_grad - jnp.sum(probs * prob_grad, axis=-1, keepdims=True))
        ).astype(jnp.bfloat16)
        query_grad = jnp.einsum(
            "nhqk,nkhd->nqhd", score_grad, block_qkv[:, :, 1], preferred_element_type=jnp.float32
        ) * HEAD ** (-0.5)
        key_grad = jnp.einsum(
            "nhqk,nqhd->nkhd", score_grad, block_qkv[:, :, 0], preferred_element_type=jnp.float32
        ) * HEAD ** (-0.5)
        return jnp.stack([query_grad, key_grad, value_grad], axis=2).astype(jnp.bfloat16)

    return lax.map(one_block, (blocks, grad_blocks, log_totals)).reshape(packed.shape)


def split_flat(flat_weights, model_width, hidden, model_split):
    width_piece = model_width // model_split
    hidden_piece = hidden // model_split
    first_end = model_width * 3 * width_piece
    second_end = first_end + width_piece * model_width
    third_end = second_end + model_width * hidden_piece
    return (
        flat_weights[:first_end].reshape(model_width, 3, width_piece),
        flat_weights[first_end:second_end].reshape(width_piece, model_width),
        flat_weights[second_end:third_end].reshape(model_width, hidden_piece),
        flat_weights[third_end:].reshape(hidden_piece, model_width),
    )


def layer_forward(tokens, weights, norms, causal):
    qkv_weight, out_weight, up_weight, down_weight = weights
    seq_count, seq_length, model_width = tokens.shape
    token_rows = tokens.reshape(seq_count * seq_length, model_width).astype(jnp.float32)
    first_normed, unit_one, inverse_one = norm_forward(token_rows, norms[0], norms[1])
    first_low = first_normed.astype(jnp.bfloat16)
    packed = jnp.einsum(
        "rd,dtk->rtk", first_low, qkv_weight, preferred_element_type=jnp.float32
    ).astype(jnp.bfloat16)
    packed = packed.reshape(token_rows.shape[0], 3, qkv_weight.shape[2] // HEAD, HEAD)
    attended, log_totals = attend(packed, seq_count, seq_length, causal)
    middle = token_rows + branch_sum(
        jnp.dot(attended, out_weight, preferred_element_type=jnp.float32)
    )
    second_normed, unit_two, inverse_two = norm_forward(middle, norms[2], norms[3])
    second_low = second_normed.astype(jnp.bfloat16)
    pre_act = jnp.dot(second_low, up_weight, preferred_element_type=jnp.float32)
    activated = quick_gelu(pre_act).astype(jnp.bfloat16)
    outputs = middle + branch_sum(
        jnp.dot(activated, down_weight, preferred_element_type=jnp.float32)
    )
    return (
        outputs,
        (
            first_low,
            unit_one,
            inverse_one,
            packed,
            attended,
            log_totals,
            second_low,
            unit_two,
            inverse_two,
            pre_act,
            activated,
        ),
    )


def layer_backward(grad_out, weights, norms, stored, seq_count, seq_length, causal):
    qkv_weight, out_weight, up_weight, down_weight = weights
    (
        first_low,
        unit_one,
        inverse_one,
        packed,
        attended,
        log_totals,
        second_low,
        unit_two,
        inverse_two,
        pre_act,
        activated,
    ) = stored
    grad_low = grad_out.astype(jnp.bfloat16)
    down_grad = jnp.einsum("rf,rd->fd", activated, grad_low, preferred_element_type=jnp.float32)
    act_grad = jnp.einsum("rd,fd->rf", grad_low, down_weight, preferred_element_type=jnp.float32)
    pre_grad = (act_grad * gelu_slope(pre_act)).astype(jnp.bfloat16)
    up_grad = jnp.einsum("rd,rf->df", second_low, pre_grad, preferred_element_type=jnp.float32)
    second_grad = branch_back(
        jnp.einsum("rf,df->rd", pre_grad, up_weight, preferred_element_type=jnp.float32)
    )
    norm_grad_two, gain_two, shift_two = norm_backward(second_grad, unit_two, inverse_two, norms[2])
    middle_grad = grad_out + norm_grad_two
    middle_low = middle_grad.astype(jnp.bfloat16)
    out_grad = jnp.einsum("ra,rd->ad", attended, middle_low, preferred_element_type=jnp.float32)
    attended_grad = jnp.einsum(
        "rd,ad->ra", middle_low, out_weight, preferred_element_type=jnp.float32
    ).astype(jnp.bfloat16)
    packed_grad = attend_back(packed, attended_grad, log_totals, seq_count, seq_length, causal)
    packed_grad = packed_grad.reshape(packed.shape[0], 3, qkv_weight.shape[2])
    qkv_grad = jnp.einsum("rd,rtk->dtk", first_low, packed_grad, preferred_element_type=jnp.float32)
    first_grad = branch_back(
        jnp.einsum("rtk,dtk->rd", packed_grad, qkv_weight, preferred_element_type=jnp.float32)
    )
    norm_grad_one, gain_one, shift_one = norm_backward(first_grad, unit_one, inverse_one, norms[0])
    flat_grads = jnp.concatenate(
        [qkv_grad.reshape(-1), out_grad.reshape(-1), up_grad.reshape(-1), down_grad.reshape(-1)]
    )
    return (middle_grad + norm_grad_one, flat_grads, [gain_one, shift_one, gain_two, shift_two])


def pool_forward(picked, norm_gain, norm_shift, projection):
    normed, unit_rows, inverse = norm_forward(picked, norm_gain, norm_shift)
    normed_low = normed.astype(jnp.bfloat16)
    raw_embed = jnp.dot(normed_low, projection, preferred_element_type=jnp.float32)
    length_inverse = lax.rsqrt(jnp.sum(raw_embed * raw_embed, axis=-1, keepdims=True) + UNIT_EPS)
    embed_rows = raw_embed * length_inverse
    return (
        embed_rows.astype(jnp.bfloat16),
        (unit_rows, inverse, normed_low, embed_rows, length_inverse),
    )


def pool_backward(embed_grad, norm_gain, projection, stored):
    unit_rows, inverse, normed_low, embed_rows, length_inverse = stored
    raw_grad = (
        length_inverse
        * (embed_grad - embed_rows * jnp.sum(embed_grad * embed_rows, axis=-1, keepdims=True))
    ).astype(jnp.bfloat16)
    proj_grad = jnp.einsum("nd,ne->de", normed_low, raw_grad, preferred_element_type=jnp.float32)
    normed_grad = jnp.einsum("ne,de->nd", raw_grad, projection, preferred_element_type=jnp.float32)
    picked_grad, gain_grad, shift_grad = norm_backward(normed_grad, unit_rows, inverse, norm_gain)
    return (picked_grad, proj_grad, gain_grad, shift_grad)


def cosine_logits(picture_feature_lines, sentence_feature_lines, couple_allowed_flags, log_scale):
    image_all, text_all, valid_all = (
        lax.all_gather(picture_feature_lines, GROUP, axis=0, tiled=True),
        lax.all_gather(sentence_feature_lines, GROUP, axis=0, tiled=True),
        lax.all_gather(
            couple_allowed_flags.astype(jnp.bfloat16), GROUP, axis=0, tiled=True
        ),
    )
    count_valid = jnp.sum(valid_all.astype(jnp.float32))
    column_valid = valid_all > 0
    row_valid = couple_allowed_flags > 0
    local_count = picture_feature_lines.shape[0]
    offset_rows = lax.axis_index(GROUP) * local_count
    on_diagonal = (
        lax.iota(jnp.int32, valid_all.shape[0])[None, :]
        == offset_rows + lax.iota(jnp.int32, local_count)[:, None]
    )
    scale_factor = jnp.exp(log_scale)

    def one_side(mine, others):
        logits = scale_factor * jnp.einsum(
            "ne,me->nm", mine, others, preferred_element_type=jnp.float32
        )
        masked = jnp.where(column_valid[None, :], logits, MASK_LOW)
        row_max = jnp.max(masked, axis=1, keepdims=True)
        exponent = jnp.exp(masked - row_max)
        totals = jnp.sum(exponent, axis=1, keepdims=True)
        own_logit = jnp.sum(jnp.where(on_diagonal, logits, 0.0), axis=1)
        log_sum = row_max[:, 0] + jnp.log(totals[:, 0])
        loss_sum = jnp.sum(jnp.where(row_valid, log_sum - own_logit, 0.0))
        logit_grad = jnp.where(
            row_valid[:, None], exponent / totals - on_diagonal.astype(jnp.float32), 0.0
        ) / (2.0 * count_valid)
        return (loss_sum, logit_grad, jnp.sum(logit_grad * logits), log_sum, logits)

    image_loss, image_logit_grad, image_scale_part, image_lse, image_logits = one_side(
        picture_feature_lines, text_all
    )
    text_loss, text_logit_grad, text_scale_part, text_lse, text_logits = one_side(
        sentence_feature_lines, image_all
    )
    picture_device_share = scale_factor * jnp.dot(
        image_logit_grad, text_all.astype(jnp.float32), precision=lax.Precision.HIGHEST
    )
    sentence_device_share = scale_factor * jnp.dot(
        text_logit_grad, image_all.astype(jnp.float32), precision=lax.Precision.HIGHEST
    )
    text_spread = scale_factor * jnp.einsum(
        "np,ne->pe",
        image_logit_grad,
        picture_feature_lines.astype(jnp.float32),
        precision=lax.Precision.HIGHEST,
    )
    image_spread = scale_factor * jnp.einsum(
        "np,ne->pe",
        text_logit_grad,
        sentence_feature_lines.astype(jnp.float32),
        precision=lax.Precision.HIGHEST,
    )
    picture_reverse, sentence_reverse = (
        lax.psum_scatter(image_spread, GROUP, scatter_dimension=0, tiled=True),
        lax.psum_scatter(text_spread, GROUP, scatter_dimension=0, tiled=True),
    )
    contrast_objective, logit_log_slope = lax.psum(
        ((image_loss + text_loss) / (2.0 * count_valid), image_scale_part + text_scale_part),
        GROUP,
    )
    return (
        picture_device_share + picture_reverse,
        sentence_device_share + sentence_reverse,
        contrast_objective,
        logit_log_slope,
    )


def optimizer_advance(master, first, second, grad, rate, decay):
    first_new = BETA_ONE * first + (1.0 - BETA_ONE) * grad
    second_new = BETA_TWO * second + (1.0 - BETA_TWO) * grad * grad
    update = (
        first_new
        / (1.0 - BETA_ONE**STEP)
        / (jnp.sqrt(second_new / (1.0 - BETA_TWO**STEP)) + ADAM_EPS)
    )
    return (master - rate * (update + decay * master), first_new, second_new)


def local(
    picture_residual_entry,
    sentence_residual_entry,
    sentence_lengths_held,
    couple_allowed_flags,
    picture_single_matrices,
    picture_mean_state,
    picture_square_state,
    sentence_single_matrices,
    sentence_mean_state,
    sentence_square_state,
    array_single_params,
    array_mean_state,
    array_square_state,
    logit_log_trio,
):
    model_split = lax.axis_size("mp")
    norm_end = 6 * (D_IMG + D_TXT)
    image_end = norm_end + D_IMG * EMBED
    image_flat, text_flat, vector_flat = (
        lax.all_gather(
            picture_single_matrices.astype(jnp.bfloat16), GROUP, axis=1, tiled=True
        ),
        lax.all_gather(
            sentence_single_matrices.astype(jnp.bfloat16), GROUP, axis=1, tiled=True
        ),
        lax.all_gather(
            array_single_params.astype(jnp.bfloat16), GROUP, axis=0, tiled=True
        ),
    )
    image_norms = vector_flat[: 6 * D_IMG].reshape(6, D_IMG).astype(jnp.float32)
    text_norms = vector_flat[6 * D_IMG : norm_end].reshape(6, D_TXT).astype(jnp.float32)
    image_proj = vector_flat[norm_end:image_end].reshape(D_IMG, EMBED)
    text_proj = vector_flat[image_end:].reshape(D_TXT, EMBED)
    seq_count = picture_residual_entry.shape[0]
    image_weights = split_flat(image_flat[0], D_IMG, FF_IMG, model_split)
    image_out, image_stored = layer_forward(
        picture_residual_entry, image_weights, image_norms, False
    )
    image_picked = jnp.mean(image_out.reshape(seq_count, IMG_LEN, D_IMG), axis=1)
    picture_feature_lines, image_pool = pool_forward(
        image_picked, image_norms[4], image_norms[5], image_proj
    )
    text_weights = split_flat(text_flat[0], D_TXT, FF_TXT, model_split)
    text_out, text_stored = layer_forward(sentence_residual_entry, text_weights, text_norms, True)
    inside = (lax.iota(jnp.int32, TXT_LEN)[None, :] < sentence_lengths_held[:, None]).astype(
        jnp.float32
    )
    picker = inside / sentence_lengths_held[:, None].astype(jnp.float32)
    text_picked = jnp.einsum(
        "nl,nld->nd",
        picker,
        text_out.reshape(seq_count, TXT_LEN, D_TXT),
        precision=lax.Precision.HIGHEST,
    )
    sentence_feature_lines, text_pool = pool_forward(
        text_picked, text_norms[4], text_norms[5], text_proj
    )
    picture_feature_slope, sentence_feature_slope, contrast_objective, logit_log_slope = (
        cosine_logits(
            picture_feature_lines, sentence_feature_lines, couple_allowed_flags, logit_log_trio[0]
        )
    )
    text_picked_grad, text_proj_grad, text_post_gain, text_post_shift = pool_backward(
        sentence_feature_slope, text_norms[4], text_proj, text_pool
    )
    text_rows_grad = (picker[:, :, None] * text_picked_grad[:, None, :]).reshape(
        seq_count * TXT_LEN, D_TXT
    )
    sentence_entry_slope, text_flat_grad, text_norm_grads = layer_backward(
        text_rows_grad, text_weights, text_norms, text_stored, seq_count, TXT_LEN, True
    )
    image_picked_grad, image_proj_grad, image_post_gain, image_post_shift = pool_backward(
        picture_feature_slope, image_norms[4], image_proj, image_pool
    )
    image_rows_grad = jnp.broadcast_to(
        image_picked_grad[:, None, :] / IMG_LEN, (seq_count, IMG_LEN, D_IMG)
    ).reshape(seq_count * IMG_LEN, D_IMG)
    picture_entry_slope, image_flat_grad, image_norm_grads = layer_backward(
        image_rows_grad, image_weights, image_norms, image_stored, seq_count, IMG_LEN, False
    )
    array_param_slope = jnp.concatenate(
        [
            jnp.stack(image_norm_grads + [image_post_gain, image_post_shift]).reshape(-1),
            jnp.stack(text_norm_grads + [text_post_gain, text_post_shift]).reshape(-1),
            image_proj_grad.reshape(-1),
            text_proj_grad.reshape(-1),
        ]
    )
    image_reduced, text_reduced, vector_reduced = (
        lax.psum_scatter(
            image_flat_grad.reshape(-1, D_IMG), GROUP, scatter_dimension=0, tiled=True
        ).reshape(1, -1),
        lax.psum_scatter(
            text_flat_grad.reshape(-1, D_TXT), GROUP, scatter_dimension=0, tiled=True
        ).reshape(1, -1),
        lax.psum_scatter(array_param_slope, GROUP, scatter_dimension=0, tiled=True),
    )
    matrix_squares = jnp.sum(image_reduced * image_reduced) + jnp.sum(text_reduced * text_reduced)
    vector_squares = jnp.sum(vector_reduced * vector_reduced) / model_split
    tensor_square_sum, array_square_sum = lax.psum(
        (matrix_squares, vector_squares), (*GROUP, "mp")
    )
    global_slope_size = jnp.sqrt(
        tensor_square_sum + array_square_sum + logit_log_slope * logit_log_slope
    )
    clipping_factor = CLIP_LEVEL / jnp.maximum(global_slope_size, CLIP_LEVEL)
    picture_matrices_fresh, picture_mean_fresh, picture_square_fresh = optimizer_advance(
        picture_single_matrices,
        picture_mean_state,
        picture_square_state,
        image_reduced * clipping_factor,
        RATE_MATRIX,
        WEIGHT_DECAY,
    )
    sentence_matrices_fresh, sentence_mean_fresh, sentence_square_fresh = optimizer_advance(
        sentence_single_matrices,
        sentence_mean_state,
        sentence_square_state,
        text_reduced * clipping_factor,
        RATE_MATRIX,
        WEIGHT_DECAY,
    )
    shard_length = array_single_params.shape[0]
    vector_index = lax.axis_index(GROUP) * shard_length + lax.iota(
        jnp.int32, shard_length
    )
    is_norm = vector_index < norm_end
    array_params_fresh, array_mean_fresh, array_square_fresh = optimizer_advance(
        array_single_params,
        array_mean_state,
        array_square_state,
        vector_reduced * clipping_factor,
        jnp.where(is_norm, RATE_VECTOR, RATE_MATRIX),
        jnp.where(is_norm, 0.0, WEIGHT_DECAY),
    )
    logit_log_fresh, logit_mean_fresh, logit_square_fresh = optimizer_advance(
        logit_log_trio[0],
        logit_log_trio[1],
        logit_log_trio[2],
        logit_log_slope * clipping_factor,
        LOGIT_SPEED,
        0.0,
    )
    return (
        contrast_objective,
        global_slope_size,
        picture_entry_slope.reshape(picture_residual_entry.shape),
        sentence_entry_slope.reshape(sentence_residual_entry.shape),
        picture_matrices_fresh,
        picture_matrices_fresh.astype(jnp.bfloat16),
        picture_mean_fresh,
        picture_square_fresh,
        sentence_matrices_fresh,
        sentence_matrices_fresh.astype(jnp.bfloat16),
        sentence_mean_fresh,
        sentence_square_fresh,
        array_params_fresh,
        array_params_fresh.astype(jnp.bfloat16),
        array_mean_fresh,
        array_square_fresh,
        logit_log_fresh,
    )


ZN = 4
MP = 4
SEQS = 8


class Tower:
    def __init__(self, tag, width, length, padded, joint, causal, norm_row):
        self.tag = tag
        self.d = width
        self.w = width // MP
        self.heads = self.w // HEAD
        self.length = length
        self.padded = padded
        self.rows = 2 * padded
        self.all_rows = MP * self.rows
        self.tile = self.rows if joint else padded
        self.tiles = self.rows // self.tile
        self.causal = causal
        self.sr = 3 * width // 8
        self.half = self.sr // 2
        self.q = width // 128
        self.norm_row = norm_row
        self.lin = self.sr * self.q


IMG = Tower("_img", D_IMG, IMG_LEN, 56, True, False, 0)
TXT = Tower("_txt", D_TXT, TXT_LEN, 80, False, True, 6 * D_IMG // 128)
NORM_ROWS = 6 * (D_IMG + D_TXT) // 128
VEC_ROWS = 648
HALF = IMG.half + 64
FEED_ROWS = IMG.d // 8 + 48
URGENT = HALF + 16


COST_SCALE = 1.5e9


def kernel_call(body, outs, ins, scratch=(), us=2.0, after=(), vmem=64):
    after = list(after) + LAST

    def spec(value):
        small = value.dtype == jnp.int32 or (value.ndim == 1 and value.shape[0] <= 8)
        return pl.BlockSpec(memory_space=pltpu.SMEM if small else pltpu.VMEM)

    count, late = len(ins), len(after)
    name = getattr(body, "func", body).__name__
    if hasattr(body, "args"):
        name = name + body.args[0].tag
    results = pl.pallas_call(
        lambda *refs: body(*refs[:count], *refs[count + late :]),
        out_shape=list(outs),
        in_specs=[spec(v) for v in ins] + [pl.BlockSpec(memory_space=pl.ANY)] * late,
        out_specs=[pl.BlockSpec(memory_space=pltpu.VMEM)] * len(outs),
        scratch_shapes=list(scratch),
        compiler_params=pltpu.CompilerParams(
            vmem_limit_bytes=vmem * MIB
        ),
        cost_estimate=pl.CostEstimate(
            flops=int(COST_SCALE * us), bytes_accessed=0, transcendentals=0
        ),
        name=name,
    )(*ins, *after)
    LAST[:] = results[:1]
    return results


LAST = []
MIB = 1024 * 1024


def gate(value, *after):
    anywhere = pl.BlockSpec(memory_space=pl.ANY)
    return pl.pallas_call(
        lambda *refs: None,
        out_shape=out(value.shape, value.dtype),
        in_specs=[anywhere] * (1 + len(after)),
        out_specs=anywhere,
        input_output_aliases={0: 0},
    )(value, *after)


def out(shape, dtype=F32):
    return jax.ShapeDtypeStruct(shape, dtype)


def dot(a, b):
    return lax.dot_general(a, b, (((1,), (0,)), ((), ())), preferred_element_type=F32)


def dot_nt(a, b):
    return lax.dot_general(a, b, (((1,), (1,)), ((), ())), preferred_element_type=F32)


def dot_tn(a, b):
    return lax.dot_general(a, b, (((0,), (0,)), ((), ())), preferred_element_type=F32)


def pieces(a, count):
    parts = []
    for _ in range(count):
        part = a.astype(BF)
        parts.append(part)
        a = a - part.astype(F32)
    return parts


def unit(values):
    width = values.shape[-1]
    centered = values - jnp.sum(values, axis=-1, keepdims=True) * (1.0 / width)
    inverse = lax.rsqrt(
        jnp.sum(centered * centered, axis=-1, keepdims=True) * (1.0 / width) + NORM_EPS
    )
    return centered * inverse, inverse


def unit_back(grad_rows, unit_rows, inverse, gain):
    width = grad_rows.shape[-1]
    scaled = grad_rows * gain
    first = jnp.sum(scaled, axis=-1, keepdims=True) * (1.0 / width)
    second = jnp.sum(scaled * unit_rows, axis=-1, keepdims=True) * (1.0 / width)
    return (scaled - first - unit_rows * second) * inverse


def norm_vector(norms_ref, tower, index):
    start = tower.norm_row + index * tower.q
    return jnp.concatenate([norms_ref[start + i : start + i + 1, :] for i in range(tower.q)], axis=1)


def natural_from_lin(tower, lin_ref, spare):
    d, w = tower.d, tower.w
    if (3 * w) % 128 == 0:
        per = 3 * w // 128
        return jnp.concatenate(
            [lin_ref[pl.ds(i, d // 2, stride=per), :] for i in range(per)], axis=1
        )
    per = 2 * 3 * w // 128
    mid = per // 2
    lines = [lin_ref[pl.ds(i, d // 4, stride=per), :] for i in range(per)]
    empty = jnp.zeros((d // 4, 64), F32)
    even = lines[: mid + 1]
    odd = jnp.concatenate([lines[mid][:, 64:]] + lines[mid + 1 :] + [empty], axis=1)
    for j in range(mid + 1):
        spare.at[j][pl.ds(0, d // 4, stride=2), :] = even[j]
        spare.at[j][pl.ds(1, d // 4, stride=2), :] = odd[:, 128 * j : 128 * (j + 1)]
    return jnp.concatenate([spare[j] for j in range(mid)] + [spare[mid][:, :64]], axis=1)


def natural_to_lin(tower, natural, lin_ref, spare):
    d, w = tower.d, tower.w
    if (3 * w) % 128 == 0:
        per = 3 * w // 128
        for i in range(per):
            lin_ref[pl.ds(i, d // 2, stride=per), :] = natural[:, 128 * i : 128 * (i + 1)]
        return
    per = 2 * 3 * w // 128
    mid = per // 2
    for j in range(mid):
        spare[j] = natural[:, 128 * j : 128 * (j + 1)]
    spare[mid] = jnp.concatenate([natural[:, 128 * mid :], jnp.zeros((d // 2, 64), F32)], axis=1)
    even = [spare.at[j][pl.ds(0, d // 4, stride=2), :] for j in range(mid + 1)]
    odd = jnp.concatenate(
        [spare.at[j][pl.ds(1, d // 4, stride=2), :] for j in range(mid + 1)], axis=1
    )
    for i in range(mid):
        lin_ref[pl.ds(i, d // 4, stride=per), :] = even[i]
    lin_ref[pl.ds(mid, d // 4, stride=per), :] = jnp.concatenate(
        [even[mid][:, :64], odd[:, :64]], axis=1
    )
    for i in range(mid):
        lin_ref[pl.ds(mid + 1 + i, d // 4, stride=per), :] = odd[:, 64 + 128 * i : 192 + 128 * i]


def lin_to_rows(tower, lin_ref, rows_ref, spare, shard):
    d, w, sr, q = tower.d, tower.w, tower.sr, tower.q

    @pl.when(shard >= 2)
    def _():
        for j in range(q):
            rows_ref[:, 128 * j : 128 * (j + 1)] = lin_ref[pl.ds(j, sr, stride=q), :]

    @pl.when(shard < 2)
    def _():
        tail = d // 8
        natural = natural_from_lin(tower, lin_ref, spare)
        rows_ref[:, : 3 * w] = natural[:sr]
        for i in range(3):
            rows_ref[tail * i : tail * (i + 1), 3 * w :] = natural[sr:, w * i : w * (i + 1)]


def rows_to_lin(tower, rows_ref, lin_ref, spare, shard):
    d, w, sr, q = tower.d, tower.w, tower.sr, tower.q

    @pl.when(shard >= 2)
    def _():
        for j in range(q):
            lin_ref[pl.ds(j, sr, stride=q), :] = rows_ref[:, 128 * j : 128 * (j + 1)]

    @pl.when(shard < 2)
    def _():
        tail = d // 8
        rest = jnp.concatenate(
            [rows_ref[tail * i : tail * (i + 1), 3 * w :] for i in range(3)], axis=1
        )
        natural = jnp.concatenate([rows_ref[:, : 3 * w], rest], axis=0)
        natural_to_lin(tower, natural, lin_ref, spare)


SPARE = ((3 * IMG.w + 127) // 128, IMG.d // 2, 128)


def prepare_body(
    ids, flags, lengths, img, txt, head, keep_t, keep_i, send_t, send_i, block, rows_i, rows_t, spare
):
    side, shard = ids[0], ids[3]
    lin_to_rows(IMG, img, rows_i, spare, shard)
    lin_to_rows(TXT, txt, rows_t, spare, shard)
    lane = lax.broadcasted_iota(jnp.int32, (1, 128), 1)
    flag_row = jnp.zeros((1, 128), F32)
    length_row = jnp.zeros((1, 128), F32)
    for i in range(SEQS):
        flag_row = jnp.where(lane == i, jnp.where(flags[i] > 0, 1.0, 0.0), flag_row)
        length_row = jnp.where(lane == i, lengths[i].astype(F32), length_row)
    lines = jnp.concatenate(
        [head[:NORM_ROWS, :], flag_row, length_row, jnp.zeros((64 - NORM_ROWS - 2, 128), F32)], axis=0
    )
    for j in range(4):
        block[:, 128 * j : 128 * (j + 1)] = lines[16 * j : 16 * (j + 1)].astype(BF)
    for tower, rows, keep, send in ((TXT, rows_t, keep_t, send_t), (IMG, rows_i, keep_i, send_i)):
        for target, which in ((keep, side), (send, 1 - side)):
            target[...] = rows[
                pl.ds(pl.multiple_of(which * tower.half, 8), tower.half), :
            ].astype(BF)


def sort_body(ids, keep_t, keep_i, got_t, got_i, block, urgent, late):
    def fill(*halves):
        for target, part_t, part_i in ((urgent, *halves[:2]), (late, *halves[2:])):
            target[: IMG.half, :] = part_i[...]
            target[IMG.half : HALF, : TXT.d] = part_t[:64, :]
            target[IMG.half : IMG.half + 32, TXT.d :] = part_t[64:, :256]
            target[IMG.half + 32 : HALF, TXT.d :] = part_t[64:, 256:]

    pl.when(ids[0] == 0)(lambda: fill(keep_t, keep_i, got_t, got_i))
    pl.when(ids[0] != 0)(lambda: fill(got_t, got_i, keep_t, keep_i))
    urgent[HALF:, : TXT.d] = block[...]
    urgent[HALF:, TXT.d :] = jnp.zeros((16, IMG.d - TXT.d), BF)


def vector_pay_body(ids, vec, vecpay, shifted):
    odd = ids[3] % 2

    @pl.when(odd == 0)
    def _():
        vecpay[...] = vec[...].astype(BF)

    @pl.when(odd == 1)
    def _():
        rolled = pltpu.roll(vec[...], 64, 1)
        shifted[0:8, :] = jnp.zeros((8, 128), F32)
        shifted[8 : 8 + VEC_ROWS, :] = rolled
        before = shifted[7 : 7 + VEC_ROWS, :]
        low_lanes = lax.broadcasted_iota(jnp.int32, (VEC_ROWS, 128), 1) < 64
        vecpay[...] = jnp.where(low_lanes, before, rolled).astype(BF)


def with_halves(blocks, side, z, shard, use):
    if len(blocks) == 2:
        rows = blocks[0].shape[0] // ZN
        mine, other = [block.at[pl.ds(shard * rows, rows)] for block in blocks]
        pl.when(side == 0)(lambda: use(mine, other))
        pl.when(side != 0)(lambda: use(other, mine))
        return
    for k in range(ZN):
        mine, other = blocks[k], blocks[ZN + k]
        here = (z ^ shard) == k
        pl.when(here & (side == 0))(functools.partial(use, mine, other))
        pl.when(here & (side != 0))(functools.partial(use, other, mine))


def half_rows(tower, first, second):
    if tower is IMG:
        return jnp.concatenate([first[: IMG.half, :], second[: IMG.half, :]], axis=0)
    parts = []
    for half in (first, second):
        parts += [
            half[IMG.half : HALF, : TXT.d],
            half[IMG.half : IMG.half + 32, TXT.d :],
            half[IMG.half + 32 : HALF, TXT.d :],
        ]
    return jnp.concatenate(
        [
            parts[0],
            jnp.concatenate([parts[1], parts[2]], axis=1),
            parts[3],
            jnp.concatenate([parts[4], parts[5]], axis=1),
        ],
        axis=0,
    )


def attention_mask(tower):
    shape = (tower.tile, tower.tile)
    row = lax.broadcasted_iota(jnp.int32, shape, 0)
    column = lax.broadcasted_iota(jnp.int32, shape, 1)
    if tower.causal:
        return (column <= row) & (column < tower.length)
    pad = tower.padded
    first = (row < pad) & (column < tower.length)
    second = (row >= pad) & (column >= pad) & (column < pad + tower.length)
    return first | second


def read_meta(meta, blocks, side, z):
    for place in range(ZN):

        def use(*halves, place=place):
            for half, block in enumerate(halves):
                lines = block[HALF:, 384:512].astype(F32)
                line = half * ZN + place
                meta[line : line + 1, :] = lines[12:13]
                meta[8 + line : 9 + line, :] = lines[13:14]

        with_halves(blocks, side, z, place, use)


def attend_body(tower, ids, x, *rest):
    count = 2 * ZN
    blocks, rest = rest[:count], rest[count:]
    if tower is TXT:
        (norms, meta, wq, wo, up, h1, u1, qkv, att, probs, xo, own, s1, s2, s3, xf, xs) = rest
    else:
        norms = rest[0]
        (wq, wo, up, h1, u1, qkv, att, probs, xo, own, s1, s2, s3, xf, xs) = rest[1:]
    side, z, m = ids[0], ids[1], ids[2]
    d, w, sr = tower.d, tower.w, tower.sr
    if tower is TXT:

        def read_norms(block, _):
            for j in range(4):
                norms[16 * j : 16 * (j + 1), :] = block[HALF:, 128 * j : 128 * (j + 1)].astype(F32)

        with_halves(blocks, side, z, 0, read_norms)
        read_meta(meta, blocks, side, z)

    tail = d // 8
    for s in range(2):

        def read_qkv(first, second, base=s * (d // 2)):
            part = half_rows(tower, first, second)
            wq[base : base + sr, :] = part[:, : 3 * w]
            wq[base + sr : base + sr + tail, :] = jnp.concatenate(
                [part[tail * i : tail * (i + 1), 3 * w :] for i in range(3)], axis=1
            )

        with_halves(blocks, side, z, s, read_qkv)

    def read_out(first, second):
        part = half_rows(tower, first, second)
        wo[...] = part[:w]
        up[:tail, :] = part[w:]

    def read_up(first, second):
        up[tail:, :] = half_rows(tower, first, second)

    with_halves(blocks, side, z, 2, read_out)
    with_halves(blocks, side, z, 3, read_up)
    for j in range(tower.q):
        xf[j] = x[:, :, 128 * j : 128 * (j + 1)].astype(F32).reshape(tower.length * SEQS, 128)
    pad = tower.padded - tower.length
    for k in range(MP):
        for j in range(2):
            start = k * tower.rows + j * tower.padded
            seq = 2 * (m ^ k) + j
            for i in range(tower.q):
                xs[start : start + tower.length, 128 * i : 128 * (i + 1)] = xf.at[i][
                    pl.ds(seq, tower.length, stride=SEQS), :
                ]
            xs[start + tower.length : start + tower.padded, :] = jnp.zeros((pad, d), F32)
    xo[...] = xs[: tower.rows, :]
    unit_rows, _ = unit(xs[...])
    u1[...] = unit_rows.astype(BF)
    h1[...] = (
        unit_rows * norm_vector(norms, tower, 0) + norm_vector(norms, tower, 1)
    ).astype(BF)
    qkv[...] = dot(h1[...], wq[...]).astype(BF)
    allowed = attention_mask(tower)
    targets = (own, s1, s2, s3)
    for k in range(MP):
        for tile in range(tower.tiles):
            start = k * tower.rows + tile * tower.tile
            rows = slice(start, start + tower.tile)
            heads = []
            for h in range(tower.heads):
                query = qkv[rows, h * HEAD : (h + 1) * HEAD]
                key = qkv[rows, w + h * HEAD : w + (h + 1) * HEAD]
                value = qkv[rows, 2 * w + h * HEAD : 2 * w + (h + 1) * HEAD]
                scores = jnp.where(allowed, dot_nt(query, key) * HEAD ** (-0.5), MASK_LOW)
                exponent = jnp.exp(scores - jnp.max(scores, axis=-1, keepdims=True))
                prob = exponent / jnp.sum(exponent, axis=-1, keepdims=True)
                probs[(k * tower.tiles + tile) * tower.heads + h] = prob
                heads.append(dot(prob.astype(BF), value))
            att[rows, :] = jnp.concatenate(heads, axis=1).astype(BF)
        rows = slice(k * tower.rows, (k + 1) * tower.rows)
        part = dot(att[rows, :], wo[...])
        targets[k][...] = part.astype(targets[k].dtype)


def attend_call(tower, ids, x, blocks, norms=None, after=()):
    d, w, rows, every = tower.d, tower.w, tower.rows, tower.all_rows
    outs = [
        out((d, 3 * w), BF),
        out((w, d), BF),
        out((d // 2, d), BF),
        out((every, d), BF),
        out((every, d), BF),
        out((every, 3 * w), BF),
        out((every, w), BF),
        out((MP * tower.tiles * tower.heads, tower.tile, tower.tile)),
        out((rows, d)),
        out((rows, d)),
        out((rows, d), BF),
        out((rows, d), BF),
        out((rows, d), BF),
    ]
    ins = [ids, x] + blocks
    if tower is TXT:
        outs = [out((64, 128)), out((16, 128))] + outs
    else:
        ins.append(norms)
    return kernel_call(
        functools.partial(attend_body, tower),
        outs,
        ins,
        [
            pltpu.VMEM((tower.q, tower.length * SEQS, 128), F32),
            pltpu.VMEM((every, d), F32),
        ],
        after=after,
        us=7.2,
    )


def row_mask(tower, lengths, pair):
    position = lax.broadcasted_iota(jnp.int32, (tower.padded, 1), 0)
    count = lengths[pair] if tower.causal else tower.length
    return position < count, count


def middle_body(tower, ids, lengths, norms, xo, own, r1, r2, r3, x1, h2, pooled):
    m = ids[2]
    total = xo[...] + ((own[...] + r1[...].astype(F32)) + (r2[...].astype(F32) + r3[...].astype(F32)))
    x1[...] = total
    unit_rows, _ = unit(total)
    h2[...] = (
        unit_rows * norm_vector(norms, tower, 2) + norm_vector(norms, tower, 3)
    ).astype(BF)
    for j in range(2):
        inside, count = row_mask(tower, lengths, 2 * m + j)
        part = total[j * tower.padded : (j + 1) * tower.padded]
        summed = jnp.sum(jnp.where(inside, part, 0.0), axis=0, keepdims=True)
        pooled[j : j + 1, :] = summed / jnp.full((1, 1), count, F32)


def middle_call(tower, ids, lengths, norms, xo, own, received, after=()):
    rows, d = tower.rows, tower.d
    return kernel_call(
        functools.partial(middle_body, tower),
        [out((rows, d)), out((rows, d), BF), out((2, d))],
        [ids, lengths, norms, xo, own] + received,
        after=after,
    )


def feed_body(tower, ids, lengths, h_own, h1, h2, h3, *rest):
    up, late, rest = rest[0], rest[1:3], rest[3:]
    if tower is TXT:
        pooled, w1, w2, slope, sums, *y_out = rest
    else:
        pooled, *y_txt, sums_txt, w1, w2, slope, sums, y0, y1, y2, y3 = rest
        y_out = (y0, y1, y2, y3)
    side, z, m = ids[0], ids[1], ids[2]
    d, w, sr = tower.d, tower.w, tower.sr
    tail = d // 8

    def read(target, start, skip, count):
        def use(first, second):
            part = half_rows(tower, first, second)
            target[start : start + count, :] = part[skip : skip + count]

        return use

    def read_both(first, second):
        part = half_rows(tower, first, second)
        w1[tail + 2 * sr :, :] = part[:tail]
        w2[:w, :] = part[tail:]

    w1[: d // 2, :] = up[...]
    with_halves(late, side, z, 0, read(w1, tail + sr, 0, sr))
    with_halves(late, side, z, 1, read_both)
    with_halves(late, side, z, 2, read(w2, w, 0, sr))
    with_halves(late, side, z, 3, read(w2, w + sr, 0, sr))
    sums_places, y_places = [], []
    for k, block in enumerate((h_own, h1, h2, h3)):
        pre = dot(block[...], w1[...])
        gate = jax.nn.sigmoid(GELU_SLOPE * pre)
        acted = (pre * gate).astype(BF).astype(F32)
        slope[k * tower.rows : (k + 1) * tower.rows, :] = gate + GELU_SLOPE * pre * gate * (
            1.0 - gate
        )
        summed = []
        counts = []
        for j in range(2):
            inside, count = row_mask(tower, lengths, 2 * (m ^ k) + j)
            part = acted[j * tower.padded : (j + 1) * tower.padded]
            summed.append(jnp.sum(jnp.where(inside, part, 0.0), axis=0, keepdims=True))
            counts.append(jnp.full((1, 1), count, F32))
        both = jnp.concatenate(summed, axis=0)
        sums_places.append(both)
        high, low, rest = pieces(both, 3)
        y = dot(high, w2[...]) + (dot(low, w2[...]) + dot(rest, w2[...]))
        y = y / jnp.concatenate(counts, axis=0)
        if k == 0:
            y = y + pooled[...]
        y_places.append(y)

    def in_order(places):
        def chunk(c):
            value = places[c ^ 3]
            for member in range(3):
                value = jnp.where(m == member, places[c ^ member], value)
            return value

        return jnp.concatenate([chunk(c) for c in range(MP)], axis=0)

    ordered = in_order(sums_places)
    if tower is TXT:
        sums[...] = ordered
        for target, value in zip(y_out, y_places):
            target[...] = value
        return
    for target, value, other in zip(y_out, y_places, y_txt):
        target[:, :d] = value
        target[:, d:] = other[...]
    sums[:, :d] = ordered
    sums[:, d:] = sums_txt[...]


def feed_call(tower, ids, lengths, blocks, up, late, pooled, before=()):
    d = tower.d
    wide = d if tower is TXT else D_IMG + D_TXT
    return kernel_call(
        functools.partial(feed_body, tower),
        [
            out((d, d), BF),
            out((d, d), BF),
            out((tower.all_rows, d)),
            out((SEQS, wide)),
        ]
        + [out((2, wide))] * MP,
        [ids, lengths] + blocks + [up] + late + [pooled] + list(before),
        us=6.4,
    )


def project_body(gathered, pi, pt, flat):
    for e in range(4):
        base = e * (2 * VEC_ROWS - 1)
        flat[base : base + VEC_ROWS, :] = gathered[2 * e].astype(F32)
        odd = gathered[2 * e + 1].astype(F32)
        row = base + VEC_ROWS - 1
        flat[row : row + 1, :] = flat[row : row + 1, :] + odd[:1]
        flat[row + 1 : row + VEC_ROWS, :] = odd[1:]
    for j in range(4):
        pi[:, 128 * j : 128 * (j + 1)] = flat[pl.ds(NORM_ROWS + j, D_IMG, stride=4), :].astype(BF)
        pt[:, 128 * j : 128 * (j + 1)] = flat[
            pl.ds(NORM_ROWS + 4 * D_IMG + j, D_TXT, stride=4), :
        ].astype(BF)


def project_call(gathered, after):
    return kernel_call(
        project_body,
        [out((D_IMG, EMBED), BF), out((D_TXT, EMBED), BF)],
        [gathered],
        [pltpu.VMEM((4 * (2 * VEC_ROWS - 1) + 4, 128), F32)],
        us=2.8,
        after=after,
    )


def head_body(
    ids, trio, parts, norms, meta, pi, pt,
    misc, dyb_i, dyb_t, own_i, own_t, window, pg_i, pg_t, ng_i, ng_t, scr_i, scr_t, yall, flat,
):
    shard = ids[3]
    total = yall.shape[0]
    for i in range(parts.shape[0]):
        yall[2 * i : 2 * i + 2, :] = parts[i]
    row = lax.broadcasted_iota(jnp.int32, (total, total), 0)
    column = lax.broadcasted_iota(jnp.int32, (total, total), 1)
    eye = row == column
    place = lax.broadcasted_iota(jnp.int32, (total, 128), 0)
    lane = lax.broadcasted_iota(jnp.int32, (total, 128), 1)

    def column_of(first):
        picked = jnp.zeros((total, 128), F32)
        for s in range(2 * ZN):
            picked = jnp.where(place // SEQS == s, meta[first + s : first + s + 1, :], picked)
        return jnp.sum(jnp.where(lane == place % SEQS, picked, 0.0), axis=1, keepdims=True)

    flag_column = column_of(0)
    length_column = column_of(8)
    flag_row = jnp.sum(jnp.where(eye, flag_column, 0.0), axis=0, keepdims=True)
    row_valid = flag_column > 0.5
    column_valid = flag_row > 0.5
    count = jnp.sum(flag_column, axis=0, keepdims=True)

    def forward(tower, values, projection):
        unit_rows, inverse = unit(values)
        z = (
            unit_rows * norm_vector(norms, tower, 4) + norm_vector(norms, tower, 5)
        ).astype(BF)
        raw = dot(z, projection[...])
        scale = lax.rsqrt(jnp.sum(raw * raw, axis=-1, keepdims=True) + UNIT_EPS)
        quotient = raw * scale
        return unit_rows, inverse, z, scale, quotient, quotient.astype(BF)

    image = forward(IMG, yall[:, :D_IMG], pi)
    text = forward(TXT, yall[:, D_IMG:], pt)
    factor = jnp.exp(jnp.full((1, 1), trio[0], F32))
    e_image, e_text = image[5], text[5]

    def side(mine, others):
        logits = factor * dot_nt(mine, others)
        masked = jnp.where(column_valid, logits, MASK_LOW)
        top = jnp.max(masked, axis=1, keepdims=True)
        exponent = jnp.exp(masked - top)
        totals = jnp.sum(exponent, axis=1, keepdims=True)
        own = jnp.sum(jnp.where(eye, logits, 0.0), axis=1, keepdims=True)
        loss = jnp.sum(
            jnp.where(row_valid, top + jnp.log(totals) - own, 0.0), axis=0, keepdims=True
        )
        grad = jnp.where(row_valid, exponent / totals - eye.astype(F32), 0.0) / (2.0 * count)
        scale_part = jnp.sum(jnp.sum(grad * logits, axis=1, keepdims=True), axis=0, keepdims=True)
        return loss, grad, scale_part

    loss_i, grad_i, part_i = side(e_image, e_text)
    loss_t, grad_t, part_t = side(e_text, e_image)
    loss = (loss_i + loss_t) / (2.0 * count)
    slope = part_i + part_t
    misc[...] = jnp.concatenate(
        [
            jnp.broadcast_to(loss, (1, 128)),
            jnp.broadcast_to(slope, (1, 128)),
            jnp.zeros((6, 128), F32),
        ],
        axis=0,
    )

    def product(grad, back, others):
        sums = None
        for part in pieces(grad, 3):
            term = dot(part, others)
            sums = term if sums is None else sums + term
        for part in pieces(back, 3):
            sums = sums + dot_tn(part, others)
        return factor * sums

    def backward(tower, stored, embed_grad, projection, counts, pg, ng, dyb, scratch, own):
        unit_rows, inverse, z, scale, quotient, _ = stored
        raw_grad = (
            scale
            * (embed_grad - quotient * jnp.sum(embed_grad * quotient, axis=-1, keepdims=True))
        ).astype(BF)
        pg[...] = dot_tn(z, raw_grad)
        normed_grad = dot_nt(raw_grad, projection[...])
        ng[0:1, :] = jnp.sum(normed_grad * unit_rows, axis=0, keepdims=True)
        ng[1:2, :] = jnp.sum(normed_grad, axis=0, keepdims=True)
        grad = unit_back(normed_grad, unit_rows, inverse, norm_vector(norms, tower, 4)) / counts
        dyb[...] = grad.astype(BF)
        scratch[...] = grad
        rows = scratch[pl.ds(pl.multiple_of(shard * SEQS, 8), SEQS), :]
        for c in range(MP):
            own[c] = rows[2 * c : 2 * c + 2]

    grad_image = product(grad_i, grad_t, e_text)
    grad_text = product(grad_t, grad_i, e_image)
    backward(
        TXT, text, grad_text, pt, length_column, pg_t, ng_t, dyb_t, scr_t, own_t
    )
    backward(
        IMG, image, grad_image, pi, jnp.full((1, 1), float(IMG_LEN), F32),
        pg_i, ng_i, dyb_i, scr_i, own_i,
    )
    vector_body(ids, pg_i, pg_t, ng_i, ng_t, window, flat)


def head_call(ids, trio, parts, norms, meta, pi, pt):
    total = 2 * parts.shape[0]
    return kernel_call(
        head_body,
        [
            out((8, 128)),
            out((total, D_IMG), BF),
            out((total, D_TXT), BF),
            out((MP, 2, D_IMG)),
            out((MP, 2, D_TXT)),
            out((VEC_ROWS, 128)),
        ],
        [ids, trio, parts, norms, meta, pi, pt],
        [
            pltpu.VMEM((D_IMG, EMBED), F32),
            pltpu.VMEM((D_TXT, EMBED), F32),
            pltpu.VMEM((2, D_IMG), F32),
            pltpu.VMEM((2, D_TXT), F32),
            pltpu.VMEM((total, D_IMG), F32),
            pltpu.VMEM((total, D_TXT), F32),
            pltpu.VMEM((total, D_IMG + D_TXT), F32),
            pltpu.VMEM((4 * (2 * VEC_ROWS - 1) + 12, 128), F32),
        ],
        us=5.0,
    )


def feed_back_body(
    tower, ids, lengths, h_own, h1, h2, h3, slope, dy, w1, w2, *rest
):
    if tower is TXT:
        grad_i, own, s1, s2, s3, payload, h_all, du = rest
    else:
        own, s1, s2, s3, grads, h_all, du = rest
    m = ids[2]
    rows, pad = tower.rows, tower.padded
    for k, block in enumerate((h_own, h1, h2, h3)):
        h_all[k * rows : (k + 1) * rows, :] = block[...]
    dy_rows = jnp.concatenate([dy[m ^ k] for k in range(MP)], axis=0).astype(BF)
    act = dot_nt(dy_rows, w2[...])
    targets = (own, s1, s2, s3)
    for k in range(MP):
        for j in range(2):
            inside, _ = row_mask(tower, lengths, 2 * (m ^ k) + j)
            start = k * rows + j * pad
            place = 2 * k + j
            piece = slope[start : start + pad, :] * act[place : place + 1, :]
            du[start : start + pad, :] = jnp.where(inside, piece, 0.0).astype(BF)
        part = dot_nt(du[k * rows : (k + 1) * rows, :], w1[...])
        targets[k][...] = part.astype(targets[k].dtype)
    grad = dot_tn(h_all[...], du[...]).astype(BF)
    if tower is IMG:
        grads[...] = grad
        return
    rows_i, rows_t = IMG.d // 8, TXT.d // 8
    for place, e in enumerate(FEED_ORDER):
        payload[place, :rows_i, :] = grad_i[rows_i * e : rows_i * (e + 1), :]
        pack_eighth(payload.at[place], rows_i, grad[rows_t * e : rows_t * (e + 1)])


def feed_back_call(tower, ids, lengths, blocks, slope, dy, w1, w2, grads, after=()):
    rows, d, every = tower.rows, tower.d, tower.all_rows
    return kernel_call(
        functools.partial(feed_back_body, tower),
        [
            out((rows, d)),
            out((rows, d), BF),
            out((rows, d), BF),
            out((rows, d), BF),
            out((d, d), BF) if tower is IMG else out((2 * ZN, FEED_ROWS, IMG.d), BF),
        ],
        [ids, lengths] + blocks + [slope, dy, w1, w2] + grads,
        [pltpu.VMEM((every, d), BF), pltpu.VMEM((every, d), BF)],
        after=after,
        us=5.3,
    )


def middle_back_body(tower, ids, lengths, norms, x1, dy, own, r1, r2, r3, dx1, dx1b):
    m = ids[2]
    grad = (own[...] + r1[...].astype(F32)) + (r2[...].astype(F32) + r3[...].astype(F32))
    unit_rows, inverse = unit(x1[...])
    extra = (
        jnp.sum(grad * unit_rows, axis=0, keepdims=True),
        jnp.sum(grad, axis=0, keepdims=True),
    )
    back = unit_back(grad, unit_rows, inverse, norm_vector(norms, tower, 2))
    rows = dy[m]
    position = lax.broadcasted_iota(jnp.int32, (tower.padded, 1), 0)
    for j in range(2):
        inside, _ = row_mask(tower, lengths, 2 * m + j)
        part = slice(j * tower.padded, (j + 1) * tower.padded)
        total = back[part] + jnp.where(inside, rows[j : j + 1, :], 0.0)
        dx1[part, :] = total
        high, low = [piece.astype(F32) for piece in pieces(extra[j], 2)]
        total = jnp.where(position == tower.length, high, total)
        total = jnp.where(position == tower.length + 1, low, total)
        dx1b[part, :] = total.astype(BF)


def middle_back_call(tower, ids, lengths, norms, x1, dy, own, received, after=()):
    rows, d = tower.rows, tower.d
    return kernel_call(
        functools.partial(middle_back_body, tower),
        [out((rows, d)), out((rows, d), BF)],
        [ids, lengths, norms, x1, dy, own] + received,
        after=after,
    )


def attend_back_body(
    tower, ids, d_own, d1, d2, d3, att, qkv, probs, h1, u1, wq, wo,
    own, s1, s2, s3, *rest
):
    keep, sent, sums, d_all, dqkv, wide, backs, grads = rest
    rows, d, w, sr = tower.rows, tower.d, tower.w, tower.sr
    tail = d // 8
    position = lax.broadcasted_iota(jnp.int32, (tower.padded, 1), 0)
    extra = [[], []]
    for k, block in enumerate((d_own, d1, d2, d3)):
        for j in range(2):
            start = j * tower.padded
            part = block[start : start + tower.padded, :].astype(F32)
            line = tower.length
            extra[j].append(part[line : line + 1] + part[line + 1 : line + 2])
            d_all[k * rows + start : k * rows + start + tower.padded, :] = jnp.where(
                position < line, part, 0.0
            ).astype(BF)
    for j in range(2):
        sums[j : j + 1, :] = (extra[j][0] + extra[j][1]) + (extra[j][2] + extra[j][3])
    targets = (own, s1, s2, s3)
    gain = jnp.zeros((1, d), F32)
    shift = jnp.zeros((1, d), F32)
    for k in range(MP):
        span = slice(k * rows, (k + 1) * rows)
        d_att = dot_nt(d_all[span, :], wo[...]).astype(BF)
        for tile in range(tower.tiles):
            start = k * rows + tile * tower.tile
            part = slice(start, start + tower.tile)
            queries, keys, values = [], [], []
            for h in range(tower.heads):
                query = qkv[part, h * HEAD : (h + 1) * HEAD]
                key = qkv[part, w + h * HEAD : w + (h + 1) * HEAD]
                value = qkv[part, 2 * w + h * HEAD : 2 * w + (h + 1) * HEAD]
                grad = d_att[
                    tile * tower.tile : (tile + 1) * tower.tile, h * HEAD : (h + 1) * HEAD
                ]
                prob = probs[(k * tower.tiles + tile) * tower.heads + h]
                values.append(dot_tn(prob.astype(BF), grad))
                prob_grad = dot_nt(grad, value)
                score = (
                    prob * (prob_grad - jnp.sum(prob * prob_grad, axis=-1, keepdims=True))
                ).astype(BF)
                queries.append(dot(score, key) * HEAD ** (-0.5))
                keys.append(dot_tn(score, query) * HEAD ** (-0.5))
            dqkv[part, :] = jnp.concatenate(queries + keys + values, axis=1).astype(BF)
        back = dot_nt(dqkv[span, :], wq[...])
        gain = gain + jnp.sum(back * u1[span, :].astype(F32), axis=0, keepdims=True)
        shift = shift + jnp.sum(back, axis=0, keepdims=True)
        backs[k, :, :] = back
    for k in range(MP):
        for j, value in enumerate((gain, shift)):
            start = j * tower.padded
            part = backs[k, start : start + tower.padded, :]
            high, low = [piece.astype(F32) for piece in pieces(value, 2)]
            part = jnp.where(position == tower.length, high, part)
            part = jnp.where(position == tower.length + 1, low, part)
            targets[k][start : start + tower.padded, :] = part.astype(targets[k].dtype)
    wide[...] = dot_tn(h1[...], dqkv[...]).astype(BF)
    out_grad = dot_tn(att[...], d_all[...]).astype(BF)
    for place, e in enumerate(WIDE_ORDER):
        if e >= 6:
            piece = out_grad[(e - 6) * tail : (e - 5) * tail]
        else:
            s, i = e // 3, e % 3
            base = s * (d // 2)
            rest = wide[base + sr : base + sr + tail, w * i : w * (i + 1)]
            piece = jnp.concatenate(
                [wide[base + i * tail : base + (i + 1) * tail, :], rest], axis=1
            )
        grads[place] = piece
    for z in range(ZN):
        keep[z] = grads[ids[0] * ZN + z]
        sent[z] = grads[(1 - ids[0]) * ZN + z]


def attend_back_call(tower, ids, blocks, att, qkv, probs, h1, u1, wq, wo, after=()):
    rows, d, w, every = tower.rows, tower.d, tower.w, tower.all_rows
    return kernel_call(
        functools.partial(attend_back_body, tower),
        [
            out((rows, d)),
            out((rows, d), BF),
            out((rows, d), BF),
            out((rows, d), BF),
            out((ZN, d // 8, d), BF),
            out((ZN, d // 8, d), BF),
            out((2, d)),
        ],
        [ids] + blocks + [att, qkv, probs, h1, u1, wq, wo],
        [
            pltpu.VMEM((every, d), BF),
            pltpu.VMEM((every, 3 * w), BF),
            pltpu.VMEM((d, 3 * w), BF),
            pltpu.VMEM((MP, rows, d), F32),
            pltpu.VMEM((2 * ZN, d // 8, d), BF),
        ],
        after=after,
        us=10.4,
    )


def entry_body(tower, norms, xo, dx1, second, own, r1, r2, r3, *rest):
    if tower is IMG:
        dx, sums = rest
    else:
        dx_i, payload, sums = rest
    grad = (own[...] + r1[...].astype(F32)) + (r2[...].astype(F32) + r3[...].astype(F32))
    line = tower.length
    sums[0:1, :] = grad[line : line + 1] + grad[line + 1 : line + 2]
    line += tower.padded
    sums[1:2, :] = grad[line : line + 1] + grad[line + 1 : line + 2]
    sums[2:4, :] = second[...]
    unit_rows, inverse = unit(xo[...])
    back = unit_back(grad, unit_rows, inverse, norm_vector(norms, tower, 0))
    result = (dx1[...] + back).astype(BF)
    if tower is IMG:
        dx[...] = result
        return
    top = IMG.rows
    rest = TXT.rows - top
    payload[:top, :] = dx_i[...]
    payload[top:, : TXT.d] = result[:top]
    payload[top : top + rest, TXT.d :] = result[top:, :256]
    payload[top + rest : top + 2 * rest, TXT.d :] = result[top:, 256:]
    payload[top + 2 * rest :, TXT.d :] = jnp.zeros((top - 2 * rest, IMG.d - TXT.d), BF)


def entry_call(tower, norms, xo, dx1, second, own, received, before=(), after=()):
    rows, d = tower.rows, tower.d
    return kernel_call(
        functools.partial(entry_body, tower),
        [out((rows, d), BF) if tower is IMG else out((2 * IMG.rows, IMG.d), BF), out((4, d))],
        [norms, xo, dx1, second, own] + received + list(before),
        after=after,
    )


def place_body(tower, ids, own, r1, r2, r3, result, flat):
    m = ids[2]
    top = IMG.rows
    rest = TXT.rows - top
    for k, block in enumerate((own, r1, r2, r3)):
        if tower is IMG:
            rows = block[:top, :].astype(F32)
        else:
            low = jnp.concatenate(
                [
                    block[top : top + rest, TXT.d :],
                    block[top + rest : top + 2 * rest, TXT.d :],
                ],
                axis=1,
            )
            rows = jnp.concatenate([block[top:, : TXT.d], low], axis=0).astype(F32)
        for j in range(2):
            seq = 2 * (m ^ k) + j
            part = rows[j * tower.padded : j * tower.padded + tower.length]
            for i in range(tower.q):
                flat.at[i][pl.ds(seq, tower.length, stride=SEQS), :] = part[
                    :, 128 * i : 128 * (i + 1)
                ]
    for i in range(tower.q):
        result[:, :, 128 * i : 128 * (i + 1)] = flat[i].reshape(tower.length, SEQS, 128)


def place_call(tower, ids, blocks):
    return kernel_call(
        functools.partial(place_body, tower),
        [out((tower.length, SEQS, tower.d))],
        [ids] + blocks,
        [pltpu.VMEM((tower.q, tower.length * SEQS, 128), F32)],
        vmem=PLACE_VMEM,
        us=2.7,
    )[0]


def pack_eighth(target, start, part):
    target[start : start + 48, : TXT.d] = part[:48]
    target[start : start + 16, TXT.d :] = part[48:, :256]
    target[start + 16 : start + 32, TXT.d :] = part[48:, 256:]
    target[start + 32 : start + 48, TXT.d :] = jnp.zeros((16, IMG.d - TXT.d), BF)


def pair_body(keep_i, got_i, keep_t, got_t, payload):
    top = IMG.d // 8
    for z in range(ZN):
        payload[z, :top, :] = (keep_i[z].astype(F32) + got_i[z].astype(F32)).astype(BF)
        total = (keep_t[z].astype(F32) + got_t[z].astype(F32)).astype(BF)
        pack_eighth(payload.at[z], top, total)


def mix_body(ids, feed, got, wide, first, second):
    shard = ids[3]
    part = [got[z].astype(F32) for z in range(ZN)]
    wide[...] = ((part[0] + part[1]) + (part[2] + part[3])).astype(BF)
    for target, (senders, _) in zip((first, second), MOVES):
        passes = (shard == senders[0]) | (shard == senders[1])

        def copy(source, target=target):
            target[...] = source[...]

        pl.when(passes)(functools.partial(copy, feed))
        pl.when(jnp.logical_not(passes))(functools.partial(copy, wide))


def mix_call(ids, feed, got):
    return kernel_call(mix_body, [out((FEED_ROWS, IMG.d), BF)] * 3, [ids, feed, got], us=2.5)


def down_body(tower, ids, b0, b1, b2, b3, b4, b5, b6, b7, dyb, result, wide, sums):
    d = tower.d
    tail = d // 8
    first = 0 if tower is IMG else D_IMG
    for k, block in enumerate((b0, b1, b2, b3, b4, b5, b6, b7)):
        side = ids[0] if k < ZN else 1 - ids[0]
        start = (side * ZN + (ids[1] ^ (k % ZN))) * SEQS
        sums[pl.ds(pl.multiple_of(start, SEQS), SEQS), :] = block[:, first : first + d]
    high, low = pieces(sums[...], 2)
    wide[:tail, :] = jnp.zeros((tail, d), F32)
    wide[tail:, :] = dot_tn(high, dyb[...]) + dot_tn(low, dyb[...])
    start = jnp.maximum(ids[3] - 5, 0) * tower.sr
    result[...] = wide[pl.ds(pl.multiple_of(start, 8), tower.sr), :]


def down_call(tower, ids, sums, dyb):
    d = tower.d
    return kernel_call(
        functools.partial(down_body, tower),
        [out((tower.sr, d))],
        [ids] + sums + [dyb],
        [pltpu.VMEM((d + d // 8, d), F32), pltpu.VMEM((2 * ZN * SEQS, d), F32)],
        us=2.6,
    )[0]


def vector_body(ids, pg_i, pg_t, ng_i, ng_t, window, flat):
    flat[:64, :] = jnp.zeros((64, 128), F32)
    for tower, sums in ((IMG, ng_i), (TXT, ng_t)):
        for i in range(2):
            start = tower.norm_row + (4 + i) * tower.q
            for j in range(tower.q):
                flat[start + j : start + j + 1, :] = sums[i : i + 1, 128 * j : 128 * (j + 1)]
    for j in range(4):
        flat[pl.ds(NORM_ROWS + j, D_IMG, stride=4), :] = pg_i[:, 128 * j : 128 * (j + 1)]
        flat[pl.ds(NORM_ROWS + 4 * D_IMG + j, D_TXT, stride=4), :] = pg_t[
            :, 128 * j : 128 * (j + 1)
        ]
    low_lanes = lax.broadcasted_iota(jnp.int32, (VEC_ROWS, 128), 1) < 64
    last = lax.broadcasted_iota(jnp.int32, (VEC_ROWS, 128), 0) == VEC_ROWS - 1
    for s in range(8):

        def copy(s=s):
            start = (s * (2 * VEC_ROWS - 1)) // 2
            part = flat[start : start + VEC_ROWS, :]
            if s % 2 == 1:
                after = pltpu.roll(flat[start + 1 : start + 1 + VEC_ROWS, :], 64, 1)
                part = jnp.where(low_lanes, pltpu.roll(part, 64, 1), after)
            window[...] = jnp.where(last & jnp.logical_not(low_lanes), 0.0, part)

        pl.when(ids[3] == s)(copy)


def collect_body(
    ids, f_own, w_own, ra, rb, down_i, down_t, window,
    sums_i, sums_t, lin_i, lin_t, message, rows_i, rows_t, spare,
):
    shard = ids[3]
    q = IMG.d // 8

    @pl.when(shard >= 5)
    def _():
        rows_i[...] = down_i[...]
        rows_t[...] = down_t[...]

    tq = TXT.d // 8

    def feed(start, *blocks):
        for i, block in enumerate(blocks):
            rows_i[q * (start + i) : q * (start + i + 1), :] = block[:q, :].astype(F32)
            low = jnp.concatenate([block[q : q + 16, TXT.d :], block[q + 16 : q + 32, TXT.d :]], axis=1)
            part = jnp.concatenate([block[q:, : TXT.d], low], axis=0)
            rows_t[tq * (start + i) : tq * (start + i + 1), :] = part.astype(F32)

    pl.when(shard < 2)(lambda: feed(0, w_own, ra, rb))
    pl.when(shard == 2)(lambda: feed(0, w_own, ra, f_own))
    pl.when((shard == 3) | (shard == 4))(lambda: feed(0, f_own, ra, rb))
    pl.when(shard == 5)(lambda: feed(0, f_own))

    rows_to_lin(IMG, rows_i, lin_i, spare, shard)
    rows_to_lin(TXT, rows_t, lin_t, spare, shard)
    def total_of(value):
        return jnp.sum(value * value, axis=0, keepdims=True)

    every = total_of(window[...]) * (1.0 / MP)
    for j in range(IMG.q):
        every = every + total_of(rows_i[:, 128 * j : 128 * (j + 1)])
    for j in range(TXT.q):
        every = every + total_of(rows_t[:, 128 * j : 128 * (j + 1)])
    m = ids[2]

    def own_line(sums):
        line = sums[3:4, :]
        for member in range(3):
            line = jnp.where(m == member, sums[member : member + 1, :], line)
        return line

    line = jnp.concatenate([own_line(sums_i), own_line(sums_t)], axis=1)
    block = jnp.concatenate(
        [every] + [line[:, 128 * j : 128 * (j + 1)] for j in range(IMG.q + TXT.q)], axis=0
    )
    for peer in range(2 * ZN * MP):
        message[peer, : MESSAGE_ROWS, :] = block
        message[peer, MESSAGE_ROWS:, :] = jnp.zeros((16 - MESSAGE_ROWS, 128), F32)


MESSAGE_ROWS = 1 + IMG.q + TXT.q


def collect_call(ids, moved, down_i, down_t, window, sums_i, sums_t, after):
    return kernel_call(
        collect_body,
        [out((IMG.lin, 128)), out((TXT.lin, 128)), out((2 * ZN * MP, 16, 128))],
        [ids] + moved + [down_i, down_t, window, sums_i, sums_t],
        [
            pltpu.VMEM((IMG.sr, IMG.d), F32),
            pltpu.VMEM((TXT.sr, TXT.d), F32),
            pltpu.VMEM(SPARE, F32),
        ],
        us=3.8,
        after=after,
    )


def advance_body(
    ids, trio, parts, misc, ip, im, iv, ig, tp, tm, tv, tg, vp, vm, vv, vg,
    loss_out, size_out, trio_out, ipn, icn, imn, ivn, tpn, tcn, tmn, tvn, vpn, vcn, vmn, vvn, grad_v,
):
    slope = misc[1:2, :]
    grad_v[...] = vg[...]
    norm_squares = jnp.zeros((1, 128), F32)
    for member in range(MP):
        lines = parts[member]
        for group in range(1, 2 * ZN):
            lines = lines + parts[group * MP + member]
        if member == 0:
            squares = lines[:1]
        else:
            squares = squares + lines[:1]
        lines = lines[1:MESSAGE_ROWS]
        norm_squares = norm_squares + jnp.sum(lines * lines, axis=0, keepdims=True)

        @pl.when((ids[3] == 0) & (pl.program_id(0) == 0))
        def _(member=member, lines=lines):
            start = member * IMG.q
            grad_v[start : start + IMG.q, :] = lines[: IMG.q]
            start = TXT.norm_row + member * TXT.q
            grad_v[start : start + TXT.q, :] = lines[IMG.q :]

    total = jnp.sum(squares + norm_squares, axis=1, keepdims=True)
    size = jnp.sqrt(total + slope * slope)
    clip = CLIP_LEVEL / jnp.maximum(size, CLIP_LEVEL)

    def step(master, first, second, grad, rate, decay):
        clipped = grad * clip
        first_new = BETA_ONE * first + (1.0 - BETA_ONE) * clipped
        second_new = BETA_TWO * second + (1.0 - BETA_TWO) * clipped * clipped
        update = (first_new * (1.0 / (1.0 - BETA_ONE**STEP))) / (
            jnp.sqrt(second_new * (1.0 / (1.0 - BETA_TWO**STEP))) + ADAM_EPS
        )
        return master - rate * (update + decay * master), first_new, second_new

    for master, first, second, grad, a, b, c, e in (
        (ip, im, iv, ig, ipn, icn, imn, ivn),
        (tp, tm, tv, tg, tpn, tcn, tmn, tvn),
    ):
        new, first_new, second_new = step(
            master[...], first[...], second[...], grad[...], RATE_MATRIX, WEIGHT_DECAY
        )
        a[...] = new
        b[:, 0, :] = new.astype(BF)
        c[...] = first_new
        e[...] = second_new
    rows = VEC_ROWS // ADVANCE_STEPS
    row = lax.broadcasted_iota(jnp.int32, (rows, 128), 0) + pl.program_id(0) * rows
    is_norm = row < jnp.where(ids[3] == 0, NORM_ROWS, 0)
    new, first_new, second_new = step(
        vp[...],
        vm[...],
        vv[...],
        grad_v[...],
        jnp.where(is_norm, RATE_VECTOR, RATE_MATRIX),
        jnp.where(is_norm, 0.0, WEIGHT_DECAY),
    )
    vpn[...] = new
    vcn[...] = new.astype(BF)
    vmn[...] = first_new
    vvn[...] = second_new
    lane_row = jnp.zeros((1, 128), F32)
    new, _, _ = step(
        lane_row + trio[0], lane_row + trio[1], lane_row + trio[2], slope, LOGIT_SPEED, 0.0
    )
    loss_out[...] = misc[0:1, :1]
    size_out[...] = size[:, :1]
    trio_out[...] = new[:, :1]


PLACE_VMEM = 64
ADVANCE_STEPS = 3


def advance_call(ids, trio, parts, misc, image, text, vector):
    ins = [ids, trio, parts, misc] + image + text + vector

    def spec(shape, cut):
        block = (shape[0] // ADVANCE_STEPS if cut else shape[0],) + tuple(shape[1:])
        rest = (0,) * (len(shape) - 1)
        return pl.BlockSpec(block, lambda i: ((i if cut else 0),) + rest)

    outs = [out((1, 1))] * 3
    for rows in (IMG.lin, TXT.lin, VEC_ROWS):
        copied = (rows, 128) if rows == VEC_ROWS else (rows, 1, 128)
        outs += [out((rows, 128)), out(copied, BF), out((rows, 128)), out((rows, 128))]
    scalars = pl.BlockSpec(memory_space=pltpu.SMEM)
    return pl.pallas_call(
        advance_body,
        grid=(ADVANCE_STEPS,),
        out_shape=outs,
        in_specs=[scalars, scalars] + [spec(v.shape, i > 1) for i, v in enumerate(ins[2:])],
        out_specs=[spec(v.shape, i > 2) for i, v in enumerate(outs)],
        scratch_shapes=[pltpu.VMEM((VEC_ROWS // ADVANCE_STEPS, 128), F32)],
        compiler_params=pltpu.CompilerParams(vmem_limit_bytes=64 * MIB),
        cost_estimate=pl.CostEstimate(
            flops=int(COST_SCALE * 7), bytes_accessed=0, transcendentals=0
        ),
    )(*ins)


def hop(value, axis, mask):
    size = lax.axis_size(axis)
    return lax.ppermute(value, axis, [(i, i ^ mask) for i in range(size)])


def peers(values):
    return [hop(value, "mp", k) for k, value in zip((1, 2, 3), values)]


def spread(value):
    near, far = hop(value, "dp", 1), hop(value, "dp", 2)
    here = [value, near, far, hop(far, "dp", 1)]
    return here + [hop(block, "tower", 1) for block in here]


def merge(value, axis, mask):
    other = hop(value, axis, mask)
    upper = (lax.axis_index(axis) & mask) != 0
    return jnp.where(
        upper, jnp.concatenate([other, value], axis=0), jnp.concatenate([value, other], axis=0)
    )


FEED_ORDER = (5, 6, 0, 1, 4, 7, 3, 2)
WIDE_ORDER = (0, 3, 6, 5, 1, 4, 7, 2)
MOVES = (
    ((7, 0), ((7, 3), (0, 4), (4, 0), (5, 1), (6, 2))),
    ((6, 1), ((6, 3), (1, 4), (7, 0), (3, 1))),
)


def fast_local(
    picture_residual_entry,
    sentence_residual_entry,
    sentence_lengths_held,
    couple_allowed_flags,
    picture_single_matrices,
    picture_mean_state,
    picture_square_state,
    sentence_single_matrices,
    sentence_mean_state,
    sentence_square_state,
    array_single_params,
    array_mean_state,
    array_square_state,
    logit_log_trio,
):
    LAST.clear()
    side, z, m = lax.axis_index("tower"), lax.axis_index("dp"), lax.axis_index("mp")
    ids = jnp.stack([side, z, m, side * ZN + z]).astype(jnp.int32)
    lengths = sentence_lengths_held
    vec_size = array_single_params.shape[0]

    def lines(value):
        return value.reshape(-1, 128)

    def vector_lines(value):
        return jnp.pad(value, (0, VEC_ROWS * 128 - vec_size)).reshape(VEC_ROWS, 128)

    vec_lines = vector_lines(array_single_params)
    keep_t, keep_i, send_t, send_i, block = kernel_call(
        prepare_body,
        [out((TXT.half, TXT.d), BF), out((IMG.half, IMG.d), BF)] * 2 + [out((16, TXT.d), BF)],
        [
            ids,
            couple_allowed_flags,
            lengths,
            lines(picture_single_matrices),
            lines(sentence_single_matrices),
            vec_lines,
        ],
        [
            pltpu.VMEM((IMG.sr, IMG.d), F32),
            pltpu.VMEM((TXT.sr, TXT.d), F32),
            pltpu.VMEM(SPARE, F32),
        ],
        us=2.5,
    )
    urgent, late = kernel_call(
        sort_body,
        [out((URGENT, IMG.d), BF), out((HALF, IMG.d), BF)],
        [ids, keep_t, keep_i, hop(send_t, "tower", 1), hop(send_i, "tower", 1), block],
    )
    urgent = spread(urgent)
    late = lax.all_gather(gate(late, *urgent[1:ZN]), "dp", axis=0, tiled=True)
    vecpay = kernel_call(
        vector_pay_body,
        [out((VEC_ROWS, 128), BF)],
        [ids, vec_lines],
        [pltpu.VMEM((VEC_ROWS + 8, 128), F32)],
    )[0]
    x_txt = jnp.transpose(sentence_residual_entry, (1, 0, 2))
    x_img = jnp.transpose(picture_residual_entry, (1, 0, 2))
    norms, meta, *t_out = attend_call(TXT, ids, x_txt, urgent)
    i_out = attend_call(IMG, ids, x_img, urgent, norms=norms)
    layers = {}
    before = ()
    middles = {}
    for tower, outs in ((TXT, t_out), (IMG, i_out)):
        xo, own, s1, s2, s3 = outs[8:]
        x1, h2, pooled = middle_call(
            tower, ids, lengths, norms, xo, own, peers([s1, s2, s3])
        )
        middles[tower] = (x1, pooled, [h2] + peers([h2, h2, h2]))
    late = gate(late, x1, *middles[TXT][2][1:])
    late = [late, hop(late, "tower", 1)]
    gathered = lax.all_gather(gate(vecpay, late[0]), GROUP, axis=0, tiled=False)
    for tower, outs in ((TXT, t_out), (IMG, i_out)):
        wq, wo, up, h1, u1, qkv, att, probs, xo = outs[:9]
        x1, pooled, blocks = middles[tower]
        w1, w2, slope, sums, *y = feed_call(
            tower, ids, lengths, blocks, up, late, pooled, before
        )
        before = (*y, sums)
        layers[tower] = dict(
            wq=wq, wo=wo, h1=h1, u1=u1, qkv=qkv, att=att, probs=probs, xo=xo,
            x1=x1, blocks=blocks, w1=w1, w2=w2, slope=slope,
        )

    received = peers(y[1:])
    y = (y[0] + received[0]) + (received[1] + received[2])
    parts = lax.all_to_all(
        jnp.broadcast_to(y, (2 * ZN * MP, *y.shape)), (*GROUP, "mp"), 0, 0, tiled=True
    )
    sums = gate(sums, y)
    sums = [sums] + [hop(sums, "dp", k) for k in range(1, ZN)]
    pi, pt = project_call(gathered, ())
    sums = sums[:1] + [gate(block, pi) for block in sums[1:]]
    sums = sums + [hop(block, "tower", 1) for block in sums]
    misc, dyb_i, dyb_t, dy_i, dy_t, window = head_call(
        ids, logit_log_trio, parts, norms, meta, pi, pt
    )

    dy = {IMG: dy_i, TXT: dy_t}
    back, dx1, dx1b, second = {}, {}, {}, {}
    entries, norm_sums = {}, {}
    grads = []
    for tower in (IMG, TXT):
        s = layers[tower]
        back[tower] = feed_back_call(
            tower, ids, lengths, s["blocks"], s["slope"], dy[tower], s["w1"], s["w2"], grads,
            sums if tower is TXT else (),
        )
        grads = [back[tower][4]]
    feed_own = lax.psum_scatter(back[TXT][4], GROUP, scatter_dimension=0, tiled=False)
    for tower in (IMG, TXT):
        own, s1, s2, s3 = back[tower][:4]
        dx1[tower], dx1b[tower] = middle_back_call(
            tower, ids, lengths, norms, layers[tower]["x1"], dy[tower], own, peers([s1, s2, s3])
        )
    halves = []
    for tower in (IMG, TXT):
        s = layers[tower]
        block = dx1b[tower]
        *back[tower], keep, sent, second[tower] = attend_back_call(
            tower, ids, [block] + peers([block] * 3),
            s["att"], s["qkv"], s["probs"], s["h1"], s["u1"], s["wq"], s["wo"],
        )
        halves += [keep, hop(sent, "tower", 1)]
    payload = kernel_call(pair_body, [out((ZN, FEED_ROWS, IMG.d), BF)], halves, us=2.8)[0]
    got = lax.all_to_all(payload, "dp", 0, 0, tiled=True)
    before = ()
    for tower in (IMG, TXT):
        own, s1, s2, s3 = back[tower]
        dx, norm_sums[tower] = entry_call(
            tower, norms, layers[tower]["xo"], dx1[tower], second[tower], own,
            peers([s1, s2, s3]), before,
        )
        before = (dx,)
        if tower is IMG:
            down = {IMG: down_call(IMG, ids, sums, dyb_i)}
    placed = [dx] + peers([dx, dx, dx])
    down[TXT] = down_call(TXT, ids, sums, dyb_t)
    wide, *passed = mix_call(ids, feed_own, got)
    moved = [lax.ppermute(v, GROUP, list(pairs)) for v, (_, pairs) in zip(passed, MOVES)]
    lin_i, lin_t, message = collect_call(
        ids, [feed_own, wide, *moved], down[IMG], down[TXT], window,
        norm_sums[IMG], norm_sums[TXT], placed[1:],
    )
    parts = lax.all_to_all(message, (*GROUP, "mp"), 0, 0, tiled=True)
    for tower in (IMG, TXT):
        entries[tower] = place_call(tower, ids, placed)
    loss, size, temperature, *new = advance_call(
        ids,
        logit_log_trio,
        parts,
        misc,
        [lines(picture_single_matrices), lines(picture_mean_state), lines(picture_square_state), lin_i],
        [
            lines(sentence_single_matrices),
            lines(sentence_mean_state),
            lines(sentence_square_state),
            lin_t,
        ],
        [vec_lines, vector_lines(array_mean_state), vector_lines(array_square_state), window],
    )

    def flat(value, like):
        return value.reshape(-1)[: like.size].reshape(like.shape)

    likes = [picture_single_matrices] * 4 + [sentence_single_matrices] * 4 + [array_single_params] * 4
    news = [flat(value, like) for value, like in zip(new, likes)]
    return (
        loss.reshape(()),
        size.reshape(()),
        jnp.transpose(entries[IMG], (1, 0, 2)),
        jnp.transpose(entries[TXT], (1, 0, 2)),
        *news,
        temperature.reshape(()),
    )


def fits(mesh):
    return mesh.shape["tower"] == 2 and mesh.shape["dp"] == ZN and mesh.shape["mp"] == MP


def solution(mesh):
    placed = (
        P(GROUP, None, None),
        P(GROUP, None, None),
        P(GROUP),
        P(GROUP),
        P("mp", GROUP),
        P("mp", GROUP),
        P("mp", GROUP),
        P("mp", GROUP),
        P("mp", GROUP),
        P("mp", GROUP),
        P(GROUP),
        P(GROUP),
        P(GROUP),
        P(),
    )
    return jax.shard_map(
        fast_local if fits(mesh) else local,
        mesh=mesh,
        in_specs=placed,
        out_specs=(
            P(),
            P(),
            P(GROUP, None, None),
            P(GROUP, None, None),
            P("mp", GROUP),
            P("mp", GROUP),
            P("mp", GROUP),
            P("mp", GROUP),
            P("mp", GROUP),
            P("mp", GROUP),
            P("mp", GROUP),
            P("mp", GROUP),
            P(GROUP),
            P(GROUP),
            P(GROUP),
            P(GROUP),
            P(),
        ),
        check_vma=False,
    )
```

```python
import functools
import jax
import jax.numpy as jnp
from jax import lax
from jax.experimental import pallas as pl
from jax.experimental.pallas import tpu as pltpu
from jax.sharding import PartitionSpec as P

BF = jnp.bfloat16
F32 = jnp.float32
GROUP = ("tower", "dp")

D_IMG = 768
FF_IMG = 3072
IMG_LEN = 50
D_TXT = 512
FF_TXT = 2048
TXT_LEN = 77
HEAD = 64
EMBED = 512
STEP = 10


NORM_EPS = 1e-05
UNIT_EPS = 1e-06
BETA_ONE = 0.5
BETA_TWO = 0.5
ADAM_EPS = 1e-08
WEIGHT_DECAY = 0.1
RATE_MATRIX = 0.04
RATE_VECTOR = 0.3
LOGIT_SPEED = 0.5
CLIP_LEVEL = 0.005
MASK_LOW = -1e30
GELU_SLOPE = 1.702
BLOCK_TARGET = 512


def branch_sum(partial_sum):
    return lax.psum(partial_sum, "mp")


def branch_back(partial_sum):
    return lax.psum(partial_sum, "mp")


def norm_forward(values, norm_gain, norm_shift):
    centered = values - jnp.mean(values, axis=-1, keepdims=True)
    inverse = lax.rsqrt(jnp.mean(centered * centered, axis=-1, keepdims=True) + NORM_EPS)
    unit_rows = centered * inverse
    return (unit_rows * norm_gain + norm_shift, unit_rows, inverse)


def norm_backward(grad_rows, unit_rows, inverse, norm_gain):
    scaled = grad_rows * norm_gain
    centered_grad = (
        scaled
        - jnp.mean(scaled, axis=-1, keepdims=True)
        - unit_rows * jnp.mean(scaled * unit_rows, axis=-1, keepdims=True)
    )
    return (
        centered_grad * inverse,
        jnp.sum(grad_rows * unit_rows, axis=0),
        jnp.sum(grad_rows, axis=0),
    )


def quick_gelu(values):
    return values * jax.nn.sigmoid(GELU_SLOPE * values)


def gelu_slope(values):
    sigmoid_value = jax.nn.sigmoid(GELU_SLOPE * values)
    return sigmoid_value + GELU_SLOPE * values * sigmoid_value * (1.0 - sigmoid_value)


def block_size(seq_count, seq_length):
    for candidate in range(1, seq_count + 1):
        if seq_count % candidate == 0 and candidate * seq_length >= BLOCK_TARGET:
            return candidate
    return seq_count


def sequence_mask(seq_length, causal):
    position = lax.iota(jnp.int32, seq_length)
    if causal:
        return position[None, :] <= position[:, None]
    return position[None, :] >= 0


def block_scores(block_qkv, allowed):
    scores = jnp.einsum(
        "nqhd,nkhd->nhqk",
        block_qkv[:, :, 0],
        block_qkv[:, :, 1],
        preferred_element_type=jnp.float32,
    ) * HEAD ** (-0.5)
    return jnp.where(allowed[None, None], scores, MASK_LOW)


def attend(packed, seq_count, seq_length, causal):
    head_count = packed.shape[2]
    per_block = block_size(seq_count, seq_length)
    blocks = packed.reshape(seq_count // per_block, per_block, seq_length, 3, head_count, HEAD)
    allowed = sequence_mask(seq_length, causal)

    def one_block(block_qkv):
        scores = block_scores(block_qkv, allowed)
        row_max = jnp.max(scores, axis=-1, keepdims=True)
        exponent = jnp.exp(scores - row_max)
        totals = jnp.sum(exponent, axis=-1, keepdims=True)
        probs = (exponent / totals).astype(jnp.bfloat16)
        result = jnp.einsum(
            "nhqk,nkhd->nqhd", probs, block_qkv[:, :, 2], preferred_element_type=jnp.float32
        ).astype(jnp.bfloat16)
        return (result, (row_max + jnp.log(totals))[..., 0])

    results, log_totals = lax.map(one_block, blocks)
    return (results.reshape(packed.shape[0], head_count * HEAD), log_totals)


def attend_back(packed, attended_grad, log_totals, seq_count, seq_length, causal):
    head_count = packed.shape[2]
    per_block = block_size(seq_count, seq_length)
    block_total = seq_count // per_block
    blocks = packed.reshape(block_total, per_block, seq_length, 3, head_count, HEAD)
    grad_blocks = attended_grad.reshape(block_total, per_block, seq_length, head_count, HEAD)
    allowed = sequence_mask(seq_length, causal)

    def one_block(block_args):
        block_qkv, block_grad, block_totals = block_args
        scores = block_scores(block_qkv, allowed)
        probs = jnp.exp(scores - block_totals[..., None])
        value_grad = jnp.einsum(
            "nhqk,nqhd->nkhd",
            probs.astype(jnp.bfloat16),
            block_grad,
            preferred_element_type=jnp.float32,
        )
        prob_grad = jnp.einsum(
            "nqhd,nkhd->nhqk", block_grad, block_qkv[:, :, 2], preferred_element_type=jnp.float32
        )
        score_grad = (
            probs * (prob_grad - jnp.sum(probs * prob_grad, axis=-1, keepdims=True))
        ).astype(jnp.bfloat16)
        query_grad = jnp.einsum(
            "nhqk,nkhd->nqhd", score_grad, block_qkv[:, :, 1], preferred_element_type=jnp.float32
        ) * HEAD ** (-0.5)
        key_grad = jnp.einsum(
            "nhqk,nqhd->nkhd", score_grad, block_qkv[:, :, 0], preferred_element_type=jnp.float32
        ) * HEAD ** (-0.5)
        return jnp.stack([query_grad, key_grad, value_grad], axis=2).astype(jnp.bfloat16)

    return lax.map(one_block, (blocks, grad_blocks, log_totals)).reshape(packed.shape)


def split_flat(flat_weights, model_width, hidden, model_split):
    width_piece = model_width // model_split
    hidden_piece = hidden // model_split
    first_end = model_width * 3 * width_piece
    second_end = first_end + width_piece * model_width
    third_end = second_end + model_width * hidden_piece
    return (
        flat_weights[:first_end].reshape(model_width, 3, width_piece),
        flat_weights[first_end:second_end].reshape(width_piece, model_width),
        flat_weights[second_end:third_end].reshape(model_width, hidden_piece),
        flat_weights[third_end:].reshape(hidden_piece, model_width),
    )


def layer_forward(tokens, weights, norms, causal):
    qkv_weight, out_weight, up_weight, down_weight = weights
    seq_count, seq_length, model_width = tokens.shape
    token_rows = tokens.reshape(seq_count * seq_length, model_width).astype(jnp.float32)
    first_normed, unit_one, inverse_one = norm_forward(token_rows, norms[0], norms[1])
    first_low = first_normed.astype(jnp.bfloat16)
    packed = jnp.einsum(
        "rd,dtk->rtk", first_low, qkv_weight, preferred_element_type=jnp.float32
    ).astype(jnp.bfloat16)
    packed = packed.reshape(token_rows.shape[0], 3, qkv_weight.shape[2] // HEAD, HEAD)
    attended, log_totals = attend(packed, seq_count, seq_length, causal)
    middle = token_rows + branch_sum(
        jnp.dot(attended, out_weight, preferred_element_type=jnp.float32)
    )
    second_normed, unit_two, inverse_two = norm_forward(middle, norms[2], norms[3])
    second_low = second_normed.astype(jnp.bfloat16)
    pre_act = jnp.dot(second_low, up_weight, preferred_element_type=jnp.float32)
    activated = quick_gelu(pre_act).astype(jnp.bfloat16)
    outputs = middle + branch_sum(
        jnp.dot(activated, down_weight, preferred_element_type=jnp.float32)
    )
    return (
        outputs,
        (
            first_low,
            unit_one,
            inverse_one,
            packed,
            attended,
            log_totals,
            second_low,
            unit_two,
            inverse_two,
            pre_act,
            activated,
        ),
    )


def layer_backward(grad_out, weights, norms, stored, seq_count, seq_length, causal):
    qkv_weight, out_weight, up_weight, down_weight = weights
    (
        first_low,
        unit_one,
        inverse_one,
        packed,
        attended,
        log_totals,
        second_low,
        unit_two,
        inverse_two,
        pre_act,
        activated,
    ) = stored
    grad_low = grad_out.astype(jnp.bfloat16)
    down_grad = jnp.einsum("rf,rd->fd", activated, grad_low, preferred_element_type=jnp.float32)
    act_grad = jnp.einsum("rd,fd->rf", grad_low, down_weight, preferred_element_type=jnp.float32)
    pre_grad = (act_grad * gelu_slope(pre_act)).astype(jnp.bfloat16)
    up_grad = jnp.einsum("rd,rf->df", second_low, pre_grad, preferred_element_type=jnp.float32)
    second_grad = branch_back(
        jnp.einsum("rf,df->rd", pre_grad, up_weight, preferred_element_type=jnp.float32)
    )
    norm_grad_two, gain_two, shift_two = norm_backward(second_grad, unit_two, inverse_two, norms[2])
    middle_grad = grad_out + norm_grad_two
    middle_low = middle_grad.astype(jnp.bfloat16)
    out_grad = jnp.einsum("ra,rd->ad", attended, middle_low, preferred_element_type=jnp.float32)
    attended_grad = jnp.einsum(
        "rd,ad->ra", middle_low, out_weight, preferred_element_type=jnp.float32
    ).astype(jnp.bfloat16)
    packed_grad = attend_back(packed, attended_grad, log_totals, seq_count, seq_length, causal)
    packed_grad = packed_grad.reshape(packed.shape[0], 3, qkv_weight.shape[2])
    qkv_grad = jnp.einsum("rd,rtk->dtk", first_low, packed_grad, preferred_element_type=jnp.float32)
    first_grad = branch_back(
        jnp.einsum("rtk,dtk->rd", packed_grad, qkv_weight, preferred_element_type=jnp.float32)
    )
    norm_grad_one, gain_one, shift_one = norm_backward(first_grad, unit_one, inverse_one, norms[0])
    flat_grads = jnp.concatenate(
        [qkv_grad.reshape(-1), out_grad.reshape(-1), up_grad.reshape(-1), down_grad.reshape(-1)]
    )
    return (middle_grad + norm_grad_one, flat_grads, [gain_one, shift_one, gain_two, shift_two])


def pool_forward(picked, norm_gain, norm_shift, projection):
    normed, unit_rows, inverse = norm_forward(picked, norm_gain, norm_shift)
    normed_low = normed.astype(jnp.bfloat16)
    raw_embed = jnp.dot(normed_low, projection, preferred_element_type=jnp.float32)
    length_inverse = lax.rsqrt(jnp.sum(raw_embed * raw_embed, axis=-1, keepdims=True) + UNIT_EPS)
    embed_rows = raw_embed * length_inverse
    return (
        embed_rows.astype(jnp.bfloat16),
        (unit_rows, inverse, normed_low, embed_rows, length_inverse),
    )


def pool_backward(embed_grad, norm_gain, projection, stored):
    unit_rows, inverse, normed_low, embed_rows, length_inverse = stored
    raw_grad = (
        length_inverse
        * (embed_grad - embed_rows * jnp.sum(embed_grad * embed_rows, axis=-1, keepdims=True))
    ).astype(jnp.bfloat16)
    proj_grad = jnp.einsum("nd,ne->de", normed_low, raw_grad, preferred_element_type=jnp.float32)
    normed_grad = jnp.einsum("ne,de->nd", raw_grad, projection, preferred_element_type=jnp.float32)
    picked_grad, gain_grad, shift_grad = norm_backward(normed_grad, unit_rows, inverse, norm_gain)
    return (picked_grad, proj_grad, gain_grad, shift_grad)


def cosine_logits(picture_feature_lines, sentence_feature_lines, couple_allowed_flags, log_scale):
    image_all, text_all, valid_all = (
        lax.all_gather(picture_feature_lines, GROUP, axis=0, tiled=True),
        lax.all_gather(sentence_feature_lines, GROUP, axis=0, tiled=True),
        lax.all_gather(
            couple_allowed_flags.astype(jnp.bfloat16), GROUP, axis=0, tiled=True
        ),
    )
    count_valid = jnp.sum(valid_all.astype(jnp.float32))
    column_valid = valid_all > 0
    row_valid = couple_allowed_flags > 0
    local_count = picture_feature_lines.shape[0]
    offset_rows = lax.axis_index(GROUP) * local_count
    on_diagonal = (
        lax.iota(jnp.int32, valid_all.shape[0])[None, :]
        == offset_rows + lax.iota(jnp.int32, local_count)[:, None]
    )
    scale_factor = jnp.exp(log_scale)

    def one_side(mine, others):
        logits = scale_factor * jnp.einsum(
            "ne,me->nm", mine, others, preferred_element_type=jnp.float32
        )
        masked = jnp.where(column_valid[None, :], logits, MASK_LOW)
        row_max = jnp.max(masked, axis=1, keepdims=True)
        exponent = jnp.exp(masked - row_max)
        totals = jnp.sum(exponent, axis=1, keepdims=True)
        own_logit = jnp.sum(jnp.where(on_diagonal, logits, 0.0), axis=1)
        log_sum = row_max[:, 0] + jnp.log(totals[:, 0])
        loss_sum = jnp.sum(jnp.where(row_valid, log_sum - own_logit, 0.0))
        logit_grad = jnp.where(
            row_valid[:, None], exponent / totals - on_diagonal.astype(jnp.float32), 0.0
        ) / (2.0 * count_valid)
        return (loss_sum, logit_grad, jnp.sum(logit_grad * logits), log_sum, logits)

    image_loss, image_logit_grad, image_scale_part, image_lse, image_logits = one_side(
        picture_feature_lines, text_all
    )
    text_loss, text_logit_grad, text_scale_part, text_lse, text_logits = one_side(
        sentence_feature_lines, image_all
    )
    picture_device_share = scale_factor * jnp.dot(
        image_logit_grad, text_all.astype(jnp.float32), precision=lax.Precision.HIGHEST
    )
    sentence_device_share = scale_factor * jnp.dot(
        text_logit_grad, image_all.astype(jnp.float32), precision=lax.Precision.HIGHEST
    )
    text_spread = scale_factor * jnp.einsum(
        "np,ne->pe",
        image_logit_grad,
        picture_feature_lines.astype(jnp.float32),
        precision=lax.Precision.HIGHEST,
    )
    image_spread = scale_factor * jnp.einsum(
        "np,ne->pe",
        text_logit_grad,
        sentence_feature_lines.astype(jnp.float32),
        precision=lax.Precision.HIGHEST,
    )
    picture_reverse, sentence_reverse = (
        lax.psum_scatter(image_spread, GROUP, scatter_dimension=0, tiled=True),
        lax.psum_scatter(text_spread, GROUP, scatter_dimension=0, tiled=True),
    )
    contrast_objective, logit_log_slope = lax.psum(
        ((image_loss + text_loss) / (2.0 * count_valid), image_scale_part + text_scale_part),
        GROUP,
    )
    return (
        picture_device_share + picture_reverse,
        sentence_device_share + sentence_reverse,
        contrast_objective,
        logit_log_slope,
    )


def optimizer_advance(master, first, second, grad, rate, decay):
    first_new = BETA_ONE * first + (1.0 - BETA_ONE) * grad
    second_new = BETA_TWO * second + (1.0 - BETA_TWO) * grad * grad
    update = (
        first_new
        / (1.0 - BETA_ONE**STEP)
        / (jnp.sqrt(second_new / (1.0 - BETA_TWO**STEP)) + ADAM_EPS)
    )
    return (master - rate * (update + decay * master), first_new, second_new)


def local(
    picture_residual_entry,
    sentence_residual_entry,
    sentence_lengths_held,
    couple_allowed_flags,
    picture_single_matrices,
    picture_mean_state,
    picture_square_state,
    sentence_single_matrices,
    sentence_mean_state,
    sentence_square_state,
    array_single_params,
    array_mean_state,
    array_square_state,
    logit_log_trio,
):
    model_split = lax.axis_size("mp")
    norm_end = 6 * (D_IMG + D_TXT)
    image_end = norm_end + D_IMG * EMBED
    image_flat, text_flat, vector_flat = (
        lax.all_gather(
            picture_single_matrices.astype(jnp.bfloat16), GROUP, axis=1, tiled=True
        ),
        lax.all_gather(
            sentence_single_matrices.astype(jnp.bfloat16), GROUP, axis=1, tiled=True
        ),
        lax.all_gather(
            array_single_params.astype(jnp.bfloat16), GROUP, axis=0, tiled=True
        ),
    )
    image_norms = vector_flat[: 6 * D_IMG].reshape(6, D_IMG).astype(jnp.float32)
    text_norms = vector_flat[6 * D_IMG : norm_end].reshape(6, D_TXT).astype(jnp.float32)
    image_proj = vector_flat[norm_end:image_end].reshape(D_IMG, EMBED)
    text_proj = vector_flat[image_end:].reshape(D_TXT, EMBED)
    seq_count = picture_residual_entry.shape[0]
    image_weights = split_flat(image_flat[0], D_IMG, FF_IMG, model_split)
    image_out, image_stored = layer_forward(
        picture_residual_entry, image_weights, image_norms, False
    )
    image_picked = jnp.mean(image_out.reshape(seq_count, IMG_LEN, D_IMG), axis=1)
    picture_feature_lines, image_pool = pool_forward(
        image_picked, image_norms[4], image_norms[5], image_proj
    )
    text_weights = split_flat(text_flat[0], D_TXT, FF_TXT, model_split)
    text_out, text_stored = layer_forward(sentence_residual_entry, text_weights, text_norms, True)
    inside = (lax.iota(jnp.int32, TXT_LEN)[None, :] < sentence_lengths_held[:, None]).astype(
        jnp.float32
    )
    picker = inside / sentence_lengths_held[:, None].astype(jnp.float32)
    text_picked = jnp.einsum(
        "nl,nld->nd",
        picker,
        text_out.reshape(seq_count, TXT_LEN, D_TXT),
        precision=lax.Precision.HIGHEST,
    )
    sentence_feature_lines, text_pool = pool_forward(
        text_picked, text_norms[4], text_norms[5], text_proj
    )
    picture_feature_slope, sentence_feature_slope, contrast_objective, logit_log_slope = (
        cosine_logits(
            picture_feature_lines, sentence_feature_lines, couple_allowed_flags, logit_log_trio[0]
        )
    )
    text_picked_grad, text_proj_grad, text_post_gain, text_post_shift = pool_backward(
        sentence_feature_slope, text_norms[4], text_proj, text_pool
    )
    text_rows_grad = (picker[:, :, None] * text_picked_grad[:, None, :]).reshape(
        seq_count * TXT_LEN, D_TXT
    )
    sentence_entry_slope, text_flat_grad, text_norm_grads = layer_backward(
        text_rows_grad, text_weights, text_norms, text_stored, seq_count, TXT_LEN, True
    )
    image_picked_grad, image_proj_grad, image_post_gain, image_post_shift = pool_backward(
        picture_feature_slope, image_norms[4], image_proj, image_pool
    )
    image_rows_grad = jnp.broadcast_to(
        image_picked_grad[:, None, :] / IMG_LEN, (seq_count, IMG_LEN, D_IMG)
    ).reshape(seq_count * IMG_LEN, D_IMG)
    picture_entry_slope, image_flat_grad, image_norm_grads = layer_backward(
        image_rows_grad, image_weights, image_norms, image_stored, seq_count, IMG_LEN, False
    )
    array_param_slope = jnp.concatenate(
        [
            jnp.stack(image_norm_grads + [image_post_gain, image_post_shift]).reshape(-1),
            jnp.stack(text_norm_grads + [text_post_gain, text_post_shift]).reshape(-1),
            image_proj_grad.reshape(-1),
            text_proj_grad.reshape(-1),
        ]
    )
    image_reduced, text_reduced, vector_reduced = (
        lax.psum_scatter(
            image_flat_grad.reshape(-1, D_IMG), GROUP, scatter_dimension=0, tiled=True
        ).reshape(1, -1),
        lax.psum_scatter(
            text_flat_grad.reshape(-1, D_TXT), GROUP, scatter_dimension=0, tiled=True
        ).reshape(1, -1),
        lax.psum_scatter(array_param_slope, GROUP, scatter_dimension=0, tiled=True),
    )
    matrix_squares = jnp.sum(image_reduced * image_reduced) + jnp.sum(text_reduced * text_reduced)
    vector_squares = jnp.sum(vector_reduced * vector_reduced) / model_split
    tensor_square_sum, array_square_sum = lax.psum(
        (matrix_squares, vector_squares), (*GROUP, "mp")
    )
    global_slope_size = jnp.sqrt(
        tensor_square_sum + array_square_sum + logit_log_slope * logit_log_slope
    )
    clipping_factor = CLIP_LEVEL / jnp.maximum(global_slope_size, CLIP_LEVEL)
    picture_matrices_fresh, picture_mean_fresh, picture_square_fresh = optimizer_advance(
        picture_single_matrices,
        picture_mean_state,
        picture_square_state,
        image_reduced * clipping_factor,
        RATE_MATRIX,
        WEIGHT_DECAY,
    )
    sentence_matrices_fresh, sentence_mean_fresh, sentence_square_fresh = optimizer_advance(
        sentence_single_matrices,
        sentence_mean_state,
        sentence_square_state,
        text_reduced * clipping_factor,
        RATE_MATRIX,
        WEIGHT_DECAY,
    )
    shard_length = array_single_params.shape[0]
    vector_index = lax.axis_index(GROUP) * shard_length + lax.iota(
        jnp.int32, shard_length
    )
    is_norm = vector_index < norm_end
    array_params_fresh, array_mean_fresh, array_square_fresh = optimizer_advance(
        array_single_params,
        array_mean_state,
        array_square_state,
        vector_reduced * clipping_factor,
        jnp.where(is_norm, RATE_VECTOR, RATE_MATRIX),
        jnp.where(is_norm, 0.0, WEIGHT_DECAY),
    )
    logit_log_fresh, logit_mean_fresh, logit_square_fresh = optimizer_advance(
        logit_log_trio[0],
        logit_log_trio[1],
        logit_log_trio[2],
        logit_log_slope * clipping_factor,
        LOGIT_SPEED,
        0.0,
    )
    return (
        contrast_objective,
        global_slope_size,
        picture_entry_slope.reshape(picture_residual_entry.shape),
        sentence_entry_slope.reshape(sentence_residual_entry.shape),
        picture_matrices_fresh,
        picture_matrices_fresh.astype(jnp.bfloat16),
        picture_mean_fresh,
        picture_square_fresh,
        sentence_matrices_fresh,
        sentence_matrices_fresh.astype(jnp.bfloat16),
        sentence_mean_fresh,
        sentence_square_fresh,
        array_params_fresh,
        array_params_fresh.astype(jnp.bfloat16),
        array_mean_fresh,
        array_square_fresh,
        logit_log_fresh,
    )


ZN = 4
MP = 4
SEQS = 8


class Tower:
    def __init__(self, tag, width, length, padded, joint, causal, norm_row):
        self.tag = tag
        self.d = width
        self.w = width // MP
        self.heads = self.w // HEAD
        self.length = length
        self.padded = padded
        self.rows = 2 * padded
        self.all_rows = MP * self.rows
        self.tile = self.rows if joint else padded
        self.tiles = self.rows // self.tile
        self.causal = causal
        self.sr = 3 * width // 8
        self.half = self.sr // 2
        self.q = width // 128
        self.norm_row = norm_row
        self.lin = self.sr * self.q


IMG = Tower("_img", D_IMG, IMG_LEN, 56, True, False, 0)
TXT = Tower("_txt", D_TXT, TXT_LEN, 80, False, True, 6 * D_IMG // 128)
NORM_ROWS = 6 * (D_IMG + D_TXT) // 128
VEC_ROWS = 648
HALF = IMG.half + 64
FEED_ROWS = IMG.d // 8 + 48
URGENT = HALF + 16


COST_SCALE = 1.5e9


def kernel_call(body, outs, ins, scratch=(), us=2.0, after=(), vmem=64):
    after = list(after) + LAST

    def spec(value):
        small = value.dtype == jnp.int32 or (value.ndim == 1 and value.shape[0] <= 8)
        return pl.BlockSpec(memory_space=pltpu.SMEM if small else pltpu.VMEM)

    count, late = len(ins), len(after)
    name = getattr(body, "func", body).__name__
    if hasattr(body, "args"):
        name = name + body.args[0].tag
    results = pl.pallas_call(
        lambda *refs: body(*refs[:count], *refs[count + late :]),
        out_shape=list(outs),
        in_specs=[spec(v) for v in ins] + [pl.BlockSpec(memory_space=pl.ANY)] * late,
        out_specs=[pl.BlockSpec(memory_space=pltpu.VMEM)] * len(outs),
        scratch_shapes=list(scratch),
        compiler_params=pltpu.CompilerParams(
            vmem_limit_bytes=vmem * MIB
        ),
        cost_estimate=pl.CostEstimate(
            flops=int(COST_SCALE * us), bytes_accessed=0, transcendentals=0
        ),
        name=name,
    )(*ins, *after)
    LAST[:] = results[:1]
    return results


LAST = []
MIB = 1024 * 1024


def gate(value, *after):
    anywhere = pl.BlockSpec(memory_space=pl.ANY)
    return pl.pallas_call(
        lambda *refs: None,
        out_shape=out(value.shape, value.dtype),
        in_specs=[anywhere] * (1 + len(after)),
        out_specs=anywhere,
        input_output_aliases={0: 0},
    )(value, *after)


def out(shape, dtype=F32):
    return jax.ShapeDtypeStruct(shape, dtype)


def dot(a, b):
    return lax.dot_general(a, b, (((1,), (0,)), ((), ())), preferred_element_type=F32)


def dot_nt(a, b):
    return lax.dot_general(a, b, (((1,), (1,)), ((), ())), preferred_element_type=F32)


def dot_tn(a, b):
    return lax.dot_general(a, b, (((0,), (0,)), ((), ())), preferred_element_type=F32)


def pieces(a, count):
    parts = []
    for _ in range(count):
        part = a.astype(BF)
        parts.append(part)
        a = a - part.astype(F32)
    return parts


def unit(values):
    width = values.shape[-1]
    centered = values - jnp.sum(values, axis=-1, keepdims=True) * (1.0 / width)
    inverse = lax.rsqrt(
        jnp.sum(centered * centered, axis=-1, keepdims=True) * (1.0 / width) + NORM_EPS
    )
    return centered * inverse, inverse


def unit_back(grad_rows, unit_rows, inverse, gain):
    width = grad_rows.shape[-1]
    scaled = grad_rows * gain
    first = jnp.sum(scaled, axis=-1, keepdims=True) * (1.0 / width)
    second = jnp.sum(scaled * unit_rows, axis=-1, keepdims=True) * (1.0 / width)
    return (scaled - first - unit_rows * second) * inverse


def norm_vector(norms_ref, tower, index):
    start = tower.norm_row + index * tower.q
    return jnp.concatenate([norms_ref[start + i : start + i + 1, :] for i in range(tower.q)], axis=1)


def natural_from_lin(tower, lin_ref, spare):
    d, w = tower.d, tower.w
    if (3 * w) % 128 == 0:
        per = 3 * w // 128
        return jnp.concatenate(
            [lin_ref[pl.ds(i, d // 2, stride=per), :] for i in range(per)], axis=1
        )
    per = 2 * 3 * w // 128
    mid = per // 2
    lines = [lin_ref[pl.ds(i, d // 4, stride=per), :] for i in range(per)]
    empty = jnp.zeros((d // 4, 64), F32)
    even = lines[: mid + 1]
    odd = jnp.concatenate([lines[mid][:, 64:]] + lines[mid + 1 :] + [empty], axis=1)
    for j in range(mid + 1):
        spare.at[j][pl.ds(0, d // 4, stride=2), :] = even[j]
        spare.at[j][pl.ds(1, d // 4, stride=2), :] = odd[:, 128 * j : 128 * (j + 1)]
    return jnp.concatenate([spare[j] for j in range(mid)] + [spare[mid][:, :64]], axis=1)


def natural_to_lin(tower, natural, lin_ref, spare):
    d, w = tower.d, tower.w
    if (3 * w) % 128 == 0:
        per = 3 * w // 128
        for i in range(per):
            lin_ref[pl.ds(i, d // 2, stride=per), :] = natural[:, 128 * i : 128 * (i + 1)]
        return
    per = 2 * 3 * w // 128
    mid = per // 2
    for j in range(mid):
        spare[j] = natural[:, 128 * j : 128 * (j + 1)]
    spare[mid] = jnp.concatenate([natural[:, 128 * mid :], jnp.zeros((d // 2, 64), F32)], axis=1)
    even = [spare.at[j][pl.ds(0, d // 4, stride=2), :] for j in range(mid + 1)]
    odd = jnp.concatenate(
        [spare.at[j][pl.ds(1, d // 4, stride=2), :] for j in range(mid + 1)], axis=1
    )
    for i in range(mid):
        lin_ref[pl.ds(i, d // 4, stride=per), :] = even[i]
    lin_ref[pl.ds(mid, d // 4, stride=per), :] = jnp.concatenate(
        [even[mid][:, :64], odd[:, :64]], axis=1
    )
    for i in range(mid):
        lin_ref[pl.ds(mid + 1 + i, d // 4, stride=per), :] = odd[:, 64 + 128 * i : 192 + 128 * i]


def lin_to_rows(tower, lin_ref, rows_ref, spare, shard):
    d, w, sr, q = tower.d, tower.w, tower.sr, tower.q

    @pl.when(shard >= 2)
    def _():
        for j in range(q):
            rows_ref[:, 128 * j : 128 * (j + 1)] = lin_ref[pl.ds(j, sr, stride=q), :]

    @pl.when(shard < 2)
    def _():
        tail = d // 8
        natural = natural_from_lin(tower, lin_ref, spare)
        rows_ref[:, : 3 * w] = natural[:sr]
        for i in range(3):
            rows_ref[tail * i : tail * (i + 1), 3 * w :] = natural[sr:, w * i : w * (i + 1)]


def rows_to_lin(tower, rows_ref, lin_ref, spare, shard):
    d, w, sr, q = tower.d, tower.w, tower.sr, tower.q

    @pl.when(shard >= 2)
    def _():
        for j in range(q):
            lin_ref[pl.ds(j, sr, stride=q), :] = rows_ref[:, 128 * j : 128 * (j + 1)]

    @pl.when(shard < 2)
    def _():
        tail = d // 8
        rest = jnp.concatenate(
            [rows_ref[tail * i : tail * (i + 1), 3 * w :] for i in range(3)], axis=1
        )
        natural = jnp.concatenate([rows_ref[:, : 3 * w], rest], axis=0)
        natural_to_lin(tower, natural, lin_ref, spare)


SPARE = ((3 * IMG.w + 127) // 128, IMG.d // 2, 128)


def prepare_body(
    ids, flags, lengths, img, txt, head, keep_t, keep_i, send_t, send_i, block, rows_i, rows_t, spare
):
    side, shard = ids[0], ids[3]
    lin_to_rows(IMG, img, rows_i, spare, shard)
    lin_to_rows(TXT, txt, rows_t, spare, shard)
    lane = lax.broadcasted_iota(jnp.int32, (1, 128), 1)
    flag_row = jnp.zeros((1, 128), F32)
    length_row = jnp.zeros((1, 128), F32)
    for i in range(SEQS):
        flag_row = jnp.where(lane == i, jnp.where(flags[i] > 0, 1.0, 0.0), flag_row)
        length_row = jnp.where(lane == i, lengths[i].astype(F32), length_row)
    lines = jnp.concatenate(
        [head[:NORM_ROWS, :], flag_row, length_row, jnp.zeros((64 - NORM_ROWS - 2, 128), F32)], axis=0
    )
    for j in range(4):
        block[:, 128 * j : 128 * (j + 1)] = lines[16 * j : 16 * (j + 1)].astype(BF)
    for tower, rows, keep, send in ((TXT, rows_t, keep_t, send_t), (IMG, rows_i, keep_i, send_i)):
        for target, which in ((keep, side), (send, 1 - side)):
            target[...] = rows[
                pl.ds(pl.multiple_of(which * tower.half, 8), tower.half), :
            ].astype(BF)


def sort_body(ids, keep_t, keep_i, got_t, got_i, block, urgent, late):
    def fill(*halves):
        for target, part_t, part_i in ((urgent, *halves[:2]), (late, *halves[2:])):
            target[: IMG.half, :] = part_i[...]
            target[IMG.half : HALF, : TXT.d] = part_t[:64, :]
            target[IMG.half : IMG.half + 32, TXT.d :] = part_t[64:, :256]
            target[IMG.half + 32 : HALF, TXT.d :] = part_t[64:, 256:]

    pl.when(ids[0] == 0)(lambda: fill(keep_t, keep_i, got_t, got_i))
    pl.when(ids[0] != 0)(lambda: fill(got_t, got_i, keep_t, keep_i))
    urgent[HALF:, : TXT.d] = block[...]
    urgent[HALF:, TXT.d :] = jnp.zeros((16, IMG.d - TXT.d), BF)


def vector_pay_body(ids, vec, vecpay, shifted):
    odd = ids[3] % 2

    @pl.when(odd == 0)
    def _():
        vecpay[...] = vec[...].astype(BF)

    @pl.when(odd == 1)
    def _():
        rolled = pltpu.roll(vec[...], 64, 1)
        shifted[0:8, :] = jnp.zeros((8, 128), F32)
        shifted[8 : 8 + VEC_ROWS, :] = rolled
        before = shifted[7 : 7 + VEC_ROWS, :]
        low_lanes = lax.broadcasted_iota(jnp.int32, (VEC_ROWS, 128), 1) < 64
        vecpay[...] = jnp.where(low_lanes, before, rolled).astype(BF)


def with_halves(blocks, side, z, shard, use):
    if len(blocks) == 2:
        rows = blocks[0].shape[0] // ZN
        mine, other = [block.at[pl.ds(shard * rows, rows)] for block in blocks]
        pl.when(side == 0)(lambda: use(mine, other))
        pl.when(side != 0)(lambda: use(other, mine))
        return
    for k in range(ZN):
        mine, other = blocks[k], blocks[ZN + k]
        here = (z ^ shard) == k
        pl.when(here & (side == 0))(functools.partial(use, mine, other))
        pl.when(here & (side != 0))(functools.partial(use, other, mine))


def half_rows(tower, first, second):
    if tower is IMG:
        return jnp.concatenate([first[: IMG.half, :], second[: IMG.half, :]], axis=0)
    parts = []
    for half in (first, second):
        parts += [
            half[IMG.half : HALF, : TXT.d],
            half[IMG.half : IMG.half + 32, TXT.d :],
            half[IMG.half + 32 : HALF, TXT.d :],
        ]
    return jnp.concatenate(
        [
            parts[0],
            jnp.concatenate([parts[1], parts[2]], axis=1),
            parts[3],
            jnp.concatenate([parts[4], parts[5]], axis=1),
        ],
        axis=0,
    )


def attention_mask(tower):
    shape = (tower.tile, tower.tile)
    row = lax.broadcasted_iota(jnp.int32, shape, 0)
    column = lax.broadcasted_iota(jnp.int32, shape, 1)
    if tower.causal:
        return (column <= row) & (column < tower.length)
    pad = tower.padded
    first = (row < pad) & (column < tower.length)
    second = (row >= pad) & (column >= pad) & (column < pad + tower.length)
    return first | second


def read_meta(meta, blocks, side, z):
    for place in range(ZN):

        def use(*halves, place=place):
            for half, block in enumerate(halves):
                lines = block[HALF:, 384:512].astype(F32)
                line = half * ZN + place
                meta[line : line + 1, :] = lines[12:13]
                meta[8 + line : 9 + line, :] = lines[13:14]

        with_halves(blocks, side, z, place, use)


def attend_body(tower, ids, x, *rest):
    count = 2 * ZN
    blocks, rest = rest[:count], rest[count:]
    if tower is TXT:
        (norms, meta, wq, wo, up, h1, u1, qkv, att, probs, xo, own, s1, s2, s3, xf, xs) = rest
    else:
        norms = rest[0]
        (wq, wo, up, h1, u1, qkv, att, probs, xo, own, s1, s2, s3, xf, xs) = rest[1:]
    side, z, m = ids[0], ids[1], ids[2]
    d, w, sr = tower.d, tower.w, tower.sr
    if tower is TXT:

        def read_norms(block, _):
            for j in range(4):
                norms[16 * j : 16 * (j + 1), :] = block[HALF:, 128 * j : 128 * (j + 1)].astype(F32)

        with_halves(blocks, side, z, 0, read_norms)
        read_meta(meta, blocks, side, z)

    tail = d // 8
    for s in range(2):

        def read_qkv(first, second, base=s * (d // 2)):
            part = half_rows(tower, first, second)
            wq[base : base + sr, :] = part[:, : 3 * w]
            wq[base + sr : base + sr + tail, :] = jnp.concatenate(
                [part[tail * i : tail * (i + 1), 3 * w :] for i in range(3)], axis=1
            )

        with_halves(blocks, side, z, s, read_qkv)

    def read_out(first, second):
        part = half_rows(tower, first, second)
        wo[...] = part[:w]
        up[:tail, :] = part[w:]

    def read_up(first, second):
        up[tail:, :] = half_rows(tower, first, second)

    with_halves(blocks, side, z, 2, read_out)
    with_halves(blocks, side, z, 3, read_up)
    for j in range(tower.q):
        xf[j] = x[:, :, 128 * j : 128 * (j + 1)].astype(F32).reshape(tower.length * SEQS, 128)
    pad = tower.padded - tower.length
    for k in range(MP):
        for j in range(2):
            start = k * tower.rows + j * tower.padded
            seq = 2 * (m ^ k) + j
            for i in range(tower.q):
                xs[start : start + tower.length, 128 * i : 128 * (i + 1)] = xf.at[i][
                    pl.ds(seq, tower.length, stride=SEQS), :
                ]
            xs[start + tower.length : start + tower.padded, :] = jnp.zeros((pad, d), F32)
    xo[...] = xs[: tower.rows, :]
    unit_rows, _ = unit(xs[...])
    u1[...] = unit_rows.astype(BF)
    h1[...] = (
        unit_rows * norm_vector(norms, tower, 0) + norm_vector(norms, tower, 1)
    ).astype(BF)
    qkv[...] = dot(h1[...], wq[...]).astype(BF)
    allowed = attention_mask(tower)
    targets = (own, s1, s2, s3)
    for k in range(MP):
        for tile in range(tower.tiles):
            start = k * tower.rows + tile * tower.tile
            rows = slice(start, start + tower.tile)
            heads = []
            for h in range(tower.heads):
                query = qkv[rows, h * HEAD : (h + 1) * HEAD]
                key = qkv[rows, w + h * HEAD : w + (h + 1) * HEAD]
                value = qkv[rows, 2 * w + h * HEAD : 2 * w + (h + 1) * HEAD]
                scores = jnp.where(allowed, dot_nt(query, key) * HEAD ** (-0.5), MASK_LOW)
                exponent = jnp.exp(scores - jnp.max(scores, axis=-1, keepdims=True))
                prob = exponent / jnp.sum(exponent, axis=-1, keepdims=True)
                probs[(k * tower.tiles + tile) * tower.heads + h] = prob
                heads.append(dot(prob.astype(BF), value))
            att[rows, :] = jnp.concatenate(heads, axis=1).astype(BF)
        rows = slice(k * tower.rows, (k + 1) * tower.rows)
        part = dot(att[rows, :], wo[...])
        targets[k][...] = part.astype(targets[k].dtype)


def attend_call(tower, ids, x, blocks, norms=None, after=()):
    d, w, rows, every = tower.d, tower.w, tower.rows, tower.all_rows
    outs = [
        out((d, 3 * w), BF),
        out((w, d), BF),
        out((d // 2, d), BF),
        out((every, d), BF),
        out((every, d), BF),
        out((every, 3 * w), BF),
        out((every, w), BF),
        out((MP * tower.tiles * tower.heads, tower.tile, tower.tile)),
        out((rows, d)),
        out((rows, d)),
        out((rows, d), BF),
        out((rows, d), BF),
        out((rows, d), BF),
    ]
    ins = [ids, x] + blocks
    if tower is TXT:
        outs = [out((64, 128)), out((16, 128))] + outs
    else:
        ins.append(norms)
    return kernel_call(
        functools.partial(attend_body, tower),
        outs,
        ins,
        [
            pltpu.VMEM((tower.q, tower.length * SEQS, 128), F32),
            pltpu.VMEM((every, d), F32),
        ],
        after=after,
        us=7.2,
    )


def row_mask(tower, lengths, pair):
    position = lax.broadcasted_iota(jnp.int32, (tower.padded, 1), 0)
    count = lengths[pair] if tower.causal else tower.length
    return position < count, count


def middle_body(tower, ids, lengths, norms, xo, own, r1, r2, r3, x1, h2, pooled):
    m = ids[2]
    total = xo[...] + ((own[...] + r1[...].astype(F32)) + (r2[...].astype(F32) + r3[...].astype(F32)))
    x1[...] = total
    unit_rows, _ = unit(total)
    h2[...] = (
        unit_rows * norm_vector(norms, tower, 2) + norm_vector(norms, tower, 3)
    ).astype(BF)
    for j in range(2):
        inside, count = row_mask(tower, lengths, 2 * m + j)
        part = total[j * tower.padded : (j + 1) * tower.padded]
        summed = jnp.sum(jnp.where(inside, part, 0.0), axis=0, keepdims=True)
        pooled[j : j + 1, :] = summed / jnp.full((1, 1), count, F32)


def middle_call(tower, ids, lengths, norms, xo, own, received, after=()):
    rows, d = tower.rows, tower.d
    return kernel_call(
        functools.partial(middle_body, tower),
        [out((rows, d)), out((rows, d), BF), out((2, d))],
        [ids, lengths, norms, xo, own] + received,
        after=after,
    )


def feed_body(tower, ids, lengths, h_own, h1, h2, h3, *rest):
    up, late, rest = rest[0], rest[1:3], rest[3:]
    if tower is TXT:
        pooled, w1, w2, slope, sums, *y_out = rest
    else:
        pooled, *y_txt, sums_txt, w1, w2, slope, sums, y0, y1, y2, y3 = rest
        y_out = (y0, y1, y2, y3)
    side, z, m = ids[0], ids[1], ids[2]
    d, w, sr = tower.d, tower.w, tower.sr
    tail = d // 8

    def read(target, start, skip, count):
        def use(first, second):
            part = half_rows(tower, first, second)
            target[start : start + count, :] = part[skip : skip + count]

        return use

    def read_both(first, second):
        part = half_rows(tower, first, second)
        w1[tail + 2 * sr :, :] = part[:tail]
        w2[:w, :] = part[tail:]

    w1[: d // 2, :] = up[...]
    with_halves(late, side, z, 0, read(w1, tail + sr, 0, sr))
    with_halves(late, side, z, 1, read_both)
    with_halves(late, side, z, 2, read(w2, w, 0, sr))
    with_halves(late, side, z, 3, read(w2, w + sr, 0, sr))
    sums_places, y_places = [], []
    for k, block in enumerate((h_own, h1, h2, h3)):
        pre = dot(block[...], w1[...])
        gate = jax.nn.sigmoid(GELU_SLOPE * pre)
        acted = (pre * gate).astype(BF).astype(F32)
        slope[k * tower.rows : (k + 1) * tower.rows, :] = gate + GELU_SLOPE * pre * gate * (
            1.0 - gate
        )
        summed = []
        counts = []
        for j in range(2):
            inside, count = row_mask(tower, lengths, 2 * (m ^ k) + j)
            part = acted[j * tower.padded : (j + 1) * tower.padded]
            summed.append(jnp.sum(jnp.where(inside, part, 0.0), axis=0, keepdims=True))
            counts.append(jnp.full((1, 1), count, F32))
        both = jnp.concatenate(summed, axis=0)
        sums_places.append(both)
        high, low, rest = pieces(both, 3)
        y = dot(high, w2[...]) + (dot(low, w2[...]) + dot(rest, w2[...]))
        y = y / jnp.concatenate(counts, axis=0)
        if k == 0:
            y = y + pooled[...]
        y_places.append(y)

    def in_order(places):
        def chunk(c):
            value = places[c ^ 3]
            for member in range(3):
                value = jnp.where(m == member, places[c ^ member], value)
            return value

        return jnp.concatenate([chunk(c) for c in range(MP)], axis=0)

    ordered = in_order(sums_places)
    if tower is TXT:
        sums[...] = ordered
        for target, value in zip(y_out, y_places):
            target[...] = value
        return
    for target, value, other in zip(y_out, y_places, y_txt):
        target[:, :d] = value
        target[:, d:] = other[...]
    sums[:, :d] = ordered
    sums[:, d:] = sums_txt[...]


def feed_call(tower, ids, lengths, blocks, up, late, pooled, before=()):
    d = tower.d
    wide = d if tower is TXT else D_IMG + D_TXT
    return kernel_call(
        functools.partial(feed_body, tower),
        [
            out((d, d), BF),
            out((d, d), BF),
            out((tower.all_rows, d)),
            out((SEQS, wide)),
        ]
        + [out((2, wide))] * MP,
        [ids, lengths] + blocks + [up] + late + [pooled] + list(before),
        us=6.4,
    )


def project_body(gathered, pi, pt, flat):
    for e in range(4):
        base = e * (2 * VEC_ROWS - 1)
        flat[base : base + VEC_ROWS, :] = gathered[2 * e].astype(F32)
        odd = gathered[2 * e + 1].astype(F32)
        row = base + VEC_ROWS - 1
        flat[row : row + 1, :] = flat[row : row + 1, :] + odd[:1]
        flat[row + 1 : row + VEC_ROWS, :] = odd[1:]
    for j in range(4):
        pi[:, 128 * j : 128 * (j + 1)] = flat[pl.ds(NORM_ROWS + j, D_IMG, stride=4), :].astype(BF)
        pt[:, 128 * j : 128 * (j + 1)] = flat[
            pl.ds(NORM_ROWS + 4 * D_IMG + j, D_TXT, stride=4), :
        ].astype(BF)


def project_call(gathered, after):
    return kernel_call(
        project_body,
        [out((D_IMG, EMBED), BF), out((D_TXT, EMBED), BF)],
        [gathered],
        [pltpu.VMEM((4 * (2 * VEC_ROWS - 1) + 4, 128), F32)],
        us=2.8,
        after=after,
    )


def head_body(
    ids, trio, parts, norms, meta, pi, pt,
    misc, dyb_i, dyb_t, own_i, own_t, window, pg_i, pg_t, ng_i, ng_t, scr_i, scr_t, yall, flat,
):
    shard = ids[3]
    total = yall.shape[0]
    for i in range(parts.shape[0]):
        yall[2 * i : 2 * i + 2, :] = parts[i]
    row = lax.broadcasted_iota(jnp.int32, (total, total), 0)
    column = lax.broadcasted_iota(jnp.int32, (total, total), 1)
    eye = row == column
    place = lax.broadcasted_iota(jnp.int32, (total, 128), 0)
    lane = lax.broadcasted_iota(jnp.int32, (total, 128), 1)

    def column_of(first):
        picked = jnp.zeros((total, 128), F32)
        for s in range(2 * ZN):
            picked = jnp.where(place // SEQS == s, meta[first + s : first + s + 1, :], picked)
        return jnp.sum(jnp.where(lane == place % SEQS, picked, 0.0), axis=1, keepdims=True)

    flag_column = column_of(0)
    length_column = column_of(8)
    flag_row = jnp.sum(jnp.where(eye, flag_column, 0.0), axis=0, keepdims=True)
    row_valid = flag_column > 0.5
    column_valid = flag_row > 0.5
    count = jnp.sum(flag_column, axis=0, keepdims=True)

    def forward(tower, values, projection):
        unit_rows, inverse = unit(values)
        z = (
            unit_rows * norm_vector(norms, tower, 4) + norm_vector(norms, tower, 5)
        ).astype(BF)
        raw = dot(z, projection[...])
        scale = lax.rsqrt(jnp.sum(raw * raw, axis=-1, keepdims=True) + UNIT_EPS)
        quotient = raw * scale
        return unit_rows, inverse, z, scale, quotient, quotient.astype(BF)

    image = forward(IMG, yall[:, :D_IMG], pi)
    text = forward(TXT, yall[:, D_IMG:], pt)
    factor = jnp.exp(jnp.full((1, 1), trio[0], F32))
    e_image, e_text = image[5], text[5]

    def side(mine, others):
        logits = factor * dot_nt(mine, others)
        masked = jnp.where(column_valid, logits, MASK_LOW)
        top = jnp.max(masked, axis=1, keepdims=True)
        exponent = jnp.exp(masked - top)
        totals = jnp.sum(exponent, axis=1, keepdims=True)
        own = jnp.sum(jnp.where(eye, logits, 0.0), axis=1, keepdims=True)
        loss = jnp.sum(
            jnp.where(row_valid, top + jnp.log(totals) - own, 0.0), axis=0, keepdims=True
        )
        grad = jnp.where(row_valid, exponent / totals - eye.astype(F32), 0.0) / (2.0 * count)
        scale_part = jnp.sum(jnp.sum(grad * logits, axis=1, keepdims=True), axis=0, keepdims=True)
        return loss, grad, scale_part

    loss_i, grad_i, part_i = side(e_image, e_text)
    loss_t, grad_t, part_t = side(e_text, e_image)
    loss = (loss_i + loss_t) / (2.0 * count)
    slope = part_i + part_t
    misc[...] = jnp.concatenate(
        [
            jnp.broadcast_to(loss, (1, 128)),
            jnp.broadcast_to(slope, (1, 128)),
            jnp.zeros((6, 128), F32),
        ],
        axis=0,
    )

    def product(grad, back, others):
        sums = None
        for part in pieces(grad, 3):
            term = dot(part, others)
            sums = term if sums is None else sums + term
        for part in pieces(back, 3):
            sums = sums + dot_tn(part, others)
        return factor * sums

    def backward(tower, stored, embed_grad, projection, counts, pg, ng, dyb, scratch, own):
        unit_rows, inverse, z, scale, quotient, _ = stored
        raw_grad = (
            scale
            * (embed_grad - quotient * jnp.sum(embed_grad * quotient, axis=-1, keepdims=True))
        ).astype(BF)
        pg[...] = dot_tn(z, raw_grad)
        normed_grad = dot_nt(raw_grad, projection[...])
        ng[0:1, :] = jnp.sum(normed_grad * unit_rows, axis=0, keepdims=True)
        ng[1:2, :] = jnp.sum(normed_grad, axis=0, keepdims=True)
        grad = unit_back(normed_grad, unit_rows, inverse, norm_vector(norms, tower, 4)) / counts
        dyb[...] = grad.astype(BF)
        scratch[...] = grad
        rows = scratch[pl.ds(pl.multiple_of(shard * SEQS, 8), SEQS), :]
        for c in range(MP):
            own[c] = rows[2 * c : 2 * c + 2]

    grad_image = product(grad_i, grad_t, e_text)
    grad_text = product(grad_t, grad_i, e_image)
    backward(
        TXT, text, grad_text, pt, length_column, pg_t, ng_t, dyb_t, scr_t, own_t
    )
    backward(
        IMG, image, grad_image, pi, jnp.full((1, 1), float(IMG_LEN), F32),
        pg_i, ng_i, dyb_i, scr_i, own_i,
    )
    vector_body(ids, pg_i, pg_t, ng_i, ng_t, window, flat)


def head_call(ids, trio, parts, norms, meta, pi, pt):
    total = 2 * parts.shape[0]
    return kernel_call(
        head_body,
        [
            out((8, 128)),
            out((total, D_IMG), BF),
            out((total, D_TXT), BF),
            out((MP, 2, D_IMG)),
            out((MP, 2, D_TXT)),
            out((VEC_ROWS, 128)),
        ],
        [ids, trio, parts, norms, meta, pi, pt],
        [
            pltpu.VMEM((D_IMG, EMBED), F32),
            pltpu.VMEM((D_TXT, EMBED), F32),
            pltpu.VMEM((2, D_IMG), F32),
            pltpu.VMEM((2, D_TXT), F32),
            pltpu.VMEM((total, D_IMG), F32),
            pltpu.VMEM((total, D_TXT), F32),
            pltpu.VMEM((total, D_IMG + D_TXT), F32),
            pltpu.VMEM((4 * (2 * VEC_ROWS - 1) + 12, 128), F32),
        ],
        us=5.0,
    )


def feed_back_body(
    tower, ids, lengths, h_own, h1, h2, h3, slope, dy, w1, w2, *rest
):
    if tower is TXT:
        grad_i, own, s1, s2, s3, payload, h_all, du = rest
    else:
        own, s1, s2, s3, grads, h_all, du = rest
    m = ids[2]
    rows, pad = tower.rows, tower.padded
    for k, block in enumerate((h_own, h1, h2, h3)):
        h_all[k * rows : (k + 1) * rows, :] = block[...]
    dy_rows = jnp.concatenate([dy[m ^ k] for k in range(MP)], axis=0).astype(BF)
    act = dot_nt(dy_rows, w2[...])
    targets = (own, s1, s2, s3)
    for k in range(MP):
        for j in range(2):
            inside, _ = row_mask(tower, lengths, 2 * (m ^ k) + j)
            start = k * rows + j * pad
            place = 2 * k + j
            piece = slope[start : start + pad, :] * act[place : place + 1, :]
            du[start : start + pad, :] = jnp.where(inside, piece, 0.0).astype(BF)
        part = dot_nt(du[k * rows : (k + 1) * rows, :], w1[...])
        targets[k][...] = part.astype(targets[k].dtype)
    grad = dot_tn(h_all[...], du[...]).astype(BF)
    if tower is IMG:
        grads[...] = grad
        return
    rows_i, rows_t = IMG.d // 8, TXT.d // 8
    for place, e in enumerate(FEED_ORDER):
        payload[place, :rows_i, :] = grad_i[rows_i * e : rows_i * (e + 1), :]
        pack_eighth(payload.at[place], rows_i, grad[rows_t * e : rows_t * (e + 1)])


def feed_back_call(tower, ids, lengths, blocks, slope, dy, w1, w2, grads, after=()):
    rows, d, every = tower.rows, tower.d, tower.all_rows
    return kernel_call(
        functools.partial(feed_back_body, tower),
        [
            out((rows, d)),
            out((rows, d), BF),
            out((rows, d), BF),
            out((rows, d), BF),
            out((d, d), BF) if tower is IMG else out((2 * ZN, FEED_ROWS, IMG.d), BF),
        ],
        [ids, lengths] + blocks + [slope, dy, w1, w2] + grads,
        [pltpu.VMEM((every, d), BF), pltpu.VMEM((every, d), BF)],
        after=after,
        us=5.3,
    )


def middle_back_body(tower, ids, lengths, norms, x1, dy, own, r1, r2, r3, dx1, dx1b):
    m = ids[2]
    grad = (own[...] + r1[...].astype(F32)) + (r2[...].astype(F32) + r3[...].astype(F32))
    unit_rows, inverse = unit(x1[...])
    extra = (
        jnp.sum(grad * unit_rows, axis=0, keepdims=True),
        jnp.sum(grad, axis=0, keepdims=True),
    )
    back = unit_back(grad, unit_rows, inverse, norm_vector(norms, tower, 2))
    rows = dy[m]
    position = lax.broadcasted_iota(jnp.int32, (tower.padded, 1), 0)
    for j in range(2):
        inside, _ = row_mask(tower, lengths, 2 * m + j)
        part = slice(j * tower.padded, (j + 1) * tower.padded)
        total = back[part] + jnp.where(inside, rows[j : j + 1, :], 0.0)
        dx1[part, :] = total
        high, low = [piece.astype(F32) for piece in pieces(extra[j], 2)]
        total = jnp.where(position == tower.length, high, total)
        total = jnp.where(position == tower.length + 1, low, total)
        dx1b[part, :] = total.astype(BF)


def middle_back_call(tower, ids, lengths, norms, x1, dy, own, received, after=()):
    rows, d = tower.rows, tower.d
    return kernel_call(
        functools.partial(middle_back_body, tower),
        [out((rows, d)), out((rows, d), BF)],
        [ids, lengths, norms, x1, dy, own] + received,
        after=after,
    )


def attend_back_body(
    tower, ids, d_own, d1, d2, d3, att, qkv, probs, h1, u1, wq, wo,
    own, s1, s2, s3, *rest
):
    keep, sent, sums, d_all, dqkv, wide, backs, grads = rest
    rows, d, w, sr = tower.rows, tower.d, tower.w, tower.sr
    tail = d // 8
    position = lax.broadcasted_iota(jnp.int32, (tower.padded, 1), 0)
    extra = [[], []]
    for k, block in enumerate((d_own, d1, d2, d3)):
        for j in range(2):
            start = j * tower.padded
            part = block[start : start + tower.padded, :].astype(F32)
            line = tower.length
            extra[j].append(part[line : line + 1] + part[line + 1 : line + 2])
            d_all[k * rows + start : k * rows + start + tower.padded, :] = jnp.where(
                position < line, part, 0.0
            ).astype(BF)
    for j in range(2):
        sums[j : j + 1, :] = (extra[j][0] + extra[j][1]) + (extra[j][2] + extra[j][3])
    targets = (own, s1, s2, s3)
    gain = jnp.zeros((1, d), F32)
    shift = jnp.zeros((1, d), F32)
    for k in range(MP):
        span = slice(k * rows, (k + 1) * rows)
        d_att = dot_nt(d_all[span, :], wo[...]).astype(BF)
        for tile in range(tower.tiles):
            start = k * rows + tile * tower.tile
            part = slice(start, start + tower.tile)
            queries, keys, values = [], [], []
            for h in range(tower.heads):
                query = qkv[part, h * HEAD : (h + 1) * HEAD]
                key = qkv[part, w + h * HEAD : w + (h + 1) * HEAD]
                value = qkv[part, 2 * w + h * HEAD : 2 * w + (h + 1) * HEAD]
                grad = d_att[
                    tile * tower.tile : (tile + 1) * tower.tile, h * HEAD : (h + 1) * HEAD
                ]
                prob = probs[(k * tower.tiles + tile) * tower.heads + h]
                values.append(dot_tn(prob.astype(BF), grad))
                prob_grad = dot_nt(grad, value)
                score = (
                    prob * (prob_grad - jnp.sum(prob * prob_grad, axis=-1, keepdims=True))
                ).astype(BF)
                queries.append(dot(score, key) * HEAD ** (-0.5))
                keys.append(dot_tn(score, query) * HEAD ** (-0.5))
            dqkv[part, :] = jnp.concatenate(queries + keys + values, axis=1).astype(BF)
        back = dot_nt(dqkv[span, :], wq[...])
        gain = gain + jnp.sum(back * u1[span, :].astype(F32), axis=0, keepdims=True)
        shift = shift + jnp.sum(back, axis=0, keepdims=True)
        backs[k, :, :] = back
    for k in range(MP):
        for j, value in enumerate((gain, shift)):
            start = j * tower.padded
            part = backs[k, start : start + tower.padded, :]
            high, low = [piece.astype(F32) for piece in pieces(value, 2)]
            part = jnp.where(position == tower.length, high, part)
            part = jnp.where(position == tower.length + 1, low, part)
            targets[k][start : start + tower.padded, :] = part.astype(targets[k].dtype)
    wide[...] = dot_tn(h1[...], dqkv[...]).astype(BF)
    out_grad = dot_tn(att[...], d_all[...]).astype(BF)
    for place, e in enumerate(WIDE_ORDER):
        if e >= 6:
            piece = out_grad[(e - 6) * tail : (e - 5) * tail]
        else:
            s, i = e // 3, e % 3
            base = s * (d // 2)
            rest = wide[base + sr : base + sr + tail, w * i : w * (i + 1)]
            piece = jnp.concatenate(
                [wide[base + i * tail : base + (i + 1) * tail, :], rest], axis=1
            )
        grads[place] = piece
    for z in range(ZN):
        keep[z] = grads[ids[0] * ZN + z]
        sent[z] = grads[(1 - ids[0]) * ZN + z]


def attend_back_call(tower, ids, blocks, att, qkv, probs, h1, u1, wq, wo, after=()):
    rows, d, w, every = tower.rows, tower.d, tower.w, tower.all_rows
    return kernel_call(
        functools.partial(attend_back_body, tower),
        [
            out((rows, d)),
            out((rows, d), BF),
            out((rows, d), BF),
            out((rows, d), BF),
            out((ZN, d // 8, d), BF),
            out((ZN, d // 8, d), BF),
            out((2, d)),
        ],
        [ids] + blocks + [att, qkv, probs, h1, u1, wq, wo],
        [
            pltpu.VMEM((every, d), BF),
            pltpu.VMEM((every, 3 * w), BF),
            pltpu.VMEM((d, 3 * w), BF),
            pltpu.VMEM((MP, rows, d), F32),
            pltpu.VMEM((2 * ZN, d // 8, d), BF),
        ],
        after=after,
        us=10.4,
    )


def entry_body(tower, norms, xo, dx1, second, own, r1, r2, r3, *rest):
    if tower is IMG:
        dx, sums = rest
    else:
        dx_i, payload, sums = rest
    grad = (own[...] + r1[...].astype(F32)) + (r2[...].astype(F32) + r3[...].astype(F32))
    line = tower.length
    sums[0:1, :] = grad[line : line + 1] + grad[line + 1 : line + 2]
    line += tower.padded
    sums[1:2, :] = grad[line : line + 1] + grad[line + 1 : line + 2]
    sums[2:4, :] = second[...]
    unit_rows, inverse = unit(xo[...])
    back = unit_back(grad, unit_rows, inverse, norm_vector(norms, tower, 0))
    result = (dx1[...] + back).astype(BF)
    if tower is IMG:
        dx[...] = result
        return
    top = IMG.rows
    rest = TXT.rows - top
    payload[:top, :] = dx_i[...]
    payload[top:, : TXT.d] = result[:top]
    payload[top : top + rest, TXT.d :] = result[top:, :256]
    payload[top + rest : top + 2 * rest, TXT.d :] = result[top:, 256:]
    payload[top + 2 * rest :, TXT.d :] = jnp.zeros((top - 2 * rest, IMG.d - TXT.d), BF)


def entry_call(tower, norms, xo, dx1, second, own, received, before=(), after=()):
    rows, d = tower.rows, tower.d
    return kernel_call(
        functools.partial(entry_body, tower),
        [out((rows, d), BF) if tower is IMG else out((2 * IMG.rows, IMG.d), BF), out((4, d))],
        [norms, xo, dx1, second, own] + received + list(before),
        after=after,
    )


def place_body(tower, ids, own, r1, r2, r3, result, flat):
    m = ids[2]
    top = IMG.rows
    rest = TXT.rows - top
    for k, block in enumerate((own, r1, r2, r3)):
        if tower is IMG:
            rows = block[:top, :].astype(F32)
        else:
            low = jnp.concatenate(
                [
                    block[top : top + rest, TXT.d :],
                    block[top + rest : top + 2 * rest, TXT.d :],
                ],
                axis=1,
            )
            rows = jnp.concatenate([block[top:, : TXT.d], low], axis=0).astype(F32)
        for j in range(2):
            seq = 2 * (m ^ k) + j
            part = rows[j * tower.padded : j * tower.padded + tower.length]
            for i in range(tower.q):
                flat.at[i][pl.ds(seq, tower.length, stride=SEQS), :] = part[
                    :, 128 * i : 128 * (i + 1)
                ]
    for i in range(tower.q):
        result[:, :, 128 * i : 128 * (i + 1)] = flat[i].reshape(tower.length, SEQS, 128)


def place_call(tower, ids, blocks):
    return kernel_call(
        functools.partial(place_body, tower),
        [out((tower.length, SEQS, tower.d))],
        [ids] + blocks,
        [pltpu.VMEM((tower.q, tower.length * SEQS, 128), F32)],
        vmem=PLACE_VMEM,
        us=2.7,
    )[0]


def pack_eighth(target, start, part):
    target[start : start + 48, : TXT.d] = part[:48]
    target[start : start + 16, TXT.d :] = part[48:, :256]
    target[start + 16 : start + 32, TXT.d :] = part[48:, 256:]
    target[start + 32 : start + 48, TXT.d :] = jnp.zeros((16, IMG.d - TXT.d), BF)


def pair_body(keep_i, got_i, keep_t, got_t, payload):
    top = IMG.d // 8
    for z in range(ZN):
        payload[z, :top, :] = (keep_i[z].astype(F32) + got_i[z].astype(F32)).astype(BF)
        total = (keep_t[z].astype(F32) + got_t[z].astype(F32)).astype(BF)
        pack_eighth(payload.at[z], top, total)


def mix_body(ids, feed, got, wide, first, second):
    shard = ids[3]
    part = [got[z].astype(F32) for z in range(ZN)]
    wide[...] = ((part[0] + part[1]) + (part[2] + part[3])).astype(BF)
    for target, (senders, _) in zip((first, second), MOVES):
        passes = (shard == senders[0]) | (shard == senders[1])

        def copy(source, target=target):
            target[...] = source[...]

        pl.when(passes)(functools.partial(copy, feed))
        pl.when(jnp.logical_not(passes))(functools.partial(copy, wide))


def mix_call(ids, feed, got):
    return kernel_call(mix_body, [out((FEED_ROWS, IMG.d), BF)] * 3, [ids, feed, got], us=2.5)


def down_body(tower, ids, b0, b1, b2, b3, b4, b5, b6, b7, dyb, result, wide, sums):
    d = tower.d
    tail = d // 8
    first = 0 if tower is IMG else D_IMG
    for k, block in enumerate((b0, b1, b2, b3, b4, b5, b6, b7)):
        side = ids[0] if k < ZN else 1 - ids[0]
        start = (side * ZN + (ids[1] ^ (k % ZN))) * SEQS
        sums[pl.ds(pl.multiple_of(start, SEQS), SEQS), :] = block[:, first : first + d]
    high, low = pieces(sums[...], 2)
    wide[:tail, :] = jnp.zeros((tail, d), F32)
    wide[tail:, :] = dot_tn(high, dyb[...]) + dot_tn(low, dyb[...])
    start = jnp.maximum(ids[3] - 5, 0) * tower.sr
    result[...] = wide[pl.ds(pl.multiple_of(start, 8), tower.sr), :]


def down_call(tower, ids, sums, dyb):
    d = tower.d
    return kernel_call(
        functools.partial(down_body, tower),
        [out((tower.sr, d))],
        [ids] + sums + [dyb],
        [pltpu.VMEM((d + d // 8, d), F32), pltpu.VMEM((2 * ZN * SEQS, d), F32)],
        us=2.6,
    )[0]


def vector_body(ids, pg_i, pg_t, ng_i, ng_t, window, flat):
    flat[:64, :] = jnp.zeros((64, 128), F32)
    for tower, sums in ((IMG, ng_i), (TXT, ng_t)):
        for i in range(2):
            start = tower.norm_row + (4 + i) * tower.q
            for j in range(tower.q):
                flat[start + j : start + j + 1, :] = sums[i : i + 1, 128 * j : 128 * (j + 1)]
    for j in range(4):
        flat[pl.ds(NORM_ROWS + j, D_IMG, stride=4), :] = pg_i[:, 128 * j : 128 * (j + 1)]
        flat[pl.ds(NORM_ROWS + 4 * D_IMG + j, D_TXT, stride=4), :] = pg_t[
            :, 128 * j : 128 * (j + 1)
        ]
    low_lanes = lax.broadcasted_iota(jnp.int32, (VEC_ROWS, 128), 1) < 64
    last = lax.broadcasted_iota(jnp.int32, (VEC_ROWS, 128), 0) == VEC_ROWS - 1
    for s in range(8):

        def copy(s=s):
            start = (s * (2 * VEC_ROWS - 1)) // 2
            part = flat[start : start + VEC_ROWS, :]
            if s % 2 == 1:
                after = pltpu.roll(flat[start + 1 : start + 1 + VEC_ROWS, :], 64, 1)
                part = jnp.where(low_lanes, pltpu.roll(part, 64, 1), after)
            window[...] = jnp.where(last & jnp.logical_not(low_lanes), 0.0, part)

        pl.when(ids[3] == s)(copy)


def collect_body(
    ids, f_own, w_own, ra, rb, down_i, down_t, window,
    sums_i, sums_t, got_i, got_t, lin_i, lin_t, message, rows_i, rows_t, spare,
):
    shard = ids[3]
    q = IMG.d // 8

    @pl.when(shard >= 5)
    def _():
        rows_i[...] = down_i[...]
        rows_t[...] = down_t[...]

    tq = TXT.d // 8

    def feed(start, *blocks):
        for i, block in enumerate(blocks):
            rows_i[q * (start + i) : q * (start + i + 1), :] = block[:q, :].astype(F32)
            low = jnp.concatenate([block[q : q + 16, TXT.d :], block[q + 16 : q + 32, TXT.d :]], axis=1)
            part = jnp.concatenate([block[q:, : TXT.d], low], axis=0)
            rows_t[tq * (start + i) : tq * (start + i + 1), :] = part.astype(F32)

    pl.when(shard < 2)(lambda: feed(0, w_own, ra, rb))
    pl.when(shard == 2)(lambda: feed(0, w_own, ra, f_own))
    pl.when((shard == 3) | (shard == 4))(lambda: feed(0, f_own, ra, rb))
    pl.when(shard == 5)(lambda: feed(0, f_own))

    rows_to_lin(IMG, rows_i, lin_i, spare, shard)
    rows_to_lin(TXT, rows_t, lin_t, spare, shard)
    def total_of(value):
        return jnp.sum(value * value, axis=0, keepdims=True)

    every = total_of(window[...]) * (1.0 / MP)
    for j in range(IMG.q):
        every = every + total_of(rows_i[:, 128 * j : 128 * (j + 1)])
    for j in range(TXT.q):
        every = every + total_of(rows_t[:, 128 * j : 128 * (j + 1)])
    m = ids[2]

    def own_line(sums):
        line = sums[3:4, :]
        for member in range(3):
            line = jnp.where(m == member, sums[member : member + 1, :], line)
        return line

    line = jnp.concatenate(
        [own_line(sums_i[...] + got_i[...]), own_line(sums_t[...] + got_t[...])], axis=1
    )
    lines = [line[:, 128 * j : 128 * (j + 1)] for j in range(2 * PART_ROWS)]
    mine = [jnp.where(ids[0] == 0, a, b) for a, b in zip(lines[:PART_ROWS], lines[PART_ROWS:])]
    block = jnp.concatenate([every] + mine, axis=0)
    for peer in range(2 * ZN * MP):
        message[peer, : MESSAGE_ROWS, :] = block
        message[peer, MESSAGE_ROWS:, :] = jnp.zeros((8 - MESSAGE_ROWS, 128), F32)


PART_ROWS = (IMG.q + TXT.q) // 2
MESSAGE_ROWS = 1 + PART_ROWS


def collect_call(ids, moved, down_i, down_t, window, sums_i, sums_t, after):
    return kernel_call(
        collect_body,
        [out((IMG.lin, 128)), out((TXT.lin, 128)), out((2 * ZN * MP, 8, 128))],
        [ids] + moved + [down_i, down_t, window, sums_i, sums_t, hop(sums_i, "tower", 1), hop(sums_t, "tower", 1)],
        [
            pltpu.VMEM((IMG.sr, IMG.d), F32),
            pltpu.VMEM((TXT.sr, TXT.d), F32),
            pltpu.VMEM(SPARE, F32),
        ],
        us=3.8,
        after=after,
    )


def advance_body(
    ids, trio, parts, misc, ip, im, iv, ig, tp, tm, tv, tg, vp, vm, vv, vg,
    loss_out, size_out, trio_out, ipn, icn, imn, ivn, tpn, tcn, tmn, tvn, vpn, vcn, vmn, vvn, grad_v,
):
    slope = misc[1:2, :]
    grad_v[...] = vg[...]
    norm_squares = jnp.zeros((1, 128), F32)
    for member in range(MP):
        halves = []
        for side in range(2):
            lines = parts[side * ZN * MP + member]
            for z in range(1, ZN):
                lines = lines + parts[(side * ZN + z) * MP + member]
            halves.append(lines)
            if member == 0 and side == 0:
                squares = lines[:1]
            else:
                squares = squares + lines[:1]
        lines = jnp.concatenate([half[1:MESSAGE_ROWS] for half in halves], axis=0)
        norm_squares = norm_squares + jnp.sum(lines * lines, axis=0, keepdims=True)

        @pl.when((ids[3] == 0) & (pl.program_id(0) == 0))
        def _(member=member, lines=lines):
            start = member * IMG.q
            grad_v[start : start + IMG.q, :] = lines[: IMG.q]
            start = TXT.norm_row + member * TXT.q
            grad_v[start : start + TXT.q, :] = lines[IMG.q :]

    total = jnp.sum(squares + norm_squares, axis=1, keepdims=True)
    size = jnp.sqrt(total + slope * slope)
    clip = CLIP_LEVEL / jnp.maximum(size, CLIP_LEVEL)

    def step(master, first, second, grad, rate, decay):
        clipped = grad * clip
        first_new = BETA_ONE * first + (1.0 - BETA_ONE) * clipped
        second_new = BETA_TWO * second + (1.0 - BETA_TWO) * clipped * clipped
        update = (first_new * (1.0 / (1.0 - BETA_ONE**STEP))) / (
            jnp.sqrt(second_new * (1.0 / (1.0 - BETA_TWO**STEP))) + ADAM_EPS
        )
        return master - rate * (update + decay * master), first_new, second_new

    for master, first, second, grad, a, b, c, e in (
        (ip, im, iv, ig, ipn, icn, imn, ivn),
        (tp, tm, tv, tg, tpn, tcn, tmn, tvn),
    ):
        new, first_new, second_new = step(
            master[...], first[...], second[...], grad[...], RATE_MATRIX, WEIGHT_DECAY
        )
        a[...] = new
        b[:, 0, :] = new.astype(BF)
        c[...] = first_new
        e[...] = second_new
    rows = VEC_ROWS // ADVANCE_STEPS
    row = lax.broadcasted_iota(jnp.int32, (rows, 128), 0) + pl.program_id(0) * rows
    is_norm = row < jnp.where(ids[3] == 0, NORM_ROWS, 0)
    new, first_new, second_new = step(
        vp[...],
        vm[...],
        vv[...],
        grad_v[...],
        jnp.where(is_norm, RATE_VECTOR, RATE_MATRIX),
        jnp.where(is_norm, 0.0, WEIGHT_DECAY),
    )
    vpn[...] = new
    vcn[...] = new.astype(BF)
    vmn[...] = first_new
    vvn[...] = second_new
    lane_row = jnp.zeros((1, 128), F32)
    new, _, _ = step(
        lane_row + trio[0], lane_row + trio[1], lane_row + trio[2], slope, LOGIT_SPEED, 0.0
    )
    loss_out[...] = misc[0:1, :1]
    size_out[...] = size[:, :1]
    trio_out[...] = new[:, :1]


PLACE_VMEM = 64
ADVANCE_STEPS = 3


def advance_call(ids, trio, parts, misc, image, text, vector):
    ins = [ids, trio, parts, misc] + image + text + vector

    def spec(shape, cut):
        block = (shape[0] // ADVANCE_STEPS if cut else shape[0],) + tuple(shape[1:])
        rest = (0,) * (len(shape) - 1)
        return pl.BlockSpec(block, lambda i: ((i if cut else 0),) + rest)

    outs = [out((1, 1))] * 3
    for rows in (IMG.lin, TXT.lin, VEC_ROWS):
        copied = (rows, 128) if rows == VEC_ROWS else (rows, 1, 128)
        outs += [out((rows, 128)), out(copied, BF), out((rows, 128)), out((rows, 128))]
    scalars = pl.BlockSpec(memory_space=pltpu.SMEM)
    return pl.pallas_call(
        advance_body,
        grid=(ADVANCE_STEPS,),
        out_shape=outs,
        in_specs=[scalars, scalars] + [spec(v.shape, i > 1) for i, v in enumerate(ins[2:])],
        out_specs=[spec(v.shape, i > 2) for i, v in enumerate(outs)],
        scratch_shapes=[pltpu.VMEM((VEC_ROWS // ADVANCE_STEPS, 128), F32)],
        compiler_params=pltpu.CompilerParams(vmem_limit_bytes=64 * MIB),
        cost_estimate=pl.CostEstimate(
            flops=int(COST_SCALE * 7), bytes_accessed=0, transcendentals=0
        ),
    )(*ins)


def hop(value, axis, mask):
    size = lax.axis_size(axis)
    return lax.ppermute(value, axis, [(i, i ^ mask) for i in range(size)])


def peers(values):
    return [hop(value, "mp", k) for k, value in zip((1, 2, 3), values)]


def spread(value):
    near, far = hop(value, "dp", 1), hop(value, "dp", 2)
    here = [value, near, far, hop(far, "dp", 1)]
    return here + [hop(block, "tower", 1) for block in here]


def merge(value, axis, mask):
    other = hop(value, axis, mask)
    upper = (lax.axis_index(axis) & mask) != 0
    return jnp.where(
        upper, jnp.concatenate([other, value], axis=0), jnp.concatenate([value, other], axis=0)
    )


FEED_ORDER = (5, 6, 0, 1, 4, 7, 3, 2)
WIDE_ORDER = (0, 3, 6, 5, 1, 4, 7, 2)
MOVES = (
    ((7, 0), ((7, 3), (0, 4), (4, 0), (5, 1), (6, 2))),
    ((6, 1), ((6, 3), (1, 4), (7, 0), (3, 1))),
)


def fast_local(
    picture_residual_entry,
    sentence_residual_entry,
    sentence_lengths_held,
    couple_allowed_flags,
    picture_single_matrices,
    picture_mean_state,
    picture_square_state,
    sentence_single_matrices,
    sentence_mean_state,
    sentence_square_state,
    array_single_params,
    array_mean_state,
    array_square_state,
    logit_log_trio,
):
    LAST.clear()
    side, z, m = lax.axis_index("tower"), lax.axis_index("dp"), lax.axis_index("mp")
    ids = jnp.stack([side, z, m, side * ZN + z]).astype(jnp.int32)
    lengths = sentence_lengths_held
    vec_size = array_single_params.shape[0]

    def lines(value):
        return value.reshape(-1, 128)

    def vector_lines(value):
        return jnp.pad(value, (0, VEC_ROWS * 128 - vec_size)).reshape(VEC_ROWS, 128)

    vec_lines = vector_lines(array_single_params)
    keep_t, keep_i, send_t, send_i, block = kernel_call(
        prepare_body,
        [out((TXT.half, TXT.d), BF), out((IMG.half, IMG.d), BF)] * 2 + [out((16, TXT.d), BF)],
        [
            ids,
            couple_allowed_flags,
            lengths,
            lines(picture_single_matrices),
            lines(sentence_single_matrices),
            vec_lines,
        ],
        [
            pltpu.VMEM((IMG.sr, IMG.d), F32),
            pltpu.VMEM((TXT.sr, TXT.d), F32),
            pltpu.VMEM(SPARE, F32),
        ],
        us=2.5,
    )
    urgent, late = kernel_call(
        sort_body,
        [out((URGENT, IMG.d), BF), out((HALF, IMG.d), BF)],
        [ids, keep_t, keep_i, hop(send_t, "tower", 1), hop(send_i, "tower", 1), block],
    )
    urgent = spread(urgent)
    late = lax.all_gather(gate(late, *urgent[1:ZN]), "dp", axis=0, tiled=True)
    vecpay = kernel_call(
        vector_pay_body,
        [out((VEC_ROWS, 128), BF)],
        [ids, vec_lines],
        [pltpu.VMEM((VEC_ROWS + 8, 128), F32)],
    )[0]
    x_txt = jnp.transpose(sentence_residual_entry, (1, 0, 2))
    x_img = jnp.transpose(picture_residual_entry, (1, 0, 2))
    norms, meta, *t_out = attend_call(TXT, ids, x_txt, urgent)
    i_out = attend_call(IMG, ids, x_img, urgent, norms=norms)
    layers = {}
    before = ()
    middles = {}
    for tower, outs in ((TXT, t_out), (IMG, i_out)):
        xo, own, s1, s2, s3 = outs[8:]
        x1, h2, pooled = middle_call(
            tower, ids, lengths, norms, xo, own, peers([s1, s2, s3])
        )
        middles[tower] = (x1, pooled, [h2] + peers([h2, h2, h2]))
    late = gate(late, x1, *middles[TXT][2][1:])
    late = [late, hop(late, "tower", 1)]
    gathered = lax.all_gather(gate(vecpay, late[0]), GROUP, axis=0, tiled=False)
    for tower, outs in ((TXT, t_out), (IMG, i_out)):
        wq, wo, up, h1, u1, qkv, att, probs, xo = outs[:9]
        x1, pooled, blocks = middles[tower]
        w1, w2, slope, sums, *y = feed_call(
            tower, ids, lengths, blocks, up, late, pooled, before
        )
        before = (*y, sums)
        layers[tower] = dict(
            wq=wq, wo=wo, h1=h1, u1=u1, qkv=qkv, att=att, probs=probs, xo=xo,
            x1=x1, blocks=blocks, w1=w1, w2=w2, slope=slope,
        )

    received = peers(y[1:])
    y = (y[0] + received[0]) + (received[1] + received[2])
    parts = lax.all_to_all(
        jnp.broadcast_to(y, (2 * ZN * MP, *y.shape)), (*GROUP, "mp"), 0, 0, tiled=True
    )
    sums = gate(sums, y)
    sums = [sums] + [hop(sums, "dp", k) for k in range(1, ZN)]
    pi, pt = project_call(gathered, ())
    sums = sums[:1] + [gate(block, pi) for block in sums[1:]]
    sums = sums + [hop(block, "tower", 1) for block in sums]
    misc, dyb_i, dyb_t, dy_i, dy_t, window = head_call(
        ids, logit_log_trio, parts, norms, meta, pi, pt
    )

    dy = {IMG: dy_i, TXT: dy_t}
    back, dx1, dx1b, second = {}, {}, {}, {}
    entries, norm_sums = {}, {}
    grads = []
    for tower in (IMG, TXT):
        s = layers[tower]
        back[tower] = feed_back_call(
            tower, ids, lengths, s["blocks"], s["slope"], dy[tower], s["w1"], s["w2"], grads,
            sums if tower is TXT else (),
        )
        grads = [back[tower][4]]
    feed_own = lax.psum_scatter(back[TXT][4], GROUP, scatter_dimension=0, tiled=False)
    for tower in (IMG, TXT):
        own, s1, s2, s3 = back[tower][:4]
        dx1[tower], dx1b[tower] = middle_back_call(
            tower, ids, lengths, norms, layers[tower]["x1"], dy[tower], own, peers([s1, s2, s3])
        )
    halves = []
    for tower in (IMG, TXT):
        s = layers[tower]
        block = dx1b[tower]
        *back[tower], keep, sent, second[tower] = attend_back_call(
            tower, ids, [block] + peers([block] * 3),
            s["att"], s["qkv"], s["probs"], s["h1"], s["u1"], s["wq"], s["wo"],
        )
        halves += [keep, hop(sent, "tower", 1)]
    payload = kernel_call(pair_body, [out((ZN, FEED_ROWS, IMG.d), BF)], halves, us=2.8)[0]
    got = lax.all_to_all(payload, "dp", 0, 0, tiled=True)
    before = ()
    for tower in (IMG, TXT):
        own, s1, s2, s3 = back[tower]
        dx, norm_sums[tower] = entry_call(
            tower, norms, layers[tower]["xo"], dx1[tower], second[tower], own,
            peers([s1, s2, s3]), before,
        )
        before = (dx,)
        if tower is IMG:
            down = {IMG: down_call(IMG, ids, sums, dyb_i)}
    placed = [dx] + peers([dx, dx, dx])
    down[TXT] = down_call(TXT, ids, sums, dyb_t)
    wide, *passed = mix_call(ids, feed_own, got)
    moved = [lax.ppermute(v, GROUP, list(pairs)) for v, (_, pairs) in zip(passed, MOVES)]
    lin_i, lin_t, message = collect_call(
        ids, [feed_own, wide, *moved], down[IMG], down[TXT], window,
        norm_sums[IMG], norm_sums[TXT], placed[1:],
    )
    parts = lax.all_to_all(message, (*GROUP, "mp"), 0, 0, tiled=True)
    for tower in (IMG, TXT):
        entries[tower] = place_call(tower, ids, placed)
    loss, size, temperature, *new = advance_call(
        ids,
        logit_log_trio,
        parts,
        misc,
        [lines(picture_single_matrices), lines(picture_mean_state), lines(picture_square_state), lin_i],
        [
            lines(sentence_single_matrices),
            lines(sentence_mean_state),
            lines(sentence_square_state),
            lin_t,
        ],
        [vec_lines, vector_lines(array_mean_state), vector_lines(array_square_state), window],
    )

    def flat(value, like):
        return value.reshape(-1)[: like.size].reshape(like.shape)

    likes = [picture_single_matrices] * 4 + [sentence_single_matrices] * 4 + [array_single_params] * 4
    news = [flat(value, like) for value, like in zip(new, likes)]
    return (
        loss.reshape(()),
        size.reshape(()),
        jnp.transpose(entries[IMG], (1, 0, 2)),
        jnp.transpose(entries[TXT], (1, 0, 2)),
        *news,
        temperature.reshape(()),
    )


def fits(mesh):
    return mesh.shape["tower"] == 2 and mesh.shape["dp"] == ZN and mesh.shape["mp"] == MP


def solution(mesh):
    placed = (
        P(GROUP, None, None),
        P(GROUP, None, None),
        P(GROUP),
        P(GROUP),
        P("mp", GROUP),
        P("mp", GROUP),
        P("mp", GROUP),
        P("mp", GROUP),
        P("mp", GROUP),
        P("mp", GROUP),
        P(GROUP),
        P(GROUP),
        P(GROUP),
        P(),
    )
    return jax.shard_map(
        fast_local if fits(mesh) else local,
        mesh=mesh,
        in_specs=placed,
        out_specs=(
            P(),
            P(),
            P(GROUP, None, None),
            P(GROUP, None, None),
            P("mp", GROUP),
            P("mp", GROUP),
            P("mp", GROUP),
            P("mp", GROUP),
            P("mp", GROUP),
            P("mp", GROUP),
            P("mp", GROUP),
            P("mp", GROUP),
            P(GROUP),
            P(GROUP),
            P(GROUP),
            P(GROUP),
            P(),
        ),
        check_vma=False,
    )
```
